32 devices in a mesh: dp: 8 (over y, x, core), ctx: 4 (over z).
Axes of the slice: x: 2, y: 2, z: 4, core: 2. Of those that a mesh axis runs over, the one named last changes fastest.
Arguments:
- inputs: bfloat16 [16, 1024, 1088], P('dp', 'ctx'), may hold values from -6 to 6
- cotangent: bfloat16 [16, 1024, 1088], P('dp', 'ctx'), may hold values from -6 to 6
- w_qkv: bfloat16 [1088, 3264], P('dp', 'ctx'), may hold values from -0.1875 to 0.1875
- w_out: bfloat16 [1088, 1088], P('dp', 'ctx'), may hold values from -0.5 to 0.5
- w_up: bfloat16 [1088, 4352], P('dp', 'ctx'), may hold values from -0.1875 to 0.1875
- w_down: bfloat16 [4352, 1088], P('dp', 'ctx'), may hold values from -0.09375 to 0.09375
- vectors: bfloat16 [8, 1088], P(None, 'ctx'), may hold values from 0.099609375 to 1.8984375
- bias_up: bfloat16 [4352], P('ctx'), may hold values from -3 to 3
- segment_ids: int32 [16, 1024], P('dp'), may hold values from 0 to 7, never falling along the last dimension, each value on 1 to 512 neighbouring positions
- padding: int32 [16, 1024], P('dp'), may hold values 0 or 1
- stretch_order: int32 [8], replicated, may hold values from 0 to 7, each once
Outputs:
- output: bfloat16 [16, 1024, 1088], P('dp', 'ctx')
- input_grad: float32 [16, 1024, 1088], P('dp', 'ctx')
- grad_qkv: float32 [1088, 3264], P('dp', 'ctx')
- grad_out: float32 [1088, 1088], P('dp', 'ctx')
- grad_up: float32 [1088, 4352], P('dp', 'ctx')
- grad_down: float32 [4352, 1088], P('dp', 'ctx')
- grad_vectors: float32 [8, 1088], P(None, 'ctx')
- grad_bias_up: float32 [4352], P('ctx')
- clipped_qkv: bfloat16 [1088, 3264], P('dp', 'ctx')
- clipped_query_bias: bfloat16 [1088], P('ctx')
- head_max: float32 [17], replicated
The draws below stay inside these ranges and needn't reach their ends.
Inputs may be any that keep to these rules, and one draw needn't show every extreme that they name: A permutation; the device at index c of ctx holds, in this order, the position blocks stretch_order[2 c] and stretch_order[2 c + 1], each 128 positions long, of each of its sequences. `segment_ids`: never falls along positions; a document spans 1 to 512 positions.
All inputs are finite; a program needn't handle non-finite values. No bound on the sum of `padding` on one device may be relied on, other than what follows from the above.
Results may differ from the reference program's by a relative error of at most 0.038.
Values may be sent and summed in bfloat16 or wider, within the bound.
A program may use at most 320 MiB of HBM per device.

```python
import math
import jax
import jax.numpy as jnp
import numpy as np
from jax import lax

D = 1088
HEADS = 17
HD = 64
FF = 4352
LEN = 1024
SEQS = 16
STRETCHES = 8


def set_ends(entries, rng, low, high):
    longest = entries.shape.index(max(entries.shape))
    spots = []
    for shift in (0, 1):
        where = [jax.random.randint(jax.random.fold_in(rng, axis), (), 0, length) for axis, length in enumerate(entries.shape)]
        where[longest] = (where[longest] + shift) % entries.shape[longest]
        spots.append(tuple(where))
    return entries.at[spots[0]].set(low).at[spots[1]].set(high)


def shard_levels(rng, dims, split, least, top_value):
    def one(dim, blocks):
        steps = jax.random.uniform(jax.random.fold_in(jax.random.fold_in(rng, 6), dim), (blocks,), jnp.float32, least / len(split), top_value / len(split))
        return jnp.repeat(jnp.exp(steps), dims[dim] // blocks).reshape((-1,) + (1,) * (len(dims) - dim - 1))

    loudness = one(*split[0])
    for cut in split[1:]:
        loudness = loudness * one(*cut)
    return loudness


def length_profile(count, total, bound, slope):
    loads = [(1 << 20) // math.isqrt(rank ** slope) + 1 for rank in range(2, count + 1)]
    rest, holding = total - bound - (count - 1), [1] * (count - 1)
    while rest > 0:
        free = [i for i in range(count - 1) if holding[i] < bound]
        whole, remaining = sum([loads[i] for i in free]), rest
        for i in free:
            extra = min(bound - holding[i], max(1, remaining * loads[i] // whole), rest)
            holding[i] = holding[i] + extra
            rest = rest - extra
    return np.array([bound] + holding)


def ragged(stream_key, number_of, total, bound, slope):
    if number_of == 2:
        one = jax.random.randint(stream_key, (), max(1, total - bound), min(bound, total - 1) + 1)
        return jnp.stack([one, total - one])
    tallies = jnp.asarray(length_profile(number_of, total, bound, slope), jnp.int32)
    pairs = (number_of - 1) // 2
    source_of, taker = tallies[1:1 + 2 * pairs:2], tallies[2:2 + 2 * pairs:2]
    room = jnp.minimum(source_of - 1, bound - taker)
    moved = jax.random.randint(jax.random.fold_in(stream_key, 1), (pairs,), 0, 1 << 20) % (room + 1)
    tallies = tallies.at[1:1 + 2 * pairs:2].set(source_of - moved).at[2:2 + 2 * pairs:2].set(taker + moved)
    return tallies[jax.random.permutation(jax.random.fold_in(stream_key, 2), number_of)]


def scatter_about(key, shape, width, most, split=(), kind=jnp.bfloat16):
    gain = shard_levels(key, shape, split, -0.22, 0.18) if split else 1.0
    values = jax.random.normal(key, shape, jnp.float32) * width * gain
    return jnp.minimum(jnp.maximum(values, -most), most).astype(kind)


def setup_inputs(seed: int = 0) -> dict:
    key_list = jax.random.split(jax.random.key(seed), 12)
    return {
        "inputs": scatter_about(key_list[0], (SEQS, LEN, D), 1.0, 6.0, ((0, 8), (1, 4))),
        "cotangent": scatter_about(key_list[1], (SEQS, LEN, D), 1.0, 6.0, ((0, 8), (1, 4))),
        "w_qkv": scatter_about(key_list[2], (D, 3 * D), D ** -0.5, 0.1875, ((0, 8), (1, 4))),
        "w_out": scatter_about(key_list[3], (D, D), (D // 8) ** -0.5, 0.5, ((0, 8), (1, 4))),
        "w_up": scatter_about(key_list[4], (D, FF), D ** -0.5, 0.1875, ((0, 8), (1, 4))),
        "w_down": scatter_about(key_list[5], (FF, D), FF ** -0.5, 0.09375, ((0, 8), (1, 4))),
        "vectors": jnp.clip(1.0 + 0.18 * jax.random.normal(key_list[6], (8, D), jnp.float32), 0.099609375, 1.8984375).astype(jnp.bfloat16),
        "bias_up": scatter_about(key_list[7], (FF,), 0.5, 3.0, ((0, 4),)),
        "segment_ids": jax.vmap(lambda own: jnp.searchsorted(jnp.cumsum(ragged(own, 8, LEN, LEN // 2, 0)), jnp.arange(LEN), side="right"))(jax.random.split(key_list[8], SEQS)).reshape((SEQS, LEN)).astype(jnp.int32),
        "padding": set_ends((jax.random.randint(key_list[9], (SEQS, LEN), 0, 8) < 7).astype(jnp.int32), jax.random.fold_in(key_list[9], 1), 0, 1),
        "stretch_order": jax.random.permutation(key_list[10], STRETCHES).astype(jnp.int32),
    }


@jax.custom_vjp
def low(v):
    return lax.optimization_barrier(v.astype(jnp.bfloat16)).astype(jnp.float32)

@jax.custom_vjp
def low_back(v):
    return v

def low_keep(v):
    return (low(v), None)

def low_pass(kept, grad):
    return (grad,)

def back_keep(v):
    return (v, None)

def back_low(kept, grad):
    return (low(grad),)
low.defvjp(low_keep, low_pass)
low_back.defvjp(back_keep, back_low)
eps_norm = 1e-05
clip_limit = 5.0
masked_fill = -1e+30

def matmul(left, right):
    return jnp.dot(left, right, precision=lax.Precision.HIGHEST, preferred_element_type=jnp.float32)

def layer_norm(values_in, gain_row, shift_row):
    average = lax.optimization_barrier(jnp.mean(values_in, axis=-1, keepdims=True))
    centred = values_in - average
    variance = lax.optimization_barrier(jnp.mean(centred * centred, axis=-1, keepdims=True))
    return centred * lax.rsqrt(variance + eps_norm) * gain_row + shift_row

def attend_one(pieces):
    queries, key_rows, value_rows, allowed = pieces
    score_scale = HD ** (-0.5)
    query_heads = queries.reshape(queries.shape[0], HEADS, HD)
    key_heads = key_rows.reshape(key_rows.shape[0], HEADS, HD)
    value_heads = value_rows.reshape(value_rows.shape[0], HEADS, HD)
    scores = low_back(jnp.einsum('qhd,khd->hqk', query_heads, key_heads, precision=lax.Precision.HIGHEST) * score_scale)
    masked = jnp.where(allowed[None], scores, masked_fill)
    row_top = lax.optimization_barrier(jnp.max(masked, axis=-1, keepdims=True))
    log_total = row_top + jnp.log(lax.optimization_barrier(jnp.sum(jnp.exp(masked - row_top), axis=-1, keepdims=True)))
    attn_probs = low(jnp.exp(masked - log_total))
    attended = jnp.einsum('hqk,khd->qhd', attn_probs, value_heads, precision=lax.Precision.HIGHEST)
    return (attended.reshape(queries.shape[0], -1), lax.optimization_barrier(jnp.max(masked, axis=(1, 2))))

def forward_group(w_qkv, w_out, w_up, w_down, vectors, bias_up, inputs, allowed):
    group_seqs = inputs.shape[0]
    flat_rows = inputs.reshape(-1, D)
    normed = low(layer_norm(flat_rows, vectors[0], vectors[1]))
    projected = matmul(normed, w_qkv) + jnp.concatenate([vectors[2], jnp.zeros_like(vectors[2]), vectors[3]])
    queries = low(low_back(projected[:, :D]))
    key_rows = low(low_back(projected[:, D:2 * D]))
    value_rows = low(low_back(projected[:, 2 * D:]))
    shaped = (queries.reshape(group_seqs, LEN, D), key_rows.reshape(group_seqs, LEN, D), value_rows.reshape(group_seqs, LEN, D), allowed)
    attended_raw, head_tops = lax.map(jax.checkpoint(attend_one), shaped)
    attended = low(low_back(attended_raw.reshape(-1, D)))
    branch = low_back(matmul(attended, w_out) + vectors[4])
    residual = flat_rows + branch
    normed_two = low(layer_norm(residual, vectors[5], vectors[6]))
    up_pre = low_back(matmul(normed_two, w_up) + bias_up)
    hidden = low(jax.nn.gelu(up_pre, approximate=True))
    output = residual + low_back(matmul(hidden, w_down) + vectors[7])
    return (output.reshape(inputs.shape), lax.optimization_barrier(jnp.max(head_tops, axis=0)))

def reference(inputs, cotangent, w_qkv, w_out, w_up, w_down, vectors, bias_up, segment_ids, padding, stretch_order):
    stretch_len = LEN // stretch_order.shape[0]
    stored = jnp.arange(LEN, dtype=jnp.int32)
    positions = (stretch_order[stored // stretch_len] * stretch_len + stored % stretch_len).astype(jnp.int32)
    seg_stored = jnp.take(segment_ids, positions, axis=1)
    pad_stored = jnp.take(padding, positions, axis=1)
    causal = positions[None, :] <= positions[:, None]
    diagonal = stored[:, None] == stored[None, :]
    params = tuple((array.astype(jnp.float32) for array in (w_qkv, w_out, w_up, w_down, vectors, bias_up)))
    inputs_wide = inputs.astype(jnp.float32)
    cot_wide = cotangent.astype(jnp.float32)
    group_size = math.gcd(SEQS, max(1, 4096 // LEN))
    group_count = SEQS // group_size

    def group_step(carried, group_index):
        totals, running = carried
        first_row = (group_index * group_size).astype(jnp.int32)
        group_in = lax.dynamic_slice_in_dim(inputs_wide, first_row, group_size, 0)
        group_cot = lax.dynamic_slice_in_dim(cot_wide, first_row, group_size, 0)
        group_seg = lax.dynamic_slice_in_dim(seg_stored, first_row, group_size, 0)
        group_pad = lax.dynamic_slice_in_dim(pad_stored, first_row, group_size, 0)
        allowed = (group_seg[:, :, None] == group_seg[:, None, :]) & causal[None] & ((group_pad[:, None, :] == 1) | diagonal[None])

        def forward_fixed(*leaves):
            return forward_group(*leaves, allowed)
        output, pullback, group_top = jax.vjp(forward_fixed, *params, group_in, has_aux=True)
        gradients = pullback(group_cot)
        totals = tuple((summed + fresh for summed, fresh in zip(totals, gradients[:6])))
        return ((totals, jnp.maximum(running, group_top)), (output, gradients[6]))
    start_state = (tuple((jnp.zeros_like(array) for array in params)), jnp.full((HEADS,), masked_fill, jnp.float32))
    final_state, stacked = lax.scan(group_step, start_state, jnp.arange(group_count, dtype=jnp.int32))
    totals, running = final_state
    output = stacked[0].reshape(SEQS, LEN, D).astype(jnp.bfloat16)
    input_grad = stacked[1].reshape(SEQS, LEN, D)
    factor = clip_limit / jnp.maximum(running, clip_limit)
    per_column = jnp.repeat(jnp.sqrt(factor), HD)
    column_scale = jnp.concatenate([per_column, per_column, jnp.ones((D,), jnp.float32)])
    clipped_qkv = (params[0] * column_scale[None, :]).astype(jnp.bfloat16)
    clipped_bias = (params[4][2] * per_column).astype(jnp.bfloat16)
    return (output, input_grad, totals[0], totals[1], totals[2], totals[3], totals[4], totals[5], clipped_qkv, clipped_bias, running)
```

```python
from functools import partial

import jax
import jax.numpy as jnp
from jax import lax
from jax.experimental import pallas as pl
from jax.experimental.pallas import tpu as pltpu
from jax.sharding import PartitionSpec as P

HD = 64
LANES = 128
AXES = ("dp", "ctx")

eps_norm = 1e-05
clip_limit = 5.0
masked_fill = -1e30
f32 = jnp.float32
bf16 = jnp.bfloat16


def layer_norm(values_in, gain_row, shift_row):
    average = jnp.mean(values_in, axis=-1, keepdims=True)
    centred = values_in - average
    variance = jnp.mean(centred * centred, axis=-1, keepdims=True)
    return centred * lax.rsqrt(variance + eps_norm) * gain_row + shift_row


def to_low(values_in):
    return values_in.astype(bf16)


def product(left, right):
    return jnp.dot(left, right, preferred_element_type=f32)


def contract_rows(left, right):
    return lax.dot_general(left, right, (((0,), (0,)), ((), ())), preferred_element_type=f32)


def contract_cols(left, right):
    return lax.dot_general(left, right, (((1,), (1,)), ((), ())), preferred_element_type=f32)


def column_sum(values_in):
    return jnp.sum(values_in.astype(f32), axis=0)


class Moves:
    def __init__(self, dp, ctx, local_seqs):
        self.dp, self.ctx, self.seqs = dp, ctx, local_seqs
        self.d = lax.axis_index("dp")
        self.z = lax.axis_index("ctx")
        self.core = self.d % 2
        self.cube = dp == 8 and ctx == 4
        self.x = (self.d // 2) % 2
        self.y = self.d // 4

    def permute(self, values, target):
        pairs = []
        for d in range(self.dp):
            for z in range(self.ctx):
                there = target(d, z)
                if there is not None:
                    pairs.append((d * self.ctx + z, there[0] * self.ctx + there[1]))
        return lax.ppermute(values, AXES, pairs)

    def swap_core(self, values):
        return self.permute(values, lambda d, z: (d ^ 1, z))

    def swap_x(self, values):
        return self.permute(values, lambda d, z: (d ^ 2, z))

    def swap_y(self, values):
        return self.permute(values, lambda d, z: (d ^ 4, z))

    def up(self, values):
        return self.permute(values, lambda d, z: (d, z + 1) if z + 1 < self.ctx else None)

    def down(self, values):
        return self.permute(values, lambda d, z: (d, z - 1) if z > 0 else None)

    def sequence_target(self, step):
        n = self.seqs

        def target(d, z):
            return (d - d % 2 + z // n, n * (d % 2) + (z + step) % n)

        return target

    def to_sequences(self, values):
        n = self.seqs
        came = []
        for step in range(n):
            block = lax.dynamic_index_in_dim(values, (self.z + step) % n, 0, keepdims=False)
            came.append(self.permute(block, self.sequence_target(step)))
        return jnp.concatenate([self.choose(came, (self.z - t) % n) for t in range(n)], axis=0)

    def from_sequences(self, values):
        n = self.seqs
        parts = values.reshape(n, values.shape[0] // n, values.shape[1])
        came = []
        for step in range(n):
            forward = self.sequence_target(step)
            block = lax.dynamic_index_in_dim(parts, (self.z - step) % n, 0, keepdims=False)
            back = {}
            for d in range(self.dp):
                for z in range(self.ctx):
                    back[forward(d, z)] = (d, z)
            came.append(self.permute(block, lambda d, z: back[(d, z)]))
        return jnp.stack([self.choose(came, (j - self.z) % n) for j in range(n)], axis=0)

    @staticmethod
    def choose(items, index):
        picked = items[0]
        for i in range(1, len(items)):
            picked = jnp.where(index == i, items[i], picked)
        return picked

    def gather_ctx(self, block):
        if not self.cube:
            return lax.all_gather(block, "ctx", axis=0, tiled=False)
        rising, falling = [block], [block]
        for _ in range(self.ctx - 1):
            rising.append(self.up(rising[-1]))
            falling.append(self.down(falling[-1]))
        line = jnp.stack(rising[:0:-1] + falling, axis=0)
        return lax.dynamic_slice_in_dim(line, self.ctx - 1 - self.z, self.ctx, 0)

    def gather_dp(self, block):
        if not self.cube:
            return lax.all_gather(block, "dp", axis=0, tiled=True)
        rows, cols = block.shape
        half = (cols // 2 + LANES - 1) // LANES * LANES
        from_x, from_y = self.swap_x(block), self.swap_y(block)
        far = jnp.concatenate(
            [self.swap_y(from_x[:, :half]), self.swap_x(from_y[:, half:])], axis=1
        )
        mine = jnp.zeros((4, rows, cols), block.dtype)
        here = 2 * self.y + self.x
        for step, part in enumerate((block, from_x, from_y, far)):
            mine = lax.dynamic_update_slice(mine, part[None], (here ^ step, 0, 0))
        other = self.swap_core(mine)
        first = jnp.where(self.core == 0, mine, other)
        second = jnp.where(self.core == 0, other, mine)
        return jnp.stack([first, second], axis=1).reshape(8 * rows, cols)

    def scatter_ctx(self, blocks):
        if not self.cube:
            return lax.psum_scatter(blocks, "ctx", scatter_dimension=0, tiled=False).astype(f32)

        def part(index):
            return lax.dynamic_index_in_dim(blocks, jnp.clip(index, 0, self.ctx - 1), 0, False)

        falling = rising = None
        for step in range(self.ctx - 1, 0, -1):
            low, high = part(self.z - step), part(self.z + step)
            if falling is not None:
                low = to_low(low.astype(f32) + falling.astype(f32))
                high = to_low(high.astype(f32) + rising.astype(f32))
            n = self.ctx
            falling = self.permute(
                low, lambda d, z: (d, z - 1) if z - step >= 0 else None
            )
            rising = self.permute(
                high, lambda d, z: (d, z + 1) if z + step < n else None
            )
        return part(self.z).astype(f32) + falling.astype(f32) + rising.astype(f32)

    def weight_terms(self, left, right):
        if not self.cube:
            return to_low(contract_rows(left, right))
        tokens, width = left.shape
        rows = width // self.dp
        parts = left.reshape(tokens, self.dp // 2, 2, rows)
        even = parts[:, :, 0].reshape(tokens, -1)
        odd = parts[:, :, 1].reshape(tokens, -1)
        own = jnp.where(self.core == 0, even, odd)
        sibling = jnp.where(self.core == 0, odd, even)
        came = self.swap_core(to_low(contract_rows(sibling, right)))
        return to_low(contract_rows(own, right) + came.astype(f32))

    def scatter_dp(self, terms):
        if not self.cube:
            return lax.psum_scatter(terms, "dp", scatter_dimension=0, tiled=True)
        rows, cols = terms.shape[0] // 4, terms.shape[1]
        half = (cols // 2 + LANES - 1) // LANES * LANES
        grid = terms.reshape(2, 2, rows, cols)

        def pick(values, index, axis):
            return lax.dynamic_index_in_dim(values, index, axis, False)

        def added(one, two):
            return to_low(one.astype(f32) + two.astype(f32))

        left, right = grid[..., :half], grid[..., half:]
        left_x = self.swap_x(pick(left, 1 - self.x, 1))
        right_y = self.swap_y(pick(right, 1 - self.y, 0))
        left = added(pick(left, self.x, 1), left_x)
        right = added(pick(right, self.y, 0), right_y)
        left_y = self.swap_y(pick(left, 1 - self.y, 0))
        right_x = self.swap_x(pick(right, 1 - self.x, 0))
        left = added(pick(left, self.y, 0), left_y)
        right = added(pick(right, self.x, 0), right_x)
        return jnp.concatenate([left, right], axis=1)


def nt(left, right):
    return lax.dot_general(left, right, (((1,), (1,)), ((), ())), preferred_element_type=f32)


def tn(left, right):
    return lax.dot_general(left, right, (((0,), (0,)), ((), ())), preferred_element_type=f32)


def fill_bias(kinfo_ref, qinfo_ref, bias_ref):
    diff = qinfo_ref[0:1, :] - kinfo_ref[:, 0:1]
    fine = (diff >= 0) & (diff <= kinfo_ref[:, 1:2])
    bias_ref[...] = jnp.where(fine, 0.0, masked_fill)


def attend_forward_kernel(
    heads, kinfo_ref, qinfo_ref, q_ref, own_ref, sib_ref, out_ref, lse_ref, top_ref, bias_ref
):
    step = pl.program_id(0)

    @pl.when(step == 0)
    def _():
        fill_bias(kinfo_ref, qinfo_ref, bias_ref)

    keys = jnp.concatenate([own_ref[0], sib_ref[0]], axis=0)
    values = jnp.concatenate([own_ref[1], sib_ref[1]], axis=0)
    queries = q_ref[...]
    lane = lax.broadcasted_iota(jnp.int32, queries.shape, 1)
    outs = []
    for side in range(2):
        mine = (lane >= HD) if side else (lane < HD)
        picked = jnp.where(mine, queries, jnp.zeros_like(queries)) * bf16(HD**-0.5)
        scores = nt(keys, picked) + bias_ref[...]
        top = jnp.max(scores, axis=0, keepdims=True)
        weights = jnp.exp(scores - top)
        total = jnp.sum(weights, axis=0, keepdims=True)
        mixed = tn(values[:, side * HD : (side + 1) * HD], weights.astype(bf16))
        outs.append(mixed * (1.0 / total))
        lse_ref[0, side : side + 1, :] = top + jnp.log(total)
        top_ref[0, side : side + 1, :] = top
    out_ref[...] = jnp.concatenate(outs, axis=0).T.astype(bf16)


def attend_backward_kernel(
    heads,
    kinfo_ref,
    qinfo_ref,
    q_ref,
    own_ref,
    sib_ref,
    grad_ref,
    lse_ref,
    dq_ref,
    down_ref,
    dsib_ref,
    bias_ref,
):
    step = pl.program_id(0)

    @pl.when(step == 0)
    def _():
        fill_bias(kinfo_ref, qinfo_ref, bias_ref)

    keys = jnp.concatenate([own_ref[0], sib_ref[0]], axis=0)
    values = jnp.concatenate([own_ref[1], sib_ref[1]], axis=0)
    queries, grads = q_ref[...], grad_ref[...]
    half = queries.shape[0]
    lane = lax.broadcasted_iota(jnp.int32, queries.shape, 1)
    dqs, dk, dv = [], 0.0, 0.0
    for side in range(2):
        mine = (lane >= HD) if side else (lane < HD)
        picked = jnp.where(mine, queries, jnp.zeros_like(queries)) * bf16(HD**-0.5)
        grad = jnp.where(mine, grads, jnp.zeros_like(grads))
        scores = nt(keys, picked) + bias_ref[...]
        weights = jnp.exp(scores - lse_ref[0, side : side + 1, :])
        dp = nt(values, grad)
        delta = jnp.sum(weights * dp, axis=0, keepdims=True)
        ds = (weights * (dp - delta)).astype(bf16)
        dqs.append(tn(keys[:, side * HD : (side + 1) * HD], ds) * (HD**-0.5))
        dk = dk + product(ds, picked)
        dv = dv + product(weights.astype(bf16), grad)
    dq_ref[...] = jnp.concatenate(dqs, axis=0).T.astype(bf16)
    dk, dv = dk.astype(bf16), dv.astype(bf16)
    down_ref[0] = dk[:half]
    dsib_ref[0] = dk[half:]
    down_ref[1] = dv[:half]
    dsib_ref[1] = dv[half:]


def pair_specs(rows):
    flat = pl.BlockSpec((rows, LANES), lambda i: (0, i))
    double = pl.BlockSpec((2, rows, LANES), lambda i: (0, 0, i))
    per_head = pl.BlockSpec((1, 2, rows), lambda i: (i, 0, 0))
    return flat, double, per_head


def attend_forward(heads, kinfo, qinfo, queries, own, sib):
    rows, width = queries.shape
    pairs = width // LANES
    flat, double, per_head = pair_specs(rows)
    small = jax.ShapeDtypeStruct((pairs, 2, rows), f32)
    return pl.pallas_call(
        partial(attend_forward_kernel, heads),
        grid=(pairs,),
        in_specs=[
            pl.BlockSpec(kinfo.shape, lambda i: (0, 0)),
            pl.BlockSpec(qinfo.shape, lambda i: (0, 0)),
            flat,
            double,
            double,
        ],
        out_specs=[flat, per_head, per_head],
        out_shape=[jax.ShapeDtypeStruct((rows, width), bf16), small, small],
        scratch_shapes=[pltpu.VMEM((2 * rows, rows), f32)],
        compiler_params=pltpu.CompilerParams(vmem_limit_bytes=48 * 2**20),
        cost_estimate=pl.CostEstimate(
            flops=pairs * 16 * rows * rows * LANES,
            bytes_accessed=rows * width * 12,
            transcendentals=pairs * 4 * rows * rows,
        ),
        name="attend_forward",
    )(kinfo, qinfo, queries, own, sib)


def attend_backward(heads, kinfo, qinfo, queries, own, sib, grad, lse):
    rows, width = queries.shape
    pairs = width // LANES
    flat, double, per_head = pair_specs(rows)
    both = jax.ShapeDtypeStruct((2, rows, width), bf16)
    return pl.pallas_call(
        partial(attend_backward_kernel, heads),
        grid=(pairs,),
        in_specs=[
            pl.BlockSpec(kinfo.shape, lambda i: (0, 0)),
            pl.BlockSpec(qinfo.shape, lambda i: (0, 0)),
            flat,
            double,
            double,
            flat,
            per_head,
        ],
        out_specs=[flat, double, double],
        out_shape=[jax.ShapeDtypeStruct((rows, width), bf16), both, both],
        scratch_shapes=[pltpu.VMEM((2 * rows, rows), f32)],
        compiler_params=pltpu.CompilerParams(vmem_limit_bytes=48 * 2**20),
        cost_estimate=pl.CostEstimate(
            flops=pairs * 40 * rows * rows * LANES,
            bytes_accessed=rows * width * 22,
            transcendentals=pairs * 4 * rows * rows,
        ),
        name="attend_backward",
    )(kinfo, qinfo, queries, own, sib, grad, lse)


def shards(
    dp,
    ctx,
    inputs,
    cotangent,
    w_qkv,
    w_out,
    w_up,
    w_down,
    vectors,
    bias_up,
    segment_ids,
    padding,
    stretch_order,
):
    local_seqs, query_len, width = inputs.shape
    length = segment_ids.shape[1]
    half = length // 2
    heads = width // HD
    wide = (width + LANES - 1) // LANES * LANES
    rows_d = w_qkv.shape[0]
    cols_d = w_out.shape[1]
    cols_f = w_up.shape[1]
    ratio = w_down.shape[0] // rows_d
    hidden_width = cols_f * ctx
    moves = Moves(dp, ctx, local_seqs)
    core, place = moves.core, moves.z

    extra = jnp.concatenate([vectors.reshape(-1, cols_f), bias_up[None]], axis=0)
    first = jnp.concatenate([jnp.concatenate([w_qkv, w_out], axis=1), extra], axis=0)
    first = moves.gather_ctx(first)
    x_flat = moves.to_sequences(inputs).astype(f32)
    down_packed = jnp.swapaxes(w_down.reshape(ratio, rows_d, cols_d), 0, 1).reshape(rows_d, -1)
    second = moves.gather_ctx(jnp.concatenate([w_up, down_packed], axis=0))
    cot = moves.to_sequences(cotangent)

    def columns(blocks):
        return jnp.swapaxes(blocks, 0, 1).reshape(blocks.shape[1], -1)

    cols_q = w_qkv.shape[1]
    part_qkv = columns(first[:, :rows_d, :cols_q])
    part_out = columns(first[:, :rows_d, cols_q:])
    small = first[:, rows_d:]
    vec_rows = columns(small[:, :-1].reshape(ctx, 8, cols_d)).astype(f32)
    bias_row = small[:, -1].reshape(-1).astype(f32)
    part_up = columns(second[:, :rows_d])
    part_down = second[:, rows_d:].reshape(ctx, rows_d, ratio, cols_d)
    part_down = jnp.transpose(part_down, (2, 1, 0, 3)).reshape(ratio * rows_d, width)

    wide_qkv = moves.gather_dp(part_qkv)
    wide_out = moves.gather_dp(part_out)
    wide_up = moves.gather_dp(part_up)
    wide_down = moves.gather_dp(part_down)

    info = jnp.stack([segment_ids, padding], axis=0)
    info_there = moves.swap_core(info)
    info = jnp.where(place // local_seqs == core, info, info_there)
    info = lax.dynamic_index_in_dim(info, place % local_seqs, 1, False)
    stretches = stretch_order.shape[0]
    stretch_len = length // stretches
    info = jnp.take(info.reshape(2, stretches, stretch_len), stretch_order, axis=1)
    positions = stretch_order[:, None] * stretch_len + jnp.arange(stretch_len, dtype=jnp.int32)
    code = (info[0] * (2 * length) + positions).reshape(2, half)
    reach = (info[1] * (length - 1)).reshape(2, half)
    code_own = lax.dynamic_index_in_dim(code, core, 0, False)
    code_sib = lax.dynamic_index_in_dim(code, 1 - core, 0, False)
    reach_own = lax.dynamic_index_in_dim(reach, core, 0, False)
    reach_sib = lax.dynamic_index_in_dim(reach, 1 - core, 0, False)
    kinfo = jnp.stack(
        [jnp.concatenate([code_own, code_sib]), jnp.concatenate([reach_own, reach_sib])], axis=1
    )
    qinfo = code_own[None]

    normed = to_low(layer_norm(x_flat, vec_rows[0], vec_rows[1]))
    projected = product(normed, wide_qkv)

    def padded(values):
        return jnp.pad(to_low(values), ((0, 0), (0, wide - width)))

    queries = padded(projected[:, :width] + vec_rows[2])
    own = jnp.stack(
        [
            padded(projected[:, width : 2 * width]),
            padded(projected[:, 2 * width :] + vec_rows[3]),
        ]
    )
    sib = moves.swap_core(own)
    attended, lse, tops = attend_forward(heads, kinfo, qinfo, queries, own, sib)
    attended = attended[:, :width]
    block_top = jnp.max(tops, axis=2).reshape(-1)[:heads]
    global_top = lax.pmax(block_top, AXES)
    residual = x_flat + product(attended, wide_out) + vec_rows[4]
    normed_two = to_low(layer_norm(residual, vec_rows[5], vec_rows[6]))
    up_pre = product(normed_two, wide_up) + bias_row
    hidden = to_low(jax.nn.gelu(up_pre, approximate=True))
    output = to_low(residual + product(hidden, wide_down) + vec_rows[7])
    output = moves.from_sequences(output)

    grad_output = cot.astype(f32)
    grad_bias_two = column_sum(cot)
    sum_down = moves.weight_terms(hidden, cot)
    sum_down = moves.scatter_dp(sum_down)
    grad_hidden = contract_cols(cot, wide_down)
    unused, gelu_back = jax.vjp(partial(jax.nn.gelu, approximate=True), up_pre)
    grad_pre = to_low(gelu_back(grad_hidden)[0])
    grad_bias_up = column_sum(grad_pre)
    sum_up = moves.weight_terms(normed_two, grad_pre)
    sum_up = moves.scatter_dp(sum_up)
    unused, norm_back_two = jax.vjp(layer_norm, residual, vec_rows[5], vec_rows[6])
    back_two = norm_back_two(contract_cols(grad_pre, wide_up))
    grad_residual = grad_output + back_two[0]
    grad_branch = to_low(grad_residual)
    sum_out = moves.weight_terms(attended, grad_branch)
    sum_out = moves.scatter_dp(sum_out)
    grad_attended = padded(contract_cols(grad_branch, wide_out))
    dq, d_own, d_sib = attend_backward(
        heads, kinfo, qinfo, queries, own, sib, grad_attended, lse
    )
    d_came = moves.swap_core(d_sib)
    d_own = to_low(d_own.astype(f32) + d_came.astype(f32))
    grad_proj = jnp.concatenate([dq[:, :width], d_own[0, :, :width], d_own[1, :, :width]], axis=1)
    sum_qkv = moves.weight_terms(normed, grad_proj)
    sum_qkv = moves.scatter_dp(sum_qkv)
    unused, norm_back_one = jax.vjp(layer_norm, x_flat, vec_rows[0], vec_rows[1])
    back_one = norm_back_one(contract_cols(grad_proj, wide_qkv))
    grad_input = to_low(grad_residual + back_one[0])
    grad_input = moves.from_sequences(grad_input).astype(f32)
    grad_vectors = jnp.stack(
        [
            back_one[1],
            back_one[2],
            column_sum(dq[:, :width]),
            column_sum(d_own[1, :, :width]),
            column_sum(grad_branch),
            back_two[1],
            back_two[2],
            grad_bias_two,
        ]
    )

    def by_place(values):
        return jnp.swapaxes(values.reshape(values.shape[0], ctx, -1), 0, 1)

    blocks_down = sum_down.reshape(ratio, rows_d, ctx, cols_d)
    blocks_down = jnp.transpose(blocks_down, (2, 1, 0, 3)).reshape(ctx, rows_d, -1)
    later = jnp.concatenate([by_place(sum_up), blocks_down, by_place(sum_out)], axis=2)
    later = moves.scatter_ctx(later)
    grad_up = later[:, :cols_f]
    grad_down = later[:, cols_f : 2 * cols_f].reshape(rows_d, ratio, cols_d)
    grad_down = jnp.swapaxes(grad_down, 0, 1).reshape(ratio * rows_d, cols_d)
    grad_out = later[:, 2 * cols_f :]
    grad_qkv = moves.scatter_ctx(by_place(sum_qkv))

    tiny = jnp.concatenate([grad_vectors, grad_bias_up.reshape(-1, width)], axis=0)
    tiny = lax.psum(tiny, AXES)
    grad_vectors = lax.dynamic_slice_in_dim(tiny[:8], place * cols_d, cols_d, 1)
    grad_bias = lax.dynamic_slice_in_dim(tiny[8:].reshape(-1), place * cols_f, cols_f)

    factor = clip_limit / jnp.maximum(global_top, clip_limit)
    per_column = jnp.repeat(jnp.sqrt(factor), HD)
    column_scale = jnp.concatenate([per_column, per_column, jnp.ones((width,), f32)])
    local_scale = lax.dynamic_slice_in_dim(column_scale, place * cols_q, cols_q)
    clipped_qkv = to_low(w_qkv.astype(f32) * local_scale[None, :])
    bias_scale = lax.dynamic_slice_in_dim(per_column, place * cols_d, cols_d)
    clipped_bias = to_low(vectors[2].astype(f32) * bias_scale)
    return (
        output,
        grad_input,
        grad_qkv,
        grad_out,
        grad_up,
        grad_down,
        grad_vectors,
        grad_bias,
        clipped_qkv,
        clipped_bias,
        global_top,
    )


def solution(mesh):
    return jax.shard_map(
        partial(shards, mesh.shape["dp"], mesh.shape["ctx"]),
        mesh=mesh,
        in_specs=(
            P("dp", "ctx", None),
            P("dp", "ctx", None),
            P("dp", "ctx"),
            P("dp", "ctx"),
            P("dp", "ctx"),
            P("dp", "ctx"),
            P(None, "ctx"),
            P("ctx"),
            P("dp", None),
            P("dp", None),
            P(),
        ),
        out_specs=(
            P("dp", "ctx", None),
            P("dp", "ctx", None),
            P("dp", "ctx"),
            P("dp", "ctx"),
            P("dp", "ctx"),
            P("dp", "ctx"),
            P(None, "ctx"),
            P("ctx"),
            P("dp", "ctx"),
            P("ctx"),
            P(),
        ),
        check_vma=False,
    )
```

```python
import math
from functools import partial

import jax
import jax.numpy as jnp
from jax import lax
from jax.experimental import pallas as pl
from jax.experimental.pallas import tpu as pltpu
from jax.sharding import PartitionSpec as P

HD = 64
LANES = 128
AXES = ("dp", "ctx")

eps_norm = 1e-05
clip_limit = 5.0
masked_fill = -1e30
f32 = jnp.float32
bf16 = jnp.bfloat16


def layer_norm(values_in, gain_row, shift_row):
    average = jnp.mean(values_in, axis=-1, keepdims=True)
    centred = values_in - average
    variance = jnp.mean(centred * centred, axis=-1, keepdims=True)
    return centred * lax.rsqrt(variance + eps_norm) * gain_row + shift_row


def to_low(values_in):
    return values_in.astype(bf16)


def product(left, right):
    return jnp.dot(left, right, preferred_element_type=f32)


def contract_rows(left, right):
    return lax.dot_general(left, right, (((0,), (0,)), ((), ())), preferred_element_type=f32)


def contract_cols(left, right):
    return lax.dot_general(left, right, (((1,), (1,)), ((), ())), preferred_element_type=f32)


def column_sum(values_in):
    return jnp.sum(values_in.astype(f32), axis=0)


class Moves:
    def __init__(self, dp, ctx, local_seqs):
        self.dp, self.ctx, self.seqs = dp, ctx, local_seqs
        self.d = lax.axis_index("dp")
        self.z = lax.axis_index("ctx")
        self.core = self.d % 2
        self.cube = dp == 8 and ctx == 4
        self.x = (self.d // 2) % 2
        self.y = self.d // 4

    def permute(self, values, target):
        pairs = []
        for d in range(self.dp):
            for z in range(self.ctx):
                there = target(d, z)
                if there is not None:
                    pairs.append((d * self.ctx + z, there[0] * self.ctx + there[1]))
        return lax.ppermute(values, AXES, pairs)

    def swap_core(self, values):
        return self.permute(values, lambda d, z: (d ^ 1, z))

    def swap_x(self, values):
        return self.permute(values, lambda d, z: (d ^ 2, z))

    def swap_y(self, values):
        return self.permute(values, lambda d, z: (d ^ 4, z))

    def up(self, values):
        return self.permute(values, lambda d, z: (d, z + 1) if z + 1 < self.ctx else None)

    def down(self, values):
        return self.permute(values, lambda d, z: (d, z - 1) if z > 0 else None)

    def sequence_target(self, step):
        n = self.seqs

        def target(d, z):
            return (d - d % 2 + z // n, n * (d % 2) + (z + step) % n)

        return target

    def to_sequences(self, values):
        n = self.seqs
        came = []
        for step in range(n):
            block = lax.dynamic_index_in_dim(values, (self.z + step) % n, 0, keepdims=False)
            came.append(self.permute(block, self.sequence_target(step)))
        return jnp.concatenate([self.choose(came, (self.z - t) % n) for t in range(n)], axis=0)

    def from_sequences(self, values):
        n = self.seqs
        parts = values.reshape(n, values.shape[0] // n, values.shape[1])
        came = []
        for step in range(n):
            forward = self.sequence_target(step)
            block = lax.dynamic_index_in_dim(parts, (self.z - step) % n, 0, keepdims=False)
            back = {}
            for d in range(self.dp):
                for z in range(self.ctx):
                    back[forward(d, z)] = (d, z)
            came.append(self.permute(block, lambda d, z: back[(d, z)]))
        return jnp.stack([self.choose(came, (j - self.z) % n) for j in range(n)], axis=0)

    @staticmethod
    def choose(items, index):
        picked = items[0]
        for i in range(1, len(items)):
            picked = jnp.where(index == i, items[i], picked)
        return picked

    def gather_ctx(self, block):
        if not self.cube:
            return lax.all_gather(block, "ctx", axis=0, tiled=False)
        rising, falling = [block], [block]
        for _ in range(self.ctx - 1):
            rising.append(self.up(rising[-1]))
            falling.append(self.down(falling[-1]))
        line = jnp.stack(rising[:0:-1] + falling, axis=0)
        return lax.dynamic_slice_in_dim(line, self.ctx - 1 - self.z, self.ctx, 0)

    def gather_dp(self, block):
        if not self.cube:
            return lax.all_gather(block, "dp", axis=0, tiled=True)
        rows, cols = block.shape
        half = (cols // 2 + LANES - 1) // LANES * LANES
        from_x, from_y = self.swap_x(block), self.swap_y(block)
        far = jnp.concatenate(
            [self.swap_y(from_x[:, :half]), self.swap_x(from_y[:, half:])], axis=1
        )
        mine = jnp.zeros((4, rows, cols), block.dtype)
        here = 2 * self.y + self.x
        for step, part in enumerate((block, from_x, from_y, far)):
            mine = lax.dynamic_update_slice(mine, part[None], (here ^ step, 0, 0))
        other = self.swap_core(mine)
        first = jnp.where(self.core == 0, mine, other)
        second = jnp.where(self.core == 0, other, mine)
        return jnp.stack([first, second], axis=1).reshape(8 * rows, cols)

    def scatter_ctx(self, blocks):
        if not self.cube:
            return lax.psum_scatter(blocks, "ctx", scatter_dimension=0, tiled=False).astype(f32)

        def part(index):
            return lax.dynamic_index_in_dim(blocks, jnp.clip(index, 0, self.ctx - 1), 0, False)

        falling = rising = None
        for step in range(self.ctx - 1, 0, -1):
            low, high = part(self.z - step), part(self.z + step)
            if falling is not None:
                low = to_low(low.astype(f32) + falling.astype(f32))
                high = to_low(high.astype(f32) + rising.astype(f32))
            n = self.ctx
            falling = self.permute(
                low, lambda d, z: (d, z - 1) if z - step >= 0 else None
            )
            rising = self.permute(
                high, lambda d, z: (d, z + 1) if z + step < n else None
            )
        return part(self.z).astype(f32) + falling.astype(f32) + rising.astype(f32)

    def weight_terms(self, left, right):
        if not self.cube:
            return to_low(contract_rows(left, right))
        tokens, width = left.shape
        rows = width // self.dp
        parts = left.reshape(tokens, self.dp // 2, 2, rows)
        even = parts[:, :, 0].reshape(tokens, -1)
        odd = parts[:, :, 1].reshape(tokens, -1)
        own = jnp.where(self.core == 0, even, odd)
        sibling = jnp.where(self.core == 0, odd, even)
        came = self.swap_core(to_low(contract_rows(sibling, right)))
        return to_low(contract_rows(own, right) + came.astype(f32))

    def scatter_dp(self, terms):
        if not self.cube:
            return lax.psum_scatter(terms, "dp", scatter_dimension=0, tiled=True)
        rows, cols = terms.shape[0] // 4, terms.shape[1]
        half = (cols // 2 + LANES - 1) // LANES * LANES
        grid = terms.reshape(2, 2, rows, cols)

        def pick(values, index, axis):
            return lax.dynamic_index_in_dim(values, index, axis, False)

        def added(one, two):
            return to_low(one.astype(f32) + two.astype(f32))

        left, right = grid[..., :half], grid[..., half:]
        left_x = self.swap_x(pick(left, 1 - self.x, 1))
        right_y = self.swap_y(pick(right, 1 - self.y, 0))
        left = added(pick(left, self.x, 1), left_x)
        right = added(pick(right, self.y, 0), right_y)
        left_y = self.swap_y(pick(left, 1 - self.y, 0))
        right_x = self.swap_x(pick(right, 1 - self.x, 0))
        left = added(pick(left, self.y, 0), left_y)
        right = added(pick(right, self.x, 0), right_x)
        return jnp.concatenate([left, right], axis=1)


def nt(left, right):
    return lax.dot_general(left, right, (((1,), (1,)), ((), ())), preferred_element_type=f32)


def tn(left, right):
    return lax.dot_general(left, right, (((0,), (0,)), ((), ())), preferred_element_type=f32)


def fill_bias(kinfo_ref, qinfo_ref, bias_ref):
    diff = qinfo_ref[0:1, :] - kinfo_ref[:, 0:1]
    fine = (diff >= 0) & (diff <= kinfo_ref[:, 1:2])
    bias_ref[...] = jnp.where(fine, 0.0, masked_fill)


def attend_forward_kernel(
    heads, kinfo_ref, qinfo_ref, q_ref, own_ref, sib_ref, out_ref, lse_ref, top_ref, bias_ref
):
    step = pl.program_id(0)

    @pl.when(step == 0)
    def _():
        fill_bias(kinfo_ref, qinfo_ref, bias_ref)

    keys = jnp.concatenate([own_ref[0], sib_ref[0]], axis=0)
    values = jnp.concatenate([own_ref[1], sib_ref[1]], axis=0)
    queries = q_ref[...]
    lane = lax.broadcasted_iota(jnp.int32, queries.shape, 1)
    outs = []
    for side in range(2):
        mine = (lane >= HD) if side else (lane < HD)
        picked = jnp.where(mine, queries, jnp.zeros_like(queries)) * bf16(HD**-0.5)
        scores = nt(keys, picked) + bias_ref[...]
        top = jnp.max(scores, axis=0, keepdims=True)
        weights = jnp.exp(scores - top)
        total = jnp.sum(weights, axis=0, keepdims=True)
        mixed = tn(values[:, side * HD : (side + 1) * HD], weights.astype(bf16))
        outs.append(mixed * (1.0 / total))
        lse_ref[0, side : side + 1, :] = top + jnp.log(total)
        top_ref[0, side : side + 1, :] = top
    out_ref[...] = jnp.concatenate(outs, axis=0).T.astype(bf16)


def attend_backward_kernel(
    heads,
    kinfo_ref,
    qinfo_ref,
    q_ref,
    own_ref,
    sib_ref,
    grad_ref,
    lse_ref,
    dq_ref,
    down_ref,
    dsib_ref,
    bias_ref,
):
    step = pl.program_id(0)

    @pl.when(step == 0)
    def _():
        fill_bias(kinfo_ref, qinfo_ref, bias_ref)

    keys = jnp.concatenate([own_ref[0], sib_ref[0]], axis=0)
    values = jnp.concatenate([own_ref[1], sib_ref[1]], axis=0)
    queries, grads = q_ref[...], grad_ref[...]
    half = queries.shape[0]
    lane = lax.broadcasted_iota(jnp.int32, queries.shape, 1)
    dqs, dk, dv = [], 0.0, 0.0
    for side in range(2):
        mine = (lane >= HD) if side else (lane < HD)
        picked = jnp.where(mine, queries, jnp.zeros_like(queries)) * bf16(HD**-0.5)
        grad = jnp.where(mine, grads, jnp.zeros_like(grads))
        scores = nt(keys, picked) + bias_ref[...]
        weights = jnp.exp(scores - lse_ref[0, side : side + 1, :])
        dp = nt(values, grad)
        delta = jnp.sum(weights * dp, axis=0, keepdims=True)
        ds = (weights * (dp - delta)).astype(bf16)
        dqs.append(tn(keys[:, side * HD : (side + 1) * HD], ds) * (HD**-0.5))
        dk = dk + product(ds, picked)
        dv = dv + product(weights.astype(bf16), grad)
    dq_ref[...] = jnp.concatenate(dqs, axis=0).T.astype(bf16)
    dk, dv = dk.astype(bf16), dv.astype(bf16)
    down_ref[0] = dk[:half]
    dsib_ref[0] = dk[half:]
    down_ref[1] = dv[:half]
    dsib_ref[1] = dv[half:]


def pair_specs(rows):
    flat = pl.BlockSpec((rows, LANES), lambda i: (0, i))
    double = pl.BlockSpec((2, rows, LANES), lambda i: (0, 0, i))
    per_head = pl.BlockSpec((1, 2, rows), lambda i: (i, 0, 0))
    return flat, double, per_head


def attend_forward(heads, kinfo, qinfo, queries, own, sib):
    rows, width = queries.shape
    pairs = width // LANES
    flat, double, per_head = pair_specs(rows)
    small = jax.ShapeDtypeStruct((pairs, 2, rows), f32)
    return pl.pallas_call(
        partial(attend_forward_kernel, heads),
        grid=(pairs,),
        in_specs=[
            pl.BlockSpec(kinfo.shape, lambda i: (0, 0)),
            pl.BlockSpec(qinfo.shape, lambda i: (0, 0)),
            flat,
            double,
            double,
        ],
        out_specs=[flat, per_head, per_head],
        out_shape=[jax.ShapeDtypeStruct((rows, width), bf16), small, small],
        scratch_shapes=[pltpu.VMEM((2 * rows, rows), f32)],
        compiler_params=pltpu.CompilerParams(vmem_limit_bytes=48 * 2**20),
        cost_estimate=pl.CostEstimate(
            flops=pairs * 16 * rows * rows * LANES,
            bytes_accessed=rows * width * 12,
            transcendentals=pairs * 4 * rows * rows,
        ),
        name="attend_forward",
    )(kinfo, qinfo, queries, own, sib)


def attend_backward(heads, kinfo, qinfo, queries, own, sib, grad, lse):
    rows, width = queries.shape
    pairs = width // LANES
    flat, double, per_head = pair_specs(rows)
    both = jax.ShapeDtypeStruct((2, rows, width), bf16)
    return pl.pallas_call(
        partial(attend_backward_kernel, heads),
        grid=(pairs,),
        in_specs=[
            pl.BlockSpec(kinfo.shape, lambda i: (0, 0)),
            pl.BlockSpec(qinfo.shape, lambda i: (0, 0)),
            flat,
            double,
            double,
            flat,
            per_head,
        ],
        out_specs=[flat, double, double],
        out_shape=[jax.ShapeDtypeStruct((rows, width), bf16), both, both],
        scratch_shapes=[pltpu.VMEM((2 * rows, rows), f32)],
        compiler_params=pltpu.CompilerParams(vmem_limit_bytes=48 * 2**20),
        cost_estimate=pl.CostEstimate(
            flops=pairs * 40 * rows * rows * LANES,
            bytes_accessed=rows * width * 22,
            transcendentals=pairs * 4 * rows * rows,
        ),
        name="attend_backward",
    )(kinfo, qinfo, queries, own, sib, grad, lse)


MESH = pl.DeviceIdType.MESH


class Sizes:
    def __init__(self, width, hidden, ctx, dp, length):
        self.width = width
        self.wide = -(-width // LANES) * LANES
        self.ctx = ctx
        self.rows = 2 * width // dp
        self.qkv = 3 * width // ctx
        self.out = width // ctx
        self.cols = -(-(self.qkv + self.out) // LANES) * LANES
        self.up = hidden // ctx
        self.half = length // 2
        self.pairs = self.wide // LANES
        self.out_tile = self.qkv // LANES * LANES
        self.qkv_cols = 1024

    def qkv_runs(self, z):
        runs, at = [], z * self.qkv
        end = at + self.qkv
        while at < end:
            kind = at // self.width
            stop = min(end, (kind + 1) * self.width)
            runs.append((at - z * self.qkv, kind * self.wide + at - kind * self.width, stop - at))
            at = stop
        return runs


class Net:
    def __init__(self):
        self.d = lax.axis_index("dp")
        self.z = lax.axis_index("ctx")
        self.c = self.d % 2
        self.p = self.d // 2
        y, x = self.p // 2, self.p % 2
        self.px, self.py, self.pd = 2 * y + 1 - x, 2 * (1 - y) + x, 2 * (1 - y) + 1 - x
        self.x_to = (2 * self.px + self.c, self.z)
        self.y_to = (2 * self.py + self.c, self.z)
        self.sib = (2 * self.p + 1 - self.c, self.z)
        self.near = self.c + 2 * (self.z // 2)
        self.far = self.c + 2 * (1 - self.z // 2)


def enter(net):
    gate = pltpu.get_barrier_semaphore()
    for c in range(2):
        for z in range(4):

            @pl.when((c != net.c) | (z != net.z))
            def _():
                pl.semaphore_signal(gate, inc=1, device_id=(2 * net.p + c, z), device_id_type=MESH)

    for to in (net.x_to, net.y_to):
        pl.semaphore_signal(gate, inc=1, device_id=to, device_id_type=MESH)
    pl.semaphore_wait(gate, 9)


class Gather:
    def __init__(self, net, sizes, w, own, swapped, sems):
        self.n, self.s, self.w, self.own, self.swapped = net, sizes, w, own, swapped
        self.zs, self.zr, self.hs, self.hr, self.cs, self.cr, self.loc = sems

    def at(self, p, z):
        r, c = (z, p) if self.swapped else (p, z)
        s = self.s
        return self.w.at[
            pl.ds(pl.multiple_of(r * s.rows, 16), s.rows),
            pl.ds(pl.multiple_of(c * s.cols, LANES), s.cols),
        ]

    def copy(self, p, z, send, recv, to):
        block = self.at(p, z)
        return pltpu.make_async_remote_copy(
            block, block, send, recv, device_id=to, device_id_type=MESH
        )

    def zcopy(self, z, up):
        n = self.n
        to = (n.d, n.z + 1 if up else n.z - 1)
        return self.copy(n.p, z, self.zs.at[z // 2, int(up)], self.zr.at[z // 2], to)

    def hop(self, p, z, to, k):
        return self.copy(p, z, self.hs.at[z // 2, k], self.hr.at[z // 2, k], to)

    def across(self, p, z):
        return self.copy(p, z, self.cs.at[p, z // 2], self.cr.at[p, z // 2], self.n.sib)

    def begin(self):
        n = self.n

        @pl.when(n.z % 2 == n.c)
        def _():
            local = pltpu.make_async_copy(self.own, self.at(n.p, n.z), self.loc)
            local.start()
            local.wait()

            @pl.when(n.z < 3)
            def _():
                self.zcopy(n.z, True).start()

            @pl.when(n.z > 0)
            def _():
                self.zcopy(n.z, False).start()

    def arrive(self, z):
        n = self.n

        @pl.when(z != n.z)
        def _():
            self.zcopy(z, True).wait_recv()

            @pl.when((z < n.z) & (n.z < 3))
            def _():
                self.zcopy(z, True).start()

            @pl.when((z > n.z) & (n.z > 0))
            def _():
                self.zcopy(z, False).start()

        self.hop(n.p, z, n.x_to, 0).start()
        self.hop(n.p, z, n.y_to, 1).start()
        self.across(n.p, z).start()

    def turn(self, z):
        n = self.n
        self.hop(n.px, z, n.x_to, 0).wait_recv()

        @pl.when(z < 2)
        def _():
            self.hop(n.px, z, n.y_to, 2).start()

        self.across(n.px, z).start()
        self.hop(n.py, z, n.y_to, 1).wait_recv()

        @pl.when(z >= 2)
        def _():
            self.hop(n.py, z, n.x_to, 2).start()

        self.across(n.py, z).start()

    def last(self, z):
        n = self.n
        self.hop(n.pd, z, n.x_to, 2).wait_recv()
        self.across(n.pd, z).start()

    def ready(self):
        n = self.n
        for half in range(2):
            for p in range(4):
                self.across(p, 1 - n.c + 2 * half).wait_recv()

    def drain(self):
        n = self.n
        for half in range(2):
            z = n.c + 2 * half

            @pl.when((z <= n.z) & (n.z < 3))
            def _():
                self.zcopy(z, True).wait_send()

            @pl.when((z >= n.z) & (n.z > 0))
            def _():
                self.zcopy(z, False).wait_send()

            for k, to in enumerate((n.x_to, n.y_to, n.x_to)):
                self.hop(n.p, z, to, k).wait_send()
            for p in range(4):
                self.across(p, z).wait_send()


def gather_sems():
    dma = pltpu.SemaphoreType.DMA
    return [dma((2, 2)), dma((2,)), dma((2, 3)), dma((2, 3)), dma((4, 2)), dma((4, 2)), dma]


class ToSequences:
    def __init__(self, net, src, dst, sems):
        self.n, self.src, self.dst = net, src, dst
        self.ss, self.rs = sems
        self.rows = src.shape[1]

    def parts(self):
        n = self.n
        for j in range(2):
            to = (2 * n.p + n.z // 2, 2 * n.c + j)
            yield j, to, (to[0] == n.d) & (to[1] == n.z)

    def place(self, t):
        return self.dst.at[pl.ds(pl.multiple_of(t * self.rows, 16), self.rows)]

    def remote(self, j, to):
        t = self.n.z % 2
        return pltpu.make_async_remote_copy(
            self.src.at[j],
            self.place(t),
            self.ss.at[j],
            self.rs.at[t],
            device_id=to,
            device_id_type=MESH,
        )

    def start(self):
        for j, to, here in self.parts():

            @pl.when(here)
            def _():
                t = self.n.z % 2
                pltpu.make_async_copy(self.src.at[j], self.place(t), self.rs.at[t]).start()

            @pl.when(jnp.logical_not(here))
            def _():
                self.remote(j, to).start()

    def wait(self):
        for t in range(2):
            pltpu.make_async_copy(self.src.at[0], self.place(t), self.rs.at[t]).wait()

    def drain(self):
        for j, to, here in self.parts():

            @pl.when(jnp.logical_not(here))
            def _():
                self.remote(j, to).wait_send()


class FromSequences:
    def __init__(self, net, src, dst, sems):
        self.n, self.src, self.dst = net, src, dst
        self.ss, self.rs = sems
        self.rows = dst.shape[1]

    def parts(self):
        n = self.n
        for t in range(2):
            to = (2 * n.p + n.z // 2, 2 * n.c + t)
            yield t, to, (to[0] == n.d) & (to[1] == n.z)

    def piece(self, t):
        return self.src.at[pl.ds(t * self.rows, self.rows)]

    def remote(self, t, to):
        j = self.n.z % 2
        return pltpu.make_async_remote_copy(
            self.piece(t),
            self.dst.at[j],
            self.ss.at[t],
            self.rs.at[j],
            device_id=to,
            device_id_type=MESH,
        )

    def start(self):
        for t, to, here in self.parts():

            @pl.when(here)
            def _():
                j = self.n.z % 2
                pltpu.make_async_copy(self.piece(t), self.dst.at[j], self.rs.at[j]).start()

            @pl.when(jnp.logical_not(here))
            def _():
                self.remote(t, to).start()

    def wait(self):
        for j in range(2):
            pltpu.make_async_copy(self.piece(0), self.dst.at[j], self.rs.at[j]).wait()

    def drain(self):
        for t, to, here in self.parts():

            @pl.when(jnp.logical_not(here))
            def _():
                self.remote(t, to).wait_send()


def by_rows(total, step, body):
    def one(i, carry):
        body(pl.ds(pl.multiple_of(i * step, step), step))
        return carry

    lax.fori_loop(0, total // step, one, 0)


def by_columns(total, body, step=256):
    def one(i, carry):
        body(pl.multiple_of(i * step, LANES), step)
        return carry

    lax.fori_loop(0, total // step, one, 0)
    if total % step:
        body(total // step * step, total % step)


def normalised(values):
    average = jnp.mean(values, axis=-1, keepdims=True)
    centred = values - average
    variance = jnp.mean(centred * centred, axis=-1, keepdims=True)
    return centred * lax.rsqrt(variance + eps_norm)


def place_run(block, source, phase, count):
    moved = pltpu.roll(block, (phase - source) % block.shape[1], axis=1)
    tiles = -(-(phase + count) // LANES) * LANES
    moved = moved[:, :tiles]
    lane = lax.broadcasted_iota(jnp.int32, moved.shape, 1)
    return jnp.where((lane >= phase) & (lane < phase + count), moved, 0.0)


def attend_pair(s, i, q_ref, kv_ref, bias_ref, att_ref, lse_ref, top_ref):
    lanes = pl.ds(pl.multiple_of(i * LANES, LANES), LANES)
    keys, values, queries = kv_ref[0, :, lanes], kv_ref[1, :, lanes], q_ref[:, lanes]
    lane = lax.broadcasted_iota(jnp.int32, queries.shape, 1)
    outs = []
    for side in range(2):
        mine = (lane >= HD) if side else (lane < HD)
        picked = jnp.where(mine, queries, jnp.zeros_like(queries)) * bf16(HD**-0.5)
        scores = nt(keys, picked) + bias_ref[...]
        top = jnp.max(scores, axis=0, keepdims=True)
        weights = jnp.exp(scores - top)
        total = jnp.sum(weights, axis=0, keepdims=True)
        mixed = tn(values[:, side * HD : (side + 1) * HD], weights.astype(bf16))
        outs.append(mixed * (1.0 / total))
        lse_ref[i, side : side + 1, :] = top + jnp.log(total)
        top_ref[i, side : side + 1, :] = top
    att_ref[:, lanes] = jnp.concatenate(outs, axis=0).T.astype(bf16)


def forward_kernel(s, *refs):
    (own_a, own_b, own_c, small, inp, cot, kinfo, qinfo) = refs[:8]
    (wa, wb, wc, x_o, cot_o, vec, normed_o, q_o, kv_o, att_o, res_o, two_o, slope_o, hid_o) = refs[8:22]
    (lse, top, out_o) = refs[22:25]
    (x, normed, pre, q, kv, bias, att, res, two, slope, hid, wt, ct, out, smalls) = refs[25:40]
    sems = refs[40:]
    net = Net()
    A, B, C = [
        Gather(net, s, w, own, swapped, sems[7 * g : 7 * g + 7])
        for g, (w, own, swapped) in enumerate(
            ((wa, own_a, False), (wb, own_b, False), (wc, own_c, True))
        )
    ]
    seq_x = ToSequences(net, inp, x, sems[21:23])
    seq_cot = ToSequences(net, cot, cot_o, sems[23:25])
    seq_out = FromSequences(net, out, out_o, sems[25:27])
    small_s, small_r, kv_s, kv_r, load, save = sems[27:33]
    near, far = net.near, net.far
    saves = []

    def keep(src, dst):
        copy = pltpu.make_async_copy(src, dst, save.at[len(saves)])
        copy.start()
        saves.append(copy)

    def small_copy(z):
        return pltpu.make_async_remote_copy(
            small,
            smalls.at[net.z],
            small_s.at[z],
            small_r.at[net.z],
            device_id=(net.d, z),
            device_id_type=MESH,
        )

    enter(net)
    A.begin()
    for z in range(4):

        @pl.when(z != net.z)
        def _():
            small_copy(z).start()

        @pl.when(z == net.z)
        def _():
            pltpu.make_async_copy(small, smalls.at[z], small_r.at[z]).start()

    A.arrive(near)
    seq_x.start()
    A.arrive(far)
    B.begin()
    diff = qinfo[0:1, :] - kinfo[:, 0:1]
    fine = (diff >= 0) & (diff <= kinfo[:, 1:2])
    bias[...] = jnp.where(fine, 0.0, masked_fill)
    A.turn(near)
    B.arrive(near)

    for z in range(4):
        pltpu.make_async_copy(small, smalls.at[z], small_r.at[z]).wait()
    row = lax.broadcasted_iota(jnp.int32, (3 * LANES, s.wide), 0)
    col = lax.broadcasted_iota(jnp.int32, (3 * LANES, s.wide), 1)
    rows = 0.0
    for z in range(4):
        spread = jnp.where((col == row + z * s.out) & (row < s.out), 1.0, 0.0).astype(bf16)
        rows = rows + product(smalls[z, :, : 3 * LANES], spread)
    vec[...] = rows

    seq_x.wait()
    keep(x, x_o)
    by_rows(
        s.half,
        LANES,
        lambda r: normed.__setitem__(
            (r, slice(None)),
            to_low(
                normalised(x[r, :].astype(f32)) * vec[0:1, : s.width] + vec[1:2, : s.width]
            ),
        ),
    )
    keep(normed, normed_o)
    A.turn(far)
    A.last(near)
    B.arrive(far)
    A.last(far)
    C.begin()
    pre[...] = jnp.zeros_like(pre)
    A.ready()

    def tile_a(z):
        return pltpu.make_async_copy(
            wa.at[:, pl.ds(z * s.cols, s.cols)], wt.at[z % 2], load.at[z % 2]
        )

    def tile_b(z):
        return pltpu.make_async_copy(
            wb.at[:, pl.ds(z * s.cols, s.cols)], wt.at[z % 2], load.at[z % 2]
        )

    tile_a(0).start()
    for z in range(4):
        if z < 3:
            tile_a(z + 1).start()
        tile_a(z).wait()

        def part(start, size):
            res[:, pl.ds(start, size)] = product(normed[...], wt[z % 2, :, pl.ds(start, size)])

        by_columns(s.qkv_cols, part)
        for source, target, count in s.qkv_runs(z):
            base = target // LANES * LANES
            moved = place_run(res[:, : s.qkv_cols], source, target - base, count)
            pre[:, base : base + moved.shape[1]] += moved
        if z == 1:
            seq_cot.start()
    tile_a(0).start()
    kv[0, : s.half, :] = to_low(pre[:, s.wide : 2 * s.wide])
    kv[1, : s.half, :] = to_low(pre[:, 2 * s.wide :] + vec[3:4, :])
    share = pltpu.make_async_remote_copy(
        kv.at[:, pl.ds(0, s.half)],
        kv.at[:, pl.ds(s.half, s.half)],
        kv_s,
        kv_r,
        device_id=net.sib,
        device_id_type=MESH,
    )
    share.start()
    q[...] = to_low(pre[:, : s.wide] + vec[2:3, :])
    B.turn(near)
    C.arrive(near)
    share.wait()
    keep(q, q_o)
    keep(kv, kv_o)

    def pair(i, carry):
        attend_pair(s, i, q, kv, bias, att, lse, top)

        @pl.when(i == 1)
        def _():
            B.turn(far)
            B.last(near)

        @pl.when(i == 4)
        def _():
            C.arrive(far)

        @pl.when(i == 6)
        def _():
            B.last(far)

        return carry

    lax.fori_loop(0, s.pairs, pair, 0)
    keep(att, att_o)
    C.turn(near)

    res[...] = jnp.zeros_like(res)
    for z in range(4):
        if z < 3:
            tile_a(z + 1).start()
        tile_a(z).wait()
        block = product(att[:, : s.width], wt[z % 2, :, s.out_tile :])
        target = z * s.out
        base = target // LANES * LANES
        moved = place_run(block, s.qkv - s.out_tile, target - base, s.out)
        res[:, base : base + moved.shape[1]] += moved
    B.ready()
    tile_b(0).start()

    def second(r):
        total = res[r, : s.width] + x[r, :].astype(f32) + vec[4:5, : s.width]
        res[r, : s.width] = total
        two[r, :] = to_low(normalised(total) * vec[5:6, : s.width] + vec[6:7, : s.width])

    by_rows(s.half, LANES, second)
    keep(res, res_o)
    keep(two, two_o)

    for z in range(4):
        if z < 3:
            tile_b(z + 1).start()
        tile_b(z).wait()

        def part(start, size):
            u = product(two[...], wt[z % 2, :, pl.ds(start, size)])
            u = u + smalls[z, 8:9, pl.ds(start, size)].astype(f32)
            inner = math.sqrt(2 / math.pi) * (u + 0.044715 * u * u * u)
            t = jnp.tanh(inner)
            bend = math.sqrt(2 / math.pi) * (1 + 3 * 0.044715 * u * u)
            lanes = pl.ds(pl.multiple_of(z * s.cols + start, LANES), size)
            hid[:, lanes] = to_low(0.5 * u * (1 + t))
            slope[:, lanes] = to_low(0.5 * (1 + t) + 0.5 * u * (1 - t * t) * bend)

        by_columns(s.cols, part)
        if z == 1:
            C.turn(far)
            C.last(near)
    keep(hid, hid_o)
    keep(slope, slope_o)
    C.last(far)
    C.ready()

    def tile_c(k):
        count = min(3 * LANES, s.width - k * 3 * LANES)
        return pltpu.make_async_copy(
            wc.at[pl.ds(k * 3 * LANES, count)], ct.at[k % 2, pl.ds(0, count)], load.at[k % 2]
        )

    tile_c(0).start()
    for k in range(3):
        if k < 2:
            tile_c(k + 1).start()
        tile_c(k).wait()
        at, count = k * 3 * LANES, min(3 * LANES, s.width - k * 3 * LANES)
        block = nt(hid[...], ct[k % 2, :count, :])
        total = res[:, at : at + count] + block + vec[7:8, at : at + count]
        out[:, at : at + count] = to_low(total)
    seq_out.start()
    seq_cot.wait()
    for group in (A, B, C):
        group.drain()
    for z in range(4):

        @pl.when(z != net.z)
        def _():
            small_copy(z).wait_send()

    seq_x.drain()
    seq_cot.drain()
    for copy in saves:
        copy.wait()
    seq_out.wait()
    seq_out.drain()


def forward_call(s, own_a, own_b, own_c, small, inp, cot, kinfo, qinfo):
    dma = pltpu.SemaphoreType.DMA
    rows = s.half
    full = s.ctx * s.cols

    def low(*shape):
        return jax.ShapeDtypeStruct(shape, bf16)

    def high(*shape):
        return jax.ShapeDtypeStruct(shape, f32)

    out_shape = [low(s.width, full)] * 3 + [
        low(rows, s.width),
        low(rows, s.width),
        high(16, s.wide),
        low(rows, s.width),
        low(rows, s.wide),
        low(2, 2 * rows, s.wide),
        low(rows, s.wide),
        high(rows, s.wide),
        low(rows, s.width),
        low(rows, full),
        low(rows, full),
        high(s.pairs, 2, rows),
        high(s.pairs, 2, rows),
        low(*inp.shape),
    ]
    anywhere = pl.BlockSpec(memory_space=pl.ANY)
    local = pl.BlockSpec(memory_space=pltpu.VMEM)
    out_specs = [local if i in (5, 14, 15) else anywhere for i in range(len(out_shape))]
    return pl.pallas_call(
        partial(forward_kernel, s),
        out_shape=out_shape,
        in_specs=[anywhere] * 6 + [local] * 2,
        out_specs=out_specs,
        scratch_shapes=[
            pltpu.VMEM((rows, s.width), bf16),
            pltpu.VMEM((rows, s.width), bf16),
            pltpu.VMEM((rows, 3 * s.wide), f32),
            pltpu.VMEM((rows, s.wide), bf16),
            pltpu.VMEM((2, 2 * rows, s.wide), bf16),
            pltpu.VMEM((2 * rows, rows), f32),
            pltpu.VMEM((rows, s.wide), bf16),
            pltpu.VMEM((rows, s.wide), f32),
            pltpu.VMEM((rows, s.width), bf16),
            pltpu.VMEM((rows, full), bf16),
            pltpu.VMEM((rows, full), bf16),
            pltpu.VMEM((2, s.width, s.cols), bf16),
            pltpu.VMEM((2, 3 * LANES, full), bf16),
            pltpu.VMEM((rows, s.width), bf16),
            pltpu.VMEM((4, 16, s.wide), bf16),
        ]
        + gather_sems() * 3
        + [dma((2,))] * 6
        + [dma((4,)), dma((4,)), dma, dma, dma((2,)), dma((12,))],
        compiler_params=pltpu.CompilerParams(
            collective_id=1, has_side_effects=True, vmem_limit_bytes=61 * 2**20
        ),
        name="forward",
    )(own_a, own_b, own_c, small, inp, cot, kinfo, qinfo)


def slot_info(moves, segment_ids, padding, stretch_order):
    core, place, local_seqs = moves.core, moves.z, segment_ids.shape[0]
    length = segment_ids.shape[1]
    half = length // 2
    info = jnp.stack([segment_ids, padding], axis=0)
    info_there = moves.swap_core(info)
    info = jnp.where(place // local_seqs == core, info, info_there)
    info = lax.dynamic_index_in_dim(info, place % local_seqs, 1, False)
    stretches = stretch_order.shape[0]
    stretch_len = length // stretches
    info = jnp.take(info.reshape(2, stretches, stretch_len), stretch_order, axis=1)
    positions = stretch_order[:, None] * stretch_len + jnp.arange(stretch_len, dtype=jnp.int32)
    code = (info[0] * (2 * length) + positions).reshape(2, half)
    reach = (info[1] * (length - 1)).reshape(2, half)
    code_own = lax.dynamic_index_in_dim(code, core, 0, False)
    code_sib = lax.dynamic_index_in_dim(code, 1 - core, 0, False)
    reach_own = lax.dynamic_index_in_dim(reach, core, 0, False)
    reach_sib = lax.dynamic_index_in_dim(reach, 1 - core, 0, False)
    kinfo = jnp.stack(
        [jnp.concatenate([code_own, code_sib]), jnp.concatenate([reach_own, reach_sib])], axis=1
    )
    return kinfo, code_own[None]


def pack_blocks(moves, s, w_qkv, w_out, w_up, w_down, vectors, bias_up):
    rows = w_qkv.shape[0]

    def filled(values):
        return jnp.pad(values, ((0, 0), (0, s.cols - values.shape[1])))

    turned = w_down.T
    parts = jnp.concatenate(
        [
            filled(jnp.concatenate([w_qkv, w_out], axis=1)),
            filled(w_up),
            filled(jnp.concatenate([turned[:rows], turned[rows:]], axis=1)),
        ],
        axis=0,
    )
    there = moves.swap_core(parts)
    even = jnp.where(moves.core == 0, parts, there)
    odd = jnp.where(moves.core == 0, there, parts)
    own_a = jnp.concatenate([even[:rows], odd[:rows]], axis=0)
    own_b = jnp.concatenate([even[rows : 2 * rows], odd[rows : 2 * rows]], axis=0)
    ff = turned.shape[1]
    own_c = filled(
        jnp.concatenate(
            [
                jnp.concatenate([v[2 * rows :, :ff], v[2 * rows :, ff : 2 * ff]], axis=0)
                for v in (even, odd)
            ],
            axis=1,
        )
    )
    small = jnp.concatenate([jnp.pad(vectors, ((0, 0), (0, s.cols - vectors.shape[1]))), filled(bias_up[None])], axis=0)
    small = jnp.pad(small, ((0, 16 - small.shape[0]), (0, 0)))
    return own_a, own_b, own_c, small


def fast_shards(
    dp,
    ctx,
    inputs,
    cotangent,
    w_qkv,
    w_out,
    w_up,
    w_down,
    vectors,
    bias_up,
    segment_ids,
    padding,
    stretch_order,
):
    local_seqs, query_len, width = inputs.shape
    heads = width // HD
    s = Sizes(width, w_up.shape[1] * ctx, ctx, dp, segment_ids.shape[1])
    moves = Moves(dp, ctx, local_seqs)
    core, place = moves.core, moves.z
    wide = s.wide
    kinfo, qinfo = slot_info(moves, segment_ids, padding, stretch_order)
    own_a, own_b, own_c, small = pack_blocks(moves, s, w_qkv, w_out, w_up, w_down, vectors, bias_up)
    (wa, wb, wc, x_low, cot, vec, normed, queries, kv, attended, residual, normed_two, slope, hidden, lse, tops, output) = forward_call(
        s, own_a, own_b, own_c, small, inputs, cotangent, kinfo, qinfo
    )
    vec_rows = vec[:8, :width]
    attended = attended[:, :width]
    residual = residual[:, :width]

    def unpad(values, size):
        return values.reshape(values.shape[0], ctx, s.cols)[:, :, :size].reshape(values.shape[0], -1)

    wide_qkv = unpad(wa, s.qkv)
    wide_out = wa.reshape(width, ctx, s.cols)[:, :, s.qkv : s.qkv + s.out].reshape(width, -1)
    wide_up = unpad(wb, s.up)
    down_t = unpad(wc, s.up)
    hidden = unpad(hidden, s.up)
    slope = unpad(slope, s.up)
    x_flat = x_low.astype(f32)
    own, sib = kv[:, : s.half], kv[:, s.half :]
    cols_q, cols_d, cols_f = w_qkv.shape[1], w_out.shape[1], w_up.shape[1]
    rows_d, ratio = w_qkv.shape[0], w_down.shape[0] // w_qkv.shape[0]
    block_top = jnp.max(tops, axis=2).reshape(-1)[:heads]
    global_top = lax.pmax(block_top, AXES)

    def padded(values):
        return jnp.pad(to_low(values), ((0, 0), (0, wide - width)))

    grad_output = cot.astype(f32)
    grad_bias_two = column_sum(cot)
    sum_down = moves.scatter_dp(moves.weight_terms(hidden, cot))
    grad_hidden = product(cot, down_t)
    grad_pre = to_low(grad_hidden * slope.astype(f32))
    grad_bias_up = column_sum(grad_pre)
    sum_up = moves.weight_terms(normed_two, grad_pre)
    sum_up = moves.scatter_dp(sum_up)
    unused, norm_back_two = jax.vjp(layer_norm, residual, vec_rows[5], vec_rows[6])
    back_two = norm_back_two(contract_cols(grad_pre, wide_up))
    grad_residual = grad_output + back_two[0]
    grad_branch = to_low(grad_residual)
    sum_out = moves.weight_terms(attended, grad_branch)
    sum_out = moves.scatter_dp(sum_out)
    grad_attended = padded(contract_cols(grad_branch, wide_out))
    dq, d_own, d_sib = attend_backward(
        heads, kinfo, qinfo, queries, own, sib, grad_attended, lse
    )
    d_came = moves.swap_core(d_sib)
    d_own = to_low(d_own.astype(f32) + d_came.astype(f32))
    grad_proj = jnp.concatenate([dq[:, :width], d_own[0, :, :width], d_own[1, :, :width]], axis=1)
    sum_qkv = moves.weight_terms(normed, grad_proj)
    sum_qkv = moves.scatter_dp(sum_qkv)
    unused, norm_back_one = jax.vjp(layer_norm, x_flat, vec_rows[0], vec_rows[1])
    back_one = norm_back_one(contract_cols(grad_proj, wide_qkv))
    grad_input = to_low(grad_residual + back_one[0])
    grad_input = moves.from_sequences(grad_input).astype(f32)
    grad_vectors = jnp.stack(
        [
            back_one[1],
            back_one[2],
            column_sum(dq[:, :width]),
            column_sum(d_own[1, :, :width]),
            column_sum(grad_branch),
            back_two[1],
            back_two[2],
            grad_bias_two,
        ]
    )

    def by_place(values):
        return jnp.swapaxes(values.reshape(values.shape[0], ctx, -1), 0, 1)

    blocks_down = sum_down.reshape(ratio, rows_d, ctx, cols_d)
    blocks_down = jnp.transpose(blocks_down, (2, 1, 0, 3)).reshape(ctx, rows_d, -1)
    later = jnp.concatenate([by_place(sum_up), blocks_down, by_place(sum_out)], axis=2)
    later = moves.scatter_ctx(later)
    grad_up = later[:, :cols_f]
    grad_down = later[:, cols_f : 2 * cols_f].reshape(rows_d, ratio, cols_d)
    grad_down = jnp.swapaxes(grad_down, 0, 1).reshape(ratio * rows_d, cols_d)
    grad_out = later[:, 2 * cols_f :]
    grad_qkv = moves.scatter_ctx(by_place(sum_qkv))

    tiny = jnp.concatenate([grad_vectors, grad_bias_up.reshape(-1, width)], axis=0)
    tiny = lax.psum(tiny, AXES)
    grad_vectors = lax.dynamic_slice_in_dim(tiny[:8], place * cols_d, cols_d, 1)
    grad_bias = lax.dynamic_slice_in_dim(tiny[8:].reshape(-1), place * cols_f, cols_f)

    factor = clip_limit / jnp.maximum(global_top, clip_limit)
    per_column = jnp.repeat(jnp.sqrt(factor), HD)
    column_scale = jnp.concatenate([per_column, per_column, jnp.ones((width,), f32)])
    local_scale = lax.dynamic_slice_in_dim(column_scale, place * cols_q, cols_q)
    clipped_qkv = to_low(w_qkv.astype(f32) * local_scale[None, :])
    bias_scale = lax.dynamic_slice_in_dim(per_column, place * cols_d, cols_d)
    clipped_bias = to_low(vectors[2].astype(f32) * bias_scale)
    return (
        output,
        grad_input,
        grad_qkv,
        grad_out,
        grad_up,
        grad_down,
        grad_vectors,
        grad_bias,
        clipped_qkv,
        clipped_bias,
        global_top,
    )


def shards(
    dp,
    ctx,
    inputs,
    cotangent,
    w_qkv,
    w_out,
    w_up,
    w_down,
    vectors,
    bias_up,
    segment_ids,
    padding,
    stretch_order,
):
    local_seqs, query_len, width = inputs.shape
    length = segment_ids.shape[1]
    half = length // 2
    heads = width // HD
    wide = (width + LANES - 1) // LANES * LANES
    rows_d = w_qkv.shape[0]
    cols_d = w_out.shape[1]
    cols_f = w_up.shape[1]
    ratio = w_down.shape[0] // rows_d
    hidden_width = cols_f * ctx
    moves = Moves(dp, ctx, local_seqs)
    core, place = moves.core, moves.z

    extra = jnp.concatenate([vectors.reshape(-1, cols_f), bias_up[None]], axis=0)
    first = jnp.concatenate([jnp.concatenate([w_qkv, w_out], axis=1), extra], axis=0)
    first = moves.gather_ctx(first)
    x_flat = moves.to_sequences(inputs).astype(f32)
    down_packed = jnp.swapaxes(w_down.reshape(ratio, rows_d, cols_d), 0, 1).reshape(rows_d, -1)
    second = moves.gather_ctx(jnp.concatenate([w_up, down_packed], axis=0))
    cot = moves.to_sequences(cotangent)

    def columns(blocks):
        return jnp.swapaxes(blocks, 0, 1).reshape(blocks.shape[1], -1)

    cols_q = w_qkv.shape[1]
    part_qkv = columns(first[:, :rows_d, :cols_q])
    part_out = columns(first[:, :rows_d, cols_q:])
    small = first[:, rows_d:]
    vec_rows = columns(small[:, :-1].reshape(ctx, 8, cols_d)).astype(f32)
    bias_row = small[:, -1].reshape(-1).astype(f32)
    part_up = columns(second[:, :rows_d])
    part_down = second[:, rows_d:].reshape(ctx, rows_d, ratio, cols_d)
    part_down = jnp.transpose(part_down, (2, 1, 0, 3)).reshape(ratio * rows_d, width)

    wide_qkv = moves.gather_dp(part_qkv)
    wide_out = moves.gather_dp(part_out)
    wide_up = moves.gather_dp(part_up)
    wide_down = moves.gather_dp(part_down)

    info = jnp.stack([segment_ids, padding], axis=0)
    info_there = moves.swap_core(info)
    info = jnp.where(place // local_seqs == core, info, info_there)
    info = lax.dynamic_index_in_dim(info, place % local_seqs, 1, False)
    stretches = stretch_order.shape[0]
    stretch_len = length // stretches
    info = jnp.take(info.reshape(2, stretches, stretch_len), stretch_order, axis=1)
    positions = stretch_order[:, None] * stretch_len + jnp.arange(stretch_len, dtype=jnp.int32)
    code = (info[0] * (2 * length) + positions).reshape(2, half)
    reach = (info[1] * (length - 1)).reshape(2, half)
    code_own = lax.dynamic_index_in_dim(code, core, 0, False)
    code_sib = lax.dynamic_index_in_dim(code, 1 - core, 0, False)
    reach_own = lax.dynamic_index_in_dim(reach, core, 0, False)
    reach_sib = lax.dynamic_index_in_dim(reach, 1 - core, 0, False)
    kinfo = jnp.stack(
        [jnp.concatenate([code_own, code_sib]), jnp.concatenate([reach_own, reach_sib])], axis=1
    )
    qinfo = code_own[None]

    normed = to_low(layer_norm(x_flat, vec_rows[0], vec_rows[1]))
    projected = product(normed, wide_qkv)

    def padded(values):
        return jnp.pad(to_low(values), ((0, 0), (0, wide - width)))

    queries = padded(projected[:, :width] + vec_rows[2])
    own = jnp.stack(
        [
            padded(projected[:, width : 2 * width]),
            padded(projected[:, 2 * width :] + vec_rows[3]),
        ]
    )
    sib = moves.swap_core(own)
    attended, lse, tops = attend_forward(heads, kinfo, qinfo, queries, own, sib)
    attended = attended[:, :width]
    block_top = jnp.max(tops, axis=2).reshape(-1)[:heads]
    global_top = lax.pmax(block_top, AXES)
    residual = x_flat + product(attended, wide_out) + vec_rows[4]
    normed_two = to_low(layer_norm(residual, vec_rows[5], vec_rows[6]))
    up_pre = product(normed_two, wide_up) + bias_row
    hidden = to_low(jax.nn.gelu(up_pre, approximate=True))
    output = to_low(residual + product(hidden, wide_down) + vec_rows[7])
    output = moves.from_sequences(output)

    grad_output = cot.astype(f32)
    grad_bias_two = column_sum(cot)
    sum_down = moves.weight_terms(hidden, cot)
    sum_down = moves.scatter_dp(sum_down)
    grad_hidden = contract_cols(cot, wide_down)
    unused, gelu_back = jax.vjp(partial(jax.nn.gelu, approximate=True), up_pre)
    grad_pre = to_low(gelu_back(grad_hidden)[0])
    grad_bias_up = column_sum(grad_pre)
    sum_up = moves.weight_terms(normed_two, grad_pre)
    sum_up = moves.scatter_dp(sum_up)
    unused, norm_back_two = jax.vjp(layer_norm, residual, vec_rows[5], vec_rows[6])
    back_two = norm_back_two(contract_cols(grad_pre, wide_up))
    grad_residual = grad_output + back_two[0]
    grad_branch = to_low(grad_residual)
    sum_out = moves.weight_terms(attended, grad_branch)
    sum_out = moves.scatter_dp(sum_out)
    grad_attended = padded(contract_cols(grad_branch, wide_out))
    dq, d_own, d_sib = attend_backward(
        heads, kinfo, qinfo, queries, own, sib, grad_attended, lse
    )
    d_came = moves.swap_core(d_sib)
    d_own = to_low(d_own.astype(f32) + d_came.astype(f32))
    grad_proj = jnp.concatenate([dq[:, :width], d_own[0, :, :width], d_own[1, :, :width]], axis=1)
    sum_qkv = moves.weight_terms(normed, grad_proj)
    sum_qkv = moves.scatter_dp(sum_qkv)
    unused, norm_back_one = jax.vjp(layer_norm, x_flat, vec_rows[0], vec_rows[1])
    back_one = norm_back_one(contract_cols(grad_proj, wide_qkv))
    grad_input = to_low(grad_residual + back_one[0])
    grad_input = moves.from_sequences(grad_input).astype(f32)
    grad_vectors = jnp.stack(
        [
            back_one[1],
            back_one[2],
            column_sum(dq[:, :width]),
            column_sum(d_own[1, :, :width]),
            column_sum(grad_branch),
            back_two[1],
            back_two[2],
            grad_bias_two,
        ]
    )

    def by_place(values):
        return jnp.swapaxes(values.reshape(values.shape[0], ctx, -1), 0, 1)

    blocks_down = sum_down.reshape(ratio, rows_d, ctx, cols_d)
    blocks_down = jnp.transpose(blocks_down, (2, 1, 0, 3)).reshape(ctx, rows_d, -1)
    later = jnp.concatenate([by_place(sum_up), blocks_down, by_place(sum_out)], axis=2)
    later = moves.scatter_ctx(later)
    grad_up = later[:, :cols_f]
    grad_down = later[:, cols_f : 2 * cols_f].reshape(rows_d, ratio, cols_d)
    grad_down = jnp.swapaxes(grad_down, 0, 1).reshape(ratio * rows_d, cols_d)
    grad_out = later[:, 2 * cols_f :]
    grad_qkv = moves.scatter_ctx(by_place(sum_qkv))

    tiny = jnp.concatenate([grad_vectors, grad_bias_up.reshape(-1, width)], axis=0)
    tiny = lax.psum(tiny, AXES)
    grad_vectors = lax.dynamic_slice_in_dim(tiny[:8], place * cols_d, cols_d, 1)
    grad_bias = lax.dynamic_slice_in_dim(tiny[8:].reshape(-1), place * cols_f, cols_f)

    factor = clip_limit / jnp.maximum(global_top, clip_limit)
    per_column = jnp.repeat(jnp.sqrt(factor), HD)
    column_scale = jnp.concatenate([per_column, per_column, jnp.ones((width,), f32)])
    local_scale = lax.dynamic_slice_in_dim(column_scale, place * cols_q, cols_q)
    clipped_qkv = to_low(w_qkv.astype(f32) * local_scale[None, :])
    bias_scale = lax.dynamic_slice_in_dim(per_column, place * cols_d, cols_d)
    clipped_bias = to_low(vectors[2].astype(f32) * bias_scale)
    return (
        output,
        grad_input,
        grad_qkv,
        grad_out,
        grad_up,
        grad_down,
        grad_vectors,
        grad_bias,
        clipped_qkv,
        clipped_bias,
        global_top,
    )


def solution(mesh):
    dp, ctx = mesh.shape["dp"], mesh.shape["ctx"]
    body = fast_shards if (dp, ctx) == (8, 4) else shards
    return jax.shard_map(
        partial(body, dp, ctx),
        mesh=mesh,
        in_specs=(
            P("dp", "ctx", None),
            P("dp", "ctx", None),
            P("dp", "ctx"),
            P("dp", "ctx"),
            P("dp", "ctx"),
            P("dp", "ctx"),
            P(None, "ctx"),
            P("ctx"),
            P("dp", None),
            P("dp", None),
            P(),
        ),
        out_specs=(
            P("dp", "ctx", None),
            P("dp", "ctx", None),
            P("dp", "ctx"),
            P("dp", "ctx"),
            P("dp", "ctx"),
            P("dp", "ctx"),
            P(None, "ctx"),
            P("ctx"),
            P("dp", "ctx"),
            P("ctx"),
            P(),
        ),
        check_vma=False,
    )
```

```python
import math
from functools import partial

import jax
import jax.numpy as jnp
from jax import lax
from jax.experimental import pallas as pl
from jax.experimental.pallas import tpu as pltpu
from jax.sharding import PartitionSpec as P

HD = 64
LANES = 128
AXES = ("dp", "ctx")

eps_norm = 1e-05
clip_limit = 5.0
masked_fill = -1e30
f32 = jnp.float32
bf16 = jnp.bfloat16


def layer_norm(values_in, gain_row, shift_row):
    average = jnp.mean(values_in, axis=-1, keepdims=True)
    centred = values_in - average
    variance = jnp.mean(centred * centred, axis=-1, keepdims=True)
    return centred * lax.rsqrt(variance + eps_norm) * gain_row + shift_row


def to_low(values_in):
    return values_in.astype(bf16)


def product(left, right):
    return jnp.dot(left, right, preferred_element_type=f32)


def contract_rows(left, right):
    return lax.dot_general(left, right, (((0,), (0,)), ((), ())), preferred_element_type=f32)


def contract_cols(left, right):
    return lax.dot_general(left, right, (((1,), (1,)), ((), ())), preferred_element_type=f32)


def column_sum(values_in):
    return jnp.sum(values_in.astype(f32), axis=0)


class Moves:
    def __init__(self, dp, ctx, local_seqs):
        self.dp, self.ctx, self.seqs = dp, ctx, local_seqs
        self.d = lax.axis_index("dp")
        self.z = lax.axis_index("ctx")
        self.core = self.d % 2
        self.cube = dp == 8 and ctx == 4
        self.x = (self.d // 2) % 2
        self.y = self.d // 4

    def permute(self, values, target):
        pairs = []
        for d in range(self.dp):
            for z in range(self.ctx):
                there = target(d, z)
                if there is not None:
                    pairs.append((d * self.ctx + z, there[0] * self.ctx + there[1]))
        return lax.ppermute(values, AXES, pairs)

    def swap_core(self, values):
        return self.permute(values, lambda d, z: (d ^ 1, z))

    def swap_x(self, values):
        return self.permute(values, lambda d, z: (d ^ 2, z))

    def swap_y(self, values):
        return self.permute(values, lambda d, z: (d ^ 4, z))

    def up(self, values):
        return self.permute(values, lambda d, z: (d, z + 1) if z + 1 < self.ctx else None)

    def down(self, values):
        return self.permute(values, lambda d, z: (d, z - 1) if z > 0 else None)

    def sequence_target(self, step):
        n = self.seqs

        def target(d, z):
            return (d - d % 2 + z // n, n * (d % 2) + (z + step) % n)

        return target

    def to_sequences(self, values):
        n = self.seqs
        came = []
        for step in range(n):
            block = lax.dynamic_index_in_dim(values, (self.z + step) % n, 0, keepdims=False)
            came.append(self.permute(block, self.sequence_target(step)))
        return jnp.concatenate([self.choose(came, (self.z - t) % n) for t in range(n)], axis=0)

    def from_sequences(self, values):
        n = self.seqs
        parts = values.reshape(n, values.shape[0] // n, values.shape[1])
        came = []
        for step in range(n):
            forward = self.sequence_target(step)
            block = lax.dynamic_index_in_dim(parts, (self.z - step) % n, 0, keepdims=False)
            back = {}
            for d in range(self.dp):
                for z in range(self.ctx):
                    back[forward(d, z)] = (d, z)
            came.append(self.permute(block, lambda d, z: back[(d, z)]))
        return jnp.stack([self.choose(came, (j - self.z) % n) for j in range(n)], axis=0)

    @staticmethod
    def choose(items, index):
        picked = items[0]
        for i in range(1, len(items)):
            picked = jnp.where(index == i, items[i], picked)
        return picked

    def gather_ctx(self, block):
        if not self.cube:
            return lax.all_gather(block, "ctx", axis=0, tiled=False)
        rising, falling = [block], [block]
        for _ in range(self.ctx - 1):
            rising.append(self.up(rising[-1]))
            falling.append(self.down(falling[-1]))
        line = jnp.stack(rising[:0:-1] + falling, axis=0)
        return lax.dynamic_slice_in_dim(line, self.ctx - 1 - self.z, self.ctx, 0)

    def gather_dp(self, block):
        if not self.cube:
            return lax.all_gather(block, "dp", axis=0, tiled=True)
        rows, cols = block.shape
        half = (cols // 2 + LANES - 1) // LANES * LANES
        from_x, from_y = self.swap_x(block), self.swap_y(block)
        far = jnp.concatenate(
            [self.swap_y(from_x[:, :half]), self.swap_x(from_y[:, half:])], axis=1
        )
        mine = jnp.zeros((4, rows, cols), block.dtype)
        here = 2 * self.y + self.x
        for step, part in enumerate((block, from_x, from_y, far)):
            mine = lax.dynamic_update_slice(mine, part[None], (here ^ step, 0, 0))
        other = self.swap_core(mine)
        first = jnp.where(self.core == 0, mine, other)
        second = jnp.where(self.core == 0, other, mine)
        return jnp.stack([first, second], axis=1).reshape(8 * rows, cols)

    def scatter_ctx(self, blocks):
        if not self.cube:
            return lax.psum_scatter(blocks, "ctx", scatter_dimension=0, tiled=False).astype(f32)

        def part(index):
            return lax.dynamic_index_in_dim(blocks, jnp.clip(index, 0, self.ctx - 1), 0, False)

        falling = rising = None
        for step in range(self.ctx - 1, 0, -1):
            low, high = part(self.z - step), part(self.z + step)
            if falling is not None:
                low = to_low(low.astype(f32) + falling.astype(f32))
                high = to_low(high.astype(f32) + rising.astype(f32))
            n = self.ctx
            falling = self.permute(
                low, lambda d, z: (d, z - 1) if z - step >= 0 else None
            )
            rising = self.permute(
                high, lambda d, z: (d, z + 1) if z + step < n else None
            )
        return part(self.z).astype(f32) + falling.astype(f32) + rising.astype(f32)

    def weight_terms(self, left, right):
        if not self.cube:
            return to_low(contract_rows(left, right))
        tokens, width = left.shape
        rows = width // self.dp
        parts = left.reshape(tokens, self.dp // 2, 2, rows)
        even = parts[:, :, 0].reshape(tokens, -1)
        odd = parts[:, :, 1].reshape(tokens, -1)
        own = jnp.where(self.core == 0, even, odd)
        sibling = jnp.where(self.core == 0, odd, even)
        came = self.swap_core(to_low(contract_rows(sibling, right)))
        return to_low(contract_rows(own, right) + came.astype(f32))

    def scatter_dp(self, terms):
        if not self.cube:
            return lax.psum_scatter(terms, "dp", scatter_dimension=0, tiled=True)
        rows, cols = terms.shape[0] // 4, terms.shape[1]
        half = (cols // 2 + LANES - 1) // LANES * LANES
        grid = terms.reshape(2, 2, rows, cols)

        def pick(values, index, axis):
            return lax.dynamic_index_in_dim(values, index, axis, False)

        def added(one, two):
            return to_low(one.astype(f32) + two.astype(f32))

        left, right = grid[..., :half], grid[..., half:]
        left_x = self.swap_x(pick(left, 1 - self.x, 1))
        right_y = self.swap_y(pick(right, 1 - self.y, 0))
        left = added(pick(left, self.x, 1), left_x)
        right = added(pick(right, self.y, 0), right_y)
        left_y = self.swap_y(pick(left, 1 - self.y, 0))
        right_x = self.swap_x(pick(right, 1 - self.x, 0))
        left = added(pick(left, self.y, 0), left_y)
        right = added(pick(right, self.x, 0), right_x)
        return jnp.concatenate([left, right], axis=1)


def nt(left, right):
    return lax.dot_general(left, right, (((1,), (1,)), ((), ())), preferred_element_type=f32)


def tn(left, right):
    return lax.dot_general(left, right, (((0,), (0,)), ((), ())), preferred_element_type=f32)


def fill_bias(kinfo_ref, qinfo_ref, bias_ref):
    diff = qinfo_ref[0:1, :] - kinfo_ref[:, 0:1]
    fine = (diff >= 0) & (diff <= kinfo_ref[:, 1:2])
    bias_ref[...] = jnp.where(fine, 0.0, masked_fill)


def attend_forward_kernel(
    heads, kinfo_ref, qinfo_ref, q_ref, own_ref, sib_ref, out_ref, lse_ref, top_ref, bias_ref
):
    step = pl.program_id(0)

    @pl.when(step == 0)
    def _():
        fill_bias(kinfo_ref, qinfo_ref, bias_ref)

    keys = jnp.concatenate([own_ref[0], sib_ref[0]], axis=0)
    values = jnp.concatenate([own_ref[1], sib_ref[1]], axis=0)
    queries = q_ref[...]
    lane = lax.broadcasted_iota(jnp.int32, queries.shape, 1)
    outs = []
    for side in range(2):
        mine = (lane >= HD) if side else (lane < HD)
        picked = jnp.where(mine, queries, jnp.zeros_like(queries)) * bf16(HD**-0.5)
        scores = nt(keys, picked) + bias_ref[...]
        top = jnp.max(scores, axis=0, keepdims=True)
        weights = jnp.exp(scores - top)
        total = jnp.sum(weights, axis=0, keepdims=True)
        mixed = tn(values[:, side * HD : (side + 1) * HD], weights.astype(bf16))
        outs.append(mixed * (1.0 / total))
        lse_ref[0, side : side + 1, :] = top + jnp.log(total)
        top_ref[0, side : side + 1, :] = top
    out_ref[...] = jnp.concatenate(outs, axis=0).T.astype(bf16)


def attend_backward_kernel(
    heads,
    kinfo_ref,
    qinfo_ref,
    q_ref,
    own_ref,
    sib_ref,
    grad_ref,
    lse_ref,
    dq_ref,
    down_ref,
    dsib_ref,
    bias_ref,
):
    step = pl.program_id(0)

    @pl.when(step == 0)
    def _():
        fill_bias(kinfo_ref, qinfo_ref, bias_ref)

    keys = jnp.concatenate([own_ref[0], sib_ref[0]], axis=0)
    values = jnp.concatenate([own_ref[1], sib_ref[1]], axis=0)
    queries, grads = q_ref[...], grad_ref[...]
    half = queries.shape[0]
    lane = lax.broadcasted_iota(jnp.int32, queries.shape, 1)
    dqs, dk, dv = [], 0.0, 0.0
    for side in range(2):
        mine = (lane >= HD) if side else (lane < HD)
        picked = jnp.where(mine, queries, jnp.zeros_like(queries)) * bf16(HD**-0.5)
        grad = jnp.where(mine, grads, jnp.zeros_like(grads))
        scores = nt(keys, picked) + bias_ref[...]
        weights = jnp.exp(scores - lse_ref[0, side : side + 1, :])
        dp = nt(values, grad)
        delta = jnp.sum(weights * dp, axis=0, keepdims=True)
        ds = (weights * (dp - delta)).astype(bf16)
        dqs.append(tn(keys[:, side * HD : (side + 1) * HD], ds) * (HD**-0.5))
        dk = dk + product(ds, picked)
        dv = dv + product(weights.astype(bf16), grad)
    dq_ref[...] = jnp.concatenate(dqs, axis=0).T.astype(bf16)
    dk, dv = dk.astype(bf16), dv.astype(bf16)
    down_ref[0] = dk[:half]
    dsib_ref[0] = dk[half:]
    down_ref[1] = dv[:half]
    dsib_ref[1] = dv[half:]


def pair_specs(rows):
    flat = pl.BlockSpec((rows, LANES), lambda i: (0, i))
    double = pl.BlockSpec((2, rows, LANES), lambda i: (0, 0, i))
    per_head = pl.BlockSpec((1, 2, rows), lambda i: (i, 0, 0))
    return flat, double, per_head


def attend_forward(heads, kinfo, qinfo, queries, own, sib):
    rows, width = queries.shape
    pairs = width // LANES
    flat, double, per_head = pair_specs(rows)
    small = jax.ShapeDtypeStruct((pairs, 2, rows), f32)
    return pl.pallas_call(
        partial(attend_forward_kernel, heads),
        grid=(pairs,),
        in_specs=[
            pl.BlockSpec(kinfo.shape, lambda i: (0, 0)),
            pl.BlockSpec(qinfo.shape, lambda i: (0, 0)),
            flat,
            double,
            double,
        ],
        out_specs=[flat, per_head, per_head],
        out_shape=[jax.ShapeDtypeStruct((rows, width), bf16), small, small],
        scratch_shapes=[pltpu.VMEM((2 * rows, rows), f32)],
        compiler_params=pltpu.CompilerParams(vmem_limit_bytes=48 * 2**20),
        cost_estimate=pl.CostEstimate(
            flops=pairs * 16 * rows * rows * LANES,
            bytes_accessed=rows * width * 12,
            transcendentals=pairs * 4 * rows * rows,
        ),
        name="attend_forward",
    )(kinfo, qinfo, queries, own, sib)


def attend_backward(heads, kinfo, qinfo, queries, kv, grad, lse):
    rows, width = queries.shape
    pairs = width // LANES
    flat, double, per_head = pair_specs(rows)
    both = jax.ShapeDtypeStruct((2, rows, width), bf16)
    return pl.pallas_call(
        partial(attend_backward_kernel, heads),
        grid=(pairs,),
        in_specs=[
            pl.BlockSpec(kinfo.shape, lambda i: (0, 0)),
            pl.BlockSpec(qinfo.shape, lambda i: (0, 0)),
            flat,
            double,
            pl.BlockSpec((2, rows, LANES), lambda i: (0, 1, i)),
            flat,
            per_head,
        ],
        out_specs=[flat, double, double],
        out_shape=[jax.ShapeDtypeStruct((rows, width), bf16), both, both],
        scratch_shapes=[pltpu.VMEM((2 * rows, rows), f32)],
        compiler_params=pltpu.CompilerParams(vmem_limit_bytes=48 * 2**20),
        cost_estimate=pl.CostEstimate(
            flops=pairs * 40 * rows * rows * LANES,
            bytes_accessed=rows * width * 22,
            transcendentals=pairs * 4 * rows * rows,
        ),
        name="attend_backward",
    )(kinfo, qinfo, queries, kv, kv, grad, lse)


MESH = pl.DeviceIdType.MESH


class Sizes:
    def __init__(self, width, hidden, ctx, dp, length):
        self.width = width
        self.wide = -(-width // LANES) * LANES
        self.ctx = ctx
        self.rows = 2 * width // dp
        self.qkv = 3 * width // ctx
        self.out = width // ctx
        self.cols = -(-(self.qkv + self.out) // LANES) * LANES
        self.up = hidden // ctx
        self.half = length // 2
        self.pairs = self.wide // LANES
        self.out_tile = self.qkv // LANES * LANES
        self.qkv_cols = 1024
        self.qkv_pad = -(-self.qkv // LANES) * LANES

    def qkv_runs(self, z):
        runs, at = [], z * self.qkv
        end = at + self.qkv
        while at < end:
            kind = at // self.width
            stop = min(end, (kind + 1) * self.width)
            runs.append((at - z * self.qkv, kind * self.wide + at - kind * self.width, stop - at))
            at = stop
        return runs


class Net:
    def __init__(self):
        self.d = lax.axis_index("dp")
        self.z = lax.axis_index("ctx")
        self.c = self.d % 2
        self.p = self.d // 2
        y, x = self.p // 2, self.p % 2
        self.px, self.py, self.pd = 2 * y + 1 - x, 2 * (1 - y) + x, 2 * (1 - y) + 1 - x
        self.x_to = (2 * self.px + self.c, self.z)
        self.y_to = (2 * self.py + self.c, self.z)
        self.sib = (2 * self.p + 1 - self.c, self.z)
        self.near = self.c + 2 * (self.z // 2)
        self.far = self.c + 2 * (1 - self.z // 2)


def enter(net):
    gate = pltpu.get_barrier_semaphore()
    for c in range(2):
        for z in range(4):

            @pl.when((c != net.c) | (z != net.z))
            def _():
                pl.semaphore_signal(gate, inc=1, device_id=(2 * net.p + c, z), device_id_type=MESH)

    for to in (net.x_to, net.y_to):
        pl.semaphore_signal(gate, inc=1, device_id=to, device_id_type=MESH)
    pl.semaphore_wait(gate, 9)


class Gather:
    def __init__(self, net, sizes, w, own, swapped, sems):
        self.n, self.s, self.w, self.own, self.swapped = net, sizes, w, own, swapped
        self.zs, self.zr, self.hs, self.hr, self.cs, self.cr, self.loc = sems

    def at(self, p, z):
        r, c = (z, p) if self.swapped else (p, z)
        s = self.s
        return self.w.at[
            pl.ds(pl.multiple_of(r * s.rows, 16), s.rows),
            pl.ds(pl.multiple_of(c * s.cols, LANES), s.cols),
        ]

    def copy(self, p, z, send, recv, to):
        block = self.at(p, z)
        return pltpu.make_async_remote_copy(
            block, block, send, recv, device_id=to, device_id_type=MESH
        )

    def zcopy(self, z, up):
        n = self.n
        to = (n.d, n.z + 1 if up else n.z - 1)
        return self.copy(n.p, z, self.zs.at[z // 2, int(up)], self.zr.at[z // 2], to)

    def hop(self, p, z, to, k):
        return self.copy(p, z, self.hs.at[z // 2, k], self.hr.at[z // 2, k], to)

    def across(self, p, z):
        return self.copy(p, z, self.cs.at[p, z // 2], self.cr.at[p, z // 2], self.n.sib)

    def begin(self):
        n = self.n

        @pl.when(n.z % 2 == n.c)
        def _():
            local = pltpu.make_async_copy(self.own, self.at(n.p, n.z), self.loc)
            local.start()
            local.wait()

            @pl.when(n.z < 3)
            def _():
                self.zcopy(n.z, True).start()

            @pl.when(n.z > 0)
            def _():
                self.zcopy(n.z, False).start()

    def arrive(self, z):
        n = self.n

        @pl.when(z != n.z)
        def _():
            self.zcopy(z, True).wait_recv()

            @pl.when((z < n.z) & (n.z < 3))
            def _():
                self.zcopy(z, True).start()

            @pl.when((z > n.z) & (n.z > 0))
            def _():
                self.zcopy(z, False).start()

        self.hop(n.p, z, n.x_to, 0).start()
        self.hop(n.p, z, n.y_to, 1).start()
        self.across(n.p, z).start()

    def turn(self, z):
        n = self.n
        self.hop(n.px, z, n.x_to, 0).wait_recv()

        @pl.when(z < 2)
        def _():
            self.hop(n.px, z, n.y_to, 2).start()

        self.across(n.px, z).start()
        self.hop(n.py, z, n.y_to, 1).wait_recv()

        @pl.when(z >= 2)
        def _():
            self.hop(n.py, z, n.x_to, 2).start()

        self.across(n.py, z).start()

    def last(self, z):
        n = self.n
        self.hop(n.pd, z, n.x_to, 2).wait_recv()
        self.across(n.pd, z).start()

    def ready(self):
        n = self.n
        for half in range(2):
            for p in range(4):
                self.across(p, 1 - n.c + 2 * half).wait_recv()

    def drain(self):
        n = self.n
        for half in range(2):
            z = n.c + 2 * half

            @pl.when((z <= n.z) & (n.z < 3))
            def _():
                self.zcopy(z, True).wait_send()

            @pl.when((z >= n.z) & (n.z > 0))
            def _():
                self.zcopy(z, False).wait_send()

            for k, to in enumerate((n.x_to, n.y_to, n.x_to)):
                self.hop(n.p, z, to, k).wait_send()
            for p in range(4):
                self.across(p, z).wait_send()


def gather_sems():
    dma = pltpu.SemaphoreType.DMA
    return [dma((2, 2)), dma((2,)), dma((2, 3)), dma((2, 3)), dma((4, 2)), dma((4, 2)), dma]


class ToSequences:
    def __init__(self, net, src, dst, sems):
        self.n, self.src, self.dst = net, src, dst
        self.ss, self.rs = sems
        self.rows = src.shape[1]

    def parts(self):
        n = self.n
        for j in range(2):
            to = (2 * n.p + n.z // 2, 2 * n.c + j)
            yield j, to, (to[0] == n.d) & (to[1] == n.z)

    def place(self, t):
        return self.dst.at[pl.ds(pl.multiple_of(t * self.rows, 16), self.rows)]

    def remote(self, j, to):
        t = self.n.z % 2
        return pltpu.make_async_remote_copy(
            self.src.at[j],
            self.place(t),
            self.ss.at[j],
            self.rs.at[t],
            device_id=to,
            device_id_type=MESH,
        )

    def start(self):
        for j, to, here in self.parts():

            @pl.when(here)
            def _():
                t = self.n.z % 2
                pltpu.make_async_copy(self.src.at[j], self.place(t), self.rs.at[t]).start()

            @pl.when(jnp.logical_not(here))
            def _():
                self.remote(j, to).start()

    def wait(self):
        for t in range(2):
            pltpu.make_async_copy(self.src.at[0], self.place(t), self.rs.at[t]).wait()

    def drain(self):
        for j, to, here in self.parts():

            @pl.when(jnp.logical_not(here))
            def _():
                self.remote(j, to).wait_send()


class FromSequences:
    def __init__(self, net, src, dst, sems):
        self.n, self.src, self.dst = net, src, dst
        self.ss, self.rs = sems
        self.rows = dst.shape[1]

    def parts(self):
        n = self.n
        for t in range(2):
            to = (2 * n.p + n.z // 2, 2 * n.c + t)
            yield t, to, (to[0] == n.d) & (to[1] == n.z)

    def piece(self, t):
        return self.src.at[pl.ds(t * self.rows, self.rows)]

    def remote(self, t, to):
        j = self.n.z % 2
        return pltpu.make_async_remote_copy(
            self.piece(t),
            self.dst.at[j],
            self.ss.at[t],
            self.rs.at[j],
            device_id=to,
            device_id_type=MESH,
        )

    def start(self):
        for t, to, here in self.parts():

            @pl.when(here)
            def _():
                j = self.n.z % 2
                pltpu.make_async_copy(self.piece(t), self.dst.at[j], self.rs.at[j]).start()

            @pl.when(jnp.logical_not(here))
            def _():
                self.remote(t, to).start()

    def wait(self):
        for j in range(2):
            pltpu.make_async_copy(self.piece(0), self.dst.at[j], self.rs.at[j]).wait()

    def drain(self):
        for t, to, here in self.parts():

            @pl.when(jnp.logical_not(here))
            def _():
                self.remote(t, to).wait_send()


def by_rows(total, step, body):
    def one(i, carry):
        body(pl.ds(pl.multiple_of(i * step, step), step))
        return carry

    lax.fori_loop(0, total // step, one, 0)


def by_columns(total, body, step=256):
    def one(i, carry):
        body(pl.multiple_of(i * step, LANES), step)
        return carry

    lax.fori_loop(0, total // step, one, 0)
    if total % step:
        body(total // step * step, total % step)


def normalised(values):
    average = jnp.mean(values, axis=-1, keepdims=True)
    centred = values - average
    variance = jnp.mean(centred * centred, axis=-1, keepdims=True)
    return centred * lax.rsqrt(variance + eps_norm)


def place_run(block, source, phase, count):
    moved = pltpu.roll(block, (phase - source) % block.shape[1], axis=1)
    tiles = -(-(phase + count) // LANES) * LANES
    moved = moved[:, :tiles]
    lane = lax.broadcasted_iota(jnp.int32, moved.shape, 1)
    return jnp.where((lane >= phase) & (lane < phase + count), moved, 0.0)


def attend_pair(s, i, q_ref, kv_ref, bias_ref, att_ref, lse_ref, top_ref):
    lanes = pl.ds(pl.multiple_of(i * LANES, LANES), LANES)
    keys, values, queries = kv_ref[0, :, lanes], kv_ref[1, :, lanes], q_ref[:, lanes]
    lane = lax.broadcasted_iota(jnp.int32, queries.shape, 1)
    outs = []
    for side in range(2):
        mine = (lane >= HD) if side else (lane < HD)
        picked = jnp.where(mine, queries, jnp.zeros_like(queries)) * bf16(HD**-0.5)
        scores = nt(keys, picked) + bias_ref[...]
        top = jnp.max(scores, axis=0, keepdims=True)
        weights = jnp.exp(scores - top)
        total = jnp.sum(weights, axis=0, keepdims=True)
        mixed = tn(values[:, side * HD : (side + 1) * HD], weights.astype(bf16))
        outs.append(mixed * (1.0 / total))
        lse_ref[i, side : side + 1, :] = top + jnp.log(total)
        top_ref[i, side : side + 1, :] = top
    att_ref[:, lanes] = jnp.concatenate(outs, axis=0).T.astype(bf16)


def forward_plan(A, B, C, near, far, seq_x, seq_cot):
    def do(method, *args):
        return partial(method, *args)

    return {
        ("start", 0): (
            do(A.arrive, near),
            do(B.begin),
            do(A.arrive, far),
            do(seq_x.start),
        ),
        ("vectors", 0): (
            do(A.turn, near),
            do(B.arrive, near),
            do(C.begin),
            do(A.turn, far),
            do(A.last, near),
            do(B.arrive, far),
            do(A.last, far),
        ),
        ("normed", 0): (do(B.turn, near),),
        ("project", 1): (do(C.arrive, near),),
        ("share", 0): (do(B.turn, far), do(B.last, near)),
        ("pair", 0): (do(C.arrive, far), do(seq_cot.start)),
        ("pair", 2): (do(B.last, far), do(C.turn, near)),
        ("pair", 6): (do(C.turn, far), do(C.last, near)),
        ("down", 0): (do(C.last, far),),
    }


def forward_kernel(s, *refs):
    (own_a, own_b, own_c, small, inp, cot, kinfo, qinfo) = refs[:8]
    (wa, wb, wc, x_o, cot_o, vec, normed_o, q_o, kv_o, att_o, res_o, two_o, slope_o, hid_o) = refs[8:22]
    (lse, top, out_o) = refs[22:25]
    (x, normed, pre, q, kv, bias, att, res, two, slope, hid, wt, ct, out, smalls) = refs[25:40]
    sems = refs[40:]
    net = Net()
    A, B, C = [
        Gather(net, s, w, own, swapped, sems[7 * g : 7 * g + 7])
        for g, (w, own, swapped) in enumerate(
            ((wa, own_a, False), (wb, own_b, False), (wc, own_c, True))
        )
    ]
    seq_x = ToSequences(net, inp, x, sems[21:23])
    seq_cot = ToSequences(net, cot, cot_o, sems[23:25])
    small_s, small_r, kv_s, kv_r, load, save = sems[25:31]
    near, far = net.near, net.far
    saves = []

    def keep(src, dst):
        copy = pltpu.make_async_copy(src, dst, save.at[len(saves)])
        copy.start()
        saves.append(copy)

    def small_copy(z):
        return pltpu.make_async_remote_copy(
            small,
            smalls.at[net.z],
            small_s.at[z],
            small_r.at[net.z],
            device_id=(net.d, z),
            device_id_type=MESH,
        )

    plan = forward_plan(A, B, C, near, far, seq_x, seq_cot)

    def at(name, step=0):
        for act in plan.get((name, step), ()):
            act()

    enter(net)
    A.begin()
    for z in range(4):

        @pl.when(z != net.z)
        def _():
            small_copy(z).start()

        @pl.when(z == net.z)
        def _():
            pltpu.make_async_copy(small, smalls.at[z], small_r.at[z]).start()

    at("start")
    diff = qinfo[0:1, :] - kinfo[:, 0:1]
    fine = (diff >= 0) & (diff <= kinfo[:, 1:2])
    bias[...] = jnp.where(fine, 0.0, masked_fill)
    pre[...] = jnp.zeros_like(pre)
    at("vectors")

    for z in range(4):
        pltpu.make_async_copy(small, smalls.at[z], small_r.at[z]).wait()
    row = lax.broadcasted_iota(jnp.int32, (3 * LANES, s.wide), 0)
    col = lax.broadcasted_iota(jnp.int32, (3 * LANES, s.wide), 1)
    rows = 0.0
    for z in range(4):
        spread = jnp.where((col == row + z * s.out) & (row < s.out), 1.0, 0.0).astype(bf16)
        rows = rows + product(smalls[z, :, : 3 * LANES], spread)
    vec[...] = rows

    seq_x.wait()
    keep(x, x_o)
    by_rows(
        s.half,
        LANES,
        lambda r: normed.__setitem__(
            (r, slice(None)),
            to_low(
                normalised(x[r, :].astype(f32)) * vec[0:1, : s.width] + vec[1:2, : s.width]
            ),
        ),
    )
    keep(normed, normed_o)
    at("normed")
    A.ready()

    def tile_a(z):
        return pltpu.make_async_copy(
            wa.at[:, pl.ds(z * s.cols, s.cols)], wt.at[z % 2], load.at[z % 2]
        )

    def tile_b(z):
        return pltpu.make_async_copy(
            wb.at[:, pl.ds(z * s.cols, s.cols)], wt.at[z % 2], load.at[z % 2]
        )

    tile_a(0).start()
    for z in range(4):
        if z < 3:
            tile_a(z + 1).start()
        tile_a(z).wait()

        def part(start, size):
            res[:, pl.ds(start, size)] = product(normed[...], wt[z % 2, :, pl.ds(start, size)])

        by_columns(s.qkv_cols, part)
        for source, target, count in s.qkv_runs(z):
            base = target // LANES * LANES
            moved = place_run(res[:, : s.qkv_cols], source, target - base, count)
            pre[:, base : base + moved.shape[1]] += moved
        at("project", z)
    tile_a(0).start()
    kv[0, : s.half, :] = to_low(pre[:, s.wide : 2 * s.wide])
    kv[1, : s.half, :] = to_low(pre[:, 2 * s.wide :] + vec[3:4, :])
    share = pltpu.make_async_remote_copy(
        kv.at[:, pl.ds(0, s.half)],
        kv.at[:, pl.ds(s.half, s.half)],
        kv_s,
        kv_r,
        device_id=net.sib,
        device_id_type=MESH,
    )
    share.start()
    q[...] = to_low(pre[:, : s.wide] + vec[2:3, :])
    at("share")
    share.wait()
    keep(q, q_o)
    keep(kv, kv_o)

    def pair(i, carry):
        attend_pair(s, i, q, kv, bias, att, lse, top)

        for k in range(s.pairs):
            if ("pair", k) in plan:
                pl.when(i == k)(partial(at, "pair", k))
        return carry

    lax.fori_loop(0, s.pairs, pair, 0)
    keep(att, att_o)

    res[...] = jnp.zeros_like(res)
    for z in range(4):
        if z < 3:
            tile_a(z + 1).start()
        tile_a(z).wait()
        block = product(att[:, : s.width], wt[z % 2, :, s.out_tile :])
        target = z * s.out
        base = target // LANES * LANES
        moved = place_run(block, s.qkv - s.out_tile, target - base, s.out)
        res[:, base : base + moved.shape[1]] += moved
    at("second")
    B.ready()
    tile_b(0).start()

    def second(r):
        total = res[r, : s.width] + x[r, :].astype(f32) + vec[4:5, : s.width]
        res[r, : s.width] = total
        two[r, :] = to_low(normalised(total) * vec[5:6, : s.width] + vec[6:7, : s.width])

    by_rows(s.half, LANES, second)
    keep(res, res_o)
    keep(two, two_o)

    for z in range(4):
        if z < 3:
            tile_b(z + 1).start()
        tile_b(z).wait()

        def part(start, size):
            u = product(two[...], wt[z % 2, :, pl.ds(start, size)])
            u = u + smalls[z, 8:9, pl.ds(start, size)].astype(f32)
            inner = math.sqrt(2 / math.pi) * (u + 0.044715 * u * u * u)
            t = jnp.tanh(inner)
            bend = math.sqrt(2 / math.pi) * (1 + 3 * 0.044715 * u * u)
            lanes = pl.ds(pl.multiple_of(z * s.cols + start, LANES), size)
            hid[:, lanes] = to_low(0.5 * u * (1 + t))
            slope[:, lanes] = to_low(0.5 * (1 + t) + 0.5 * u * (1 - t * t) * bend)

        by_columns(s.cols, part)
        at("up", z)
    keep(hid, hid_o)
    keep(slope, slope_o)
    at("down")
    C.ready()

    def tile_c(k):
        count = min(3 * LANES, s.width - k * 3 * LANES)
        return pltpu.make_async_copy(
            wc.at[pl.ds(k * 3 * LANES, count)], ct.at[k % 2, pl.ds(0, count)], load.at[k % 2]
        )

    tile_c(0).start()
    for k in range(3):
        if k < 2:
            tile_c(k + 1).start()
        tile_c(k).wait()
        at, count = k * 3 * LANES, min(3 * LANES, s.width - k * 3 * LANES)
        block = nt(hid[...], ct[k % 2, :count, :])
        total = res[:, at : at + count] + block + vec[7:8, at : at + count]
        out[:, at : at + count] = to_low(total)
    keep(out, out_o)
    seq_cot.wait()
    for group in (A, B, C):
        group.drain()
    for z in range(4):

        @pl.when(z != net.z)
        def _():
            small_copy(z).wait_send()

    seq_x.drain()
    seq_cot.drain()
    for copy in saves:
        copy.wait()


def forward_call(s, own_a, own_b, own_c, small, inp, cot, kinfo, qinfo):
    dma = pltpu.SemaphoreType.DMA
    rows = s.half
    full = s.ctx * s.cols

    def low(*shape):
        return jax.ShapeDtypeStruct(shape, bf16)

    def high(*shape):
        return jax.ShapeDtypeStruct(shape, f32)

    out_shape = [low(s.width, full)] * 3 + [
        low(rows, s.width),
        low(rows, s.width),
        high(16, s.wide),
        low(rows, s.width),
        low(rows, s.wide),
        low(2, 2 * rows, s.wide),
        low(rows, s.wide),
        high(rows, s.wide),
        low(rows, s.width),
        low(rows, full),
        low(rows, full),
        high(s.pairs, 2, rows),
        high(s.pairs, 2, rows),
        low(rows, s.width),
    ]
    anywhere = pl.BlockSpec(memory_space=pl.ANY)
    local = pl.BlockSpec(memory_space=pltpu.VMEM)
    out_specs = [local if i in (5, 14, 15) else anywhere for i in range(len(out_shape))]
    return pl.pallas_call(
        partial(forward_kernel, s),
        out_shape=out_shape,
        in_specs=[anywhere] * 6 + [local] * 2,
        out_specs=out_specs,
        scratch_shapes=[
            pltpu.VMEM((rows, s.width), bf16),
            pltpu.VMEM((rows, s.width), bf16),
            pltpu.VMEM((rows, 3 * s.wide), f32),
            pltpu.VMEM((rows, s.wide), bf16),
            pltpu.VMEM((2, 2 * rows, s.wide), bf16),
            pltpu.VMEM((2 * rows, rows), f32),
            pltpu.VMEM((rows, s.wide), bf16),
            pltpu.VMEM((rows, s.wide), f32),
            pltpu.VMEM((rows, s.width), bf16),
            pltpu.VMEM((rows, full), bf16),
            pltpu.VMEM((rows, full), bf16),
            pltpu.VMEM((2, s.width, s.cols), bf16),
            pltpu.VMEM((2, 3 * LANES, full), bf16),
            pltpu.VMEM((rows, s.width), bf16),
            pltpu.VMEM((4, 16, s.wide), bf16),
        ]
        + gather_sems() * 3
        + [dma((2,))] * 4
        + [dma((4,)), dma((4,)), dma, dma, dma((2,)), dma((12,))],
        compiler_params=pltpu.CompilerParams(
            collective_id=1, has_side_effects=True, vmem_limit_bytes=61 * 2**20
        ),
        name="forward",
    )(own_a, own_b, own_c, small, inp, cot, kinfo, qinfo)


class Scatter:
    def __init__(self, net, s, own, ship, came, first, second, line, total, out, stage, sems):
        self.n, self.s = net, s
        self.own, self.ship_ref, self.came = own, ship, came
        self.first_ref, self.second_ref, self.line = first, second, line
        self.total, self.out, self.stage = total, out, stage
        (self.ps, self.pr, self.fs, self.fr, self.hs, self.hr, self.zs, self.zr, self.ld, self.es, self.er, self.eo) = sems

    def target(self, k):
        return (self.n.far, self.n.near)[k]

    def sibling_target(self, k):
        n = self.n
        return 1 - n.c + 2 * (n.z // 2 if k else 1 - n.z // 2)

    def route(self, k):
        n = self.n
        early = self.target(k) < 2
        one = jnp.where(early, n.py, n.px)
        two = jnp.where(early, n.px, n.py)
        return (one, (2 * one + n.c, n.z)), (two, (2 * two + n.c, n.z))

    def block(self, k, p):
        rows = self.s.rows
        return self.own.at[k, pl.ds(pl.multiple_of(p * rows, 16), rows)]

    def remote(self, src, dst, send, recv, to):
        return pltpu.make_async_remote_copy(
            src, dst, send, recv, device_id=to, device_id_type=MESH
        )

    def panel(self, k):
        return self.remote(
            self.ship_ref.at[k], self.came.at[k], self.ps.at[k], self.pr.at[k], self.n.sib
        )

    def pieces(self, k):
        (one, to), _ = self.route(k)
        for i, p in enumerate((one, self.n.pd)):
            yield self.remote(
                self.block(k, p), self.first_ref.at[k, i], self.fs.at[k, i], self.fr.at[k, i], to
            )

    def piece(self, k):
        _, (two, to) = self.route(k)
        return self.remote(
            self.block(k, two), self.second_ref.at[k], self.hs.at[k], self.hr.at[k], to
        )

    def step(self, k, up):
        n = self.n
        t = self.target(k) // 2
        to = (n.d, n.z + 1 if up else n.z - 1)
        side = 0 if up else 1
        return self.remote(
            self.block(k, n.p), self.line.at[t, side], self.zs.at[k], self.zr.at[t, side], to
        )

    def ship(self, k):
        self.panel(k).start()

    def wait_panel(self, k):
        self.panel(k).wait_recv()

    def start(self, k):
        for copy in self.pieces(k):
            copy.start()

    def add(self, k, p, other):
        rows = self.s.rows

        def some(r):
            at = pl.ds(pl.multiple_of(p * rows + r.start, 16), r.size)
            self.own[k, at, :] = to_low(
                self.own[k, at, :].astype(f32) + other[r, :].astype(f32)
            )

        by_rows(rows, 16, some)

    def turn(self, k):
        for copy in self.pieces(k):
            copy.wait_recv()
        _, (two, _) = self.route(k)
        self.add(k, two, self.first_ref.at[k, 1])
        self.piece(k).start()
        self.add(k, self.n.p, self.first_ref.at[k, 0])

    def land(self, k):
        self.piece(k).wait_recv()
        self.add(k, self.n.p, self.second_ref.at[k])

    def fetch(self, k, side):
        t = self.target(k) // 2
        n = self.n
        block = self.block(k, n.p)
        self.remote(block, self.line.at[t, side], self.zs.at[k], self.zr.at[t, side], n.sib).wait_recv()
        load = pltpu.make_async_copy(self.line.at[t, side], self.stage, self.ld)
        load.start()
        load.wait()

    def along(self, k):
        n, z, t = self.n, self.n.z, self.target(k)

        @pl.when(t < z)
        def _():
            @pl.when(z < 3)
            def _():
                self.fetch(k, 1)
                self.add(k, n.p, self.stage)

            self.step(k, False).start()

        @pl.when(t > z)
        def _():
            @pl.when(z > 0)
            def _():
                self.fetch(k, 0)
                self.add(k, n.p, self.stage)

            self.step(k, True).start()

        if k == 1:

            @pl.when(t == z)
            def _():
                rows = self.s.rows

                def begin(r):
                    at = pl.ds(pl.multiple_of(n.p * rows + r.start, 16), r.size)
                    self.total[r, :] = self.own[k, at, :].astype(f32)

                by_rows(rows, 16, begin)

                def more(r):
                    self.total[r, :] += self.stage[r, :].astype(f32)

                @pl.when(z > 0)
                def _():
                    self.fetch(k, 0)
                    by_rows(rows, 16, more)

                @pl.when(z < 3)
                def _():
                    self.fetch(k, 1)
                    by_rows(rows, 16, more)

                pltpu.make_async_copy(self.total, self.out, self.eo).start()
                self.final().start()

    def final(self):
        return self.remote(self.total, self.out, self.es, self.er, self.n.sib)

    def finish(self, panels=True):
        n = self.n
        mine = n.z % 2 == n.c

        @pl.when(mine)
        def _():
            pltpu.make_async_copy(self.total, self.out, self.eo).wait()
            self.final().wait_send()

        @pl.when(jnp.logical_not(mine))
        def _():
            self.final().wait_recv()

        for k in range(2):
            if panels:
                self.panel(k).wait_send()
            for copy in self.pieces(k):
                copy.wait_send()
            self.piece(k).wait_send()

            @pl.when(self.target(k) != n.z)
            def _():
                self.step(k, True).wait_send()


def scatter_sems():
    dma = pltpu.SemaphoreType.DMA
    return [
        dma((2,)), dma((2,)), dma((2, 2)), dma((2, 2)), dma((2,)), dma((2,)),
        dma((2,)), dma((2, 2)), dma, dma, dma, dma,
    ]


def scatter_scratch(s, groups):
    panels = (2, s.width, s.cols)
    scratch = [pltpu.VMEM(panels, bf16)]
    for group in range(groups):
        scratch += [pltpu.VMEM(panels, bf16)] * (1 if group else 2)
        scratch += [
            pltpu.VMEM((2, 2, s.rows, s.cols), bf16),
            pltpu.VMEM((2, s.rows, s.cols), bf16),
        ]
    return scratch + [pltpu.VMEM((s.rows, s.cols), f32), pltpu.VMEM((s.rows, s.cols), bf16)]


def norm_back(values, grads, gain):
    average = jnp.mean(values, axis=-1, keepdims=True)
    centred = values - average
    variance = jnp.mean(centred * centred, axis=-1, keepdims=True)
    scale = lax.rsqrt(variance + eps_norm)
    n = centred * scale
    gn = grads * gain
    inner = jnp.mean(gn * n, axis=-1, keepdims=True)
    back = scale * (gn - jnp.mean(gn, axis=-1, keepdims=True) - n * inner)
    return back, jnp.sum(grads * n, axis=0, keepdims=True), jnp.sum(grads, axis=0, keepdims=True)


def fetch_all(pairs, sems):
    copies = [pltpu.make_async_copy(src, dst, sems.at[i]) for i, (src, dst) in enumerate(pairs)]
    for copy in copies:
        copy.start()
    return copies


def middle_kernel(s, *refs):
    (wa, wb, wc, cot_i, res_i, two_i, slope_i, hid_i, out_i, vec) = refs[:10]
    (down_o, up_o, gres_o, branch_o, gatt_o, oz_o, sums, back_o, line_c, line_b) = refs[10:20]
    (cot, res, two, gp, hid, cot_t, two_t, wt, acc, branch, oz) = refs[20:31]
    (ship, own_c, came, first_c, second_c, own_b, first_b, second_b, total, stage) = refs[31:41]
    sems = refs[41:]
    net = Net()
    C = Scatter(net, s, own_c, ship, came, first_c, second_c, line_c, total, down_o, stage, sems[:12])
    B = Scatter(net, s, own_b, ship, came, first_b, second_b, line_b, total, up_o, stage, sems[12:24])
    seq_out = FromSequences(net, out_i, back_o, sems[24:26])
    load, tiles, save, credit = sems[26:30]
    loads = fetch_all(
        ((cot_i, cot), (hid_i, hid), (slope_i, gp), (two_i, two), (res_i, res)), load
    )
    enter(net)
    seq_out.start()

    def tile(w, j, first=0):
        lanes = pl.ds(j * s.cols + first, s.cols - first)
        return pltpu.make_async_copy(
            w.at[:, lanes], wt.at[j % 2, :, pl.ds(0, s.cols - first)], tiles.at[j % 2]
        )

    tile(wc, 0).start()
    loads[0].wait()
    cot_t[...] = cot[...].T
    loads[1].wait()
    sums[...] = jnp.zeros_like(sums)

    def down_panel(z, dst, k, came=None):
        rows = pl.ds(pl.multiple_of(z * s.rows, 16), s.rows)
        for p in range(4):
            at = slice(p * s.rows, (p + 1) * s.rows)

            def part(start, size):
                lanes = pl.ds(start, size)
                many = pl.ds(pl.multiple_of(p * s.cols + start, LANES), size)
                value = product(cot_t[rows, :], hid[:, many])
                if came is not None:
                    value = value + came[k, at, lanes].astype(f32)
                dst[k, at, lanes] = to_low(value)

            by_columns(s.cols, part)

    def up_panel(z, dst, k, came=None):
        def part(start, size):
            lanes = pl.ds(start, size)
            many = pl.ds(pl.multiple_of(z * s.cols + start, LANES), size)
            value = product(two_t[...], gp[:, many])
            if came is not None:
                value = value + came[k, :, lanes].astype(f32)
            dst[k, :, lanes] = to_low(value)

        by_columns(s.cols, part)

    for k in range(2):
        down_panel(C.sibling_target(k), ship, k)
        C.ship(k)
    loads[2].wait()

    for j in range(4):
        if j < 3:
            tile(wc, j + 1).start()
        tile(wc, j).wait()

        def part(start, size):
            lanes = pl.ds(pl.multiple_of(j * s.cols + start, LANES), size)
            value = product(cot[...], wt[j % 2, :, pl.ds(start, size)])
            value = to_low(value * gp[:, lanes].astype(f32))
            gp[:, lanes] = value
            sums[8 + j : 9 + j, pl.ds(start, size)] = jnp.sum(
                value.astype(f32), axis=0, keepdims=True
            )

        by_columns(s.cols, part)
    tile(wb, 0).start()
    for k in range(2):
        C.wait_panel(k)
        down_panel(C.target(k), own_c, k, came)
        pl.semaphore_signal(
            credit.at[k], inc=1, device_id=net.sib, device_id_type=MESH
        )
        C.start(k)
    loads[3].wait()
    two_t[...] = two[...].T
    for k in range(2):
        C.panel(k).wait_send()
        up_panel(B.sibling_target(k), ship, k)
        pl.semaphore_wait(credit.at[k], 1)
        B.ship(k)

    for z in range(4):
        if z < 3:
            tile(wb, z + 1).start()
        tile(wb, z).wait()

        def part(start, size):
            value = nt(gp[:, z * s.cols : (z + 1) * s.cols], wt[z % 2, pl.ds(start, size), :])
            if z:
                value = value + acc[:, pl.ds(start, size)]
            acc[:, pl.ds(start, size)] = value

        by_columns(s.width, part)
        if z == 1:
            C.turn(0)
    tile(wa, 0, s.out_tile).start()
    for k in range(2):
        B.wait_panel(k)
        up_panel(B.target(k), own_b, k, came)
        B.start(k)
        if k == 0:
            C.turn(1)
    C.land(0)
    C.along(0)
    loads[4].wait()

    def norm(r):
        given = cot[r, :].astype(f32)
        back, gain, shift = norm_back(
            res[r, : s.width], acc[r, : s.width], vec[5:6, : s.width]
        )
        total_r = given + back
        res[r, : s.width] = total_r
        low = to_low(total_r)
        branch[r, : s.width] = low
        sums[4:5, : s.width] += jnp.sum(low.astype(f32), axis=0, keepdims=True)
        sums[5:6, : s.width] += gain
        sums[6:7, : s.width] += shift
        sums[7:8, : s.width] += jnp.sum(given, axis=0, keepdims=True)

    branch[...] = jnp.zeros_like(branch)
    by_rows(s.half, LANES, norm)
    C.land(1)
    C.along(1)
    B.turn(0)

    for z in range(4):
        if z < 3:
            tile(wa, z + 1, s.out_tile).start()
        tile(wa, z, s.out_tile).wait()
        source = z * s.out
        base = source // LANES * LANES
        size = s.cols - s.out_tile
        moved = place_run(
            branch[:, base : base + size].astype(f32), source - base, s.qkv - s.out_tile, s.out
        )
        oz[z] = to_low(moved)

        def part(start, count):
            value = nt(oz[z], wt[z % 2, pl.ds(start, count), :size])
            if z:
                value = value + acc[:, pl.ds(start, count)]
            acc[:, pl.ds(start, count)] = value

        by_columns(s.width, part)
    B.turn(1)
    branch_low = two
    branch_low[...] = branch[:, : s.width]
    lane = lax.broadcasted_iota(jnp.int32, (s.half, s.wide), 1)
    branch[...] = to_low(jnp.where(lane < s.width, acc[...], 0.0))
    saves = fetch_all(((res, gres_o), (branch_low, branch_o), (branch, gatt_o), (oz, oz_o)), save)
    B.land(0)
    B.along(0)
    C.finish(False)
    B.land(1)
    B.along(1)
    B.finish()
    for copy in saves:
        copy.wait()
    seq_out.wait()
    seq_out.drain()


def last_kernel(s, *refs):
    (wa, oz_i, dq_i, own_i, sib_i, normed_i, att_i, x_i, gres_i, vec, sums, tops) = refs[:12]
    (qkv_o, gin_o, small_o, line_a) = refs[12:16]
    (came_d, own_d, dq, wide, qz, oz, norm_t, att_t, normed, att, x, gres, wt, acc, gin, buf, got) = refs[16:33]
    (ship, own_a, came_a, first_a, second_a, total, stage) = refs[33:40]
    sems = refs[40:]
    net = Net()
    A = Scatter(net, s, own_a, ship, came_a, first_a, second_a, line_a, total, qkv_o, stage, sems[:12])
    seq_in = FromSequences(net, gin, gin_o, sems[12:14])
    load, tiles, ds, dr, gs, gr = sems[14:20]
    loads = fetch_all(
        ((dq_i, dq), (own_i, own_d), (normed_i, normed), (att_i, att), (oz_i, oz), (x_i, x), (gres_i, gres)),
        load,
    )
    enter(net)
    swap = pltpu.make_async_remote_copy(
        sib_i, came_d, ds, dr, device_id=net.sib, device_id_type=MESH
    )
    swap.start()

    def tile(j):
        return pltpu.make_async_copy(
            wa.at[:, pl.ds(j * s.cols, s.qkv_pad)], wt.at[j % 2], tiles.at[j % 2]
        )

    tile(0).start()
    loads[2].wait()
    norm_t[...] = normed[...].T
    loads[3].wait()
    att_t[...] = att[...].T
    loads[0].wait()
    loads[1].wait()
    buf[...] = sums[...]
    wide[:, : s.wide] = dq[...].astype(f32)
    swap.wait()
    for kind in range(2):
        lanes = slice((kind + 1) * s.wide, (kind + 2) * s.wide)
        value = to_low(own_d[kind].astype(f32) + came_d[kind].astype(f32)).astype(f32)
        wide[:, lanes] = value
    buf[2:3, :] = jnp.sum(wide[:, : s.wide], axis=0, keepdims=True)
    buf[3:4, :] = jnp.sum(wide[:, 2 * s.wide :], axis=0, keepdims=True)
    for z in range(4):
        block = 0.0
        for source, target, count in s.qkv_runs(z):
            base = target // LANES * LANES
            moved = place_run(
                wide[:, base : base + s.qkv_pad], target - base, source, count
            )
            if moved.shape[1] < s.qkv_pad:
                moved = jnp.concatenate(
                    [moved, jnp.zeros((s.half, s.qkv_pad - moved.shape[1]), f32)], axis=1
                )
            block = block + moved
        qz[z] = to_low(block)
    loads[4].wait()

    def panel(z, dst, k, came=None):
        def put(start, size, value):
            lanes = pl.ds(start, size)
            if came is not None:
                value = value + came[k, :, lanes].astype(f32)
            dst[k, :, lanes] = to_low(value)

        def part(start, size):
            put(start, size, product(norm_t[...], qz[z, :, pl.ds(start, size)]))

        by_columns(s.out_tile, part)
        mixed = product(norm_t[...], qz[z, :, s.out_tile :]) + product(
            att_t[: s.width, :], oz[z, :, : s.qkv_pad - s.out_tile]
        )
        put(s.out_tile, s.qkv_pad - s.out_tile, mixed)
        rest = product(att_t[: s.width, :], oz[z, :, s.qkv_pad - s.out_tile :])
        put(s.qkv_pad, s.cols - s.qkv_pad, rest)

    for k in range(2):
        panel(A.sibling_target(k), ship, k)
        A.ship(k)
    for z in range(2):
        tile(z + 1).start()
        tile(z).wait()
        through(s, acc, qz, wt, z)
    for k in range(2):
        A.wait_panel(k)
        panel(A.target(k), own_a, k, came_a)
        A.start(k)
    for z in range(2, 4):
        if z < 3:
            tile(z + 1).start()
        tile(z).wait()
        through(s, acc, qz, wt, z)
    loads[5].wait()
    loads[6].wait()

    def norm(r):
        back, gain, shift = norm_back(
            x[r, :].astype(f32), acc[r, : s.width], vec[0:1, : s.width]
        )
        gin[r, :] = to_low(gres[r, : s.width] + back)
        buf[0:1, : s.width] += gain
        buf[1:2, : s.width] += shift

    by_rows(s.half, LANES, norm)
    seq_in.start()

    def exchange(i, to):
        return pltpu.make_async_remote_copy(
            buf, got.at[i], gs.at[i], gr.at[i], device_id=to, device_id_type=MESH
        )

    def join(one, two):
        row = lax.broadcasted_iota(jnp.int32, one.shape, 0)
        return jnp.where(row == 12, jnp.maximum(one, two), one + two)

    row = lax.broadcasted_iota(jnp.int32, buf.shape, 0)
    buf[...] = jnp.where(row == 12, tops[0:1, :], buf[...])
    partners = (net.sib, net.x_to, net.y_to)

    def merge(i):
        exchange(i, partners[i]).wait()
        buf[...] = join(buf[...], got[i])

    exchange(0, partners[0]).start()
    A.turn(0)
    merge(0)
    exchange(1, partners[1]).start()
    A.turn(1)
    merge(1)
    exchange(2, partners[2]).start()
    A.land(0)
    A.along(0)
    merge(2)

    def around(z):
        return pltpu.make_async_remote_copy(
            buf, got.at[3 + net.z], gs.at[3 + z], gr.at[3 + net.z], device_id=(net.d, z), device_id_type=MESH
        )

    for z in range(4):

        @pl.when(z != net.z)
        def _():
            around(z).start()

        @pl.when(z == net.z)
        def _():
            pltpu.make_async_copy(buf, got.at[3 + z], gr.at[3 + z]).start()

    A.land(1)
    A.along(1)
    for z in range(4):
        pltpu.make_async_copy(buf, got.at[3 + z], gr.at[3 + z]).wait()

        @pl.when(z != net.z)
        def _():
            around(z).wait_send()

    small_o[...] = join(join(got[3], got[4]), join(got[5], got[6]))
    A.finish()
    seq_in.wait()
    seq_in.drain()


def through(s, acc, qz, wt, z):
    def part(start, size):
        value = nt(qz[z], wt[z % 2, pl.ds(start, size), :])
        if z:
            value = value + acc[:, pl.ds(start, size)]
        acc[:, pl.ds(start, size)] = value

    by_columns(s.width, part)


def middle_call(s, shape, wa, wb, wc, cot, res, two, slope, hid, out, vec):
    dma = pltpu.SemaphoreType.DMA
    rows, full = s.half, s.ctx * s.cols
    anywhere = pl.BlockSpec(memory_space=pl.ANY)
    local = pl.BlockSpec(memory_space=pltpu.VMEM)
    low = lambda *dims: jax.ShapeDtypeStruct(dims, bf16)
    high = lambda *dims: jax.ShapeDtypeStruct(dims, f32)
    size = s.cols - s.out_tile
    line = low(2, 2, s.rows, s.cols)
    return pl.pallas_call(
        partial(middle_kernel, s),
        out_shape=[
            high(s.rows, s.cols), high(s.rows, s.cols), high(rows, s.wide), low(rows, s.width),
            low(rows, s.wide), low(4, rows, size), high(16, s.wide), low(*shape), line, line,
        ],
        in_specs=[anywhere] * 9 + [local],
        out_specs=[anywhere] * 6 + [local] + [anywhere] * 3,
        scratch_shapes=[
            pltpu.VMEM((rows, s.width), bf16),
            pltpu.VMEM((rows, s.wide), f32),
            pltpu.VMEM((rows, s.width), bf16),
            pltpu.VMEM((rows, full), bf16),
            pltpu.VMEM((rows, full), bf16),
            pltpu.VMEM((s.width, rows), bf16),
            pltpu.VMEM((s.width, rows), bf16),
            pltpu.VMEM((2, s.width, s.cols), bf16),
            pltpu.VMEM((rows, s.wide), f32),
            pltpu.VMEM((rows, s.wide), bf16),
            pltpu.VMEM((4, rows, size), bf16),
        ]
        + scatter_scratch(s, 2)
        + scatter_sems() * 2
        + [dma((2,)), dma((2,)), dma((5,)), dma((2,)), dma((4,)), pltpu.SemaphoreType.REGULAR((2,))],
        compiler_params=pltpu.CompilerParams(
            collective_id=2, has_side_effects=True, vmem_limit_bytes=63 * 2**20
        ),
        name="middle",
    )(wa, wb, wc, cot, res, two, slope, hid, out, vec)


def last_call(s, shape, wa, oz, dq, d_own, d_sib, normed, att, x, gres, vec, sums, tops):
    dma = pltpu.SemaphoreType.DMA
    rows = s.half
    anywhere = pl.BlockSpec(memory_space=pl.ANY)
    local = pl.BlockSpec(memory_space=pltpu.VMEM)
    low = lambda *dims: jax.ShapeDtypeStruct(dims, bf16)
    high = lambda *dims: jax.ShapeDtypeStruct(dims, f32)
    size = s.cols - s.out_tile
    return pl.pallas_call(
        partial(last_kernel, s),
        out_shape=[
            high(s.rows, s.cols), low(*shape), high(16, s.wide), low(2, 2, s.rows, s.cols),
        ],
        in_specs=[anywhere] * 9 + [local] * 3,
        out_specs=[anywhere, anywhere, local, anywhere],
        scratch_shapes=[
            pltpu.VMEM((2, rows, s.wide), bf16),
            pltpu.VMEM((2, rows, s.wide), bf16),
            pltpu.VMEM((rows, s.wide), bf16),
            pltpu.VMEM((rows, 3 * s.wide), f32),
            pltpu.VMEM((4, rows, s.qkv_pad), bf16),
            pltpu.VMEM((4, rows, size), bf16),
            pltpu.VMEM((s.width, rows), bf16),
            pltpu.VMEM((s.wide, rows), bf16),
            pltpu.VMEM((rows, s.width), bf16),
            pltpu.VMEM((rows, s.wide), bf16),
            pltpu.VMEM((rows, s.width), bf16),
            pltpu.VMEM((rows, s.wide), f32),
            pltpu.VMEM((2, s.width, s.qkv_pad), bf16),
            pltpu.VMEM((rows, s.wide), f32),
            pltpu.VMEM((rows, s.width), bf16),
            pltpu.VMEM((16, s.wide), f32),
            pltpu.VMEM((7, 16, s.wide), f32),
        ]
        + scatter_scratch(s, 1)
        + scatter_sems()
        + [dma((2,)), dma((2,)), dma((7,)), dma((2,)), dma, dma, dma((7,)), dma((7,))],
        compiler_params=pltpu.CompilerParams(
            collective_id=3, has_side_effects=True, vmem_limit_bytes=63 * 2**20
        ),
        name="last",
    )(wa, oz, dq, d_own, d_sib, normed, att, x, gres, vec, sums, tops)


def slot_info(moves, segment_ids, padding, stretch_order):
    core, place, local_seqs = moves.core, moves.z, segment_ids.shape[0]
    length = segment_ids.shape[1]
    half = length // 2
    info = jnp.stack([segment_ids, padding], axis=0)
    info_there = moves.swap_core(info)
    info = jnp.where(place // local_seqs == core, info, info_there)
    info = lax.dynamic_index_in_dim(info, place % local_seqs, 1, False)
    stretches = stretch_order.shape[0]
    stretch_len = length // stretches
    info = jnp.take(info.reshape(2, stretches, stretch_len), stretch_order, axis=1)
    positions = stretch_order[:, None] * stretch_len + jnp.arange(stretch_len, dtype=jnp.int32)
    code = (info[0] * (2 * length) + positions).reshape(2, half)
    reach = (info[1] * (length - 1)).reshape(2, half)
    code_own = lax.dynamic_index_in_dim(code, core, 0, False)
    code_sib = lax.dynamic_index_in_dim(code, 1 - core, 0, False)
    reach_own = lax.dynamic_index_in_dim(reach, core, 0, False)
    reach_sib = lax.dynamic_index_in_dim(reach, 1 - core, 0, False)
    kinfo = jnp.stack(
        [jnp.concatenate([code_own, code_sib]), jnp.concatenate([reach_own, reach_sib])], axis=1
    )
    return kinfo, code_own[None]


def pack_blocks(moves, s, w_qkv, w_out, w_up, w_down, vectors, bias_up):
    rows = w_qkv.shape[0]

    def filled(values):
        return jnp.pad(values, ((0, 0), (0, s.cols - values.shape[1])))

    turned = w_down.T
    parts = jnp.concatenate(
        [
            filled(jnp.concatenate([w_qkv, w_out], axis=1)),
            filled(w_up),
            filled(jnp.concatenate([turned[:rows], turned[rows:]], axis=1)),
        ],
        axis=0,
    )
    there = moves.swap_core(parts)
    even = jnp.where(moves.core == 0, parts, there)
    odd = jnp.where(moves.core == 0, there, parts)
    own_a = jnp.concatenate([even[:rows], odd[:rows]], axis=0)
    own_b = jnp.concatenate([even[rows : 2 * rows], odd[rows : 2 * rows]], axis=0)
    ff = turned.shape[1]
    own_c = filled(
        jnp.concatenate(
            [
                jnp.concatenate([v[2 * rows :, :ff], v[2 * rows :, ff : 2 * ff]], axis=0)
                for v in (even, odd)
            ],
            axis=1,
        )
    )
    small = jnp.concatenate([jnp.pad(vectors, ((0, 0), (0, s.cols - vectors.shape[1]))), filled(bias_up[None])], axis=0)
    small = jnp.pad(small, ((0, 16 - small.shape[0]), (0, 0)))
    return own_a, own_b, own_c, small


def fast_shards(
    dp,
    ctx,
    inputs,
    cotangent,
    w_qkv,
    w_out,
    w_up,
    w_down,
    vectors,
    bias_up,
    segment_ids,
    padding,
    stretch_order,
):
    local_seqs, query_len, width = inputs.shape
    heads = width // HD
    s = Sizes(width, w_up.shape[1] * ctx, ctx, dp, segment_ids.shape[1])
    moves = Moves(dp, ctx, local_seqs)
    core, place = moves.core, moves.z
    wide = s.wide
    kinfo, qinfo = slot_info(moves, segment_ids, padding, stretch_order)
    own_a, own_b, own_c, small = pack_blocks(moves, s, w_qkv, w_out, w_up, w_down, vectors, bias_up)
    (wa, wb, wc, x, cot, vec, normed, queries, kv, attended, residual, two, slope, hidden, lse, tops, out) = forward_call(
        s, own_a, own_b, own_c, small, inputs, cotangent, kinfo, qinfo
    )
    down_block, up_block, gres, _, gatt, oz, sums, output, _, _ = middle_call(
        s, inputs.shape, wa, wb, wc, cot, residual, two, slope, hidden, out, vec
    )
    dq, d_own, d_sib = attend_backward(heads, kinfo, qinfo, queries, kv, gatt, lse)
    block_top = jnp.max(tops, axis=2).reshape(1, -1)[:, :heads]
    block_top = jnp.pad(block_top, ((0, 7), (0, wide - heads)))
    qkv_block, grad_input, small_sums, _ = last_call(
        s, inputs.shape, wa, oz, dq, d_own, d_sib, normed, attended, x, gres, vec, sums, block_top
    )
    rows_d = w_qkv.shape[0]
    cols_q, cols_d, cols_f = w_qkv.shape[1], w_out.shape[1], w_up.shape[1]
    ff = w_down.shape[0]

    def own_rows(block):
        return jnp.where(core == 0, block[:rows_d], block[rows_d:])

    qkv_block, up_block = own_rows(qkv_block), own_rows(up_block)
    grad_qkv, grad_out = qkv_block[:, :cols_q], qkv_block[:, cols_q : cols_q + cols_d]
    grad_up = up_block[:, :cols_f]
    grad_down = jnp.where(core == 0, down_block[:, :ff], down_block[:, ff : 2 * ff]).T
    grad_vectors = lax.dynamic_slice_in_dim(small_sums[:8, :width], place * cols_d, cols_d, 1)
    grad_bias = lax.dynamic_index_in_dim(small_sums[8:12], place, 0, False)[:cols_f]
    global_top = small_sums[12, :heads]

    factor = clip_limit / jnp.maximum(global_top, clip_limit)
    per_column = jnp.repeat(jnp.sqrt(factor), HD)
    column_scale = jnp.concatenate([per_column, per_column, jnp.ones((width,), f32)])
    local_scale = lax.dynamic_slice_in_dim(column_scale, place * cols_q, cols_q)
    clipped_qkv = to_low(w_qkv.astype(f32) * local_scale[None, :])
    bias_scale = lax.dynamic_slice_in_dim(per_column, place * cols_d, cols_d)
    clipped_bias = to_low(vectors[2].astype(f32) * bias_scale)
    return (
        output,
        grad_input.astype(f32),
        grad_qkv,
        grad_out,
        grad_up,
        grad_down,
        grad_vectors,
        grad_bias,
        clipped_qkv,
        clipped_bias,
        global_top,
    )


def shards(
    dp,
    ctx,
    inputs,
    cotangent,
    w_qkv,
    w_out,
    w_up,
    w_down,
    vectors,
    bias_up,
    segment_ids,
    padding,
    stretch_order,
):
    local_seqs, query_len, width = inputs.shape
    length = segment_ids.shape[1]
    half = length // 2
    heads = width // HD
    wide = (width + LANES - 1) // LANES * LANES
    rows_d = w_qkv.shape[0]
    cols_d = w_out.shape[1]
    cols_f = w_up.shape[1]
    ratio = w_down.shape[0] // rows_d
    hidden_width = cols_f * ctx
    moves = Moves(dp, ctx, local_seqs)
    core, place = moves.core, moves.z

    extra = jnp.concatenate([vectors.reshape(-1, cols_f), bias_up[None]], axis=0)
    first = jnp.concatenate([jnp.concatenate([w_qkv, w_out], axis=1), extra], axis=0)
    first = moves.gather_ctx(first)
    x_flat = moves.to_sequences(inputs).astype(f32)
    down_packed = jnp.swapaxes(w_down.reshape(ratio, rows_d, cols_d), 0, 1).reshape(rows_d, -1)
    second = moves.gather_ctx(jnp.concatenate([w_up, down_packed], axis=0))
    cot = moves.to_sequences(cotangent)

    def columns(blocks):
        return jnp.swapaxes(blocks, 0, 1).reshape(blocks.shape[1], -1)

    cols_q = w_qkv.shape[1]
    part_qkv = columns(first[:, :rows_d, :cols_q])
    part_out = columns(first[:, :rows_d, cols_q:])
    small = first[:, rows_d:]
    vec_rows = columns(small[:, :-1].reshape(ctx, 8, cols_d)).astype(f32)
    bias_row = small[:, -1].reshape(-1).astype(f32)
    part_up = columns(second[:, :rows_d])
    part_down = second[:, rows_d:].reshape(ctx, rows_d, ratio, cols_d)
    part_down = jnp.transpose(part_down, (2, 1, 0, 3)).reshape(ratio * rows_d, width)

    wide_qkv = moves.gather_dp(part_qkv)
    wide_out = moves.gather_dp(part_out)
    wide_up = moves.gather_dp(part_up)
    wide_down = moves.gather_dp(part_down)

    info = jnp.stack([segment_ids, padding], axis=0)
    info_there = moves.swap_core(info)
    info = jnp.where(place // local_seqs == core, info, info_there)
    info = lax.dynamic_index_in_dim(info, place % local_seqs, 1, False)
    stretches = stretch_order.shape[0]
    stretch_len = length // stretches
    info = jnp.take(info.reshape(2, stretches, stretch_len), stretch_order, axis=1)
    positions = stretch_order[:, None] * stretch_len + jnp.arange(stretch_len, dtype=jnp.int32)
    code = (info[0] * (2 * length) + positions).reshape(2, half)
    reach = (info[1] * (length - 1)).reshape(2, half)
    code_own = lax.dynamic_index_in_dim(code, core, 0, False)
    code_sib = lax.dynamic_index_in_dim(code, 1 - core, 0, False)
    reach_own = lax.dynamic_index_in_dim(reach, core, 0, False)
    reach_sib = lax.dynamic_index_in_dim(reach, 1 - core, 0, False)
    kinfo = jnp.stack(
        [jnp.concatenate([code_own, code_sib]), jnp.concatenate([reach_own, reach_sib])], axis=1
    )
    qinfo = code_own[None]

    normed = to_low(layer_norm(x_flat, vec_rows[0], vec_rows[1]))
    projected = product(normed, wide_qkv)

    def padded(values):
        return jnp.pad(to_low(values), ((0, 0), (0, wide - width)))

    queries = padded(projected[:, :width] + vec_rows[2])
    own = jnp.stack(
        [
            padded(projected[:, width : 2 * width]),
            padded(projected[:, 2 * width :] + vec_rows[3]),
        ]
    )
    sib = moves.swap_core(own)
    attended, lse, tops = attend_forward(heads, kinfo, qinfo, queries, own, sib)
    attended = attended[:, :width]
    block_top = jnp.max(tops, axis=2).reshape(-1)[:heads]
    global_top = lax.pmax(block_top, AXES)
    residual = x_flat + product(attended, wide_out) + vec_rows[4]
    normed_two = to_low(layer_norm(residual, vec_rows[5], vec_rows[6]))
    up_pre = product(normed_two, wide_up) + bias_row
    hidden = to_low(jax.nn.gelu(up_pre, approximate=True))
    output = to_low(residual + product(hidden, wide_down) + vec_rows[7])
    output = moves.from_sequences(output)

    grad_output = cot.astype(f32)
    grad_bias_two = column_sum(cot)
    sum_down = moves.weight_terms(hidden, cot)
    sum_down = moves.scatter_dp(sum_down)
    grad_hidden = contract_cols(cot, wide_down)
    unused, gelu_back = jax.vjp(partial(jax.nn.gelu, approximate=True), up_pre)
    grad_pre = to_low(gelu_back(grad_hidden)[0])
    grad_bias_up = column_sum(grad_pre)
    sum_up = moves.weight_terms(normed_two, grad_pre)
    sum_up = moves.scatter_dp(sum_up)
    unused, norm_back_two = jax.vjp(layer_norm, residual, vec_rows[5], vec_rows[6])
    back_two = norm_back_two(contract_cols(grad_pre, wide_up))
    grad_residual = grad_output + back_two[0]
    grad_branch = to_low(grad_residual)
    sum_out = moves.weight_terms(attended, grad_branch)
    sum_out = moves.scatter_dp(sum_out)
    grad_attended = padded(contract_cols(grad_branch, wide_out))
    dq, d_own, d_sib = attend_backward(
        heads, kinfo, qinfo, queries, jnp.concatenate([own, sib], axis=1), grad_attended, lse
    )
    d_came = moves.swap_core(d_sib)
    d_own = to_low(d_own.astype(f32) + d_came.astype(f32))
    grad_proj = jnp.concatenate([dq[:, :width], d_own[0, :, :width], d_own[1, :, :width]], axis=1)
    sum_qkv = moves.weight_terms(normed, grad_proj)
    sum_qkv = moves.scatter_dp(sum_qkv)
    unused, norm_back_one = jax.vjp(layer_norm, x_flat, vec_rows[0], vec_rows[1])
    back_one = norm_back_one(contract_cols(grad_proj, wide_qkv))
    grad_input = to_low(grad_residual + back_one[0])
    grad_input = moves.from_sequences(grad_input).astype(f32)
    grad_vectors = jnp.stack(
        [
            back_one[1],
            back_one[2],
            column_sum(dq[:, :width]),
            column_sum(d_own[1, :, :width]),
            column_sum(grad_branch),
            back_two[1],
            back_two[2],
            grad_bias_two,
        ]
    )

    def by_place(values):
        return jnp.swapaxes(values.reshape(values.shape[0], ctx, -1), 0, 1)

    blocks_down = sum_down.reshape(ratio, rows_d, ctx, cols_d)
    blocks_down = jnp.transpose(blocks_down, (2, 1, 0, 3)).reshape(ctx, rows_d, -1)
    later = jnp.concatenate([by_place(sum_up), blocks_down, by_place(sum_out)], axis=2)
    later = moves.scatter_ctx(later)
    grad_up = later[:, :cols_f]
    grad_down = later[:, cols_f : 2 * cols_f].reshape(rows_d, ratio, cols_d)
    grad_down = jnp.swapaxes(grad_down, 0, 1).reshape(ratio * rows_d, cols_d)
    grad_out = later[:, 2 * cols_f :]
    grad_qkv = moves.scatter_ctx(by_place(sum_qkv))

    tiny = jnp.concatenate([grad_vectors, grad_bias_up.reshape(-1, width)], axis=0)
    tiny = lax.psum(tiny, AXES)
    grad_vectors = lax.dynamic_slice_in_dim(tiny[:8], place * cols_d, cols_d, 1)
    grad_bias = lax.dynamic_slice_in_dim(tiny[8:].reshape(-1), place * cols_f, cols_f)

    factor = clip_limit / jnp.maximum(global_top, clip_limit)
    per_column = jnp.repeat(jnp.sqrt(factor), HD)
    column_scale = jnp.concatenate([per_column, per_column, jnp.ones((width,), f32)])
    local_scale = lax.dynamic_slice_in_dim(column_scale, place * cols_q, cols_q)
    clipped_qkv = to_low(w_qkv.astype(f32) * local_scale[None, :])
    bias_scale = lax.dynamic_slice_in_dim(per_column, place * cols_d, cols_d)
    clipped_bias = to_low(vectors[2].astype(f32) * bias_scale)
    return (
        output,
        grad_input,
        grad_qkv,
        grad_out,
        grad_up,
        grad_down,
        grad_vectors,
        grad_bias,
        clipped_qkv,
        clipped_bias,
        global_top,
    )


def solution(mesh):
    dp, ctx = mesh.shape["dp"], mesh.shape["ctx"]
    body = fast_shards if (dp, ctx) == (8, 4) else shards
    return jax.shard_map(
        partial(body, dp, ctx),
        mesh=mesh,
        in_specs=(
            P("dp", "ctx", None),
            P("dp", "ctx", None),
            P("dp", "ctx"),
            P("dp", "ctx"),
            P("dp", "ctx"),
            P("dp", "ctx"),
            P(None, "ctx"),
            P("ctx"),
            P("dp", None),
            P("dp", None),
            P(),
        ),
        out_specs=(
            P("dp", "ctx", None),
            P("dp", "ctx", None),
            P("dp", "ctx"),
            P("dp", "ctx"),
            P("dp", "ctx"),
            P("dp", "ctx"),
            P(None, "ctx"),
            P("ctx"),
            P("dp", "ctx"),
            P("ctx"),
            P(),
        ),
        check_vma=False,
    )
```

```python
import math
from functools import partial

import jax
import jax.numpy as jnp
from jax import lax
from jax.experimental import pallas as pl
from jax.experimental.pallas import tpu as pltpu
from jax.sharding import PartitionSpec as P

HD = 64
LANES = 128
AXES = ("dp", "ctx")

eps_norm = 1e-05
clip_limit = 5.0
masked_fill = -1e30
f32 = jnp.float32
bf16 = jnp.bfloat16


def layer_norm(values_in, gain_row, shift_row):
    average = jnp.mean(values_in, axis=-1, keepdims=True)
    centred = values_in - average
    variance = jnp.mean(centred * centred, axis=-1, keepdims=True)
    return centred * lax.rsqrt(variance + eps_norm) * gain_row + shift_row


def to_low(values_in):
    return values_in.astype(bf16)


def product(left, right):
    return jnp.dot(left, right, preferred_element_type=f32)


def contract_rows(left, right):
    return lax.dot_general(left, right, (((0,), (0,)), ((), ())), preferred_element_type=f32)


def contract_cols(left, right):
    return lax.dot_general(left, right, (((1,), (1,)), ((), ())), preferred_element_type=f32)


def column_sum(values_in):
    return jnp.sum(values_in.astype(f32), axis=0)


class Moves:
    def __init__(self, dp, ctx, local_seqs):
        self.dp, self.ctx, self.seqs = dp, ctx, local_seqs
        self.d = lax.axis_index("dp")
        self.z = lax.axis_index("ctx")
        self.core = self.d % 2
        self.cube = dp == 8 and ctx == 4
        self.x = (self.d // 2) % 2
        self.y = self.d // 4

    def permute(self, values, target):
        pairs = []
        for d in range(self.dp):
            for z in range(self.ctx):
                there = target(d, z)
                if there is not None:
                    pairs.append((d * self.ctx + z, there[0] * self.ctx + there[1]))
        return lax.ppermute(values, AXES, pairs)

    def swap_core(self, values):
        return self.permute(values, lambda d, z: (d ^ 1, z))

    def swap_x(self, values):
        return self.permute(values, lambda d, z: (d ^ 2, z))

    def swap_y(self, values):
        return self.permute(values, lambda d, z: (d ^ 4, z))

    def up(self, values):
        return self.permute(values, lambda d, z: (d, z + 1) if z + 1 < self.ctx else None)

    def down(self, values):
        return self.permute(values, lambda d, z: (d, z - 1) if z > 0 else None)

    def sequence_target(self, step):
        n = self.seqs

        def target(d, z):
            return (d - d % 2 + z // n, n * (d % 2) + (z + step) % n)

        return target

    def to_sequences(self, values):
        n = self.seqs
        came = []
        for step in range(n):
            block = lax.dynamic_index_in_dim(values, (self.z + step) % n, 0, keepdims=False)
            came.append(self.permute(block, self.sequence_target(step)))
        return jnp.concatenate([self.choose(came, (self.z - t) % n) for t in range(n)], axis=0)

    def from_sequences(self, values):
        n = self.seqs
        parts = values.reshape(n, values.shape[0] // n, values.shape[1])
        came = []
        for step in range(n):
            forward = self.sequence_target(step)
            block = lax.dynamic_index_in_dim(parts, (self.z - step) % n, 0, keepdims=False)
            back = {}
            for d in range(self.dp):
                for z in range(self.ctx):
                    back[forward(d, z)] = (d, z)
            came.append(self.permute(block, lambda d, z: back[(d, z)]))
        return jnp.stack([self.choose(came, (j - self.z) % n) for j in range(n)], axis=0)

    @staticmethod
    def choose(items, index):
        picked = items[0]
        for i in range(1, len(items)):
            picked = jnp.where(index == i, items[i], picked)
        return picked

    def gather_ctx(self, block):
        if not self.cube:
            return lax.all_gather(block, "ctx", axis=0, tiled=False)
        rising, falling = [block], [block]
        for _ in range(self.ctx - 1):
            rising.append(self.up(rising[-1]))
            falling.append(self.down(falling[-1]))
        line = jnp.stack(rising[:0:-1] + falling, axis=0)
        return lax.dynamic_slice_in_dim(line, self.ctx - 1 - self.z, self.ctx, 0)

    def gather_dp(self, block):
        if not self.cube:
            return lax.all_gather(block, "dp", axis=0, tiled=True)
        rows, cols = block.shape
        half = (cols // 2 + LANES - 1) // LANES * LANES
        from_x, from_y = self.swap_x(block), self.swap_y(block)
        far = jnp.concatenate(
            [self.swap_y(from_x[:, :half]), self.swap_x(from_y[:, half:])], axis=1
        )
        mine = jnp.zeros((4, rows, cols), block.dtype)
        here = 2 * self.y + self.x
        for step, part in enumerate((block, from_x, from_y, far)):
            mine = lax.dynamic_update_slice(mine, part[None], (here ^ step, 0, 0))
        other = self.swap_core(mine)
        first = jnp.where(self.core == 0, mine, other)
        second = jnp.where(self.core == 0, other, mine)
        return jnp.stack([first, second], axis=1).reshape(8 * rows, cols)

    def scatter_ctx(self, blocks):
        if not self.cube:
            return lax.psum_scatter(blocks, "ctx", scatter_dimension=0, tiled=False).astype(f32)

        def part(index):
            return lax.dynamic_index_in_dim(blocks, jnp.clip(index, 0, self.ctx - 1), 0, False)

        falling = rising = None
        for step in range(self.ctx - 1, 0, -1):
            low, high = part(self.z - step), part(self.z + step)
            if falling is not None:
                low = to_low(low.astype(f32) + falling.astype(f32))
                high = to_low(high.astype(f32) + rising.astype(f32))
            n = self.ctx
            falling = self.permute(
                low, lambda d, z: (d, z - 1) if z - step >= 0 else None
            )
            rising = self.permute(
                high, lambda d, z: (d, z + 1) if z + step < n else None
            )
        return part(self.z).astype(f32) + falling.astype(f32) + rising.astype(f32)

    def weight_terms(self, left, right):
        if not self.cube:
            return to_low(contract_rows(left, right))
        tokens, width = left.shape
        rows = width // self.dp
        parts = left.reshape(tokens, self.dp // 2, 2, rows)
        even = parts[:, :, 0].reshape(tokens, -1)
        odd = parts[:, :, 1].reshape(tokens, -1)
        own = jnp.where(self.core == 0, even, odd)
        sibling = jnp.where(self.core == 0, odd, even)
        came = self.swap_core(to_low(contract_rows(sibling, right)))
        return to_low(contract_rows(own, right) + came.astype(f32))

    def scatter_dp(self, terms):
        if not self.cube:
            return lax.psum_scatter(terms, "dp", scatter_dimension=0, tiled=True)
        rows, cols = terms.shape[0] // 4, terms.shape[1]
        half = (cols // 2 + LANES - 1) // LANES * LANES
        grid = terms.reshape(2, 2, rows, cols)

        def pick(values, index, axis):
            return lax.dynamic_index_in_dim(values, index, axis, False)

        def added(one, two):
            return to_low(one.astype(f32) + two.astype(f32))

        left, right = grid[..., :half], grid[..., half:]
        left_x = self.swap_x(pick(left, 1 - self.x, 1))
        right_y = self.swap_y(pick(right, 1 - self.y, 0))
        left = added(pick(left, self.x, 1), left_x)
        right = added(pick(right, self.y, 0), right_y)
        left_y = self.swap_y(pick(left, 1 - self.y, 0))
        right_x = self.swap_x(pick(right, 1 - self.x, 0))
        left = added(pick(left, self.y, 0), left_y)
        right = added(pick(right, self.x, 0), right_x)
        return jnp.concatenate([left, right], axis=1)


def nt(left, right):
    return lax.dot_general(left, right, (((1,), (1,)), ((), ())), preferred_element_type=f32)


def tn(left, right):
    return lax.dot_general(left, right, (((0,), (0,)), ((), ())), preferred_element_type=f32)


def fill_bias(kinfo_ref, qinfo_ref, bias_ref):
    diff = qinfo_ref[0:1, :] - kinfo_ref[:, 0:1]
    fine = (diff >= 0) & (diff <= kinfo_ref[:, 1:2])
    bias_ref[...] = jnp.where(fine, 0.0, masked_fill)


def attend_forward_kernel(
    heads, kinfo_ref, qinfo_ref, q_ref, own_ref, sib_ref, out_ref, lse_ref, top_ref, bias_ref
):
    step = pl.program_id(0)

    @pl.when(step == 0)
    def _():
        fill_bias(kinfo_ref, qinfo_ref, bias_ref)

    keys = jnp.concatenate([own_ref[0], sib_ref[0]], axis=0)
    values = jnp.concatenate([own_ref[1], sib_ref[1]], axis=0)
    queries = q_ref[...]
    lane = lax.broadcasted_iota(jnp.int32, queries.shape, 1)
    outs = []
    for side in range(2):
        mine = (lane >= HD) if side else (lane < HD)
        picked = jnp.where(mine, queries, jnp.zeros_like(queries)) * bf16(HD**-0.5)
        scores = nt(keys, picked) + bias_ref[...]
        top = jnp.max(scores, axis=0, keepdims=True)
        weights = jnp.exp(scores - top)
        total = jnp.sum(weights, axis=0, keepdims=True)
        mixed = tn(values[:, side * HD : (side + 1) * HD], weights.astype(bf16))
        outs.append(mixed * (1.0 / total))
        lse_ref[0, side : side + 1, :] = top + jnp.log(total)
        top_ref[0, side : side + 1, :] = top
    out_ref[...] = jnp.concatenate(outs, axis=0).T.astype(bf16)


def attend_backward_kernel(
    heads,
    kinfo_ref,
    qinfo_ref,
    q_ref,
    own_ref,
    sib_ref,
    grad_ref,
    lse_ref,
    dq_ref,
    down_ref,
    dsib_ref,
    bias_ref,
):
    step = pl.program_id(0)

    @pl.when(step == 0)
    def _():
        fill_bias(kinfo_ref, qinfo_ref, bias_ref)

    keys = jnp.concatenate([own_ref[0], sib_ref[0]], axis=0)
    values = jnp.concatenate([own_ref[1], sib_ref[1]], axis=0)
    queries, grads = q_ref[...], grad_ref[...]
    half = queries.shape[0]
    lane = lax.broadcasted_iota(jnp.int32, queries.shape, 1)
    dqs, dk, dv = [], 0.0, 0.0
    for side in range(2):
        mine = (lane >= HD) if side else (lane < HD)
        picked = jnp.where(mine, queries, jnp.zeros_like(queries)) * bf16(HD**-0.5)
        grad = jnp.where(mine, grads, jnp.zeros_like(grads))
        scores = nt(keys, picked) + bias_ref[...]
        weights = jnp.exp(scores - lse_ref[0, side : side + 1, :])
        dp = nt(values, grad)
        delta = jnp.sum(weights * dp, axis=0, keepdims=True)
        ds = (weights * (dp - delta)).astype(bf16)
        dqs.append(tn(keys[:, side * HD : (side + 1) * HD], ds) * (HD**-0.5))
        dk = dk + product(ds, picked)
        dv = dv + product(weights.astype(bf16), grad)
    dq_ref[...] = jnp.concatenate(dqs, axis=0).T.astype(bf16)
    dk, dv = dk.astype(bf16), dv.astype(bf16)
    down_ref[0] = dk[:half]
    dsib_ref[0] = dk[half:]
    down_ref[1] = dv[:half]
    dsib_ref[1] = dv[half:]


def pair_specs(rows):
    flat = pl.BlockSpec((rows, LANES), lambda i: (0, i))
    double = pl.BlockSpec((2, rows, LANES), lambda i: (0, 0, i))
    per_head = pl.BlockSpec((1, 2, rows), lambda i: (i, 0, 0))
    return flat, double, per_head


def attend_forward(heads, kinfo, qinfo, queries, own, sib):
    rows, width = queries.shape
    pairs = width // LANES
    flat, double, per_head = pair_specs(rows)
    small = jax.ShapeDtypeStruct((pairs, 2, rows), f32)
    return pl.pallas_call(
        partial(attend_forward_kernel, heads),
        grid=(pairs,),
        in_specs=[
            pl.BlockSpec(kinfo.shape, lambda i: (0, 0)),
            pl.BlockSpec(qinfo.shape, lambda i: (0, 0)),
            flat,
            double,
            double,
        ],
        out_specs=[flat, per_head, per_head],
        out_shape=[jax.ShapeDtypeStruct((rows, width), bf16), small, small],
        scratch_shapes=[pltpu.VMEM((2 * rows, rows), f32)],
        compiler_params=pltpu.CompilerParams(vmem_limit_bytes=48 * 2**20),
        cost_estimate=pl.CostEstimate(
            flops=pairs * 16 * rows * rows * LANES,
            bytes_accessed=rows * width * 12,
            transcendentals=pairs * 4 * rows * rows,
        ),
        name="attend_forward",
    )(kinfo, qinfo, queries, own, sib)


def attend_backward(heads, kinfo, qinfo, queries, kv, grad, lse):
    rows, width = queries.shape
    pairs = width // LANES
    flat, double, per_head = pair_specs(rows)
    both = jax.ShapeDtypeStruct((2, rows, width), bf16)
    return pl.pallas_call(
        partial(attend_backward_kernel, heads),
        grid=(pairs,),
        in_specs=[
            pl.BlockSpec(kinfo.shape, lambda i: (0, 0)),
            pl.BlockSpec(qinfo.shape, lambda i: (0, 0)),
            flat,
            double,
            pl.BlockSpec((2, rows, LANES), lambda i: (0, 1, i)),
            flat,
            per_head,
        ],
        out_specs=[flat, double, double],
        out_shape=[jax.ShapeDtypeStruct((rows, width), bf16), both, both],
        scratch_shapes=[pltpu.VMEM((2 * rows, rows), f32)],
        compiler_params=pltpu.CompilerParams(vmem_limit_bytes=48 * 2**20),
        cost_estimate=pl.CostEstimate(
            flops=pairs * 40 * rows * rows * LANES,
            bytes_accessed=rows * width * 22,
            transcendentals=pairs * 4 * rows * rows,
        ),
        name="attend_backward",
    )(kinfo, qinfo, queries, kv, kv, grad, lse)


MESH = pl.DeviceIdType.MESH


class Sizes:
    def __init__(self, width, hidden, ctx, dp, length):
        self.width = width
        self.wide = -(-width // LANES) * LANES
        self.ctx = ctx
        self.rows = 2 * width // dp
        self.qkv = 3 * width // ctx
        self.out = width // ctx
        self.cols = -(-(self.qkv + self.out) // LANES) * LANES
        self.up = hidden // ctx
        self.half = length // 2
        self.pairs = self.wide // LANES
        self.out_tile = self.qkv // LANES * LANES
        self.qkv_cols = 1024
        self.qkv_pad = -(-self.qkv // LANES) * LANES

    def qkv_runs(self, z):
        runs, at = [], z * self.qkv
        end = at + self.qkv
        while at < end:
            kind = at // self.width
            stop = min(end, (kind + 1) * self.width)
            runs.append((at - z * self.qkv, kind * self.wide + at - kind * self.width, stop - at))
            at = stop
        return runs


class Net:
    def __init__(self):
        self.d = lax.axis_index("dp")
        self.z = lax.axis_index("ctx")
        self.c = self.d % 2
        self.p = self.d // 2
        y, x = self.p // 2, self.p % 2
        self.px, self.py, self.pd = 2 * y + 1 - x, 2 * (1 - y) + x, 2 * (1 - y) + 1 - x
        self.x_to = (2 * self.px + self.c, self.z)
        self.y_to = (2 * self.py + self.c, self.z)
        self.sib = (2 * self.p + 1 - self.c, self.z)
        self.near = self.c + 2 * (self.z // 2)
        self.far = self.c + 2 * (1 - self.z // 2)


def enter(net):
    gate = pltpu.get_barrier_semaphore()
    for c in range(2):
        for z in range(4):

            @pl.when((c != net.c) | (z != net.z))
            def _():
                pl.semaphore_signal(gate, inc=1, device_id=(2 * net.p + c, z), device_id_type=MESH)

    for to in (net.x_to, net.y_to):
        pl.semaphore_signal(gate, inc=1, device_id=to, device_id_type=MESH)
    pl.semaphore_wait(gate, 9)


class Gather:
    def __init__(self, net, sizes, w, own, swapped, sems):
        self.n, self.s, self.w, self.own, self.swapped = net, sizes, w, own, swapped
        self.zs, self.zr, self.hs, self.hr, self.cs, self.cr, self.loc = sems

    def at(self, p, z):
        r, c = (z, p) if self.swapped else (p, z)
        s = self.s
        return self.w.at[
            pl.ds(pl.multiple_of(r * s.rows, 16), s.rows),
            pl.ds(pl.multiple_of(c * s.cols, LANES), s.cols),
        ]

    def copy(self, p, z, send, recv, to):
        block = self.at(p, z)
        return pltpu.make_async_remote_copy(
            block, block, send, recv, device_id=to, device_id_type=MESH
        )

    def zcopy(self, z, up):
        n = self.n
        to = (n.d, n.z + 1 if up else n.z - 1)
        return self.copy(n.p, z, self.zs.at[z // 2, int(up)], self.zr.at[z // 2], to)

    def hop(self, p, z, to, k):
        return self.copy(p, z, self.hs.at[z // 2, k], self.hr.at[z // 2, k], to)

    def across(self, p, z):
        return self.copy(p, z, self.cs.at[p, z // 2], self.cr.at[p, z // 2], self.n.sib)

    def begin(self):
        n = self.n

        @pl.when(n.z % 2 == n.c)
        def _():
            local = pltpu.make_async_copy(self.own, self.at(n.p, n.z), self.loc)
            local.start()
            local.wait()

            @pl.when(n.z < 3)
            def _():
                self.zcopy(n.z, True).start()

            @pl.when(n.z > 0)
            def _():
                self.zcopy(n.z, False).start()

    def arrive(self, z):
        n = self.n

        @pl.when(z != n.z)
        def _():
            self.zcopy(z, True).wait_recv()

            @pl.when((z < n.z) & (n.z < 3))
            def _():
                self.zcopy(z, True).start()

            @pl.when((z > n.z) & (n.z > 0))
            def _():
                self.zcopy(z, False).start()

        self.hop(n.p, z, n.x_to, 0).start()
        self.hop(n.p, z, n.y_to, 1).start()
        self.across(n.p, z).start()

    def turn(self, z):
        n = self.n
        self.hop(n.px, z, n.x_to, 0).wait_recv()

        @pl.when(z < 2)
        def _():
            self.hop(n.px, z, n.y_to, 2).start()

        self.across(n.px, z).start()
        self.hop(n.py, z, n.y_to, 1).wait_recv()

        @pl.when(z >= 2)
        def _():
            self.hop(n.py, z, n.x_to, 2).start()

        self.across(n.py, z).start()

    def last(self, z):
        n = self.n
        self.hop(n.pd, z, n.x_to, 2).wait_recv()
        self.across(n.pd, z).start()

    def ready(self):
        n = self.n
        for half in range(2):
            for p in range(4):
                self.across(p, 1 - n.c + 2 * half).wait_recv()

    def drain(self):
        n = self.n
        for half in range(2):
            z = n.c + 2 * half

            @pl.when((z <= n.z) & (n.z < 3))
            def _():
                self.zcopy(z, True).wait_send()

            @pl.when((z >= n.z) & (n.z > 0))
            def _():
                self.zcopy(z, False).wait_send()

            for k, to in enumerate((n.x_to, n.y_to, n.x_to)):
                self.hop(n.p, z, to, k).wait_send()
            for p in range(4):
                self.across(p, z).wait_send()


def gather_sems():
    dma = pltpu.SemaphoreType.DMA
    return [dma((2, 2)), dma((2,)), dma((2, 3)), dma((2, 3)), dma((4, 2)), dma((4, 2)), dma]


class ToSequences:
    def __init__(self, net, src, dst, sems):
        self.n, self.src, self.dst = net, src, dst
        self.ss, self.rs = sems
        self.rows = src.shape[1]

    def parts(self):
        n = self.n
        for j in range(2):
            to = (2 * n.p + n.z // 2, 2 * n.c + j)
            yield j, to, (to[0] == n.d) & (to[1] == n.z)

    def place(self, t):
        return self.dst.at[pl.ds(pl.multiple_of(t * self.rows, 16), self.rows)]

    def remote(self, j, to):
        t = self.n.z % 2
        return pltpu.make_async_remote_copy(
            self.src.at[j],
            self.place(t),
            self.ss.at[j],
            self.rs.at[t],
            device_id=to,
            device_id_type=MESH,
        )

    def start(self):
        for j, to, here in self.parts():

            @pl.when(here)
            def _():
                t = self.n.z % 2
                pltpu.make_async_copy(self.src.at[j], self.place(t), self.rs.at[t]).start()

            @pl.when(jnp.logical_not(here))
            def _():
                self.remote(j, to).start()

    def wait(self):
        for t in range(2):
            pltpu.make_async_copy(self.src.at[0], self.place(t), self.rs.at[t]).wait()

    def drain(self):
        for j, to, here in self.parts():

            @pl.when(jnp.logical_not(here))
            def _():
                self.remote(j, to).wait_send()


class FromSequences:
    def __init__(self, net, src, dst, sems):
        self.n, self.src, self.dst = net, src, dst
        self.ss, self.rs = sems
        self.rows = dst.shape[1]

    def parts(self):
        n = self.n
        for t in range(2):
            to = (2 * n.p + n.z // 2, 2 * n.c + t)
            yield t, to, (to[0] == n.d) & (to[1] == n.z)

    def piece(self, t):
        return self.src.at[pl.ds(t * self.rows, self.rows)]

    def remote(self, t, to):
        j = self.n.z % 2
        return pltpu.make_async_remote_copy(
            self.piece(t),
            self.dst.at[j],
            self.ss.at[t],
            self.rs.at[j],
            device_id=to,
            device_id_type=MESH,
        )

    def start(self):
        for t, to, here in self.parts():

            @pl.when(here)
            def _():
                j = self.n.z % 2
                pltpu.make_async_copy(self.piece(t), self.dst.at[j], self.rs.at[j]).start()

            @pl.when(jnp.logical_not(here))
            def _():
                self.remote(t, to).start()

    def wait(self):
        for j in range(2):
            pltpu.make_async_copy(self.piece(0), self.dst.at[j], self.rs.at[j]).wait()

    def drain(self):
        for t, to, here in self.parts():

            @pl.when(jnp.logical_not(here))
            def _():
                self.remote(t, to).wait_send()


def by_rows(total, step, body):
    def one(i, carry):
        body(pl.ds(pl.multiple_of(i * step, step), step))
        return carry

    lax.fori_loop(0, total // step, one, 0)


def by_columns(total, body, step=256):
    def one(i, carry):
        body(pl.multiple_of(i * step, LANES), step)
        return carry

    lax.fori_loop(0, total // step, one, 0)
    if total % step:
        body(total // step * step, total % step)


def normalised(values):
    average = jnp.mean(values, axis=-1, keepdims=True)
    centred = values - average
    variance = jnp.mean(centred * centred, axis=-1, keepdims=True)
    return centred * lax.rsqrt(variance + eps_norm)


def place_run(block, source, phase, count):
    moved = pltpu.roll(block, (phase - source) % block.shape[1], axis=1)
    tiles = -(-(phase + count) // LANES) * LANES
    moved = moved[:, :tiles]
    lane = lax.broadcasted_iota(jnp.int32, moved.shape, 1)
    return jnp.where((lane >= phase) & (lane < phase + count), moved, 0.0)


def attend_pair(s, i, q_ref, kv_ref, bias_ref, att_ref, lse_ref, top_ref):
    lanes = pl.ds(pl.multiple_of(i * LANES, LANES), LANES)
    keys, values, queries = kv_ref[0, :, lanes], kv_ref[1, :, lanes], q_ref[:, lanes]
    lane = lax.broadcasted_iota(jnp.int32, queries.shape, 1)
    outs = []
    for side in range(2):
        mine = (lane >= HD) if side else (lane < HD)
        picked = jnp.where(mine, queries, jnp.zeros_like(queries)) * bf16(HD**-0.5)
        scores = nt(keys, picked) + bias_ref[...]
        top = jnp.max(scores, axis=0, keepdims=True)
        weights = jnp.exp(scores - top)
        total = jnp.sum(weights, axis=0, keepdims=True)
        mixed = tn(values[:, side * HD : (side + 1) * HD], weights.astype(bf16))
        outs.append(mixed * (1.0 / total))
        lse_ref[i, side : side + 1, :] = top + jnp.log(total)
        top_ref[i, side : side + 1, :] = top
    att_ref[:, lanes] = jnp.concatenate(outs, axis=0).T.astype(bf16)


def forward_plan(A, B, C, near, far, seq_x, seq_cot):
    def do(method, *args):
        return partial(method, *args)

    return {
        ("start", 0): (
            do(A.arrive, near),
            do(B.begin),
            do(A.arrive, far),
            do(seq_x.start),
        ),
        ("vectors", 0): (
            do(A.turn, near),
            do(B.arrive, near),
            do(C.begin),
            do(A.turn, far),
            do(A.last, near),
            do(B.arrive, far),
            do(A.last, far),
        ),
        ("normed", 0): (do(B.turn, near),),
        ("project", 1): (do(C.arrive, near),),
        ("share", 0): (do(B.turn, far), do(B.last, near)),
        ("pair", 0): (do(C.arrive, far), do(seq_cot.start)),
        ("pair", 2): (do(B.last, far), do(C.turn, near)),
        ("pair", 6): (do(C.turn, far), do(C.last, near)),
        ("down", 0): (do(C.last, far),),
    }


def forward_kernel(s, *refs):
    (own_a, own_b, own_c, small, inp, cot, kinfo, qinfo) = refs[:8]
    (wa_o, wb_o, wc_o, x_o, cot_o, vec, normed_o, q_o, kv_o, att_o, res_o, two_o, slope_o, hid_o) = refs[8:22]
    (lse, top, out_o) = refs[22:25]
    (x, normed, q, kv, bias, att, res, two, wa, wb, wc, out, smalls) = refs[25:38]
    sems = refs[38:]
    net = Net()
    A, B, C = [
        Gather(net, s, w, own, swapped, sems[7 * g : 7 * g + 7])
        for g, (w, own, swapped) in enumerate(
            ((wa, own_a, False), (wb, own_b, False), (wc, own_c, True))
        )
    ]
    seq_x = ToSequences(net, inp, x, sems[21:23])
    seq_cot = ToSequences(net, cot, cot_o, sems[23:25])
    small_s, small_r, kv_s, kv_r, save = sems[25:30]
    near, far = net.near, net.far
    saves = []

    def keep(src, dst):
        copy = pltpu.make_async_copy(src, dst, save.at[len(saves)])
        copy.start()
        saves.append(copy)

    def small_copy(z):
        return pltpu.make_async_remote_copy(
            small,
            smalls.at[net.z],
            small_s.at[z],
            small_r.at[net.z],
            device_id=(net.d, z),
            device_id_type=MESH,
        )

    plan = forward_plan(A, B, C, near, far, seq_x, seq_cot)

    def at(name, step=0):
        for act in plan.get((name, step), ()):
            act()

    enter(net)
    A.begin()
    for z in range(4):

        @pl.when(z != net.z)
        def _():
            small_copy(z).start()

        @pl.when(z == net.z)
        def _():
            pltpu.make_async_copy(small, smalls.at[z], small_r.at[z]).start()

    at("start")
    diff = qinfo[0:1, :] - kinfo[:, 0:1]
    fine = (diff >= 0) & (diff <= kinfo[:, 1:2])
    bias[...] = jnp.where(fine, 0.0, masked_fill)
    at("vectors")

    for z in range(4):
        pltpu.make_async_copy(small, smalls.at[z], small_r.at[z]).wait()
    row = lax.broadcasted_iota(jnp.int32, (3 * LANES, s.wide), 0)
    col = lax.broadcasted_iota(jnp.int32, (3 * LANES, s.wide), 1)
    rows = 0.0
    for z in range(4):
        spread = jnp.where((col == row + z * s.out) & (row < s.out), 1.0, 0.0).astype(bf16)
        rows = rows + product(smalls[z, :, : 3 * LANES], spread)
    vec[...] = rows

    seq_x.wait()
    keep(x, x_o)
    by_rows(
        s.half,
        LANES,
        lambda r: normed.__setitem__(
            (r, slice(None)),
            to_low(
                normalised(x[r, :].astype(f32)) * vec[0:1, : s.width] + vec[1:2, : s.width]
            ),
        ),
    )
    keep(normed, normed_o)
    at("normed")
    A.ready()

    wa_saved = len(saves)
    keep(wa, wa_o)
    q[...] = jnp.zeros_like(q)
    kv[:, : s.half, :] = jnp.zeros((2, s.half, s.wide), bf16)
    places = (q, kv.at[0, pl.ds(0, s.half)], kv.at[1, pl.ds(0, s.half)])
    for z in range(4):

        def part(start, size):
            lanes = pl.ds(pl.multiple_of(z * s.cols + start, LANES), size)
            res[:, pl.ds(start, size)] = product(normed[...], wa[:, lanes])

        by_columns(s.qkv_cols, part)
        for source, target, count in s.qkv_runs(z):
            kind, first = target // s.wide, target % s.wide
            base = first // LANES * LANES
            moved = place_run(res[:, : s.qkv_cols], source, first - base, count)
            lanes = slice(base, base + moved.shape[1])
            if kind != 1:
                lane = lax.broadcasted_iota(jnp.int32, (1, moved.shape[1]), 1)
                fits = (lane >= first - base) & (lane < first - base + count)
                moved = moved + jnp.where(fits, vec[2 + kind // 2 : 3 + kind // 2, lanes], 0.0)
            place = places[kind]
            place[:, lanes] = place[:, lanes] + to_low(moved)
        at("project", z)
    share = pltpu.make_async_remote_copy(
        kv.at[:, pl.ds(0, s.half)],
        kv.at[:, pl.ds(s.half, s.half)],
        kv_s,
        kv_r,
        device_id=net.sib,
        device_id_type=MESH,
    )
    share.start()
    at("share")
    share.wait()
    keep(q, q_o)
    keep(kv, kv_o)

    def pair(i, carry):
        attend_pair(s, i, q, kv, bias, att, lse, top)

        for k in range(s.pairs):
            if ("pair", k) in plan:
                pl.when(i == k)(partial(at, "pair", k))
        return carry

    lax.fori_loop(0, s.pairs, pair, 0)
    keep(att, att_o)

    res[...] = jnp.zeros_like(res)
    for z in range(4):
        lanes = slice(z * s.cols + s.out_tile, (z + 1) * s.cols)
        block = product(att[:, : s.width], wa[:, lanes])
        target = z * s.out
        base = target // LANES * LANES
        moved = place_run(block, s.qkv - s.out_tile, target - base, s.out)
        res[:, base : base + moved.shape[1]] += moved
    at("second")
    B.ready()
    keep(wb, wb_o)

    def second(r):
        total = res[r, : s.width] + x[r, :].astype(f32) + vec[4:5, : s.width]
        res[r, : s.width] = total
        two[r, :] = to_low(normalised(total) * vec[5:6, : s.width] + vec[6:7, : s.width])

    by_rows(s.half, LANES, second)
    keep(res, res_o)
    keep(two, two_o)

    A.drain()
    saves[wa_saved].wait()
    hid, slope = wa.at[pl.ds(0, s.half)], wa.at[pl.ds(s.half, s.half)]
    for z in range(4):

        def part(start, size):
            lanes = pl.ds(pl.multiple_of(z * s.cols + start, LANES), size)
            u = product(two[...], wb[:, lanes])
            u = u + smalls[z, 8:9, pl.ds(start, size)].astype(f32)
            inner = math.sqrt(2 / math.pi) * (u + 0.044715 * u * u * u)
            t = jnp.tanh(inner)
            bend = math.sqrt(2 / math.pi) * (1 + 3 * 0.044715 * u * u)
            hid[:, lanes] = to_low(0.5 * u * (1 + t))
            slope[:, lanes] = to_low(0.5 * (1 + t) + 0.5 * u * (1 - t * t) * bend)

        by_columns(s.cols, part)
        at("up", z)
    keep(hid, hid_o)
    keep(slope, slope_o)
    at("down")
    C.ready()

    keep(wc, wc_o)
    for k in range(3):
        first, count = k * 3 * LANES, min(3 * LANES, s.width - k * 3 * LANES)
        block = nt(hid[...], wc[pl.ds(first, count), :])
        total = res[:, first : first + count] + block + vec[7:8, first : first + count]
        out[:, first : first + count] = to_low(total)
    keep(out, out_o)
    seq_cot.wait()
    for group in (B, C):
        group.drain()
    for z in range(4):

        @pl.when(z != net.z)
        def _():
            small_copy(z).wait_send()

    seq_x.drain()
    seq_cot.drain()
    for i, copy in enumerate(saves):
        if i != wa_saved:
            copy.wait()


def forward_call(s, own_a, own_b, own_c, small, inp, cot, kinfo, qinfo):
    dma = pltpu.SemaphoreType.DMA
    rows = s.half
    full = s.ctx * s.cols

    def low(*shape):
        return jax.ShapeDtypeStruct(shape, bf16)

    def high(*shape):
        return jax.ShapeDtypeStruct(shape, f32)

    out_shape = [low(s.width, full)] * 3 + [
        low(rows, s.width),
        low(rows, s.width),
        high(16, s.wide),
        low(rows, s.width),
        low(rows, s.wide),
        low(2, 2 * rows, s.wide),
        low(rows, s.wide),
        high(rows, s.wide),
        low(rows, s.width),
        low(rows, full),
        low(rows, full),
        high(s.pairs, 2, rows),
        high(s.pairs, 2, rows),
        low(rows, s.width),
    ]
    anywhere = pl.BlockSpec(memory_space=pl.ANY)
    local = pl.BlockSpec(memory_space=pltpu.VMEM)
    out_specs = [local if i in (5, 14, 15) else anywhere for i in range(len(out_shape))]
    return pl.pallas_call(
        partial(forward_kernel, s),
        out_shape=out_shape,
        in_specs=[anywhere] * 6 + [local] * 2,
        out_specs=out_specs,
        scratch_shapes=[
            pltpu.VMEM((rows, s.width), bf16),
            pltpu.VMEM((rows, s.width), bf16),
            pltpu.VMEM((rows, s.wide), bf16),
            pltpu.VMEM((2, 2 * rows, s.wide), bf16),
            pltpu.VMEM((2 * rows, rows), f32),
            pltpu.VMEM((rows, s.wide), bf16),
            pltpu.VMEM((rows, s.wide), f32),
            pltpu.VMEM((rows, s.width), bf16),
            pltpu.VMEM((s.width, full), bf16),
            pltpu.VMEM((s.width, full), bf16),
            pltpu.VMEM((s.width, full), bf16),
            pltpu.VMEM((rows, s.width), bf16),
            pltpu.VMEM((4, 16, s.wide), bf16),
        ]
        + gather_sems() * 3
        + [dma((2,))] * 4
        + [dma((4,)), dma((4,)), dma, dma, dma((14,))],
        compiler_params=pltpu.CompilerParams(
            collective_id=1, has_side_effects=True, vmem_limit_bytes=61 * 2**20
        ),
        name="forward",
    )(own_a, own_b, own_c, small, inp, cot, kinfo, qinfo)


class Scatter:
    def __init__(self, net, s, own, ship, came, first, second, line, total, out, sums, sems):
        self.n, self.s, self.sums = net, s, sums
        self.own, self.ship_ref, self.came = own, ship, came
        self.first_ref, self.second_ref, self.line = first, second, line
        self.total, self.out = total, out
        self.total_like = sums.at[0] if own is None else self.block(0, 0)
        (self.ps, self.pr, self.fs, self.fr, self.hs, self.hr, self.zs, self.zr, self.ld, self.es, self.er, self.eo) = sems

    def target(self, k):
        return (self.n.far, self.n.near)[k]

    def sibling_target(self, k):
        n = self.n
        return 1 - n.c + 2 * (n.z // 2 if k else 1 - n.z // 2)

    def route(self, k):
        n = self.n
        early = self.target(k) < 2
        one = jnp.where(early, n.py, n.px)
        two = jnp.where(early, n.px, n.py)
        return (one, (2 * one + n.c, n.z)), (two, (2 * two + n.c, n.z))

    def block(self, k, p):
        rows = self.s.rows
        return self.own.at[k, pl.ds(pl.multiple_of(p * rows, 16), rows)]

    def remote(self, src, dst, send, recv, to):
        return pltpu.make_async_remote_copy(
            src, dst, send, recv, device_id=to, device_id_type=MESH
        )

    def panel(self, k):
        return self.remote(
            self.ship_ref.at[k], self.came.at[k], self.ps.at[k], self.pr.at[k], self.n.sib
        )

    def pieces(self, k):
        (one, to), _ = self.route(k)
        for i, p in enumerate((one, self.n.pd)):
            yield self.remote(
                self.block(k, p), self.first_ref.at[k, i], self.fs.at[k, i], self.fr.at[k, i], to
            )

    def piece(self, k):
        _, (two, to) = self.route(k)
        return self.remote(
            self.block(k, two), self.second_ref.at[k], self.hs.at[k], self.hr.at[k], to
        )

    def along(self, k):
        n = self.n
        src = self.block(k, n.p) if self.own is not None else self.sums.at[k]
        return self.remote(
            src, self.line.at[n.z], self.zs.at[k], self.zr.at[n.z], (n.d, self.target(k))
        )

    def ship(self, k):
        self.panel(k).start()

    def wait_panel(self, k):
        self.panel(k).wait_recv()

    def start(self, k):
        for copy in self.pieces(k):
            copy.start()

    def add(self, k, p, other):
        rows = self.s.rows

        def some(r):
            at = pl.ds(pl.multiple_of(p * rows + r.start, 16), r.size)
            self.own[k, at, :] = to_low(
                self.own[k, at, :].astype(f32) + other[r, :].astype(f32)
            )

        by_rows(rows, 16, some)

    def turn(self, k):
        for copy in self.pieces(k):
            copy.wait_recv()
        _, (two, _) = self.route(k)
        self.add(k, two, self.first_ref.at[k, 1])
        self.piece(k).start()
        self.add(k, self.n.p, self.first_ref.at[k, 0])

    def land(self, k):
        self.piece(k).wait_recv()
        self.add(k, self.n.p, self.second_ref.at[k])

    def send(self, k):
        @pl.when(self.target(k) != self.n.z)
        def _():
            self.along(k).start()

    def mine(self):
        return self.n.z % 2 == self.n.c

    def collect(self, stage=None):
        n, rows = self.n, self.s.rows

        @pl.when(self.mine())
        def _():
            if self.own is None:
                load = pltpu.make_async_copy(self.sums.at[1], stage, self.ld)
                load.start()
                load.wait()

            def begin(r):
                if self.own is None:
                    value = stage[r, :]
                else:
                    value = self.own[1, pl.ds(pl.multiple_of(n.p * rows + r.start, 16), r.size), :]
                self.total[r, :] = value.astype(f32)

            by_rows(rows, 16, begin)
            for z in range(4):

                @pl.when(z != n.z)
                def _():
                    self.remote(
                        self.total_like, self.line.at[z], self.zs.at[0], self.zr.at[z], n.sib
                    ).wait_recv()
                    if stage is None:
                        other = self.line.at[z]
                    else:
                        other = stage
                        load = pltpu.make_async_copy(self.line.at[z], stage, self.ld)
                        load.start()
                        load.wait()

                    def more(r):
                        self.total[r, :] += other[r, :].astype(f32)

                    by_rows(rows, 16, more)

            pltpu.make_async_copy(self.total, self.out, self.eo).start()
            self.final().start()

    def final(self):
        return self.remote(self.total, self.out, self.es, self.er, self.n.sib)

    def drain(self, panels=True):
        for k in range(2):
            if panels:
                self.panel(k).wait_send()
            for copy in self.pieces(k):
                copy.wait_send()
            self.piece(k).wait_send()

    def finish(self):
        for k in range(2):

            @pl.when(self.target(k) != self.n.z)
            def _():
                self.along(k).wait_send()

        @pl.when(self.mine())
        def _():
            pltpu.make_async_copy(self.total, self.out, self.eo).wait()
            self.final().wait_send()

        @pl.when(jnp.logical_not(self.mine()))
        def _():
            self.final().wait_recv()


def scatter_sems():
    dma = pltpu.SemaphoreType.DMA
    return [
        dma((2,)), dma((2,)), dma((2, 2)), dma((2, 2)), dma((2,)), dma((2,)),
        dma((2,)), dma((4,)), dma, dma, dma, dma,
    ]


def scatter_scratch(s, groups):
    panels = (2, s.width, s.cols)
    scratch = [pltpu.VMEM(panels, bf16)]
    for group in range(groups):
        scratch += [pltpu.VMEM(panels, bf16)] * (1 if group else 2)
        scratch += [
            pltpu.VMEM((2, 2, s.rows, s.cols), bf16),
            pltpu.VMEM((2, s.rows, s.cols), bf16),
        ]
    return scratch + [pltpu.VMEM((s.rows, s.cols), f32), pltpu.VMEM((s.rows, s.cols), bf16)]


def norm_back(values, grads, gain):
    average = jnp.mean(values, axis=-1, keepdims=True)
    centred = values - average
    variance = jnp.mean(centred * centred, axis=-1, keepdims=True)
    scale = lax.rsqrt(variance + eps_norm)
    n = centred * scale
    gn = grads * gain
    inner = jnp.mean(gn * n, axis=-1, keepdims=True)
    back = scale * (gn - jnp.mean(gn, axis=-1, keepdims=True) - n * inner)
    return back, jnp.sum(grads * n, axis=0, keepdims=True), jnp.sum(grads, axis=0, keepdims=True)


def fetch_all(pairs, sems):
    copies = [pltpu.make_async_copy(src, dst, sems.at[i]) for i, (src, dst) in enumerate(pairs)]
    for copy in copies:
        copy.start()
    return copies


def middle_kernel(s, *refs):
    (wa, wb, wc, cot_i, res_i, two_i, slope_i, hid_i, out_i, vec) = refs[:10]
    (down_o, up_s, gres_o, gatt_o, oz_o, sums, back_o, line_c) = refs[10:18]
    (cot, res, two, gp, hid, cot_t, two_t, wt, acc, branch, oz) = refs[18:29]
    (ship, own_c, came, first_c, second_c, own_b, first_b, second_b, total, stage) = refs[29:39]
    sems = refs[39:]
    net = Net()
    C = Scatter(net, s, own_c, ship, came, first_c, second_c, line_c, total, down_o, None, sems[:12])
    B = Scatter(net, s, own_b, ship, came, first_b, second_b, None, None, None, None, sems[12:24])
    seq_out = FromSequences(net, out_i, back_o, sems[24:26])
    load, tiles, save, keep, credit = sems[26:31]
    loads = fetch_all(
        ((cot_i, cot), (hid_i, hid), (slope_i, gp), (two_i, two), (res_i, res)), load
    )
    enter(net)
    seq_out.start()

    def tile(w, j, first=0):
        lanes = pl.ds(j * s.cols + first, s.cols - first)
        return pltpu.make_async_copy(
            w.at[:, lanes], wt.at[j % 2, :, pl.ds(0, s.cols - first)], tiles.at[j % 2]
        )

    tile(wc, 0).start()
    loads[0].wait()
    cot_t[...] = cot[...].T
    loads[1].wait()
    sums[...] = jnp.zeros_like(sums)

    def down_panel(z, dst, k, came=None):
        rows = pl.ds(pl.multiple_of(z * s.rows, 16), s.rows)
        for p in range(4):
            at = slice(p * s.rows, (p + 1) * s.rows)

            def part(start, size):
                lanes = pl.ds(start, size)
                many = pl.ds(pl.multiple_of(p * s.cols + start, LANES), size)
                value = product(cot_t[rows, :], hid[:, many])
                if came is not None:
                    value = value + came[k, at, lanes].astype(f32)
                dst[k, at, lanes] = to_low(value)

            by_columns(s.cols, part)

    def up_panel(z, dst, k, came=None):
        def part(start, size):
            lanes = pl.ds(start, size)
            many = pl.ds(pl.multiple_of(z * s.cols + start, LANES), size)
            value = product(two_t[...], gp[:, many])
            if came is not None:
                value = value + came[k, :, lanes].astype(f32)
            dst[k, :, lanes] = to_low(value)

        by_columns(s.cols, part)

    for k in range(2):
        down_panel(C.sibling_target(k), ship, k)
        C.ship(k)
    loads[2].wait()

    for j in range(4):
        if j < 3:
            tile(wc, j + 1).start()
        tile(wc, j).wait()

        def part(start, size):
            lanes = pl.ds(pl.multiple_of(j * s.cols + start, LANES), size)
            value = product(cot[...], wt[j % 2, :, pl.ds(start, size)])
            value = to_low(value * gp[:, lanes].astype(f32))
            gp[:, lanes] = value
            sums[8 + j : 9 + j, pl.ds(start, size)] = jnp.sum(
                value.astype(f32), axis=0, keepdims=True
            )

        by_columns(s.cols, part)
    tile(wb, 0).start()
    for k in range(2):
        C.wait_panel(k)
        down_panel(C.target(k), own_c, k, came)
        pl.semaphore_signal(
            credit.at[k], inc=1, device_id=net.sib, device_id_type=MESH
        )
        C.start(k)
    loads[3].wait()
    two_t[...] = two[...].T
    for k in range(2):
        C.panel(k).wait_send()
        up_panel(B.sibling_target(k), ship, k)
        pl.semaphore_wait(credit.at[k], 1)
        B.ship(k)

    for z in range(4):
        if z < 3:
            tile(wb, z + 1).start()
        tile(wb, z).wait()

        def part(start, size):
            value = nt(gp[:, z * s.cols : (z + 1) * s.cols], wt[z % 2, pl.ds(start, size), :])
            if z:
                value = value + acc[:, pl.ds(start, size)]
            acc[:, pl.ds(start, size)] = value

        by_columns(s.width, part)
        if z == 1:
            C.turn(0)
    tile(wa, 0, s.out_tile).start()
    for k in range(2):
        B.wait_panel(k)
        up_panel(B.target(k), own_b, k, came)
        B.start(k)
        if k == 0:
            C.turn(1)
    C.land(0)
    C.send(0)
    loads[4].wait()

    def norm(r):
        given = cot[r, :].astype(f32)
        back, gain, shift = norm_back(
            res[r, : s.width], acc[r, : s.width], vec[5:6, : s.width]
        )
        total_r = given + back
        res[r, : s.width] = total_r
        low = to_low(total_r)
        branch[r, : s.width] = low
        sums[4:5, : s.width] += jnp.sum(low.astype(f32), axis=0, keepdims=True)
        sums[5:6, : s.width] += gain
        sums[6:7, : s.width] += shift
        sums[7:8, : s.width] += jnp.sum(given, axis=0, keepdims=True)

    branch[...] = jnp.zeros_like(branch)
    by_rows(s.half, LANES, norm)
    C.land(1)
    C.send(1)
    B.turn(0)

    for z in range(4):
        if z < 3:
            tile(wa, z + 1, s.out_tile).start()
        tile(wa, z, s.out_tile).wait()
        source = z * s.out
        base = source // LANES * LANES
        size = s.cols - s.out_tile
        moved = place_run(
            branch[:, base : base + size].astype(f32), source - base, s.qkv - s.out_tile, s.out
        )
        oz[z] = to_low(moved)

        def part(start, count):
            value = nt(oz[z], wt[z % 2, pl.ds(start, count), :size])
            if z:
                value = value + acc[:, pl.ds(start, count)]
            acc[:, pl.ds(start, count)] = value

        by_columns(s.width, part)
    B.turn(1)
    lane = lax.broadcasted_iota(jnp.int32, (s.half, s.wide), 1)
    branch[...] = to_low(jnp.where(lane < s.width, acc[...], 0.0))
    saves = fetch_all(((res, gres_o), (branch, gatt_o), (oz, oz_o)), save)
    C.collect(stage)
    kept = []
    for k in range(2):
        B.land(k)
        kept.append(pltpu.make_async_copy(B.block(k, net.p), up_s.at[k], keep.at[k]))
        kept[k].start()
    C.drain(False)
    B.drain()
    C.finish()
    for copy in saves + kept:
        copy.wait()
    seq_out.wait()
    seq_out.drain()


def last_kernel(s, *refs):
    (wa, oz_i, dq_i, own_i, sib_i, normed_i, att_i, x_i, gres_i, up_s, vec, sums, tops) = refs[:13]
    (qkv_o, up_o, gin_o, small_o) = refs[13:17]
    (came_d, own_d, dq, wide, qz, oz, norm_t, att_t, normed, att, x, gres, wt, acc, gin, buf, got) = refs[17:34]
    (ship, own_a, came_a, first_a, second_a, total, stage, line_a, line_b) = refs[34:43]
    sems = refs[43:]
    net = Net()
    A = Scatter(net, s, own_a, ship, came_a, first_a, second_a, line_a, total, qkv_o, None, sems[:12])
    B = Scatter(net, s, None, None, None, None, None, line_b, total, up_o, up_s, sems[20:32])
    seq_in = FromSequences(net, gin, gin_o, sems[12:14])
    load, tiles, ds, dr, gs, gr = sems[14:20]
    loads = fetch_all(
        ((dq_i, dq), (own_i, own_d), (normed_i, normed), (att_i, att), (oz_i, oz), (x_i, x), (gres_i, gres)),
        load,
    )
    enter(net)
    swap = pltpu.make_async_remote_copy(
        sib_i, came_d, ds, dr, device_id=net.sib, device_id_type=MESH
    )
    swap.start()
    B.send(0)
    B.send(1)

    def tile(j):
        return pltpu.make_async_copy(
            wa.at[:, pl.ds(j * s.cols, s.qkv_pad)], wt.at[j % 2], tiles.at[j % 2]
        )

    tile(0).start()
    loads[2].wait()
    norm_t[...] = normed[...].T
    loads[3].wait()
    att_t[...] = att[...].T
    loads[0].wait()
    loads[1].wait()
    buf[...] = sums[...]
    wide[:, : s.wide] = dq[...].astype(f32)
    swap.wait()
    for kind in range(2):
        lanes = slice((kind + 1) * s.wide, (kind + 2) * s.wide)
        value = to_low(own_d[kind].astype(f32) + came_d[kind].astype(f32)).astype(f32)
        wide[:, lanes] = value
    buf[2:3, :] = jnp.sum(wide[:, : s.wide], axis=0, keepdims=True)
    buf[3:4, :] = jnp.sum(wide[:, 2 * s.wide :], axis=0, keepdims=True)
    for z in range(4):
        block = 0.0
        for source, target, count in s.qkv_runs(z):
            base = target // LANES * LANES
            moved = place_run(
                wide[:, base : base + s.qkv_pad], target - base, source, count
            )
            if moved.shape[1] < s.qkv_pad:
                moved = jnp.concatenate(
                    [moved, jnp.zeros((s.half, s.qkv_pad - moved.shape[1]), f32)], axis=1
                )
            block = block + moved
        qz[z] = to_low(block)
    loads[4].wait()

    def panel(z, dst, k, came=None):
        def put(start, size, value):
            lanes = pl.ds(start, size)
            if came is not None:
                value = value + came[k, :, lanes].astype(f32)
            dst[k, :, lanes] = to_low(value)

        def part(start, size):
            put(start, size, product(norm_t[...], qz[z, :, pl.ds(start, size)]))

        by_columns(s.out_tile, part)
        mixed = product(norm_t[...], qz[z, :, s.out_tile :]) + product(
            att_t[: s.width, :], oz[z, :, : s.qkv_pad - s.out_tile]
        )
        put(s.out_tile, s.qkv_pad - s.out_tile, mixed)
        rest = product(att_t[: s.width, :], oz[z, :, s.qkv_pad - s.out_tile :])
        put(s.qkv_pad, s.cols - s.qkv_pad, rest)

    for k in range(2):
        panel(A.sibling_target(k), ship, k)
        A.ship(k)
    for z in range(2):
        tile(z + 1).start()
        tile(z).wait()
        through(s, acc, qz, wt, z)
    for k in range(2):
        A.wait_panel(k)
        panel(A.target(k), own_a, k, came_a)
        A.start(k)
    for z in range(2, 4):
        if z < 3:
            tile(z + 1).start()
        tile(z).wait()
        through(s, acc, qz, wt, z)
    loads[5].wait()
    loads[6].wait()

    def norm(r):
        back, gain, shift = norm_back(
            x[r, :].astype(f32), acc[r, : s.width], vec[0:1, : s.width]
        )
        gin[r, :] = to_low(gres[r, : s.width] + back)
        buf[0:1, : s.width] += gain
        buf[1:2, : s.width] += shift

    by_rows(s.half, LANES, norm)
    seq_in.start()

    def exchange(i, to):
        return pltpu.make_async_remote_copy(
            buf, got.at[i], gs.at[i], gr.at[i], device_id=to, device_id_type=MESH
        )

    def join(one, two):
        row = lax.broadcasted_iota(jnp.int32, one.shape, 0)
        return jnp.where(row == 12, jnp.maximum(one, two), one + two)

    row = lax.broadcasted_iota(jnp.int32, buf.shape, 0)
    buf[...] = jnp.where(row == 12, tops[0:1, :], buf[...])
    partners = (net.sib, net.x_to, net.y_to)

    def merge(i):
        exchange(i, partners[i]).wait()
        buf[...] = join(buf[...], got[i])

    exchange(0, partners[0]).start()
    A.turn(0)
    A.turn(1)
    merge(0)
    exchange(1, partners[1]).start()
    B.collect(stage)
    merge(1)
    exchange(2, partners[2]).start()
    A.land(0)
    A.send(0)
    merge(2)

    def around(z):
        return pltpu.make_async_remote_copy(
            buf, got.at[3 + net.z], gs.at[3 + z], gr.at[3 + net.z], device_id=(net.d, z), device_id_type=MESH
        )

    for z in range(4):

        @pl.when(z != net.z)
        def _():
            around(z).start()

        @pl.when(z == net.z)
        def _():
            pltpu.make_async_copy(buf, got.at[3 + z], gr.at[3 + z]).start()

    A.land(1)
    A.send(1)
    B.finish()
    for z in range(4):
        pltpu.make_async_copy(buf, got.at[3 + z], gr.at[3 + z]).wait()

        @pl.when(z != net.z)
        def _():
            around(z).wait_send()

    small_o[...] = join(join(got[3], got[4]), join(got[5], got[6]))
    A.collect()
    A.drain()
    A.finish()
    seq_in.wait()
    seq_in.drain()


def through(s, acc, qz, wt, z):
    def part(start, size):
        value = nt(qz[z], wt[z % 2, pl.ds(start, size), :])
        if z:
            value = value + acc[:, pl.ds(start, size)]
        acc[:, pl.ds(start, size)] = value

    by_columns(s.width, part)


def middle_call(s, shape, wa, wb, wc, cot, res, two, slope, hid, out, vec):
    dma = pltpu.SemaphoreType.DMA
    rows, full = s.half, s.ctx * s.cols
    anywhere = pl.BlockSpec(memory_space=pl.ANY)
    local = pl.BlockSpec(memory_space=pltpu.VMEM)
    low = lambda *dims: jax.ShapeDtypeStruct(dims, bf16)
    high = lambda *dims: jax.ShapeDtypeStruct(dims, f32)
    size = s.cols - s.out_tile
    return pl.pallas_call(
        partial(middle_kernel, s),
        out_shape=[
            high(s.rows, s.cols), low(2, s.rows, s.cols), high(rows, s.wide),
            low(rows, s.wide), low(4, rows, size), high(16, s.wide), low(*shape),
            low(4, s.rows, s.cols),
        ],
        in_specs=[anywhere] * 9 + [local],
        out_specs=[anywhere] * 5 + [local] + [anywhere] * 2,
        scratch_shapes=[
            pltpu.VMEM((rows, s.width), bf16),
            pltpu.VMEM((rows, s.wide), f32),
            pltpu.VMEM((rows, s.width), bf16),
            pltpu.VMEM((rows, full), bf16),
            pltpu.VMEM((rows, full), bf16),
            pltpu.VMEM((s.width, rows), bf16),
            pltpu.VMEM((s.width, rows), bf16),
            pltpu.VMEM((2, s.width, s.cols), bf16),
            pltpu.VMEM((rows, s.wide), f32),
            pltpu.VMEM((rows, s.wide), bf16),
            pltpu.VMEM((4, rows, size), bf16),
        ]
        + scatter_scratch(s, 2)
        + scatter_sems() * 2
        + [dma((2,)), dma((2,)), dma((5,)), dma((2,)), dma((3,)), dma((2,)), pltpu.SemaphoreType.REGULAR((2,))],
        compiler_params=pltpu.CompilerParams(
            collective_id=2, has_side_effects=True, vmem_limit_bytes=63 * 2**20
        ),
        name="middle",
    )(wa, wb, wc, cot, res, two, slope, hid, out, vec)


def last_call(s, shape, wa, oz, dq, d_own, d_sib, normed, att, x, gres, up_sums, vec, sums, tops):
    dma = pltpu.SemaphoreType.DMA
    rows = s.half
    anywhere = pl.BlockSpec(memory_space=pl.ANY)
    local = pl.BlockSpec(memory_space=pltpu.VMEM)
    low = lambda *dims: jax.ShapeDtypeStruct(dims, bf16)
    high = lambda *dims: jax.ShapeDtypeStruct(dims, f32)
    size = s.cols - s.out_tile
    return pl.pallas_call(
        partial(last_kernel, s),
        out_shape=[
            high(s.rows, s.cols), high(s.rows, s.cols), low(*shape), high(16, s.wide),
        ],
        in_specs=[anywhere] * 10 + [local] * 3,
        out_specs=[anywhere, anywhere, anywhere, local],
        scratch_shapes=[
            pltpu.VMEM((2, rows, s.wide), bf16),
            pltpu.VMEM((2, rows, s.wide), bf16),
            pltpu.VMEM((rows, s.wide), bf16),
            pltpu.VMEM((rows, 3 * s.wide), f32),
            pltpu.VMEM((4, rows, s.qkv_pad), bf16),
            pltpu.VMEM((4, rows, size), bf16),
            pltpu.VMEM((s.width, rows), bf16),
            pltpu.VMEM((s.wide, rows), bf16),
            pltpu.VMEM((rows, s.width), bf16),
            pltpu.VMEM((rows, s.wide), bf16),
            pltpu.VMEM((rows, s.width), bf16),
            pltpu.VMEM((rows, s.wide), f32),
            pltpu.VMEM((2, s.width, s.qkv_pad), bf16),
            pltpu.VMEM((rows, s.wide), f32),
            pltpu.VMEM((rows, s.width), bf16),
            pltpu.VMEM((16, s.wide), f32),
            pltpu.VMEM((7, 16, s.wide), f32),
        ]
        + scatter_scratch(s, 1)
        + [pltpu.VMEM((4, s.rows, s.cols), bf16)] * 2
        + scatter_sems()
        + [dma((2,)), dma((2,)), dma((7,)), dma((2,)), dma, dma, dma((7,)), dma((7,))]
        + scatter_sems(),
        compiler_params=pltpu.CompilerParams(
            collective_id=3, has_side_effects=True, vmem_limit_bytes=63 * 2**20
        ),
        name="last",
    )(wa, oz, dq, d_own, d_sib, normed, att, x, gres, up_sums, vec, sums, tops)


def slot_info(moves, segment_ids, padding, stretch_order):
    core, place, local_seqs = moves.core, moves.z, segment_ids.shape[0]
    length = segment_ids.shape[1]
    half = length // 2
    info = jnp.stack([segment_ids, padding], axis=0)
    info_there = moves.swap_core(info)
    info = jnp.where(place // local_seqs == core, info, info_there)
    info = lax.dynamic_index_in_dim(info, place % local_seqs, 1, False)
    stretches = stretch_order.shape[0]
    stretch_len = length // stretches
    info = jnp.take(info.reshape(2, stretches, stretch_len), stretch_order, axis=1)
    positions = stretch_order[:, None] * stretch_len + jnp.arange(stretch_len, dtype=jnp.int32)
    code = (info[0] * (2 * length) + positions).reshape(2, half)
    reach = (info[1] * (length - 1)).reshape(2, half)
    code_own = lax.dynamic_index_in_dim(code, core, 0, False)
    code_sib = lax.dynamic_index_in_dim(code, 1 - core, 0, False)
    reach_own = lax.dynamic_index_in_dim(reach, core, 0, False)
    reach_sib = lax.dynamic_index_in_dim(reach, 1 - core, 0, False)
    kinfo = jnp.stack(
        [jnp.concatenate([code_own, code_sib]), jnp.concatenate([reach_own, reach_sib])], axis=1
    )
    return kinfo, code_own[None]


def pack_blocks(moves, s, w_qkv, w_out, w_up, w_down, vectors, bias_up):
    rows = w_qkv.shape[0]

    def filled(values):
        return jnp.pad(values, ((0, 0), (0, s.cols - values.shape[1])))

    turned = w_down.T
    parts = jnp.concatenate(
        [
            filled(jnp.concatenate([w_qkv, w_out], axis=1)),
            filled(w_up),
            filled(jnp.concatenate([turned[:rows], turned[rows:]], axis=1)),
        ],
        axis=0,
    )
    there = moves.swap_core(parts)
    even = jnp.where(moves.core == 0, parts, there)
    odd = jnp.where(moves.core == 0, there, parts)
    own_a = jnp.concatenate([even[:rows], odd[:rows]], axis=0)
    own_b = jnp.concatenate([even[rows : 2 * rows], odd[rows : 2 * rows]], axis=0)
    ff = turned.shape[1]
    own_c = filled(
        jnp.concatenate(
            [
                jnp.concatenate([v[2 * rows :, :ff], v[2 * rows :, ff : 2 * ff]], axis=0)
                for v in (even, odd)
            ],
            axis=1,
        )
    )
    small = jnp.concatenate([jnp.pad(vectors, ((0, 0), (0, s.cols - vectors.shape[1]))), filled(bias_up[None])], axis=0)
    small = jnp.pad(small, ((0, 16 - small.shape[0]), (0, 0)))
    return own_a, own_b, own_c, small


def fast_shards(
    dp,
    ctx,
    inputs,
    cotangent,
    w_qkv,
    w_out,
    w_up,
    w_down,
    vectors,
    bias_up,
    segment_ids,
    padding,
    stretch_order,
):
    local_seqs, query_len, width = inputs.shape
    heads = width // HD
    s = Sizes(width, w_up.shape[1] * ctx, ctx, dp, segment_ids.shape[1])
    moves = Moves(dp, ctx, local_seqs)
    core, place = moves.core, moves.z
    wide = s.wide
    kinfo, qinfo = slot_info(moves, segment_ids, padding, stretch_order)
    own_a, own_b, own_c, small = pack_blocks(moves, s, w_qkv, w_out, w_up, w_down, vectors, bias_up)
    (wa, wb, wc, x, cot, vec, normed, queries, kv, attended, residual, two, slope, hidden, lse, tops, out) = forward_call(
        s, own_a, own_b, own_c, small, inputs, cotangent, kinfo, qinfo
    )
    down_block, up_sums, gres, gatt, oz, sums, output, _ = middle_call(
        s, inputs.shape, wa, wb, wc, cot, residual, two, slope, hidden, out, vec
    )
    dq, d_own, d_sib = attend_backward(heads, kinfo, qinfo, queries, kv, gatt, lse)
    block_top = jnp.max(tops, axis=2).reshape(1, -1)[:, :heads]
    block_top = jnp.pad(block_top, ((0, 7), (0, wide - heads)))
    qkv_block, up_block, grad_input, small_sums = last_call(
        s, inputs.shape, wa, oz, dq, d_own, d_sib, normed, attended, x, gres, up_sums, vec, sums, block_top
    )
    rows_d = w_qkv.shape[0]
    cols_q, cols_d, cols_f = w_qkv.shape[1], w_out.shape[1], w_up.shape[1]
    ff = w_down.shape[0]

    def own_rows(block):
        return jnp.where(core == 0, block[:rows_d], block[rows_d:])

    qkv_block, up_block = own_rows(qkv_block), own_rows(up_block)
    grad_qkv, grad_out = qkv_block[:, :cols_q], qkv_block[:, cols_q : cols_q + cols_d]
    grad_up = up_block[:, :cols_f]
    grad_down = jnp.where(core == 0, down_block[:, :ff], down_block[:, ff : 2 * ff]).T
    grad_vectors = lax.dynamic_slice_in_dim(small_sums[:8, :width], place * cols_d, cols_d, 1)
    grad_bias = lax.dynamic_index_in_dim(small_sums[8:12], place, 0, False)[:cols_f]
    global_top = small_sums[12, :heads]

    factor = clip_limit / jnp.maximum(global_top, clip_limit)
    per_column = jnp.repeat(jnp.sqrt(factor), HD)
    column_scale = jnp.concatenate([per_column, per_column, jnp.ones((width,), f32)])
    local_scale = lax.dynamic_slice_in_dim(column_scale, place * cols_q, cols_q)
    clipped_qkv = to_low(w_qkv.astype(f32) * local_scale[None, :])
    bias_scale = lax.dynamic_slice_in_dim(per_column, place * cols_d, cols_d)
    clipped_bias = to_low(vectors[2].astype(f32) * bias_scale)
    return (
        output,
        grad_input.astype(f32),
        grad_qkv,
        grad_out,
        grad_up,
        grad_down,
        grad_vectors,
        grad_bias,
        clipped_qkv,
        clipped_bias,
        global_top,
    )


def shards(
    dp,
    ctx,
    inputs,
    cotangent,
    w_qkv,
    w_out,
    w_up,
    w_down,
    vectors,
    bias_up,
    segment_ids,
    padding,
    stretch_order,
):
    local_seqs, query_len, width = inputs.shape
    length = segment_ids.shape[1]
    half = length // 2
    heads = width // HD
    wide = (width + LANES - 1) // LANES * LANES
    rows_d = w_qkv.shape[0]
    cols_d = w_out.shape[1]
    cols_f = w_up.shape[1]
    ratio = w_down.shape[0] // rows_d
    hidden_width = cols_f * ctx
    moves = Moves(dp, ctx, local_seqs)
    core, place = moves.core, moves.z

    extra = jnp.concatenate([vectors.reshape(-1, cols_f), bias_up[None]], axis=0)
    first = jnp.concatenate([jnp.concatenate([w_qkv, w_out], axis=1), extra], axis=0)
    first = moves.gather_ctx(first)
    x_flat = moves.to_sequences(inputs).astype(f32)
    down_packed = jnp.swapaxes(w_down.reshape(ratio, rows_d, cols_d), 0, 1).reshape(rows_d, -1)
    second = moves.gather_ctx(jnp.concatenate([w_up, down_packed], axis=0))
    cot = moves.to_sequences(cotangent)

    def columns(blocks):
        return jnp.swapaxes(blocks, 0, 1).reshape(blocks.shape[1], -1)

    cols_q = w_qkv.shape[1]
    part_qkv = columns(first[:, :rows_d, :cols_q])
    part_out = columns(first[:, :rows_d, cols_q:])
    small = first[:, rows_d:]
    vec_rows = columns(small[:, :-1].reshape(ctx, 8, cols_d)).astype(f32)
    bias_row = small[:, -1].reshape(-1).astype(f32)
    part_up = columns(second[:, :rows_d])
    part_down = second[:, rows_d:].reshape(ctx, rows_d, ratio, cols_d)
    part_down = jnp.transpose(part_down, (2, 1, 0, 3)).reshape(ratio * rows_d, width)

    wide_qkv = moves.gather_dp(part_qkv)
    wide_out = moves.gather_dp(part_out)
    wide_up = moves.gather_dp(part_up)
    wide_down = moves.gather_dp(part_down)

    info = jnp.stack([segment_ids, padding], axis=0)
    info_there = moves.swap_core(info)
    info = jnp.where(place // local_seqs == core, info, info_there)
    info = lax.dynamic_index_in_dim(info, place % local_seqs, 1, False)
    stretches = stretch_order.shape[0]
    stretch_len = length // stretches
    info = jnp.take(info.reshape(2, stretches, stretch_len), stretch_order, axis=1)
    positions = stretch_order[:, None] * stretch_len + jnp.arange(stretch_len, dtype=jnp.int32)
    code = (info[0] * (2 * length) + positions).reshape(2, half)
    reach = (info[1] * (length - 1)).reshape(2, half)
    code_own = lax.dynamic_index_in_dim(code, core, 0, False)
    code_sib = lax.dynamic_index_in_dim(code, 1 - core, 0, False)
    reach_own = lax.dynamic_index_in_dim(reach, core, 0, False)
    reach_sib = lax.dynamic_index_in_dim(reach, 1 - core, 0, False)
    kinfo = jnp.stack(
        [jnp.concatenate([code_own, code_sib]), jnp.concatenate([reach_own, reach_sib])], axis=1
    )
    qinfo = code_own[None]

    normed = to_low(layer_norm(x_flat, vec_rows[0], vec_rows[1]))
    projected = product(normed, wide_qkv)

    def padded(values):
        return jnp.pad(to_low(values), ((0, 0), (0, wide - width)))

    queries = padded(projected[:, :width] + vec_rows[2])
    own = jnp.stack(
        [
            padded(projected[:, width : 2 * width]),
            padded(projected[:, 2 * width :] + vec_rows[3]),
        ]
    )
    sib = moves.swap_core(own)
    attended, lse, tops = attend_forward(heads, kinfo, qinfo, queries, own, sib)
    attended = attended[:, :width]
    block_top = jnp.max(tops, axis=2).reshape(-1)[:heads]
    global_top = lax.pmax(block_top, AXES)
    residual = x_flat + product(attended, wide_out) + vec_rows[4]
    normed_two = to_low(layer_norm(residual, vec_rows[5], vec_rows[6]))
    up_pre = product(normed_two, wide_up) + bias_row
    hidden = to_low(jax.nn.gelu(up_pre, approximate=True))
    output = to_low(residual + product(hidden, wide_down) + vec_rows[7])
    output = moves.from_sequences(output)

    grad_output = cot.astype(f32)
    grad_bias_two = column_sum(cot)
    sum_down = moves.weight_terms(hidden, cot)
    sum_down = moves.scatter_dp(sum_down)
    grad_hidden = contract_cols(cot, wide_down)
    unused, gelu_back = jax.vjp(partial(jax.nn.gelu, approximate=True), up_pre)
    grad_pre = to_low(gelu_back(grad_hidden)[0])
    grad_bias_up = column_sum(grad_pre)
    sum_up = moves.weight_terms(normed_two, grad_pre)
    sum_up = moves.scatter_dp(sum_up)
    unused, norm_back_two = jax.vjp(layer_norm, residual, vec_rows[5], vec_rows[6])
    back_two = norm_back_two(contract_cols(grad_pre, wide_up))
    grad_residual = grad_output + back_two[0]
    grad_branch = to_low(grad_residual)
    sum_out = moves.weight_terms(attended, grad_branch)
    sum_out = moves.scatter_dp(sum_out)
    grad_attended = padded(contract_cols(grad_branch, wide_out))
    dq, d_own, d_sib = attend_backward(
        heads, kinfo, qinfo, queries, jnp.concatenate([own, sib], axis=1), grad_attended, lse
    )
    d_came = moves.swap_core(d_sib)
    d_own = to_low(d_own.astype(f32) + d_came.astype(f32))
    grad_proj = jnp.concatenate([dq[:, :width], d_own[0, :, :width], d_own[1, :, :width]], axis=1)
    sum_qkv = moves.weight_terms(normed, grad_proj)
    sum_qkv = moves.scatter_dp(sum_qkv)
    unused, norm_back_one = jax.vjp(layer_norm, x_flat, vec_rows[0], vec_rows[1])
    back_one = norm_back_one(contract_cols(grad_proj, wide_qkv))
    grad_input = to_low(grad_residual + back_one[0])
    grad_input = moves.from_sequences(grad_input).astype(f32)
    grad_vectors = jnp.stack(
        [
            back_one[1],
            back_one[2],
            column_sum(dq[:, :width]),
            column_sum(d_own[1, :, :width]),
            column_sum(grad_branch),
            back_two[1],
            back_two[2],
            grad_bias_two,
        ]
    )

    def by_place(values):
        return jnp.swapaxes(values.reshape(values.shape[0], ctx, -1), 0, 1)

    blocks_down = sum_down.reshape(ratio, rows_d, ctx, cols_d)
    blocks_down = jnp.transpose(blocks_down, (2, 1, 0, 3)).reshape(ctx, rows_d, -1)
    later = jnp.concatenate([by_place(sum_up), blocks_down, by_place(sum_out)], axis=2)
    later = moves.scatter_ctx(later)
    grad_up = later[:, :cols_f]
    grad_down = later[:, cols_f : 2 * cols_f].reshape(rows_d, ratio, cols_d)
    grad_down = jnp.swapaxes(grad_down, 0, 1).reshape(ratio * rows_d, cols_d)
    grad_out = later[:, 2 * cols_f :]
    grad_qkv = moves.scatter_ctx(by_place(sum_qkv))

    tiny = jnp.concatenate([grad_vectors, grad_bias_up.reshape(-1, width)], axis=0)
    tiny = lax.psum(tiny, AXES)
    grad_vectors = lax.dynamic_slice_in_dim(tiny[:8], place * cols_d, cols_d, 1)
    grad_bias = lax.dynamic_slice_in_dim(tiny[8:].reshape(-1), place * cols_f, cols_f)

    factor = clip_limit / jnp.maximum(global_top, clip_limit)
    per_column = jnp.repeat(jnp.sqrt(factor), HD)
    column_scale = jnp.concatenate([per_column, per_column, jnp.ones((width,), f32)])
    local_scale = lax.dynamic_slice_in_dim(column_scale, place * cols_q, cols_q)
    clipped_qkv = to_low(w_qkv.astype(f32) * local_scale[None, :])
    bias_scale = lax.dynamic_slice_in_dim(per_column, place * cols_d, cols_d)
    clipped_bias = to_low(vectors[2].astype(f32) * bias_scale)
    return (
        output,
        grad_input,
        grad_qkv,
        grad_out,
        grad_up,
        grad_down,
        grad_vectors,
        grad_bias,
        clipped_qkv,
        clipped_bias,
        global_top,
    )


def solution(mesh):
    dp, ctx = mesh.shape["dp"], mesh.shape["ctx"]
    body = fast_shards if (dp, ctx) == (8, 4) else shards
    return jax.shard_map(
        partial(body, dp, ctx),
        mesh=mesh,
        in_specs=(
            P("dp", "ctx", None),
            P("dp", "ctx", None),
            P("dp", "ctx"),
            P("dp", "ctx"),
            P("dp", "ctx"),
            P("dp", "ctx"),
            P(None, "ctx"),
            P("ctx"),
            P("dp", None),
            P("dp", None),
            P(),
        ),
        out_specs=(
            P("dp", "ctx", None),
            P("dp", "ctx", None),
            P("dp", "ctx"),
            P("dp", "ctx"),
            P("dp", "ctx"),
            P("dp", "ctx"),
            P(None, "ctx"),
            P("ctx"),
            P("dp", "ctx"),
            P("ctx"),
            P(),
        ),
        check_vma=False,
    )
```

```python
import math
from functools import partial

import jax
import jax.numpy as jnp
from jax import lax
from jax.experimental import pallas as pl
from jax.experimental.pallas import tpu as pltpu
from jax.sharding import PartitionSpec as P

HD = 64
LANES = 128
AXES = ("dp", "ctx")

eps_norm = 1e-05
clip_limit = 5.0
masked_fill = -1e30
f32 = jnp.float32
bf16 = jnp.bfloat16


def layer_norm(values_in, gain_row, shift_row):
    average = jnp.mean(values_in, axis=-1, keepdims=True)
    centred = values_in - average
    variance = jnp.mean(centred * centred, axis=-1, keepdims=True)
    return centred * lax.rsqrt(variance + eps_norm) * gain_row + shift_row


def to_low(values_in):
    return values_in.astype(bf16)


def product(left, right):
    return jnp.dot(left, right, preferred_element_type=f32)


def contract_rows(left, right):
    return lax.dot_general(left, right, (((0,), (0,)), ((), ())), preferred_element_type=f32)


def contract_cols(left, right):
    return lax.dot_general(left, right, (((1,), (1,)), ((), ())), preferred_element_type=f32)


def column_sum(values_in):
    return jnp.sum(values_in.astype(f32), axis=0)


class Moves:
    def __init__(self, dp, ctx, local_seqs):
        self.dp, self.ctx, self.seqs = dp, ctx, local_seqs
        self.d = lax.axis_index("dp")
        self.z = lax.axis_index("ctx")
        self.core = self.d % 2
        self.cube = dp == 8 and ctx == 4
        self.x = (self.d // 2) % 2
        self.y = self.d // 4

    def permute(self, values, target):
        pairs = []
        for d in range(self.dp):
            for z in range(self.ctx):
                there = target(d, z)
                if there is not None:
                    pairs.append((d * self.ctx + z, there[0] * self.ctx + there[1]))
        return lax.ppermute(values, AXES, pairs)

    def swap_core(self, values):
        return self.permute(values, lambda d, z: (d ^ 1, z))

    def swap_x(self, values):
        return self.permute(values, lambda d, z: (d ^ 2, z))

    def swap_y(self, values):
        return self.permute(values, lambda d, z: (d ^ 4, z))

    def up(self, values):
        return self.permute(values, lambda d, z: (d, z + 1) if z + 1 < self.ctx else None)

    def down(self, values):
        return self.permute(values, lambda d, z: (d, z - 1) if z > 0 else None)

    def sequence_target(self, step):
        n = self.seqs

        def target(d, z):
            return (d - d % 2 + z // n, n * (d % 2) + (z + step) % n)

        return target

    def to_sequences(self, values):
        n = self.seqs
        came = []
        for step in range(n):
            block = lax.dynamic_index_in_dim(values, (self.z + step) % n, 0, keepdims=False)
            came.append(self.permute(block, self.sequence_target(step)))
        return jnp.concatenate([self.choose(came, (self.z - t) % n) for t in range(n)], axis=0)

    def from_sequences(self, values):
        n = self.seqs
        parts = values.reshape(n, values.shape[0] // n, values.shape[1])
        came = []
        for step in range(n):
            forward = self.sequence_target(step)
            block = lax.dynamic_index_in_dim(parts, (self.z - step) % n, 0, keepdims=False)
            back = {}
            for d in range(self.dp):
                for z in range(self.ctx):
                    back[forward(d, z)] = (d, z)
            came.append(self.permute(block, lambda d, z: back[(d, z)]))
        return jnp.stack([self.choose(came, (j - self.z) % n) for j in range(n)], axis=0)

    @staticmethod
    def choose(items, index):
        picked = items[0]
        for i in range(1, len(items)):
            picked = jnp.where(index == i, items[i], picked)
        return picked

    def gather_ctx(self, block):
        if not self.cube:
            return lax.all_gather(block, "ctx", axis=0, tiled=False)
        rising, falling = [block], [block]
        for _ in range(self.ctx - 1):
            rising.append(self.up(rising[-1]))
            falling.append(self.down(falling[-1]))
        line = jnp.stack(rising[:0:-1] + falling, axis=0)
        return lax.dynamic_slice_in_dim(line, self.ctx - 1 - self.z, self.ctx, 0)

    def gather_dp(self, block):
        if not self.cube:
            return lax.all_gather(block, "dp", axis=0, tiled=True)
        rows, cols = block.shape
        half = (cols // 2 + LANES - 1) // LANES * LANES
        from_x, from_y = self.swap_x(block), self.swap_y(block)
        far = jnp.concatenate(
            [self.swap_y(from_x[:, :half]), self.swap_x(from_y[:, half:])], axis=1
        )
        mine = jnp.zeros((4, rows, cols), block.dtype)
        here = 2 * self.y + self.x
        for step, part in enumerate((block, from_x, from_y, far)):
            mine = lax.dynamic_update_slice(mine, part[None], (here ^ step, 0, 0))
        other = self.swap_core(mine)
        first = jnp.where(self.core == 0, mine, other)
        second = jnp.where(self.core == 0, other, mine)
        return jnp.stack([first, second], axis=1).reshape(8 * rows, cols)

    def scatter_ctx(self, blocks):
        if not self.cube:
            return lax.psum_scatter(blocks, "ctx", scatter_dimension=0, tiled=False).astype(f32)

        def part(index):
            return lax.dynamic_index_in_dim(blocks, jnp.clip(index, 0, self.ctx - 1), 0, False)

        falling = rising = None
        for step in range(self.ctx - 1, 0, -1):
            low, high = part(self.z - step), part(self.z + step)
            if falling is not None:
                low = to_low(low.astype(f32) + falling.astype(f32))
                high = to_low(high.astype(f32) + rising.astype(f32))
            n = self.ctx
            falling = self.permute(
                low, lambda d, z: (d, z - 1) if z - step >= 0 else None
            )
            rising = self.permute(
                high, lambda d, z: (d, z + 1) if z + step < n else None
            )
        return part(self.z).astype(f32) + falling.astype(f32) + rising.astype(f32)

    def weight_terms(self, left, right):
        if not self.cube:
            return to_low(contract_rows(left, right))
        tokens, width = left.shape
        rows = width // self.dp
        parts = left.reshape(tokens, self.dp // 2, 2, rows)
        even = parts[:, :, 0].reshape(tokens, -1)
        odd = parts[:, :, 1].reshape(tokens, -1)
        own = jnp.where(self.core == 0, even, odd)
        sibling = jnp.where(self.core == 0, odd, even)
        came = self.swap_core(to_low(contract_rows(sibling, right)))
        return to_low(contract_rows(own, right) + came.astype(f32))

    def scatter_dp(self, terms):
        if not self.cube:
            return lax.psum_scatter(terms, "dp", scatter_dimension=0, tiled=True)
        rows, cols = terms.shape[0] // 4, terms.shape[1]
        half = (cols // 2 + LANES - 1) // LANES * LANES
        grid = terms.reshape(2, 2, rows, cols)

        def pick(values, index, axis):
            return lax.dynamic_index_in_dim(values, index, axis, False)

        def added(one, two):
            return to_low(one.astype(f32) + two.astype(f32))

        left, right = grid[..., :half], grid[..., half:]
        left_x = self.swap_x(pick(left, 1 - self.x, 1))
        right_y = self.swap_y(pick(right, 1 - self.y, 0))
        left = added(pick(left, self.x, 1), left_x)
        right = added(pick(right, self.y, 0), right_y)
        left_y = self.swap_y(pick(left, 1 - self.y, 0))
        right_x = self.swap_x(pick(right, 1 - self.x, 0))
        left = added(pick(left, self.y, 0), left_y)
        right = added(pick(right, self.x, 0), right_x)
        return jnp.concatenate([left, right], axis=1)


def nt(left, right):
    return lax.dot_general(left, right, (((1,), (1,)), ((), ())), preferred_element_type=f32)


def tn(left, right):
    return lax.dot_general(left, right, (((0,), (0,)), ((), ())), preferred_element_type=f32)


def fill_bias(kinfo_ref, qinfo_ref, bias_ref):
    diff = qinfo_ref[0:1, :] - kinfo_ref[:, 0:1]
    fine = (diff >= 0) & (diff <= kinfo_ref[:, 1:2])
    bias_ref[...] = jnp.where(fine, 0.0, masked_fill)


def attend_forward_kernel(
    heads, kinfo_ref, qinfo_ref, q_ref, own_ref, sib_ref, out_ref, lse_ref, top_ref, bias_ref
):
    step = pl.program_id(0)

    @pl.when(step == 0)
    def _():
        fill_bias(kinfo_ref, qinfo_ref, bias_ref)

    keys = jnp.concatenate([own_ref[0], sib_ref[0]], axis=0)
    values = jnp.concatenate([own_ref[1], sib_ref[1]], axis=0)
    queries = q_ref[...]
    lane = lax.broadcasted_iota(jnp.int32, queries.shape, 1)
    outs = []
    for side in range(2):
        mine = (lane >= HD) if side else (lane < HD)
        picked = jnp.where(mine, queries, jnp.zeros_like(queries)) * bf16(HD**-0.5)
        scores = nt(keys, picked) + bias_ref[...]
        top = jnp.max(scores, axis=0, keepdims=True)
        weights = jnp.exp(scores - top)
        total = jnp.sum(weights, axis=0, keepdims=True)
        mixed = tn(values[:, side * HD : (side + 1) * HD], weights.astype(bf16))
        outs.append(mixed * (1.0 / total))
        lse_ref[0, side : side + 1, :] = top + jnp.log(total)
        top_ref[0, side : side + 1, :] = top
    out_ref[...] = jnp.concatenate(outs, axis=0).T.astype(bf16)


def attend_backward_kernel(
    heads,
    kinfo_ref,
    qinfo_ref,
    q_ref,
    own_ref,
    sib_ref,
    grad_ref,
    lse_ref,
    dq_ref,
    down_ref,
    dsib_ref,
    bias_ref,
):
    step = pl.program_id(0)

    @pl.when(step == 0)
    def _():
        fill_bias(kinfo_ref, qinfo_ref, bias_ref)

    keys = jnp.concatenate([own_ref[0], sib_ref[0]], axis=0)
    values = jnp.concatenate([own_ref[1], sib_ref[1]], axis=0)
    queries, grads = q_ref[...], grad_ref[...]
    half = queries.shape[0]
    lane = lax.broadcasted_iota(jnp.int32, queries.shape, 1)
    dqs, dk, dv = [], 0.0, 0.0
    for side in range(2):
        mine = (lane >= HD) if side else (lane < HD)
        picked = jnp.where(mine, queries, jnp.zeros_like(queries)) * bf16(HD**-0.5)
        grad = jnp.where(mine, grads, jnp.zeros_like(grads))
        scores = nt(keys, picked) + bias_ref[...]
        weights = jnp.exp(scores - lse_ref[0, side : side + 1, :])
        dp = nt(values, grad)
        delta = jnp.sum(weights * dp, axis=0, keepdims=True)
        ds = (weights * (dp - delta)).astype(bf16)
        dqs.append(tn(keys[:, side * HD : (side + 1) * HD], ds) * (HD**-0.5))
        dk = dk + product(ds, picked)
        dv = dv + product(weights.astype(bf16), grad)
    dq_ref[...] = jnp.concatenate(dqs, axis=0).T.astype(bf16)
    dk, dv = dk.astype(bf16), dv.astype(bf16)
    down_ref[0] = dk[:half]
    dsib_ref[0] = dk[half:]
    down_ref[1] = dv[:half]
    dsib_ref[1] = dv[half:]


def pair_specs(rows):
    flat = pl.BlockSpec((rows, LANES), lambda i: (0, i))
    double = pl.BlockSpec((2, rows, LANES), lambda i: (0, 0, i))
    per_head = pl.BlockSpec((1, 2, rows), lambda i: (i, 0, 0))
    return flat, double, per_head


def attend_forward(heads, kinfo, qinfo, queries, own, sib):
    rows, width = queries.shape
    pairs = width // LANES
    flat, double, per_head = pair_specs(rows)
    small = jax.ShapeDtypeStruct((pairs, 2, rows), f32)
    return pl.pallas_call(
        partial(attend_forward_kernel, heads),
        grid=(pairs,),
        in_specs=[
            pl.BlockSpec(kinfo.shape, lambda i: (0, 0)),
            pl.BlockSpec(qinfo.shape, lambda i: (0, 0)),
            flat,
            double,
            double,
        ],
        out_specs=[flat, per_head, per_head],
        out_shape=[jax.ShapeDtypeStruct((rows, width), bf16), small, small],
        scratch_shapes=[pltpu.VMEM((2 * rows, rows), f32)],
        compiler_params=pltpu.CompilerParams(vmem_limit_bytes=48 * 2**20),
        cost_estimate=pl.CostEstimate(
            flops=pairs * 16 * rows * rows * LANES,
            bytes_accessed=rows * width * 12,
            transcendentals=pairs * 4 * rows * rows,
        ),
        name="attend_forward",
    )(kinfo, qinfo, queries, own, sib)


def attend_backward(heads, kinfo, qinfo, queries, kv, grad, lse):
    rows, width = queries.shape
    pairs = width // LANES
    flat, double, per_head = pair_specs(rows)
    both = jax.ShapeDtypeStruct((2, rows, width), bf16)
    return pl.pallas_call(
        partial(attend_backward_kernel, heads),
        grid=(pairs,),
        in_specs=[
            pl.BlockSpec(kinfo.shape, lambda i: (0, 0)),
            pl.BlockSpec(qinfo.shape, lambda i: (0, 0)),
            flat,
            double,
            pl.BlockSpec((2, rows, LANES), lambda i: (0, 1, i)),
            flat,
            per_head,
        ],
        out_specs=[flat, double, double],
        out_shape=[jax.ShapeDtypeStruct((rows, width), bf16), both, both],
        scratch_shapes=[pltpu.VMEM((2 * rows, rows), f32)],
        compiler_params=pltpu.CompilerParams(vmem_limit_bytes=48 * 2**20),
        cost_estimate=pl.CostEstimate(
            flops=pairs * 40 * rows * rows * LANES,
            bytes_accessed=rows * width * 22,
            transcendentals=pairs * 4 * rows * rows,
        ),
        name="attend_backward",
    )(kinfo, qinfo, queries, kv, kv, grad, lse)


MESH = pl.DeviceIdType.MESH


class Sizes:
    def __init__(self, width, hidden, ctx, dp, length):
        self.width = width
        self.wide = -(-width // LANES) * LANES
        self.ctx = ctx
        self.rows = 2 * width // dp
        self.qkv = 3 * width // ctx
        self.out = width // ctx
        self.cols = -(-(self.qkv + self.out) // LANES) * LANES
        self.up = hidden // ctx
        self.half = length // 2
        self.pairs = self.wide // LANES
        self.out_tile = self.qkv // LANES * LANES
        self.qkv_cols = 1024
        self.qkv_pad = -(-self.qkv // LANES) * LANES

    def qkv_runs(self, z):
        runs, at = [], z * self.qkv
        end = at + self.qkv
        while at < end:
            kind = at // self.width
            stop = min(end, (kind + 1) * self.width)
            runs.append((at - z * self.qkv, kind * self.wide + at - kind * self.width, stop - at))
            at = stop
        return runs


class Net:
    def __init__(self):
        self.d = lax.axis_index("dp")
        self.z = lax.axis_index("ctx")
        self.c = self.d % 2
        self.p = self.d // 2
        y, x = self.p // 2, self.p % 2
        self.px, self.py, self.pd = 2 * y + 1 - x, 2 * (1 - y) + x, 2 * (1 - y) + 1 - x
        self.x_to = (2 * self.px + self.c, self.z)
        self.y_to = (2 * self.py + self.c, self.z)
        self.sib = (2 * self.p + 1 - self.c, self.z)
        self.near = self.c + 2 * (self.z // 2)
        self.far = self.c + 2 * (1 - self.z // 2)


def enter(net):
    gate = pltpu.get_barrier_semaphore()
    for c in range(2):
        for z in range(4):

            @pl.when((c != net.c) | (z != net.z))
            def _():
                pl.semaphore_signal(gate, inc=1, device_id=(2 * net.p + c, z), device_id_type=MESH)

    for to in (net.x_to, net.y_to):
        pl.semaphore_signal(gate, inc=1, device_id=to, device_id_type=MESH)
    pl.semaphore_wait(gate, 9)


class Gather:
    def __init__(self, net, sizes, w, own, swapped, sems):
        self.n, self.s, self.w, self.own, self.swapped = net, sizes, w, own, swapped
        self.zs, self.zr, self.hs, self.hr, self.cs, self.cr, self.loc = sems

    def at(self, p, z):
        r, c = (z, p) if self.swapped else (p, z)
        s = self.s
        return self.w.at[
            pl.ds(pl.multiple_of(r * s.rows, 16), s.rows),
            pl.ds(pl.multiple_of(c * s.cols, LANES), s.cols),
        ]

    def copy(self, p, z, send, recv, to):
        block = self.at(p, z)
        return pltpu.make_async_remote_copy(
            block, block, send, recv, device_id=to, device_id_type=MESH
        )

    def zcopy(self, z, up):
        n = self.n
        to = (n.d, n.z + 1 if up else n.z - 1)
        return self.copy(n.p, z, self.zs.at[z // 2, int(up)], self.zr.at[z // 2], to)

    def hop(self, p, z, to, k):
        return self.copy(p, z, self.hs.at[z // 2, k], self.hr.at[z // 2, k], to)

    def across(self, p, z):
        return self.copy(p, z, self.cs.at[p, z // 2], self.cr.at[p, z // 2], self.n.sib)

    def begin(self):
        n = self.n

        @pl.when(n.z % 2 == n.c)
        def _():
            local = pltpu.make_async_copy(self.own, self.at(n.p, n.z), self.loc)
            local.start()
            local.wait()

            @pl.when(n.z < 3)
            def _():
                self.zcopy(n.z, True).start()

            @pl.when(n.z > 0)
            def _():
                self.zcopy(n.z, False).start()

    def arrive(self, z):
        n = self.n

        @pl.when(z != n.z)
        def _():
            self.zcopy(z, True).wait_recv()

            @pl.when((z < n.z) & (n.z < 3))
            def _():
                self.zcopy(z, True).start()

            @pl.when((z > n.z) & (n.z > 0))
            def _():
                self.zcopy(z, False).start()

        self.hop(n.p, z, n.x_to, 0).start()
        self.hop(n.p, z, n.y_to, 1).start()
        self.across(n.p, z).start()

    def turn(self, z):
        n = self.n
        self.hop(n.px, z, n.x_to, 0).wait_recv()

        @pl.when(z < 2)
        def _():
            self.hop(n.px, z, n.y_to, 2).start()

        self.across(n.px, z).start()
        self.hop(n.py, z, n.y_to, 1).wait_recv()

        @pl.when(z >= 2)
        def _():
            self.hop(n.py, z, n.x_to, 2).start()

        self.across(n.py, z).start()

    def last(self, z):
        n = self.n
        self.hop(n.pd, z, n.x_to, 2).wait_recv()
        self.across(n.pd, z).start()

    def ready(self):
        n = self.n
        for half in range(2):
            for p in range(4):
                self.across(p, 1 - n.c + 2 * half).wait_recv()

    def drain(self):
        n = self.n
        for half in range(2):
            z = n.c + 2 * half

            @pl.when((z <= n.z) & (n.z < 3))
            def _():
                self.zcopy(z, True).wait_send()

            @pl.when((z >= n.z) & (n.z > 0))
            def _():
                self.zcopy(z, False).wait_send()

            for k, to in enumerate((n.x_to, n.y_to, n.x_to)):
                self.hop(n.p, z, to, k).wait_send()
            for p in range(4):
                self.across(p, z).wait_send()


def gather_sems():
    dma = pltpu.SemaphoreType.DMA
    return [dma((2, 2)), dma((2,)), dma((2, 3)), dma((2, 3)), dma((4, 2)), dma((4, 2)), dma]


class ToSequences:
    def __init__(self, net, src, dst, sems):
        self.n, self.src, self.dst = net, src, dst
        self.ss, self.rs = sems
        self.rows = src.shape[1]

    def parts(self):
        n = self.n
        for j in range(2):
            to = (2 * n.p + n.z // 2, 2 * n.c + j)
            yield j, to, (to[0] == n.d) & (to[1] == n.z)

    def place(self, t):
        return self.dst.at[pl.ds(pl.multiple_of(t * self.rows, 16), self.rows)]

    def remote(self, j, to):
        t = self.n.z % 2
        return pltpu.make_async_remote_copy(
            self.src.at[j],
            self.place(t),
            self.ss.at[j],
            self.rs.at[t],
            device_id=to,
            device_id_type=MESH,
        )

    def start(self):
        for j, to, here in self.parts():

            @pl.when(here)
            def _():
                t = self.n.z % 2
                pltpu.make_async_copy(self.src.at[j], self.place(t), self.rs.at[t]).start()

            @pl.when(jnp.logical_not(here))
            def _():
                self.remote(j, to).start()

    def wait(self):
        for t in range(2):
            pltpu.make_async_copy(self.src.at[0], self.place(t), self.rs.at[t]).wait()

    def drain(self):
        for j, to, here in self.parts():

            @pl.when(jnp.logical_not(here))
            def _():
                self.remote(j, to).wait_send()


class FromSequences:
    def __init__(self, net, src, dst, sems):
        self.n, self.src, self.dst = net, src, dst
        self.ss, self.rs = sems
        self.rows = dst.shape[1]

    def parts(self):
        n = self.n
        for t in range(2):
            to = (2 * n.p + n.z // 2, 2 * n.c + t)
            yield t, to, (to[0] == n.d) & (to[1] == n.z)

    def piece(self, t):
        return self.src.at[pl.ds(t * self.rows, self.rows)]

    def remote(self, t, to):
        j = self.n.z % 2
        return pltpu.make_async_remote_copy(
            self.piece(t),
            self.dst.at[j],
            self.ss.at[t],
            self.rs.at[j],
            device_id=to,
            device_id_type=MESH,
        )

    def start(self):
        for t, to, here in self.parts():

            @pl.when(here)
            def _():
                j = self.n.z % 2
                pltpu.make_async_copy(self.piece(t), self.dst.at[j], self.rs.at[j]).start()

            @pl.when(jnp.logical_not(here))
            def _():
                self.remote(t, to).start()

    def wait(self):
        for j in range(2):
            pltpu.make_async_copy(self.piece(0), self.dst.at[j], self.rs.at[j]).wait()

    def drain(self):
        for t, to, here in self.parts():

            @pl.when(jnp.logical_not(here))
            def _():
                self.remote(t, to).wait_send()


def by_rows(total, step, body):
    def one(i, carry):
        body(pl.ds(pl.multiple_of(i * step, step), step))
        return carry

    lax.fori_loop(0, total // step, one, 0)


def by_columns(total, body, step=640):
    def one(i, carry):
        body(pl.multiple_of(i * step, LANES), step)
        return carry

    lax.fori_loop(0, total // step, one, 0)
    if total % step:
        body(total // step * step, total % step)


def normalised(values):
    average = jnp.mean(values, axis=-1, keepdims=True)
    centred = values - average
    variance = jnp.mean(centred * centred, axis=-1, keepdims=True)
    return centred * lax.rsqrt(variance + eps_norm)


def place_run(block, source, phase, count):
    moved = pltpu.roll(block, (phase - source) % block.shape[1], axis=1)
    tiles = -(-(phase + count) // LANES) * LANES
    moved = moved[:, :tiles]
    lane = lax.broadcasted_iota(jnp.int32, moved.shape, 1)
    return jnp.where((lane >= phase) & (lane < phase + count), moved, 0.0)


def attend_pair(s, i, q_ref, kv_ref, bias_ref, att_ref, lse_ref, top_ref):
    lanes = pl.ds(pl.multiple_of(i * LANES, LANES), LANES)
    keys, values, queries = kv_ref[0, :, lanes], kv_ref[1, :, lanes], q_ref[:, lanes]
    lane = lax.broadcasted_iota(jnp.int32, queries.shape, 1)
    outs = []
    for side in range(2):
        mine = (lane >= HD) if side else (lane < HD)
        picked = jnp.where(mine, queries, jnp.zeros_like(queries)) * bf16(HD**-0.5)
        scores = nt(keys, picked) + bias_ref[...]
        top = jnp.max(scores, axis=0, keepdims=True)
        weights = jnp.exp(scores - top)
        total = jnp.sum(weights, axis=0, keepdims=True)
        mixed = tn(values[:, side * HD : (side + 1) * HD], weights.astype(bf16))
        outs.append(mixed * (1.0 / total))
        lse_ref[i, side : side + 1, :] = top + jnp.log(total)
        top_ref[i, side : side + 1, :] = top
    att_ref[:, lanes] = jnp.concatenate(outs, axis=0).T.astype(bf16)


def forward_plan(A, B, C, near, far, seq_x, seq_cot):
    def do(method, *args):
        return partial(method, *args)

    return {
        ("start", 0): (
            do(A.arrive, near),
            do(B.begin),
            do(A.arrive, far),
            do(seq_x.start),
        ),
        ("vectors", 0): (
            do(A.turn, near),
            do(B.arrive, near),
            do(C.begin),
            do(A.turn, far),
            do(A.last, near),
            do(B.arrive, far),
            do(A.last, far),
        ),
        ("normed", 0): (do(B.turn, near),),
        ("project", 1): (do(C.arrive, near),),
        ("share", 0): (do(B.turn, far), do(B.last, near)),
        ("pair", 0): (do(C.arrive, far), do(seq_cot.start)),
        ("pair", 2): (do(B.last, far), do(C.turn, near)),
        ("pair", 6): (do(C.turn, far), do(C.last, near)),
        ("down", 0): (do(C.last, far),),
    }


def forward_kernel(s, *refs):
    (own_a, own_b, own_c, small, inp, cot, kinfo, qinfo) = refs[:8]
    (wa_o, wb_o, wc_o, x_o, cot_o, vec, normed_o, q_o, kv_o, att_o, res_o, two_o, slope_o, hid_o) = refs[8:22]
    (lse, top, out_o) = refs[22:25]
    (x, normed, q, kv, bias, att, res, two, wa, wb, wc, out, smalls) = refs[25:38]
    sems = refs[38:]
    net = Net()
    A, B, C = [
        Gather(net, s, w, own, swapped, sems[7 * g : 7 * g + 7])
        for g, (w, own, swapped) in enumerate(
            ((wa, own_a, False), (wb, own_b, False), (wc, own_c, True))
        )
    ]
    seq_x = ToSequences(net, inp, x, sems[21:23])
    seq_cot = ToSequences(net, cot, cot_o, sems[23:25])
    small_s, small_r, kv_s, kv_r, save = sems[25:30]
    near, far = net.near, net.far
    saves = []

    def keep(src, dst):
        copy = pltpu.make_async_copy(src, dst, save.at[len(saves)])
        copy.start()
        saves.append(copy)

    def small_copy(z):
        return pltpu.make_async_remote_copy(
            small,
            smalls.at[net.z],
            small_s.at[z],
            small_r.at[net.z],
            device_id=(net.d, z),
            device_id_type=MESH,
        )

    plan = forward_plan(A, B, C, near, far, seq_x, seq_cot)

    def at(name, step=0):
        for act in plan.get((name, step), ()):
            act()

    enter(net)
    A.begin()
    for z in range(4):

        @pl.when(z != net.z)
        def _():
            small_copy(z).start()

        @pl.when(z == net.z)
        def _():
            pltpu.make_async_copy(small, smalls.at[z], small_r.at[z]).start()

    at("start")
    diff = qinfo[0:1, :] - kinfo[:, 0:1]
    fine = (diff >= 0) & (diff <= kinfo[:, 1:2])
    bias[...] = jnp.where(fine, 0.0, masked_fill)
    at("vectors")

    for z in range(4):
        pltpu.make_async_copy(small, smalls.at[z], small_r.at[z]).wait()
    row = lax.broadcasted_iota(jnp.int32, (3 * LANES, s.wide), 0)
    col = lax.broadcasted_iota(jnp.int32, (3 * LANES, s.wide), 1)
    rows = 0.0
    for z in range(4):
        spread = jnp.where((col == row + z * s.out) & (row < s.out), 1.0, 0.0).astype(bf16)
        rows = rows + product(smalls[z, :, : 3 * LANES], spread)
    vec[...] = rows

    seq_x.wait()
    keep(x, x_o)
    by_rows(
        s.half,
        LANES,
        lambda r: normed.__setitem__(
            (r, slice(None)),
            to_low(
                normalised(x[r, :].astype(f32)) * vec[0:1, : s.width] + vec[1:2, : s.width]
            ),
        ),
    )
    keep(normed, normed_o)
    at("normed")
    A.ready()

    wa_saved = len(saves)
    keep(wa, wa_o)
    q[...] = jnp.zeros_like(q)
    kv[:, : s.half, :] = jnp.zeros((2, s.half, s.wide), bf16)
    places = (q, kv.at[0, pl.ds(0, s.half)], kv.at[1, pl.ds(0, s.half)])
    for z in range(4):

        def part(start, size):
            lanes = pl.ds(pl.multiple_of(z * s.cols + start, LANES), size)
            res[:, pl.ds(start, size)] = product(normed[...], wa[:, lanes])

        by_columns(s.qkv_cols, part)
        for source, target, count in s.qkv_runs(z):
            kind, first = target // s.wide, target % s.wide
            base = first // LANES * LANES
            moved = place_run(res[:, : s.qkv_cols], source, first - base, count)
            lanes = slice(base, base + moved.shape[1])
            if kind != 1:
                lane = lax.broadcasted_iota(jnp.int32, (1, moved.shape[1]), 1)
                fits = (lane >= first - base) & (lane < first - base + count)
                moved = moved + jnp.where(fits, vec[2 + kind // 2 : 3 + kind // 2, lanes], 0.0)
            place = places[kind]
            place[:, lanes] = place[:, lanes] + to_low(moved)
        at("project", z)
    share = pltpu.make_async_remote_copy(
        kv.at[:, pl.ds(0, s.half)],
        kv.at[:, pl.ds(s.half, s.half)],
        kv_s,
        kv_r,
        device_id=net.sib,
        device_id_type=MESH,
    )
    share.start()
    at("share")
    share.wait()
    keep(q, q_o)
    keep(kv, kv_o)

    def pair(i, carry):
        attend_pair(s, i, q, kv, bias, att, lse, top)

        for k in range(s.pairs):
            if ("pair", k) in plan:
                pl.when(i == k)(partial(at, "pair", k))
        return carry

    lax.fori_loop(0, s.pairs, pair, 0)
    keep(att, att_o)

    res[...] = jnp.zeros_like(res)
    for z in range(4):
        lanes = slice(z * s.cols + s.out_tile, (z + 1) * s.cols)
        block = product(att[:, : s.width], wa[:, lanes])
        target = z * s.out
        base = target // LANES * LANES
        moved = place_run(block, s.qkv - s.out_tile, target - base, s.out)
        res[:, base : base + moved.shape[1]] += moved
    at("second")
    B.ready()
    keep(wb, wb_o)

    def second(r):
        total = res[r, : s.width] + x[r, :].astype(f32) + vec[4:5, : s.width]
        res[r, : s.width] = total
        two[r, :] = to_low(normalised(total) * vec[5:6, : s.width] + vec[6:7, : s.width])

    by_rows(s.half, LANES, second)
    keep(res, res_o)
    keep(two, two_o)

    A.drain()
    saves[wa_saved].wait()
    hid, slope = wa.at[pl.ds(0, s.half)], wa.at[pl.ds(s.half, s.half)]
    for z in range(4):

        def part(start, size):
            lanes = pl.ds(pl.multiple_of(z * s.cols + start, LANES), size)
            u = product(two[...], wb[:, lanes])
            u = u + smalls[z, 8:9, pl.ds(start, size)].astype(f32)
            inner = math.sqrt(2 / math.pi) * (u + 0.044715 * u * u * u)
            t = jnp.tanh(inner)
            bend = math.sqrt(2 / math.pi) * (1 + 3 * 0.044715 * u * u)
            hid[:, lanes] = to_low(0.5 * u * (1 + t))
            slope[:, lanes] = to_low(0.5 * (1 + t) + 0.5 * u * (1 - t * t) * bend)

        by_columns(s.cols, part)
        at("up", z)
    keep(hid, hid_o)
    keep(slope, slope_o)
    at("down")
    C.ready()

    keep(wc, wc_o)
    for k in range(3):
        first, count = k * 3 * LANES, min(3 * LANES, s.width - k * 3 * LANES)
        block = nt(hid[...], wc[pl.ds(first, count), :])
        total = res[:, first : first + count] + block + vec[7:8, first : first + count]
        out[:, first : first + count] = to_low(total)
    keep(out, out_o)
    seq_cot.wait()
    for group in (B, C):
        group.drain()
    for z in range(4):

        @pl.when(z != net.z)
        def _():
            small_copy(z).wait_send()

    seq_x.drain()
    seq_cot.drain()
    for i, copy in enumerate(saves):
        if i != wa_saved:
            copy.wait()


def forward_call(s, own_a, own_b, own_c, small, inp, cot, kinfo, qinfo):
    dma = pltpu.SemaphoreType.DMA
    rows = s.half
    full = s.ctx * s.cols

    def low(*shape):
        return jax.ShapeDtypeStruct(shape, bf16)

    def high(*shape):
        return jax.ShapeDtypeStruct(shape, f32)

    out_shape = [low(s.width, full)] * 3 + [
        low(rows, s.width),
        low(rows, s.width),
        high(16, s.wide),
        low(rows, s.width),
        low(rows, s.wide),
        low(2, 2 * rows, s.wide),
        low(rows, s.wide),
        high(rows, s.wide),
        low(rows, s.width),
        low(rows, full),
        low(rows, full),
        high(s.pairs, 2, rows),
        high(s.pairs, 2, rows),
        low(rows, s.width),
    ]
    anywhere = pl.BlockSpec(memory_space=pl.ANY)
    local = pl.BlockSpec(memory_space=pltpu.VMEM)
    out_specs = [local if i in (5, 14, 15) else anywhere for i in range(len(out_shape))]
    return pl.pallas_call(
        partial(forward_kernel, s),
        out_shape=out_shape,
        in_specs=[anywhere] * 6 + [local] * 2,
        out_specs=out_specs,
        scratch_shapes=[
            pltpu.VMEM((rows, s.width), bf16),
            pltpu.VMEM((rows, s.width), bf16),
            pltpu.VMEM((rows, s.wide), bf16),
            pltpu.VMEM((2, 2 * rows, s.wide), bf16),
            pltpu.VMEM((2 * rows, rows), f32),
            pltpu.VMEM((rows, s.wide), bf16),
            pltpu.VMEM((rows, s.wide), f32),
            pltpu.VMEM((rows, s.width), bf16),
            pltpu.VMEM((s.width, full), bf16),
            pltpu.VMEM((s.width, full), bf16),
            pltpu.VMEM((s.width, full), bf16),
            pltpu.VMEM((rows, s.width), bf16),
            pltpu.VMEM((4, 16, s.wide), bf16),
        ]
        + gather_sems() * 3
        + [dma((2,))] * 4
        + [dma((4,)), dma((4,)), dma, dma, dma((14,))],
        compiler_params=pltpu.CompilerParams(
            collective_id=1, has_side_effects=True, vmem_limit_bytes=61 * 2**20
        ),
        name="forward",
    )(own_a, own_b, own_c, small, inp, cot, kinfo, qinfo)


class Scatter:
    def __init__(self, net, s, own, ship, came, first, second, line, total, out, sums, sems):
        self.n, self.s, self.sums = net, s, sums
        self.own, self.ship_ref, self.came = own, ship, came
        self.first_ref, self.second_ref, self.line = first, second, line
        self.total, self.out = total, out
        self.total_like = sums.at[0] if own is None else self.block(0, 0)
        (self.ps, self.pr, self.fs, self.fr, self.hs, self.hr, self.zs, self.zr, self.ld, self.es, self.er, self.eo) = sems

    def target(self, k):
        return (self.n.far, self.n.near)[k]

    def sibling_target(self, k):
        n = self.n
        return 1 - n.c + 2 * (n.z // 2 if k else 1 - n.z // 2)

    def route(self, k):
        n = self.n
        early = self.target(k) < 2
        one = jnp.where(early, n.py, n.px)
        two = jnp.where(early, n.px, n.py)
        return (one, (2 * one + n.c, n.z)), (two, (2 * two + n.c, n.z))

    def block(self, k, p):
        rows = self.s.rows
        return self.own.at[k, pl.ds(pl.multiple_of(p * rows, 16), rows)]

    def remote(self, src, dst, send, recv, to):
        return pltpu.make_async_remote_copy(
            src, dst, send, recv, device_id=to, device_id_type=MESH
        )

    def panel(self, k):
        return self.remote(
            self.ship_ref.at[k], self.came.at[k], self.ps.at[k], self.pr.at[k], self.n.sib
        )

    def pieces(self, k):
        (one, to), _ = self.route(k)
        for i, p in enumerate((one, self.n.pd)):
            yield self.remote(
                self.block(k, p), self.first_ref.at[k, i], self.fs.at[k, i], self.fr.at[k, i], to
            )

    def piece(self, k):
        _, (two, to) = self.route(k)
        return self.remote(
            self.block(k, two), self.second_ref.at[k], self.hs.at[k], self.hr.at[k], to
        )

    def along(self, k):
        n = self.n
        src = self.block(k, n.p) if self.own is not None else self.sums.at[k]
        return self.remote(
            src, self.line.at[n.z], self.zs.at[k], self.zr.at[n.z], (n.d, self.target(k))
        )

    def ship(self, k):
        self.panel(k).start()

    def wait_panel(self, k):
        self.panel(k).wait_recv()

    def start(self, k):
        for copy in self.pieces(k):
            copy.start()

    def add(self, k, p, other):
        rows = self.s.rows

        def some(r):
            at = pl.ds(pl.multiple_of(p * rows + r.start, 16), r.size)
            self.own[k, at, :] = to_low(
                self.own[k, at, :].astype(f32) + other[r, :].astype(f32)
            )

        by_rows(rows, 16, some)

    def turn(self, k):
        for copy in self.pieces(k):
            copy.wait_recv()
        _, (two, _) = self.route(k)
        self.add(k, two, self.first_ref.at[k, 1])
        self.piece(k).start()
        self.add(k, self.n.p, self.first_ref.at[k, 0])

    def land(self, k):
        self.piece(k).wait_recv()
        self.add(k, self.n.p, self.second_ref.at[k])

    def send(self, k):
        @pl.when(self.target(k) != self.n.z)
        def _():
            self.along(k).start()

    def mine(self):
        return self.n.z % 2 == self.n.c

    def collect(self, stage=None, held=None):
        n, rows = self.n, self.s.rows

        @pl.when(self.mine())
        def _():
            if self.own is None:
                load = pltpu.make_async_copy(self.sums.at[1], held, self.ld)
                load.start()
                load.wait()

            def begin(r):
                if self.own is None:
                    value = held[r, :]
                else:
                    value = self.own[1, pl.ds(pl.multiple_of(n.p * rows + r.start, 16), r.size), :]
                self.total[r, :] = value.astype(f32)

            by_rows(rows, 16, begin)
            for z in range(4):

                @pl.when(z != n.z)
                def _():
                    self.remote(
                        self.total_like, self.line.at[z], self.zs.at[0], self.zr.at[z], n.sib
                    ).wait_recv()
                    if stage is None:
                        other = self.line.at[z]
                    else:
                        other = stage
                        load = pltpu.make_async_copy(self.line.at[z], stage, self.ld)
                        load.start()
                        load.wait()

                    def more(r):
                        self.total[r, :] += other[r, :].astype(f32)

                    by_rows(rows, 16, more)

            pltpu.make_async_copy(self.total, self.out, self.eo).start()
            self.final().start()

    def final(self):
        return self.remote(self.total, self.out, self.es, self.er, self.n.sib)

    def drain(self, panels=True):
        for k in range(2):
            if panels:
                self.panel(k).wait_send()
            for copy in self.pieces(k):
                copy.wait_send()
            self.piece(k).wait_send()

    def finish(self):
        for k in range(2):

            @pl.when(self.target(k) != self.n.z)
            def _():
                self.along(k).wait_send()

        @pl.when(self.mine())
        def _():
            pltpu.make_async_copy(self.total, self.out, self.eo).wait()
            self.final().wait_send()

        @pl.when(jnp.logical_not(self.mine()))
        def _():
            self.final().wait_recv()


def scatter_sems():
    dma = pltpu.SemaphoreType.DMA
    return [
        dma((2,)), dma((2,)), dma((2, 2)), dma((2, 2)), dma((2,)), dma((2,)),
        dma((2,)), dma((4,)), dma, dma, dma, dma,
    ]


def scatter_scratch(s, groups):
    panels = (2, s.width, s.cols)
    scratch = [pltpu.VMEM(panels, bf16)]
    for group in range(groups):
        scratch += [pltpu.VMEM(panels, bf16)] * (1 if group else 2)
        scratch += [
            pltpu.VMEM((2, 2, s.rows, s.cols), bf16),
            pltpu.VMEM((2, s.rows, s.cols), bf16),
        ]
    return scratch + [pltpu.VMEM((s.rows, s.cols), f32), pltpu.VMEM((s.rows, s.cols), bf16)]


def norm_back(values, grads, gain):
    average = jnp.mean(values, axis=-1, keepdims=True)
    centred = values - average
    variance = jnp.mean(centred * centred, axis=-1, keepdims=True)
    scale = lax.rsqrt(variance + eps_norm)
    n = centred * scale
    gn = grads * gain
    inner = jnp.mean(gn * n, axis=-1, keepdims=True)
    back = scale * (gn - jnp.mean(gn, axis=-1, keepdims=True) - n * inner)
    return back, jnp.sum(grads * n, axis=0, keepdims=True), jnp.sum(grads, axis=0, keepdims=True)


def fetch_all(pairs, sems):
    copies = [pltpu.make_async_copy(src, dst, sems.at[i]) for i, (src, dst) in enumerate(pairs)]
    for copy in copies:
        copy.start()
    return copies


def middle_kernel(s, *refs):
    (wa, wb, wc, cot_i, res_i, two_i, slope_i, hid_i, out_i, vec) = refs[:10]
    (down_s, up_own, gres_o, gatt_o, oz_o, sums, back_o) = refs[10:17]
    (cot, res, two, gp, hid, cot_t, two_t, wt, acc, branch, oz) = refs[17:28]
    (ship, own_c, came, first_c, second_c, own_b) = refs[28:34]
    sems = refs[34:]
    net = Net()
    C = Scatter(net, s, own_c, ship, came, first_c, second_c, None, None, None, None, sems[:12])
    B = Scatter(net, s, own_b, ship, came, None, None, None, None, None, None, sems[12:24])
    seq_out = FromSequences(net, out_i, back_o, sems[24:26])
    load, tiles, save, keep, credit = sems[26:31]
    loads = fetch_all(
        ((cot_i, cot), (hid_i, hid), (slope_i, gp), (two_i, two), (res_i, res)), load
    )
    enter(net)
    seq_out.start()

    def tile(w, j, first=0):
        lanes = pl.ds(j * s.cols + first, s.cols - first)
        return pltpu.make_async_copy(
            w.at[:, lanes], wt.at[j % 2, :, pl.ds(0, s.cols - first)], tiles.at[j % 2]
        )

    tile(wc, 0).start()
    loads[0].wait()
    cot_t[...] = cot[...].T
    loads[1].wait()
    sums[...] = jnp.zeros_like(sums)

    def down_panel(z, dst, k, came=None):
        rows = pl.ds(pl.multiple_of(z * s.rows, 16), s.rows)
        for p in range(4):
            at = slice(p * s.rows, (p + 1) * s.rows)

            def part(start, size):
                lanes = pl.ds(start, size)
                many = pl.ds(pl.multiple_of(p * s.cols + start, LANES), size)
                value = product(cot_t[rows, :], hid[:, many])
                if came is not None:
                    value = value + came[k, at, lanes].astype(f32)
                dst[k, at, lanes] = to_low(value)

            by_columns(s.cols, part)

    def up_panel(z, dst, k, came=None):
        def part(start, size):
            lanes = pl.ds(start, size)
            many = pl.ds(pl.multiple_of(z * s.cols + start, LANES), size)
            value = product(two_t[...], gp[:, many])
            if came is not None:
                value = value + came[k, :, lanes].astype(f32)
            dst[k, :, lanes] = to_low(value)

        by_columns(s.cols, part)

    for k in range(2):
        down_panel(C.sibling_target(k), ship, k)
        C.ship(k)
    loads[2].wait()

    for j in range(4):
        if j < 3:
            tile(wc, j + 1).start()
        tile(wc, j).wait()

        def part(start, size):
            lanes = pl.ds(pl.multiple_of(j * s.cols + start, LANES), size)
            value = product(cot[...], wt[j % 2, :, pl.ds(start, size)])
            value = to_low(value * gp[:, lanes].astype(f32))
            gp[:, lanes] = value
            sums[8 + j : 9 + j, pl.ds(start, size)] = jnp.sum(
                value.astype(f32), axis=0, keepdims=True
            )

        by_columns(s.cols, part)
    tile(wb, 0).start()
    for k in range(2):
        C.wait_panel(k)
        down_panel(C.target(k), own_c, k, came)
        pl.semaphore_signal(
            credit.at[k], inc=1, device_id=net.sib, device_id_type=MESH
        )
        C.start(k)
    loads[3].wait()
    two_t[...] = two[...].T
    for k in range(2):
        C.panel(k).wait_send()
        up_panel(B.sibling_target(k), ship, k)
        pl.semaphore_wait(credit.at[k], 1)
        B.ship(k)

    for z in range(4):
        if z < 3:
            tile(wb, z + 1).start()
        tile(wb, z).wait()

        def part(start, size):
            value = nt(gp[:, z * s.cols : (z + 1) * s.cols], wt[z % 2, pl.ds(start, size), :])
            if z:
                value = value + acc[:, pl.ds(start, size)]
            acc[:, pl.ds(start, size)] = value

        by_columns(s.width, part)
        if z == 1:
            C.turn(0)
    tile(wa, 0, s.out_tile).start()
    for k in range(2):
        B.wait_panel(k)
        up_panel(B.target(k), own_b, k, came)
        if k == 0:
            C.turn(1)
    own_copy = pltpu.make_async_copy(own_b, up_own, save.at[3])
    own_copy.start()
    loads[4].wait()

    def norm(r):
        given = cot[r, :].astype(f32)
        back, gain, shift = norm_back(
            res[r, : s.width], acc[r, : s.width], vec[5:6, : s.width]
        )
        total_r = given + back
        res[r, : s.width] = total_r
        low = to_low(total_r)
        branch[r, : s.width] = low
        sums[4:5, : s.width] += jnp.sum(low.astype(f32), axis=0, keepdims=True)
        sums[5:6, : s.width] += gain
        sums[6:7, : s.width] += shift
        sums[7:8, : s.width] += jnp.sum(given, axis=0, keepdims=True)

    branch[...] = jnp.zeros_like(branch)
    by_rows(s.half, LANES, norm)
    kept = []
    for k in range(2):
        C.land(k)
        kept.append(pltpu.make_async_copy(C.block(k, net.p), down_s.at[k], keep.at[k]))
        kept[k].start()

    for z in range(4):
        if z < 3:
            tile(wa, z + 1, s.out_tile).start()
        tile(wa, z, s.out_tile).wait()
        source = z * s.out
        base = source // LANES * LANES
        size = s.cols - s.out_tile
        moved = place_run(
            branch[:, base : base + size].astype(f32), source - base, s.qkv - s.out_tile, s.out
        )
        oz[z] = to_low(moved)

        def part(start, count):
            value = nt(oz[z], wt[z % 2, pl.ds(start, count), :size])
            if z:
                value = value + acc[:, pl.ds(start, count)]
            acc[:, pl.ds(start, count)] = value

        by_columns(s.width, part)
    lane = lax.broadcasted_iota(jnp.int32, (s.half, s.wide), 1)
    branch[...] = to_low(jnp.where(lane < s.width, acc[...], 0.0))
    saves = fetch_all(((res, gres_o), (branch, gatt_o), (oz, oz_o)), save)
    C.drain(False)
    for k in range(2):
        B.panel(k).wait_send()
    for copy in saves + kept + [own_copy]:
        copy.wait()
    seq_out.wait()
    seq_out.drain()


def back_pair(s, i, q_ref, kv_ref, grad_ref, lse_ref, bias_ref, dq_ref, dkv_ref):
    lanes = pl.ds(pl.multiple_of(i * LANES, LANES), LANES)
    keys, values = kv_ref[0, :, lanes], kv_ref[1, :, lanes]
    queries, grads = q_ref[:, lanes], grad_ref[:, lanes]
    lane = lax.broadcasted_iota(jnp.int32, queries.shape, 1)
    dqs, dk, dv = [], 0.0, 0.0
    for side in range(2):
        mine = (lane >= HD) if side else (lane < HD)
        picked = jnp.where(mine, queries, jnp.zeros_like(queries)) * bf16(HD**-0.5)
        grad = jnp.where(mine, grads, jnp.zeros_like(grads))
        scores = nt(keys, picked) + bias_ref[...]
        weights = jnp.exp(scores - lse_ref[i, side : side + 1, :])
        dp = nt(values, grad)
        delta = jnp.sum(weights * dp, axis=0, keepdims=True)
        ds = (weights * (dp - delta)).astype(bf16)
        dqs.append(tn(keys[:, side * HD : (side + 1) * HD], ds) * (HD**-0.5))
        dk = dk + product(ds, picked)
        dv = dv + product(weights.astype(bf16), grad)
    dq_ref[:, lanes] = jnp.concatenate(dqs, axis=0).T.astype(bf16)
    dkv_ref[0, :, lanes] = dk.astype(bf16)
    dkv_ref[1, :, lanes] = dv.astype(bf16)


def attention_kernel(s, *refs):
    (kinfo, qinfo, lse, q_i, kv_i, grad_i, own_i, down_s) = refs[:8]
    (dq_o, dkv_o, up_s, down_o) = refs[8:12]
    (q, kv, grad, dq, dkv, came, bias, own_b, first_b, second_b, line, total, stage) = refs[12:25]
    sems = refs[25:]
    net = Net()
    B = Scatter(net, s, own_b, None, None, first_b, second_b, None, None, None, None, sems[:12])
    C = Scatter(net, s, None, None, None, None, None, line, total, down_o, down_s, sems[12:24])
    load, save, ds, dr = sems[24:28]
    loads = fetch_all(((own_i, own_b), (q_i, q), (kv_i, kv), (grad_i, grad)), load)
    enter(net)
    loads[0].wait()
    B.start(0)
    B.start(1)
    C.send(0)
    C.send(1)
    fill_bias(kinfo, qinfo, bias)
    for copy in loads[1:]:
        copy.wait()

    def pair(i, carry):
        back_pair(s, i, q, kv, grad, lse, bias, dq, dkv)

        @pl.when(i == 6)
        def _():
            B.turn(0)

        @pl.when(i == 7)
        def _():
            B.turn(1)

        return carry

    lax.fori_loop(0, s.pairs, pair, 0)
    rows = pl.ds(0, s.half)
    swap = pltpu.make_async_remote_copy(
        dkv.at[:, pl.ds(s.half, s.half)], came, ds, dr, device_id=net.sib, device_id_type=MESH
    )
    swap.start()
    saves = [pltpu.make_async_copy(dq, dq_o, save.at[0])]
    saves[0].start()
    C.collect(held=stage)
    swap.wait()

    def join(r):
        for kind in range(2):
            dkv[kind, r, :] = to_low(dkv[kind, r, :].astype(f32) + came[kind, r, :].astype(f32))

    by_rows(s.half, LANES, join)
    saves.append(pltpu.make_async_copy(dkv.at[:, rows], dkv_o, save.at[1]))
    saves[1].start()
    for k in range(2):
        B.land(k)
        saves.append(pltpu.make_async_copy(B.block(k, net.p), up_s.at[k], save.at[2 + k]))
        saves[2 + k].start()
    B.drain(False)
    C.finish()
    for copy in saves:
        copy.wait()


def attention_call(s, kinfo, qinfo, lse, q, kv, grad, own, down_s):
    dma = pltpu.SemaphoreType.DMA
    rows = s.half
    anywhere = pl.BlockSpec(memory_space=pl.ANY)
    local = pl.BlockSpec(memory_space=pltpu.VMEM)
    low = lambda *dims: jax.ShapeDtypeStruct(dims, bf16)
    block = pltpu.VMEM((s.rows, s.cols), bf16)
    return pl.pallas_call(
        partial(attention_kernel, s),
        out_shape=[
            low(rows, s.wide), low(2, rows, s.wide), low(2, s.rows, s.cols),
            jax.ShapeDtypeStruct((s.rows, s.cols), f32),
        ],
        in_specs=[local] * 3 + [anywhere] * 5,
        out_specs=[anywhere] * 4,
        scratch_shapes=[
            pltpu.VMEM((rows, s.wide), bf16),
            pltpu.VMEM((2, 2 * rows, s.wide), bf16),
            pltpu.VMEM((rows, s.wide), bf16),
            pltpu.VMEM((rows, s.wide), bf16),
            pltpu.VMEM((2, 2 * rows, s.wide), bf16),
            pltpu.VMEM((2, rows, s.wide), bf16),
            pltpu.VMEM((2 * rows, rows), f32),
            pltpu.VMEM((2, s.width, s.cols), bf16),
            pltpu.VMEM((2, 2, s.rows, s.cols), bf16),
            pltpu.VMEM((2, s.rows, s.cols), bf16),
            pltpu.VMEM((4, s.rows, s.cols), bf16),
            pltpu.VMEM((s.rows, s.cols), f32),
            block,
        ]
        + scatter_sems() * 2
        + [dma((4,)), dma((4,)), dma, dma],
        compiler_params=pltpu.CompilerParams(
            collective_id=4, has_side_effects=True, vmem_limit_bytes=60 * 2**20
        ),
        name="attention",
    )(kinfo, qinfo, lse, q, kv, grad, own, down_s)


def last_kernel(s, *refs):
    (wa, oz_i, dq_i, own_i, normed_i, att_i, x_i, gres_i, up_s, vec, sums, tops) = refs[:12]
    (qkv_o, up_o, gin_o, small_o) = refs[12:16]
    (own_d, dq, wide, qz, oz, norm_t, att_t, normed, att, x, gres, wt, acc, gin, buf, got) = refs[16:32]
    (ship, own_a, came_a, first_a, second_a, total, stage, line_a, line_b) = refs[32:41]
    sems = refs[41:]
    net = Net()
    A = Scatter(net, s, own_a, ship, came_a, first_a, second_a, line_a, total, qkv_o, None, sems[:12])
    B = Scatter(net, s, None, None, None, None, None, line_b, total, up_o, up_s, sems[18:30])
    seq_in = FromSequences(net, gin, gin_o, sems[12:14])
    load, tiles, gs, gr = sems[14:18]
    loads = fetch_all(
        ((dq_i, dq), (own_i, own_d), (normed_i, normed), (att_i, att), (oz_i, oz), (x_i, x), (gres_i, gres)),
        load,
    )
    enter(net)
    B.send(0)
    B.send(1)

    def tile(j):
        return pltpu.make_async_copy(
            wa.at[:, pl.ds(j * s.cols, s.qkv_pad)], wt.at[j % 2], tiles.at[j % 2]
        )

    tile(0).start()
    loads[2].wait()
    norm_t[...] = normed[...].T
    loads[3].wait()
    att_t[...] = att[...].T
    loads[0].wait()
    loads[1].wait()
    buf[...] = sums[...]
    wide[:, : s.wide] = dq[...].astype(f32)
    for kind in range(2):
        wide[:, (kind + 1) * s.wide : (kind + 2) * s.wide] = own_d[kind].astype(f32)
    buf[2:3, :] = jnp.sum(wide[:, : s.wide], axis=0, keepdims=True)
    buf[3:4, :] = jnp.sum(wide[:, 2 * s.wide :], axis=0, keepdims=True)
    for z in range(4):
        block = 0.0
        for source, target, count in s.qkv_runs(z):
            base = target // LANES * LANES
            moved = place_run(
                wide[:, base : base + s.qkv_pad], target - base, source, count
            )
            if moved.shape[1] < s.qkv_pad:
                moved = jnp.concatenate(
                    [moved, jnp.zeros((s.half, s.qkv_pad - moved.shape[1]), f32)], axis=1
                )
            block = block + moved
        qz[z] = to_low(block)
    loads[4].wait()

    def panel(z, dst, k, came=None):
        def put(start, size, value):
            lanes = pl.ds(start, size)
            if came is not None:
                value = value + came[k, :, lanes].astype(f32)
            dst[k, :, lanes] = to_low(value)

        def part(start, size):
            put(start, size, product(norm_t[...], qz[z, :, pl.ds(start, size)]))

        by_columns(s.out_tile, part)
        mixed = product(norm_t[...], qz[z, :, s.out_tile :]) + product(
            att_t[: s.width, :], oz[z, :, : s.qkv_pad - s.out_tile]
        )
        put(s.out_tile, s.qkv_pad - s.out_tile, mixed)
        rest = product(att_t[: s.width, :], oz[z, :, s.qkv_pad - s.out_tile :])
        put(s.qkv_pad, s.cols - s.qkv_pad, rest)

    for k in range(2):
        panel(A.sibling_target(k), ship, k)
        A.ship(k)
    for k in range(2):
        tile(k + 1).start()
        tile(k).wait()
        through(s, acc, qz, wt, k)
        A.wait_panel(k)
        panel(A.target(k), own_a, k, came_a)
        A.start(k)
    for z in range(2, 4):
        if z < 3:
            tile(z + 1).start()
        tile(z).wait()
        through(s, acc, qz, wt, z)
    loads[5].wait()
    loads[6].wait()

    def norm(r):
        back, gain, shift = norm_back(
            x[r, :].astype(f32), acc[r, : s.width], vec[0:1, : s.width]
        )
        gin[r, :] = to_low(gres[r, : s.width] + back)
        buf[0:1, : s.width] += gain
        buf[1:2, : s.width] += shift

    by_rows(s.half, LANES, norm)
    seq_in.start()

    def exchange(i, to):
        return pltpu.make_async_remote_copy(
            buf, got.at[i], gs.at[i], gr.at[i], device_id=to, device_id_type=MESH
        )

    def join(one, two):
        row = lax.broadcasted_iota(jnp.int32, one.shape, 0)
        return jnp.where(row == 12, jnp.maximum(one, two), one + two)

    row = lax.broadcasted_iota(jnp.int32, buf.shape, 0)
    buf[...] = jnp.where(row == 12, tops[0:1, :], buf[...])
    partners = (net.sib, net.x_to, net.y_to)

    def merge(i):
        exchange(i, partners[i]).wait()
        buf[...] = join(buf[...], got[i])

    exchange(0, partners[0]).start()
    A.turn(0)
    A.turn(1)
    merge(0)
    exchange(1, partners[1]).start()
    B.collect(held=stage)
    merge(1)
    exchange(2, partners[2]).start()
    A.land(0)
    A.send(0)
    merge(2)

    def around(z):
        return pltpu.make_async_remote_copy(
            buf, got.at[3 + net.z], gs.at[3 + z], gr.at[3 + net.z], device_id=(net.d, z), device_id_type=MESH
        )

    for z in range(4):

        @pl.when(z != net.z)
        def _():
            around(z).start()

        @pl.when(z == net.z)
        def _():
            pltpu.make_async_copy(buf, got.at[3 + z], gr.at[3 + z]).start()

    A.land(1)
    A.send(1)
    B.finish()
    for z in range(4):
        pltpu.make_async_copy(buf, got.at[3 + z], gr.at[3 + z]).wait()

        @pl.when(z != net.z)
        def _():
            around(z).wait_send()

    small_o[...] = join(join(got[3], got[4]), join(got[5], got[6]))
    A.collect()
    A.drain()
    A.finish()
    seq_in.wait()
    seq_in.drain()


def through(s, acc, qz, wt, z):
    def part(start, size):
        value = nt(qz[z], wt[z % 2, pl.ds(start, size), :])
        if z:
            value = value + acc[:, pl.ds(start, size)]
        acc[:, pl.ds(start, size)] = value

    by_columns(s.width, part)


def middle_call(s, shape, wa, wb, wc, cot, res, two, slope, hid, out, vec):
    dma = pltpu.SemaphoreType.DMA
    rows, full = s.half, s.ctx * s.cols
    anywhere = pl.BlockSpec(memory_space=pl.ANY)
    local = pl.BlockSpec(memory_space=pltpu.VMEM)
    low = lambda *dims: jax.ShapeDtypeStruct(dims, bf16)
    high = lambda *dims: jax.ShapeDtypeStruct(dims, f32)
    size = s.cols - s.out_tile
    return pl.pallas_call(
        partial(middle_kernel, s),
        out_shape=[
            low(2, s.rows, s.cols), low(2, s.width, s.cols), high(rows, s.wide),
            low(rows, s.wide), low(4, rows, size), high(16, s.wide), low(*shape),
        ],
        in_specs=[anywhere] * 9 + [local],
        out_specs=[anywhere] * 5 + [local, anywhere],
        scratch_shapes=[
            pltpu.VMEM((rows, s.width), bf16),
            pltpu.VMEM((rows, s.wide), f32),
            pltpu.VMEM((rows, s.width), bf16),
            pltpu.VMEM((rows, full), bf16),
            pltpu.VMEM((rows, full), bf16),
            pltpu.VMEM((s.width, rows), bf16),
            pltpu.VMEM((s.width, rows), bf16),
            pltpu.VMEM((2, s.width, s.cols), bf16),
            pltpu.VMEM((rows, s.wide), f32),
            pltpu.VMEM((rows, s.wide), bf16),
            pltpu.VMEM((4, rows, size), bf16),
        ]
        + scatter_scratch(s, 1)[:-2]
        + [pltpu.VMEM((2, s.width, s.cols), bf16)]
        + scatter_sems() * 2
        + [dma((2,)), dma((2,)), dma((5,)), dma((2,)), dma((4,)), dma((2,)), pltpu.SemaphoreType.REGULAR((2,))],
        compiler_params=pltpu.CompilerParams(
            collective_id=2, has_side_effects=True, vmem_limit_bytes=63 * 2**20
        ),
        name="middle",
    )(wa, wb, wc, cot, res, two, slope, hid, out, vec)


def last_call(s, shape, wa, oz, dq, d_own, normed, att, x, gres, up_sums, vec, sums, tops):
    dma = pltpu.SemaphoreType.DMA
    rows = s.half
    anywhere = pl.BlockSpec(memory_space=pl.ANY)
    local = pl.BlockSpec(memory_space=pltpu.VMEM)
    low = lambda *dims: jax.ShapeDtypeStruct(dims, bf16)
    high = lambda *dims: jax.ShapeDtypeStruct(dims, f32)
    size = s.cols - s.out_tile
    return pl.pallas_call(
        partial(last_kernel, s),
        out_shape=[
            high(s.rows, s.cols), high(s.rows, s.cols), low(*shape), high(16, s.wide),
        ],
        in_specs=[anywhere] * 9 + [local] * 3,
        out_specs=[anywhere, anywhere, anywhere, local],
        scratch_shapes=[
            pltpu.VMEM((2, rows, s.wide), bf16),
            pltpu.VMEM((rows, s.wide), bf16),
            pltpu.VMEM((rows, 3 * s.wide), f32),
            pltpu.VMEM((4, rows, s.qkv_pad), bf16),
            pltpu.VMEM((4, rows, size), bf16),
            pltpu.VMEM((s.width, rows), bf16),
            pltpu.VMEM((s.wide, rows), bf16),
            pltpu.VMEM((rows, s.width), bf16),
            pltpu.VMEM((rows, s.wide), bf16),
            pltpu.VMEM((rows, s.width), bf16),
            pltpu.VMEM((rows, s.wide), f32),
            pltpu.VMEM((2, s.width, s.qkv_pad), bf16),
            pltpu.VMEM((rows, s.wide), f32),
            pltpu.VMEM((rows, s.width), bf16),
            pltpu.VMEM((16, s.wide), f32),
            pltpu.VMEM((7, 16, s.wide), f32),
        ]
        + scatter_scratch(s, 1)
        + [pltpu.VMEM((4, s.rows, s.cols), bf16)] * 2
        + scatter_sems()
        + [dma((2,)), dma((2,)), dma((7,)), dma((2,)), dma((7,)), dma((7,))]
        + scatter_sems(),
        compiler_params=pltpu.CompilerParams(
            collective_id=3, has_side_effects=True, vmem_limit_bytes=63 * 2**20
        ),
        name="last",
    )(wa, oz, dq, d_own, normed, att, x, gres, up_sums, vec, sums, tops)


def slot_info(moves, segment_ids, padding, stretch_order):
    core, place, local_seqs = moves.core, moves.z, segment_ids.shape[0]
    length = segment_ids.shape[1]
    half = length // 2
    info = jnp.stack([segment_ids, padding], axis=0)
    info_there = moves.swap_core(info)
    info = jnp.where(place // local_seqs == core, info, info_there)
    info = lax.dynamic_index_in_dim(info, place % local_seqs, 1, False)
    stretches = stretch_order.shape[0]
    stretch_len = length // stretches
    info = jnp.take(info.reshape(2, stretches, stretch_len), stretch_order, axis=1)
    positions = stretch_order[:, None] * stretch_len + jnp.arange(stretch_len, dtype=jnp.int32)
    code = (info[0] * (2 * length) + positions).reshape(2, half)
    reach = (info[1] * (length - 1)).reshape(2, half)
    code_own = lax.dynamic_index_in_dim(code, core, 0, False)
    code_sib = lax.dynamic_index_in_dim(code, 1 - core, 0, False)
    reach_own = lax.dynamic_index_in_dim(reach, core, 0, False)
    reach_sib = lax.dynamic_index_in_dim(reach, 1 - core, 0, False)
    kinfo = jnp.stack(
        [jnp.concatenate([code_own, code_sib]), jnp.concatenate([reach_own, reach_sib])], axis=1
    )
    return kinfo, code_own[None]


def pack_blocks(moves, s, w_qkv, w_out, w_up, w_down, vectors, bias_up):
    rows = w_qkv.shape[0]

    def filled(values):
        return jnp.pad(values, ((0, 0), (0, s.cols - values.shape[1])))

    turned = w_down.T
    parts = jnp.concatenate(
        [
            filled(jnp.concatenate([w_qkv, w_out], axis=1)),
            filled(w_up),
            filled(jnp.concatenate([turned[:rows], turned[rows:]], axis=1)),
        ],
        axis=0,
    )
    there = moves.swap_core(parts)
    even = jnp.where(moves.core == 0, parts, there)
    odd = jnp.where(moves.core == 0, there, parts)
    own_a = jnp.concatenate([even[:rows], odd[:rows]], axis=0)
    own_b = jnp.concatenate([even[rows : 2 * rows], odd[rows : 2 * rows]], axis=0)
    ff = turned.shape[1]
    own_c = filled(
        jnp.concatenate(
            [
                jnp.concatenate([v[2 * rows :, :ff], v[2 * rows :, ff : 2 * ff]], axis=0)
                for v in (even, odd)
            ],
            axis=1,
        )
    )
    small = jnp.concatenate([jnp.pad(vectors, ((0, 0), (0, s.cols - vectors.shape[1]))), filled(bias_up[None])], axis=0)
    small = jnp.pad(small, ((0, 16 - small.shape[0]), (0, 0)))
    return own_a, own_b, own_c, small


def fast_shards(
    dp,
    ctx,
    inputs,
    cotangent,
    w_qkv,
    w_out,
    w_up,
    w_down,
    vectors,
    bias_up,
    segment_ids,
    padding,
    stretch_order,
):
    local_seqs, query_len, width = inputs.shape
    heads = width // HD
    s = Sizes(width, w_up.shape[1] * ctx, ctx, dp, segment_ids.shape[1])
    moves = Moves(dp, ctx, local_seqs)
    core, place = moves.core, moves.z
    wide = s.wide
    kinfo, qinfo = slot_info(moves, segment_ids, padding, stretch_order)
    own_a, own_b, own_c, small = pack_blocks(moves, s, w_qkv, w_out, w_up, w_down, vectors, bias_up)
    (wa, wb, wc, x, cot, vec, normed, queries, kv, attended, residual, two, slope, hidden, lse, tops, out) = forward_call(
        s, own_a, own_b, own_c, small, inputs, cotangent, kinfo, qinfo
    )
    down_sums, up_own, gres, gatt, oz, sums, output = middle_call(
        s, inputs.shape, wa, wb, wc, cot, residual, two, slope, hidden, out, vec
    )
    dq, d_own, up_sums, down_block = attention_call(
        s, kinfo, qinfo, lse, queries, kv, gatt, up_own, down_sums
    )
    block_top = jnp.max(tops, axis=2).reshape(1, -1)[:, :heads]
    block_top = jnp.pad(block_top, ((0, 7), (0, wide - heads)))
    qkv_block, up_block, grad_input, small_sums = last_call(
        s, inputs.shape, wa, oz, dq, d_own, normed, attended, x, gres, up_sums, vec, sums, block_top
    )
    rows_d = w_qkv.shape[0]
    cols_q, cols_d, cols_f = w_qkv.shape[1], w_out.shape[1], w_up.shape[1]
    ff = w_down.shape[0]

    def own_rows(block):
        return jnp.where(core == 0, block[:rows_d], block[rows_d:])

    qkv_block, up_block = own_rows(qkv_block), own_rows(up_block)
    grad_qkv, grad_out = qkv_block[:, :cols_q], qkv_block[:, cols_q : cols_q + cols_d]
    grad_up = up_block[:, :cols_f]
    grad_down = jnp.where(core == 0, down_block[:, :ff], down_block[:, ff : 2 * ff]).T
    grad_vectors = lax.dynamic_slice_in_dim(small_sums[:8, :width], place * cols_d, cols_d, 1)
    grad_bias = lax.dynamic_index_in_dim(small_sums[8:12], place, 0, False)[:cols_f]
    global_top = small_sums[12, :heads]

    factor = clip_limit / jnp.maximum(global_top, clip_limit)
    per_column = jnp.repeat(jnp.sqrt(factor), HD)
    column_scale = jnp.concatenate([per_column, per_column, jnp.ones((width,), f32)])
    local_scale = lax.dynamic_slice_in_dim(column_scale, place * cols_q, cols_q)
    clipped_qkv = to_low(w_qkv.astype(f32) * local_scale[None, :])
    bias_scale = lax.dynamic_slice_in_dim(per_column, place * cols_d, cols_d)
    clipped_bias = to_low(vectors[2].astype(f32) * bias_scale)
    return (
        output,
        grad_input.astype(f32),
        grad_qkv,
        grad_out,
        grad_up,
        grad_down,
        grad_vectors,
        grad_bias,
        clipped_qkv,
        clipped_bias,
        global_top,
    )


def shards(
    dp,
    ctx,
    inputs,
    cotangent,
    w_qkv,
    w_out,
    w_up,
    w_down,
    vectors,
    bias_up,
    segment_ids,
    padding,
    stretch_order,
):
    local_seqs, query_len, width = inputs.shape
    length = segment_ids.shape[1]
    half = length // 2
    heads = width // HD
    wide = (width + LANES - 1) // LANES * LANES
    rows_d = w_qkv.shape[0]
    cols_d = w_out.shape[1]
    cols_f = w_up.shape[1]
    ratio = w_down.shape[0] // rows_d
    hidden_width = cols_f * ctx
    moves = Moves(dp, ctx, local_seqs)
    core, place = moves.core, moves.z

    extra = jnp.concatenate([vectors.reshape(-1, cols_f), bias_up[None]], axis=0)
    first = jnp.concatenate([jnp.concatenate([w_qkv, w_out], axis=1), extra], axis=0)
    first = moves.gather_ctx(first)
    x_flat = moves.to_sequences(inputs).astype(f32)
    down_packed = jnp.swapaxes(w_down.reshape(ratio, rows_d, cols_d), 0, 1).reshape(rows_d, -1)
    second = moves.gather_ctx(jnp.concatenate([w_up, down_packed], axis=0))
    cot = moves.to_sequences(cotangent)

    def columns(blocks):
        return jnp.swapaxes(blocks, 0, 1).reshape(blocks.shape[1], -1)

    cols_q = w_qkv.shape[1]
    part_qkv = columns(first[:, :rows_d, :cols_q])
    part_out = columns(first[:, :rows_d, cols_q:])
    small = first[:, rows_d:]
    vec_rows = columns(small[:, :-1].reshape(ctx, 8, cols_d)).astype(f32)
    bias_row = small[:, -1].reshape(-1).astype(f32)
    part_up = columns(second[:, :rows_d])
    part_down = second[:, rows_d:].reshape(ctx, rows_d, ratio, cols_d)
    part_down = jnp.transpose(part_down, (2, 1, 0, 3)).reshape(ratio * rows_d, width)

    wide_qkv = moves.gather_dp(part_qkv)
    wide_out = moves.gather_dp(part_out)
    wide_up = moves.gather_dp(part_up)
    wide_down = moves.gather_dp(part_down)

    info = jnp.stack([segment_ids, padding], axis=0)
    info_there = moves.swap_core(info)
    info = jnp.where(place // local_seqs == core, info, info_there)
    info = lax.dynamic_index_in_dim(info, place % local_seqs, 1, False)
    stretches = stretch_order.shape[0]
    stretch_len = length // stretches
    info = jnp.take(info.reshape(2, stretches, stretch_len), stretch_order, axis=1)
    positions = stretch_order[:, None] * stretch_len + jnp.arange(stretch_len, dtype=jnp.int32)
    code = (info[0] * (2 * length) + positions).reshape(2, half)
    reach = (info[1] * (length - 1)).reshape(2, half)
    code_own = lax.dynamic_index_in_dim(code, core, 0, False)
    code_sib = lax.dynamic_index_in_dim(code, 1 - core, 0, False)
    reach_own = lax.dynamic_index_in_dim(reach, core, 0, False)
    reach_sib = lax.dynamic_index_in_dim(reach, 1 - core, 0, False)
    kinfo = jnp.stack(
        [jnp.concatenate([code_own, code_sib]), jnp.concatenate([reach_own, reach_sib])], axis=1
    )
    qinfo = code_own[None]

    normed = to_low(layer_norm(x_flat, vec_rows[0], vec_rows[1]))
    projected = product(normed, wide_qkv)

    def padded(values):
        return jnp.pad(to_low(values), ((0, 0), (0, wide - width)))

    queries = padded(projected[:, :width] + vec_rows[2])
    own = jnp.stack(
        [
            padded(projected[:, width : 2 * width]),
            padded(projected[:, 2 * width :] + vec_rows[3]),
        ]
    )
    sib = moves.swap_core(own)
    attended, lse, tops = attend_forward(heads, kinfo, qinfo, queries, own, sib)
    attended = attended[:, :width]
    block_top = jnp.max(tops, axis=2).reshape(-1)[:heads]
    global_top = lax.pmax(block_top, AXES)
    residual = x_flat + product(attended, wide_out) + vec_rows[4]
    normed_two = to_low(layer_norm(residual, vec_rows[5], vec_rows[6]))
    up_pre = product(normed_two, wide_up) + bias_row
    hidden = to_low(jax.nn.gelu(up_pre, approximate=True))
    output = to_low(residual + product(hidden, wide_down) + vec_rows[7])
    output = moves.from_sequences(output)

    grad_output = cot.astype(f32)
    grad_bias_two = column_sum(cot)
    sum_down = moves.weight_terms(hidden, cot)
    sum_down = moves.scatter_dp(sum_down)
    grad_hidden = contract_cols(cot, wide_down)
    unused, gelu_back = jax.vjp(partial(jax.nn.gelu, approximate=True), up_pre)
    grad_pre = to_low(gelu_back(grad_hidden)[0])
    grad_bias_up = column_sum(grad_pre)
    sum_up = moves.weight_terms(normed_two, grad_pre)
    sum_up = moves.scatter_dp(sum_up)
    unused, norm_back_two = jax.vjp(layer_norm, residual, vec_rows[5], vec_rows[6])
    back_two = norm_back_two(contract_cols(grad_pre, wide_up))
    grad_residual = grad_output + back_two[0]
    grad_branch = to_low(grad_residual)
    sum_out = moves.weight_terms(attended, grad_branch)
    sum_out = moves.scatter_dp(sum_out)
    grad_attended = padded(contract_cols(grad_branch, wide_out))
    dq, d_own, d_sib = attend_backward(
        heads, kinfo, qinfo, queries, jnp.concatenate([own, sib], axis=1), grad_attended, lse
    )
    d_came = moves.swap_core(d_sib)
    d_own = to_low(d_own.astype(f32) + d_came.astype(f32))
    grad_proj = jnp.concatenate([dq[:, :width], d_own[0, :, :width], d_own[1, :, :width]], axis=1)
    sum_qkv = moves.weight_terms(normed, grad_proj)
    sum_qkv = moves.scatter_dp(sum_qkv)
    unused, norm_back_one = jax.vjp(layer_norm, x_flat, vec_rows[0], vec_rows[1])
    back_one = norm_back_one(contract_cols(grad_proj, wide_qkv))
    grad_input = to_low(grad_residual + back_one[0])
    grad_input = moves.from_sequences(grad_input).astype(f32)
    grad_vectors = jnp.stack(
        [
            back_one[1],
            back_one[2],
            column_sum(dq[:, :width]),
            column_sum(d_own[1, :, :width]),
            column_sum(grad_branch),
            back_two[1],
            back_two[2],
            grad_bias_two,
        ]
    )

    def by_place(values):
        return jnp.swapaxes(values.reshape(values.shape[0], ctx, -1), 0, 1)

    blocks_down = sum_down.reshape(ratio, rows_d, ctx, cols_d)
    blocks_down = jnp.transpose(blocks_down, (2, 1, 0, 3)).reshape(ctx, rows_d, -1)
    later = jnp.concatenate([by_place(sum_up), blocks_down, by_place(sum_out)], axis=2)
    later = moves.scatter_ctx(later)
    grad_up = later[:, :cols_f]
    grad_down = later[:, cols_f : 2 * cols_f].reshape(rows_d, ratio, cols_d)
    grad_down = jnp.swapaxes(grad_down, 0, 1).reshape(ratio * rows_d, cols_d)
    grad_out = later[:, 2 * cols_f :]
    grad_qkv = moves.scatter_ctx(by_place(sum_qkv))

    tiny = jnp.concatenate([grad_vectors, grad_bias_up.reshape(-1, width)], axis=0)
    tiny = lax.psum(tiny, AXES)
    grad_vectors = lax.dynamic_slice_in_dim(tiny[:8], place * cols_d, cols_d, 1)
    grad_bias = lax.dynamic_slice_in_dim(tiny[8:].reshape(-1), place * cols_f, cols_f)

    factor = clip_limit / jnp.maximum(global_top, clip_limit)
    per_column = jnp.repeat(jnp.sqrt(factor), HD)
    column_scale = jnp.concatenate([per_column, per_column, jnp.ones((width,), f32)])
    local_scale = lax.dynamic_slice_in_dim(column_scale, place * cols_q, cols_q)
    clipped_qkv = to_low(w_qkv.astype(f32) * local_scale[None, :])
    bias_scale = lax.dynamic_slice_in_dim(per_column, place * cols_d, cols_d)
    clipped_bias = to_low(vectors[2].astype(f32) * bias_scale)
    return (
        output,
        grad_input,
        grad_qkv,
        grad_out,
        grad_up,
        grad_down,
        grad_vectors,
        grad_bias,
        clipped_qkv,
        clipped_bias,
        global_top,
    )


def solution(mesh):
    dp, ctx = mesh.shape["dp"], mesh.shape["ctx"]
    body = fast_shards if (dp, ctx) == (8, 4) else shards
    return jax.shard_map(
        partial(body, dp, ctx),
        mesh=mesh,
        in_specs=(
            P("dp", "ctx", None),
            P("dp", "ctx", None),
            P("dp", "ctx"),
            P("dp", "ctx"),
            P("dp", "ctx"),
            P("dp", "ctx"),
            P(None, "ctx"),
            P("ctx"),
            P("dp", None),
            P("dp", None),
            P(),
        ),
        out_specs=(
            P("dp", "ctx", None),
            P("dp", "ctx", None),
            P("dp", "ctx"),
            P("dp", "ctx"),
            P("dp", "ctx"),
            P("dp", "ctx"),
            P(None, "ctx"),
            P("ctx"),
            P("dp", "ctx"),
            P("ctx"),
            P(),
        ),
        check_vma=False,
    )
```

```python
import math
from functools import partial

import jax
import jax.numpy as jnp
from jax import lax
from jax.experimental import pallas as pl
from jax.experimental.pallas import tpu as pltpu
from jax.sharding import PartitionSpec as P

HD = 64
LANES = 128
AXES = ("dp", "ctx")

eps_norm = 1e-05
clip_limit = 5.0
masked_fill = -1e30
f32 = jnp.float32
bf16 = jnp.bfloat16


def layer_norm(values_in, gain_row, shift_row):
    average = jnp.mean(values_in, axis=-1, keepdims=True)
    centred = values_in - average
    variance = jnp.mean(centred * centred, axis=-1, keepdims=True)
    return centred * lax.rsqrt(variance + eps_norm) * gain_row + shift_row


def to_low(values_in):
    return values_in.astype(bf16)


def product(left, right):
    return jnp.dot(left, right, preferred_element_type=f32)


def contract_rows(left, right):
    return lax.dot_general(left, right, (((0,), (0,)), ((), ())), preferred_element_type=f32)


def contract_cols(left, right):
    return lax.dot_general(left, right, (((1,), (1,)), ((), ())), preferred_element_type=f32)


def column_sum(values_in):
    return jnp.sum(values_in.astype(f32), axis=0)


class Moves:
    def __init__(self, dp, ctx, local_seqs):
        self.dp, self.ctx, self.seqs = dp, ctx, local_seqs
        self.d = lax.axis_index("dp")
        self.z = lax.axis_index("ctx")
        self.core = self.d % 2
        self.cube = dp == 8 and ctx == 4
        self.x = (self.d // 2) % 2
        self.y = self.d // 4

    def permute(self, values, target):
        pairs = []
        for d in range(self.dp):
            for z in range(self.ctx):
                there = target(d, z)
                if there is not None:
                    pairs.append((d * self.ctx + z, there[0] * self.ctx + there[1]))
        return lax.ppermute(values, AXES, pairs)

    def swap_core(self, values):
        return self.permute(values, lambda d, z: (d ^ 1, z))

    def swap_x(self, values):
        return self.permute(values, lambda d, z: (d ^ 2, z))

    def swap_y(self, values):
        return self.permute(values, lambda d, z: (d ^ 4, z))

    def up(self, values):
        return self.permute(values, lambda d, z: (d, z + 1) if z + 1 < self.ctx else None)

    def down(self, values):
        return self.permute(values, lambda d, z: (d, z - 1) if z > 0 else None)

    def sequence_target(self, step):
        n = self.seqs

        def target(d, z):
            return (d - d % 2 + z // n, n * (d % 2) + (z + step) % n)

        return target

    def to_sequences(self, values):
        n = self.seqs
        came = []
        for step in range(n):
            block = lax.dynamic_index_in_dim(values, (self.z + step) % n, 0, keepdims=False)
            came.append(self.permute(block, self.sequence_target(step)))
        return jnp.concatenate([self.choose(came, (self.z - t) % n) for t in range(n)], axis=0)

    def from_sequences(self, values):
        n = self.seqs
        parts = values.reshape(n, values.shape[0] // n, values.shape[1])
        came = []
        for step in range(n):
            forward = self.sequence_target(step)
            block = lax.dynamic_index_in_dim(parts, (self.z - step) % n, 0, keepdims=False)
            back = {}
            for d in range(self.dp):
                for z in range(self.ctx):
                    back[forward(d, z)] = (d, z)
            came.append(self.permute(block, lambda d, z: back[(d, z)]))
        return jnp.stack([self.choose(came, (j - self.z) % n) for j in range(n)], axis=0)

    @staticmethod
    def choose(items, index):
        picked = items[0]
        for i in range(1, len(items)):
            picked = jnp.where(index == i, items[i], picked)
        return picked

    def gather_ctx(self, block):
        if not self.cube:
            return lax.all_gather(block, "ctx", axis=0, tiled=False)
        rising, falling = [block], [block]
        for _ in range(self.ctx - 1):
            rising.append(self.up(rising[-1]))
            falling.append(self.down(falling[-1]))
        line = jnp.stack(rising[:0:-1] + falling, axis=0)
        return lax.dynamic_slice_in_dim(line, self.ctx - 1 - self.z, self.ctx, 0)

    def gather_dp(self, block):
        if not self.cube:
            return lax.all_gather(block, "dp", axis=0, tiled=True)
        rows, cols = block.shape
        half = (cols // 2 + LANES - 1) // LANES * LANES
        from_x, from_y = self.swap_x(block), self.swap_y(block)
        far = jnp.concatenate(
            [self.swap_y(from_x[:, :half]), self.swap_x(from_y[:, half:])], axis=1
        )
        mine = jnp.zeros((4, rows, cols), block.dtype)
        here = 2 * self.y + self.x
        for step, part in enumerate((block, from_x, from_y, far)):
            mine = lax.dynamic_update_slice(mine, part[None], (here ^ step, 0, 0))
        other = self.swap_core(mine)
        first = jnp.where(self.core == 0, mine, other)
        second = jnp.where(self.core == 0, other, mine)
        return jnp.stack([first, second], axis=1).reshape(8 * rows, cols)

    def scatter_ctx(self, blocks):
        if not self.cube:
            return lax.psum_scatter(blocks, "ctx", scatter_dimension=0, tiled=False).astype(f32)

        def part(index):
            return lax.dynamic_index_in_dim(blocks, jnp.clip(index, 0, self.ctx - 1), 0, False)

        falling = rising = None
        for step in range(self.ctx - 1, 0, -1):
            low, high = part(self.z - step), part(self.z + step)
            if falling is not None:
                low = to_low(low.astype(f32) + falling.astype(f32))
                high = to_low(high.astype(f32) + rising.astype(f32))
            n = self.ctx
            falling = self.permute(
                low, lambda d, z: (d, z - 1) if z - step >= 0 else None
            )
            rising = self.permute(
                high, lambda d, z: (d, z + 1) if z + step < n else None
            )
        return part(self.z).astype(f32) + falling.astype(f32) + rising.astype(f32)

    def weight_terms(self, left, right):
        if not self.cube:
            return to_low(contract_rows(left, right))
        tokens, width = left.shape
        rows = width // self.dp
        parts = left.reshape(tokens, self.dp // 2, 2, rows)
        even = parts[:, :, 0].reshape(tokens, -1)
        odd = parts[:, :, 1].reshape(tokens, -1)
        own = jnp.where(self.core == 0, even, odd)
        sibling = jnp.where(self.core == 0, odd, even)
        came = self.swap_core(to_low(contract_rows(sibling, right)))
        return to_low(contract_rows(own, right) + came.astype(f32))

    def scatter_dp(self, terms):
        if not self.cube:
            return lax.psum_scatter(terms, "dp", scatter_dimension=0, tiled=True)
        rows, cols = terms.shape[0] // 4, terms.shape[1]
        half = (cols // 2 + LANES - 1) // LANES * LANES
        grid = terms.reshape(2, 2, rows, cols)

        def pick(values, index, axis):
            return lax.dynamic_index_in_dim(values, index, axis, False)

        def added(one, two):
            return to_low(one.astype(f32) + two.astype(f32))

        left, right = grid[..., :half], grid[..., half:]
        left_x = self.swap_x(pick(left, 1 - self.x, 1))
        right_y = self.swap_y(pick(right, 1 - self.y, 0))
        left = added(pick(left, self.x, 1), left_x)
        right = added(pick(right, self.y, 0), right_y)
        left_y = self.swap_y(pick(left, 1 - self.y, 0))
        right_x = self.swap_x(pick(right, 1 - self.x, 0))
        left = added(pick(left, self.y, 0), left_y)
        right = added(pick(right, self.x, 0), right_x)
        return jnp.concatenate([left, right], axis=1)


def nt(left, right):
    return lax.dot_general(left, right, (((1,), (1,)), ((), ())), preferred_element_type=f32)


def tn(left, right):
    return lax.dot_general(left, right, (((0,), (0,)), ((), ())), preferred_element_type=f32)


def fill_bias(kinfo_ref, qinfo_ref, bias_ref):
    diff = qinfo_ref[0:1, :] - kinfo_ref[:, 0:1]
    fine = (diff >= 0) & (diff <= kinfo_ref[:, 1:2])
    bias_ref[...] = jnp.where(fine, 0.0, masked_fill)


def attend_forward_kernel(
    heads, kinfo_ref, qinfo_ref, q_ref, own_ref, sib_ref, out_ref, lse_ref, top_ref, bias_ref
):
    step = pl.program_id(0)

    @pl.when(step == 0)
    def _():
        fill_bias(kinfo_ref, qinfo_ref, bias_ref)

    keys = jnp.concatenate([own_ref[0], sib_ref[0]], axis=0)
    values = jnp.concatenate([own_ref[1], sib_ref[1]], axis=0)
    queries = q_ref[...]
    lane = lax.broadcasted_iota(jnp.int32, queries.shape, 1)
    outs = []
    for side in range(2):
        mine = (lane >= HD) if side else (lane < HD)
        picked = jnp.where(mine, queries, jnp.zeros_like(queries)) * bf16(HD**-0.5)
        scores = nt(keys, picked) + bias_ref[...]
        top = jnp.max(scores, axis=0, keepdims=True)
        weights = jnp.exp(scores - top)
        total = jnp.sum(weights, axis=0, keepdims=True)
        mixed = tn(values[:, side * HD : (side + 1) * HD], weights.astype(bf16))
        outs.append(mixed * (1.0 / total))
        lse_ref[0, side : side + 1, :] = top + jnp.log(total)
        top_ref[0, side : side + 1, :] = top
    out_ref[...] = jnp.concatenate(outs, axis=0).T.astype(bf16)


def attend_backward_kernel(
    heads,
    kinfo_ref,
    qinfo_ref,
    q_ref,
    own_ref,
    sib_ref,
    grad_ref,
    lse_ref,
    dq_ref,
    down_ref,
    dsib_ref,
    bias_ref,
):
    step = pl.program_id(0)

    @pl.when(step == 0)
    def _():
        fill_bias(kinfo_ref, qinfo_ref, bias_ref)

    keys = jnp.concatenate([own_ref[0], sib_ref[0]], axis=0)
    values = jnp.concatenate([own_ref[1], sib_ref[1]], axis=0)
    queries, grads = q_ref[...], grad_ref[...]
    half = queries.shape[0]
    lane = lax.broadcasted_iota(jnp.int32, queries.shape, 1)
    dqs, dk, dv = [], 0.0, 0.0
    for side in range(2):
        mine = (lane >= HD) if side else (lane < HD)
        picked = jnp.where(mine, queries, jnp.zeros_like(queries)) * bf16(HD**-0.5)
        grad = jnp.where(mine, grads, jnp.zeros_like(grads))
        scores = nt(keys, picked) + bias_ref[...]
        weights = jnp.exp(scores - lse_ref[0, side : side + 1, :])
        dp = nt(values, grad)
        delta = jnp.sum(weights * dp, axis=0, keepdims=True)
        ds = (weights * (dp - delta)).astype(bf16)
        dqs.append(tn(keys[:, side * HD : (side + 1) * HD], ds) * (HD**-0.5))
        dk = dk + product(ds, picked)
        dv = dv + product(weights.astype(bf16), grad)
    dq_ref[...] = jnp.concatenate(dqs, axis=0).T.astype(bf16)
    dk, dv = dk.astype(bf16), dv.astype(bf16)
    down_ref[0] = dk[:half]
    dsib_ref[0] = dk[half:]
    down_ref[1] = dv[:half]
    dsib_ref[1] = dv[half:]


def pair_specs(rows):
    flat = pl.BlockSpec((rows, LANES), lambda i: (0, i))
    double = pl.BlockSpec((2, rows, LANES), lambda i: (0, 0, i))
    per_head = pl.BlockSpec((1, 2, rows), lambda i: (i, 0, 0))
    return flat, double, per_head


def attend_forward(heads, kinfo, qinfo, queries, own, sib):
    rows, width = queries.shape
    pairs = width // LANES
    flat, double, per_head = pair_specs(rows)
    small = jax.ShapeDtypeStruct((pairs, 2, rows), f32)
    return pl.pallas_call(
        partial(attend_forward_kernel, heads),
        grid=(pairs,),
        in_specs=[
            pl.BlockSpec(kinfo.shape, lambda i: (0, 0)),
            pl.BlockSpec(qinfo.shape, lambda i: (0, 0)),
            flat,
            double,
            double,
        ],
        out_specs=[flat, per_head, per_head],
        out_shape=[jax.ShapeDtypeStruct((rows, width), bf16), small, small],
        scratch_shapes=[pltpu.VMEM((2 * rows, rows), f32)],
        compiler_params=pltpu.CompilerParams(vmem_limit_bytes=48 * 2**20),
        cost_estimate=pl.CostEstimate(
            flops=pairs * 16 * rows * rows * LANES,
            bytes_accessed=rows * width * 12,
            transcendentals=pairs * 4 * rows * rows,
        ),
        name="attend_forward",
    )(kinfo, qinfo, queries, own, sib)


def attend_backward(heads, kinfo, qinfo, queries, kv, grad, lse):
    rows, width = queries.shape
    pairs = width // LANES
    flat, double, per_head = pair_specs(rows)
    both = jax.ShapeDtypeStruct((2, rows, width), bf16)
    return pl.pallas_call(
        partial(attend_backward_kernel, heads),
        grid=(pairs,),
        in_specs=[
            pl.BlockSpec(kinfo.shape, lambda i: (0, 0)),
            pl.BlockSpec(qinfo.shape, lambda i: (0, 0)),
            flat,
            double,
            pl.BlockSpec((2, rows, LANES), lambda i: (0, 1, i)),
            flat,
            per_head,
        ],
        out_specs=[flat, double, double],
        out_shape=[jax.ShapeDtypeStruct((rows, width), bf16), both, both],
        scratch_shapes=[pltpu.VMEM((2 * rows, rows), f32)],
        compiler_params=pltpu.CompilerParams(vmem_limit_bytes=48 * 2**20),
        cost_estimate=pl.CostEstimate(
            flops=pairs * 40 * rows * rows * LANES,
            bytes_accessed=rows * width * 22,
            transcendentals=pairs * 4 * rows * rows,
        ),
        name="attend_backward",
    )(kinfo, qinfo, queries, kv, kv, grad, lse)


MESH = pl.DeviceIdType.MESH


class Sizes:
    def __init__(self, width, hidden, ctx, dp, length):
        self.width = width
        self.wide = -(-width // LANES) * LANES
        self.ctx = ctx
        self.rows = 2 * width // dp
        self.qkv = 3 * width // ctx
        self.out = width // ctx
        self.cols = -(-(self.qkv + self.out) // LANES) * LANES
        self.up = hidden // ctx
        self.half = length // 2
        self.pairs = self.wide // LANES
        self.out_tile = self.qkv // LANES * LANES
        self.qkv_cols = 1024
        self.qkv_pad = -(-self.qkv // LANES) * LANES

    def qkv_runs(self, z):
        runs, at = [], z * self.qkv
        end = at + self.qkv
        while at < end:
            kind = at // self.width
            stop = min(end, (kind + 1) * self.width)
            runs.append((at - z * self.qkv, kind * self.wide + at - kind * self.width, stop - at))
            at = stop
        return runs


class Net:
    def __init__(self):
        self.d = lax.axis_index("dp")
        self.z = lax.axis_index("ctx")
        self.c = self.d % 2
        self.p = self.d // 2
        y, x = self.p // 2, self.p % 2
        self.px, self.py, self.pd = 2 * y + 1 - x, 2 * (1 - y) + x, 2 * (1 - y) + 1 - x
        self.x_to = (2 * self.px + self.c, self.z)
        self.y_to = (2 * self.py + self.c, self.z)
        self.sib = (2 * self.p + 1 - self.c, self.z)
        self.near = self.c + 2 * (self.z // 2)
        self.far = self.c + 2 * (1 - self.z // 2)


def enter(net):
    gate = pltpu.get_barrier_semaphore()
    for c in range(2):
        for z in range(4):

            @pl.when((c != net.c) | (z != net.z))
            def _():
                pl.semaphore_signal(gate, inc=1, device_id=(2 * net.p + c, z), device_id_type=MESH)

    for to in (net.x_to, net.y_to):
        pl.semaphore_signal(gate, inc=1, device_id=to, device_id_type=MESH)
    pl.semaphore_wait(gate, 9)


class Gather:
    def __init__(self, net, sizes, w, own, swapped, sems):
        self.n, self.s, self.w, self.own, self.swapped = net, sizes, w, own, swapped
        self.zs, self.zr, self.hs, self.hr, self.cs, self.cr, self.loc = sems

    def at(self, p, z):
        r, c = (z, p) if self.swapped else (p, z)
        s = self.s
        return self.w.at[
            pl.ds(pl.multiple_of(r * s.rows, 16), s.rows),
            pl.ds(pl.multiple_of(c * s.cols, LANES), s.cols),
        ]

    def copy(self, p, z, send, recv, to):
        block = self.at(p, z)
        return pltpu.make_async_remote_copy(
            block, block, send, recv, device_id=to, device_id_type=MESH
        )

    def zcopy(self, z, up):
        n = self.n
        to = (n.d, n.z + 1 if up else n.z - 1)
        return self.copy(n.p, z, self.zs.at[z // 2, int(up)], self.zr.at[z // 2], to)

    def hop(self, p, z, to, k):
        return self.copy(p, z, self.hs.at[z // 2, k], self.hr.at[z // 2, k], to)

    def across(self, p, z):
        return self.copy(p, z, self.cs.at[p, z // 2], self.cr.at[p, z // 2], self.n.sib)

    def begin(self):
        n = self.n

        @pl.when(n.z % 2 == n.c)
        def _():
            local = pltpu.make_async_copy(self.own, self.at(n.p, n.z), self.loc)
            local.start()
            local.wait()

            @pl.when(n.z < 3)
            def _():
                self.zcopy(n.z, True).start()

            @pl.when(n.z > 0)
            def _():
                self.zcopy(n.z, False).start()

    def arrive(self, z):
        n = self.n

        @pl.when(z != n.z)
        def _():
            self.zcopy(z, True).wait_recv()

            @pl.when((z < n.z) & (n.z < 3))
            def _():
                self.zcopy(z, True).start()

            @pl.when((z > n.z) & (n.z > 0))
            def _():
                self.zcopy(z, False).start()

        self.hop(n.p, z, n.x_to, 0).start()
        self.hop(n.p, z, n.y_to, 1).start()
        self.across(n.p, z).start()

    def turn(self, z):
        n = self.n
        self.hop(n.px, z, n.x_to, 0).wait_recv()

        @pl.when(z < 2)
        def _():
            self.hop(n.px, z, n.y_to, 2).start()

        self.across(n.px, z).start()
        self.hop(n.py, z, n.y_to, 1).wait_recv()

        @pl.when(z >= 2)
        def _():
            self.hop(n.py, z, n.x_to, 2).start()

        self.across(n.py, z).start()

    def last(self, z):
        n = self.n
        self.hop(n.pd, z, n.x_to, 2).wait_recv()
        self.across(n.pd, z).start()

    def ready(self):
        n = self.n
        for half in range(2):
            for p in range(4):
                self.across(p, 1 - n.c + 2 * half).wait_recv()

    def drain(self):
        n = self.n
        for half in range(2):
            z = n.c + 2 * half

            @pl.when((z <= n.z) & (n.z < 3))
            def _():
                self.zcopy(z, True).wait_send()

            @pl.when((z >= n.z) & (n.z > 0))
            def _():
                self.zcopy(z, False).wait_send()

            for k, to in enumerate((n.x_to, n.y_to, n.x_to)):
                self.hop(n.p, z, to, k).wait_send()
            for p in range(4):
                self.across(p, z).wait_send()


def gather_sems():
    dma = pltpu.SemaphoreType.DMA
    return [dma((2, 2)), dma((2,)), dma((2, 3)), dma((2, 3)), dma((4, 2)), dma((4, 2)), dma]


class ToSequences:
    def __init__(self, net, src, dst, sems):
        self.n, self.src, self.dst = net, src, dst
        self.ss, self.rs = sems
        self.rows = src.shape[1]

    def parts(self):
        n = self.n
        for j in range(2):
            to = (2 * n.p + n.z // 2, 2 * n.c + j)
            yield j, to, (to[0] == n.d) & (to[1] == n.z)

    def place(self, t):
        return self.dst.at[pl.ds(pl.multiple_of(t * self.rows, 16), self.rows)]

    def remote(self, j, to):
        t = self.n.z % 2
        return pltpu.make_async_remote_copy(
            self.src.at[j],
            self.place(t),
            self.ss.at[j],
            self.rs.at[t],
            device_id=to,
            device_id_type=MESH,
        )

    def start(self):
        for j, to, here in self.parts():

            @pl.when(here)
            def _():
                t = self.n.z % 2
                pltpu.make_async_copy(self.src.at[j], self.place(t), self.rs.at[t]).start()

            @pl.when(jnp.logical_not(here))
            def _():
                self.remote(j, to).start()

    def wait(self):
        for t in range(2):
            pltpu.make_async_copy(self.src.at[0], self.place(t), self.rs.at[t]).wait()

    def drain(self):
        for j, to, here in self.parts():

            @pl.when(jnp.logical_not(here))
            def _():
                self.remote(j, to).wait_send()


class FromSequences:
    def __init__(self, net, src, dst, sems):
        self.n, self.src, self.dst = net, src, dst
        self.ss, self.rs = sems
        self.rows = dst.shape[1]

    def parts(self):
        n = self.n
        for t in range(2):
            to = (2 * n.p + n.z // 2, 2 * n.c + t)
            yield t, to, (to[0] == n.d) & (to[1] == n.z)

    def piece(self, t):
        return self.src.at[pl.ds(t * self.rows, self.rows)]

    def remote(self, t, to):
        j = self.n.z % 2
        return pltpu.make_async_remote_copy(
            self.piece(t),
            self.dst.at[j],
            self.ss.at[t],
            self.rs.at[j],
            device_id=to,
            device_id_type=MESH,
        )

    def start(self):
        for t, to, here in self.parts():

            @pl.when(here)
            def _():
                j = self.n.z % 2
                pltpu.make_async_copy(self.piece(t), self.dst.at[j], self.rs.at[j]).start()

            @pl.when(jnp.logical_not(here))
            def _():
                self.remote(t, to).start()

    def wait(self):
        for j in range(2):
            pltpu.make_async_copy(self.piece(0), self.dst.at[j], self.rs.at[j]).wait()

    def drain(self):
        for t, to, here in self.parts():

            @pl.when(jnp.logical_not(here))
            def _():
                self.remote(t, to).wait_send()


def by_rows(total, step, body):
    def one(i, carry):
        body(pl.ds(pl.multiple_of(i * step, step), step))
        return carry

    lax.fori_loop(0, total // step, one, 0)


def by_columns(total, body, step=640):
    def one(i, carry):
        body(pl.multiple_of(i * step, LANES), step)
        return carry

    lax.fori_loop(0, total // step, one, 0)
    if total % step:
        body(total // step * step, total % step)


def normalised(values):
    average = jnp.mean(values, axis=-1, keepdims=True)
    centred = values - average
    variance = jnp.mean(centred * centred, axis=-1, keepdims=True)
    return centred * lax.rsqrt(variance + eps_norm)


def place_run(block, source, phase, count):
    moved = pltpu.roll(block, (phase - source) % block.shape[1], axis=1)
    tiles = -(-(phase + count) // LANES) * LANES
    moved = moved[:, :tiles]
    lane = lax.broadcasted_iota(jnp.int32, moved.shape, 1)
    return jnp.where((lane >= phase) & (lane < phase + count), moved, 0.0)


def attend_pair(s, i, q_ref, kv_ref, bias_ref, att_ref, lse_ref, top_ref):
    lanes = pl.ds(pl.multiple_of(i * LANES, LANES), LANES)
    keys, values, queries = kv_ref[0, :, lanes], kv_ref[1, :, lanes], q_ref[:, lanes]
    lane = lax.broadcasted_iota(jnp.int32, queries.shape, 1)
    outs = []
    for side in range(2):
        mine = (lane >= HD) if side else (lane < HD)
        picked = jnp.where(mine, queries, jnp.zeros_like(queries)) * bf16(HD**-0.5)
        scores = nt(keys, picked) + bias_ref[...]
        top = jnp.max(scores, axis=0, keepdims=True)
        weights = jnp.exp(scores - top)
        total = jnp.sum(weights, axis=0, keepdims=True)
        mixed = tn(values[:, side * HD : (side + 1) * HD], weights.astype(bf16))
        outs.append(mixed * (1.0 / total))
        lse_ref[i, side : side + 1, :] = top + jnp.log(total)
        top_ref[i, side : side + 1, :] = top
    att_ref[:, lanes] = jnp.concatenate(outs, axis=0).T.astype(bf16)


def forward_plan(A, B, C, near, far, seq_x, seq_cot):
    def do(method, *args):
        return partial(method, *args)

    return {
        ("start", 0): (
            do(A.arrive, near),
            do(B.begin),
            do(A.arrive, far),
            do(seq_x.start),
        ),
        ("vectors", 0): (
            do(A.turn, near),
            do(B.arrive, near),
            do(C.begin),
            do(A.turn, far),
            do(A.last, near),
            do(B.arrive, far),
            do(A.last, far),
        ),
        ("normed", 0): (do(B.turn, near),),
        ("project", 1): (do(C.arrive, near),),
        ("share", 0): (do(B.turn, far), do(B.last, near)),
        ("pair", 0): (do(C.arrive, far), do(seq_cot.start)),
        ("pair", 2): (do(B.last, far), do(C.turn, near)),
        ("pair", 6): (do(C.turn, far), do(C.last, near)),
        ("down", 0): (do(C.last, far),),
    }


def forward_kernel(s, *refs):
    (own_a, own_b, own_c, small, inp, cot, kinfo, qinfo) = refs[:8]
    (wa_o, wb_o, wc_o, x_o, cot_o, vec, normed_o, q_o, kv_o, att_o, res_o, two_o, slope_o, hid_o) = refs[8:22]
    (lse, top, out_o) = refs[22:25]
    (x, normed, q, kv, bias, att, res, two, wa, wb, wc, out, smalls) = refs[25:38]
    sems = refs[38:]
    net = Net()
    A, B, C = [
        Gather(net, s, w, own, swapped, sems[7 * g : 7 * g + 7])
        for g, (w, own, swapped) in enumerate(
            ((wa, own_a, False), (wb, own_b, False), (wc, own_c, True))
        )
    ]
    seq_x = ToSequences(net, inp, x, sems[21:23])
    seq_cot = ToSequences(net, cot, cot_o, sems[23:25])
    small_s, small_r, kv_s, kv_r, save = sems[25:30]
    near, far = net.near, net.far
    saves = []

    def keep(src, dst):
        copy = pltpu.make_async_copy(src, dst, save.at[len(saves)])
        copy.start()
        saves.append(copy)

    def small_copy(z):
        return pltpu.make_async_remote_copy(
            small,
            smalls.at[net.z],
            small_s.at[z],
            small_r.at[net.z],
            device_id=(net.d, z),
            device_id_type=MESH,
        )

    plan = forward_plan(A, B, C, near, far, seq_x, seq_cot)

    def at(name, step=0):
        for act in plan.get((name, step), ()):
            act()

    enter(net)
    A.begin()
    for z in range(4):

        @pl.when(z != net.z)
        def _():
            small_copy(z).start()

        @pl.when(z == net.z)
        def _():
            pltpu.make_async_copy(small, smalls.at[z], small_r.at[z]).start()

    at("start")
    diff = qinfo[0:1, :] - kinfo[:, 0:1]
    fine = (diff >= 0) & (diff <= kinfo[:, 1:2])
    bias[...] = jnp.where(fine, 0.0, masked_fill)
    at("vectors")

    for z in range(4):
        pltpu.make_async_copy(small, smalls.at[z], small_r.at[z]).wait()
    row = lax.broadcasted_iota(jnp.int32, (3 * LANES, s.wide), 0)
    col = lax.broadcasted_iota(jnp.int32, (3 * LANES, s.wide), 1)
    rows = 0.0
    for z in range(4):
        spread = jnp.where((col == row + z * s.out) & (row < s.out), 1.0, 0.0).astype(bf16)
        rows = rows + product(smalls[z, :, : 3 * LANES], spread)
    vec[...] = rows

    seq_x.wait()
    keep(x, x_o)
    by_rows(
        s.half,
        LANES,
        lambda r: normed.__setitem__(
            (r, slice(None)),
            to_low(
                normalised(x[r, :].astype(f32)) * vec[0:1, : s.width] + vec[1:2, : s.width]
            ),
        ),
    )
    keep(normed, normed_o)
    at("normed")
    A.ready()

    wa_saved = len(saves)
    keep(wa, wa_o)
    q[...] = jnp.zeros_like(q)
    kv[:, : s.half, :] = jnp.zeros((2, s.half, s.wide), bf16)
    places = (q, kv.at[0, pl.ds(0, s.half)], kv.at[1, pl.ds(0, s.half)])
    for z in range(4):

        def part(start, size):
            lanes = pl.ds(pl.multiple_of(z * s.cols + start, LANES), size)
            res[:, pl.ds(start, size)] = product(normed[...], wa[:, lanes])

        by_columns(s.qkv_cols, part)
        for source, target, count in s.qkv_runs(z):
            kind, first = target // s.wide, target % s.wide
            base = first // LANES * LANES
            moved = place_run(res[:, : s.qkv_cols], source, first - base, count)
            lanes = slice(base, base + moved.shape[1])
            if kind != 1:
                lane = lax.broadcasted_iota(jnp.int32, (1, moved.shape[1]), 1)
                fits = (lane >= first - base) & (lane < first - base + count)
                moved = moved + jnp.where(fits, vec[2 + kind // 2 : 3 + kind // 2, lanes], 0.0)
            place = places[kind]
            place[:, lanes] = place[:, lanes] + to_low(moved)
        at("project", z)
    share = pltpu.make_async_remote_copy(
        kv.at[:, pl.ds(0, s.half)],
        kv.at[:, pl.ds(s.half, s.half)],
        kv_s,
        kv_r,
        device_id=net.sib,
        device_id_type=MESH,
    )
    share.start()
    at("share")
    share.wait()
    keep(q, q_o)
    keep(kv, kv_o)

    def pair(i, carry):
        attend_pair(s, i, q, kv, bias, att, lse, top)

        for k in range(s.pairs):
            if ("pair", k) in plan:
                pl.when(i == k)(partial(at, "pair", k))
        return carry

    lax.fori_loop(0, s.pairs, pair, 0)
    keep(att, att_o)

    res[...] = jnp.zeros_like(res)
    for z in range(4):
        lanes = slice(z * s.cols + s.out_tile, (z + 1) * s.cols)
        block = product(att[:, : s.width], wa[:, lanes])
        target = z * s.out
        base = target // LANES * LANES
        moved = place_run(block, s.qkv - s.out_tile, target - base, s.out)
        res[:, base : base + moved.shape[1]] += moved
    at("second")
    B.ready()
    keep(wb, wb_o)

    def second(r):
        total = res[r, : s.width] + x[r, :].astype(f32) + vec[4:5, : s.width]
        res[r, : s.width] = total
        two[r, :] = to_low(normalised(total) * vec[5:6, : s.width] + vec[6:7, : s.width])

    by_rows(s.half, LANES, second)
    keep(res, res_o)
    keep(two, two_o)

    A.drain()
    saves[wa_saved].wait()
    hid, slope = wa.at[pl.ds(0, s.half)], wa.at[pl.ds(s.half, s.half)]
    for z in range(4):

        def part(start, size):
            lanes = pl.ds(pl.multiple_of(z * s.cols + start, LANES), size)
            u = product(two[...], wb[:, lanes])
            u = u + smalls[z, 8:9, pl.ds(start, size)].astype(f32)
            inner = math.sqrt(2 / math.pi) * (u + 0.044715 * u * u * u)
            t = jnp.tanh(inner)
            bend = math.sqrt(2 / math.pi) * (1 + 3 * 0.044715 * u * u)
            hid[:, lanes] = to_low(0.5 * u * (1 + t))
            slope[:, lanes] = to_low(0.5 * (1 + t) + 0.5 * u * (1 - t * t) * bend)

        by_columns(s.cols, part)
        at("up", z)
    keep(hid, hid_o)
    keep(slope, slope_o)
    at("down")
    C.ready()

    keep(wc, wc_o)
    for k in range(3):
        first, count = k * 3 * LANES, min(3 * LANES, s.width - k * 3 * LANES)
        block = nt(hid[...], wc[pl.ds(first, count), :])
        total = res[:, first : first + count] + block + vec[7:8, first : first + count]
        out[:, first : first + count] = to_low(total)
    keep(out, out_o)
    seq_cot.wait()
    for group in (B, C):
        group.drain()
    for z in range(4):

        @pl.when(z != net.z)
        def _():
            small_copy(z).wait_send()

    seq_x.drain()
    seq_cot.drain()
    for i, copy in enumerate(saves):
        if i != wa_saved:
            copy.wait()


def forward_call(s, own_a, own_b, own_c, small, inp, cot, kinfo, qinfo):
    dma = pltpu.SemaphoreType.DMA
    rows = s.half
    full = s.ctx * s.cols

    def low(*shape):
        return jax.ShapeDtypeStruct(shape, bf16)

    def high(*shape):
        return jax.ShapeDtypeStruct(shape, f32)

    out_shape = [low(s.width, full)] * 3 + [
        low(rows, s.width),
        low(rows, s.width),
        high(16, s.wide),
        low(rows, s.width),
        low(rows, s.wide),
        low(2, 2 * rows, s.wide),
        low(rows, s.wide),
        high(rows, s.wide),
        low(rows, s.width),
        low(rows, full),
        low(rows, full),
        high(s.pairs, 2, rows),
        high(s.pairs, 2, rows),
        low(rows, s.width),
    ]
    anywhere = pl.BlockSpec(memory_space=pl.ANY)
    local = pl.BlockSpec(memory_space=pltpu.VMEM)
    out_specs = [local if i in (5, 14, 15) else anywhere for i in range(len(out_shape))]
    return pl.pallas_call(
        partial(forward_kernel, s),
        out_shape=out_shape,
        in_specs=[anywhere] * 6 + [local] * 2,
        out_specs=out_specs,
        scratch_shapes=[
            pltpu.VMEM((rows, s.width), bf16),
            pltpu.VMEM((rows, s.width), bf16),
            pltpu.VMEM((rows, s.wide), bf16),
            pltpu.VMEM((2, 2 * rows, s.wide), bf16),
            pltpu.VMEM((2 * rows, rows), f32),
            pltpu.VMEM((rows, s.wide), bf16),
            pltpu.VMEM((rows, s.wide), f32),
            pltpu.VMEM((rows, s.width), bf16),
            pltpu.VMEM((s.width, full), bf16),
            pltpu.VMEM((s.width, full), bf16),
            pltpu.VMEM((s.width, full), bf16),
            pltpu.VMEM((rows, s.width), bf16),
            pltpu.VMEM((4, 16, s.wide), bf16),
        ]
        + gather_sems() * 3
        + [dma((2,))] * 4
        + [dma((4,)), dma((4,)), dma, dma, dma((14,))],
        compiler_params=pltpu.CompilerParams(
            collective_id=1, has_side_effects=True, vmem_limit_bytes=61 * 2**20
        ),
        name="forward",
    )(own_a, own_b, own_c, small, inp, cot, kinfo, qinfo)


class Scatter:
    def __init__(self, net, s, own, ship, came, first, second, line, total, out, sums, sems):
        self.n, self.s, self.sums = net, s, sums
        self.own, self.ship_ref, self.came = own, ship, came
        self.first_ref, self.second_ref, self.line = first, second, line
        self.total, self.out = total, out
        self.total_like = sums.at[0] if own is None else self.block(0, 0)
        (self.ps, self.pr, self.fs, self.fr, self.hs, self.hr, self.zs, self.zr, self.ld, self.es, self.er, self.eo) = sems

    def target(self, k):
        return (self.n.far, self.n.near)[k]

    def sibling_target(self, k):
        n = self.n
        return 1 - n.c + 2 * (n.z // 2 if k else 1 - n.z // 2)

    def route(self, h):
        n = self.n
        both = ((n.px, n.x_to), (n.py, n.y_to))
        return both[h], both[1 - h]

    def lanes(self, h):
        cut = (self.s.cols // 2 + LANES - 1) // LANES * LANES
        return pl.ds(0, cut) if h == 0 else pl.ds(cut, self.s.cols - cut)

    def block(self, k, p):
        rows = self.s.rows
        return self.own.at[k, pl.ds(pl.multiple_of(p * rows, 16), rows)]

    def remote(self, src, dst, send, recv, to):
        return pltpu.make_async_remote_copy(
            src, dst, send, recv, device_id=to, device_id_type=MESH
        )

    def panel(self, k):
        return self.remote(
            self.ship_ref.at[k], self.came.at[k], self.ps.at[k], self.pr.at[k], self.n.sib
        )

    def part(self, k, p, h):
        rows = self.s.rows
        return self.own.at[k, pl.ds(pl.multiple_of(p * rows, 16), rows), self.lanes(h)]

    def pieces(self, k, h):
        (one, to), _ = self.route(h)
        for i, p in enumerate((one, self.n.pd)):
            yield self.remote(
                self.part(k, p, h),
                self.first_ref.at[k, i, :, self.lanes(h)],
                self.fs.at[k, h, i],
                self.fr.at[k, h, i],
                to,
            )

    def piece(self, k, h):
        _, (two, to) = self.route(h)
        return self.remote(
            self.part(k, two, h),
            self.second_ref.at[k, :, self.lanes(h)],
            self.hs.at[k, h],
            self.hr.at[k, h],
            to,
        )

    def along(self, k):
        n = self.n
        src = self.block(k, n.p) if self.own is not None else self.sums.at[k]
        return self.remote(
            src, self.line.at[n.z], self.zs.at[k], self.zr.at[n.z], (n.d, self.target(k))
        )

    def ship(self, k):
        self.panel(k).start()

    def wait_panel(self, k):
        self.panel(k).wait_recv()

    def start(self, k):
        for h in range(2):
            for copy in self.pieces(k, h):
                copy.start()

    def add(self, k, p, h, other):
        rows, lanes = self.s.rows, self.lanes(h)

        def some(r):
            at = pl.ds(pl.multiple_of(p * rows + r.start, 16), r.size)
            self.own[k, at, lanes] = to_low(
                self.own[k, at, lanes].astype(f32) + other[r, lanes].astype(f32)
            )

        by_rows(rows, 16, some)

    def turn(self, k):
        for h in range(2):
            for copy in self.pieces(k, h):
                copy.wait_recv()
            _, (two, _) = self.route(h)
            self.add(k, two, h, self.first_ref.at[k, 1])
            self.piece(k, h).start()
        for h in range(2):
            self.add(k, self.n.p, h, self.first_ref.at[k, 0])

    def land(self, k):
        for h in range(2):
            self.piece(k, h).wait_recv()
            self.add(k, self.n.p, h, self.second_ref.at[k])

    def send(self, k):
        @pl.when(self.target(k) != self.n.z)
        def _():
            self.along(k).start()

    def mine(self):
        return self.n.z % 2 == self.n.c

    def collect(self, stage=None, held=None):
        n, rows = self.n, self.s.rows

        @pl.when(self.mine())
        def _():
            if self.own is None:
                load = pltpu.make_async_copy(self.sums.at[1], held, self.ld)
                load.start()
                load.wait()

            def begin(r):
                if self.own is None:
                    value = held[r, :]
                else:
                    value = self.own[1, pl.ds(pl.multiple_of(n.p * rows + r.start, 16), r.size), :]
                self.total[r, :] = value.astype(f32)

            by_rows(rows, 16, begin)
            for z in range(4):

                @pl.when(z != n.z)
                def _():
                    self.remote(
                        self.total_like, self.line.at[z], self.zs.at[0], self.zr.at[z], n.sib
                    ).wait_recv()
                    if stage is None:
                        other = self.line.at[z]
                    else:
                        other = stage
                        load = pltpu.make_async_copy(self.line.at[z], stage, self.ld)
                        load.start()
                        load.wait()

                    def more(r):
                        self.total[r, :] += other[r, :].astype(f32)

                    by_rows(rows, 16, more)

            pltpu.make_async_copy(self.total, self.out, self.eo).start()
            self.final().start()

    def final(self):
        return self.remote(self.total, self.out, self.es, self.er, self.n.sib)

    def drain(self, panels=True):
        for k in range(2):
            if panels:
                self.panel(k).wait_send()
            for h in range(2):
                for copy in self.pieces(k, h):
                    copy.wait_send()
                self.piece(k, h).wait_send()

    def finish(self):
        for k in range(2):

            @pl.when(self.target(k) != self.n.z)
            def _():
                self.along(k).wait_send()

        @pl.when(self.mine())
        def _():
            pltpu.make_async_copy(self.total, self.out, self.eo).wait()
            self.final().wait_send()

        @pl.when(jnp.logical_not(self.mine()))
        def _():
            self.final().wait_recv()


def scatter_sems():
    dma = pltpu.SemaphoreType.DMA
    return [
        dma((2,)), dma((2,)), dma((2, 2, 2)), dma((2, 2, 2)), dma((2, 2)), dma((2, 2)),
        dma((2,)), dma((4,)), dma, dma, dma, dma,
    ]


def scatter_scratch(s, groups):
    panels = (2, s.width, s.cols)
    scratch = [pltpu.VMEM(panels, bf16)]
    for group in range(groups):
        scratch += [pltpu.VMEM(panels, bf16)] * (1 if group else 2)
        scratch += [
            pltpu.VMEM((2, 2, s.rows, s.cols), bf16),
            pltpu.VMEM((2, s.rows, s.cols), bf16),
        ]
    return scratch + [pltpu.VMEM((s.rows, s.cols), f32), pltpu.VMEM((s.rows, s.cols), bf16)]


def norm_back(values, grads, gain):
    average = jnp.mean(values, axis=-1, keepdims=True)
    centred = values - average
    variance = jnp.mean(centred * centred, axis=-1, keepdims=True)
    scale = lax.rsqrt(variance + eps_norm)
    n = centred * scale
    gn = grads * gain
    inner = jnp.mean(gn * n, axis=-1, keepdims=True)
    back = scale * (gn - jnp.mean(gn, axis=-1, keepdims=True) - n * inner)
    return back, jnp.sum(grads * n, axis=0, keepdims=True), jnp.sum(grads, axis=0, keepdims=True)


def fetch_all(pairs, sems):
    copies = [pltpu.make_async_copy(src, dst, sems.at[i]) for i, (src, dst) in enumerate(pairs)]
    for copy in copies:
        copy.start()
    return copies


def middle_kernel(s, *refs):
    (wa, wb, wc, cot_i, res_i, two_i, slope_i, hid_i, out_i, vec) = refs[:10]
    (down_s, up_own, gres_o, gatt_o, oz_o, sums, back_o) = refs[10:17]
    (cot, res, two, gp, hid, cot_t, two_t, wt, acc, branch, oz) = refs[17:28]
    (ship, own_c, came, first_c, second_c, own_b) = refs[28:34]
    sems = refs[34:]
    net = Net()
    C = Scatter(net, s, own_c, ship, came, first_c, second_c, None, None, None, None, sems[:12])
    B = Scatter(net, s, own_b, ship, came, None, None, None, None, None, None, sems[12:24])
    seq_out = FromSequences(net, out_i, back_o, sems[24:26])
    load, tiles, save, keep, credit = sems[26:31]
    loads = fetch_all(
        ((cot_i, cot), (hid_i, hid), (slope_i, gp), (two_i, two), (res_i, res)), load
    )
    enter(net)
    seq_out.start()

    def tile(w, j, first=0):
        lanes = pl.ds(j * s.cols + first, s.cols - first)
        return pltpu.make_async_copy(
            w.at[:, lanes], wt.at[j % 2, :, pl.ds(0, s.cols - first)], tiles.at[j % 2]
        )

    tile(wc, 0).start()
    loads[0].wait()
    cot_t[...] = cot[...].T
    loads[1].wait()
    sums[...] = jnp.zeros_like(sums)

    def down_panel(z, dst, k, came=None):
        rows = pl.ds(pl.multiple_of(z * s.rows, 16), s.rows)
        for p in range(4):
            at = slice(p * s.rows, (p + 1) * s.rows)

            def part(start, size):
                lanes = pl.ds(start, size)
                many = pl.ds(pl.multiple_of(p * s.cols + start, LANES), size)
                value = product(cot_t[rows, :], hid[:, many])
                if came is not None:
                    value = value + came[k, at, lanes].astype(f32)
                dst[k, at, lanes] = to_low(value)

            by_columns(s.cols, part)

    def up_panel(z, dst, k, came=None):
        def part(start, size):
            lanes = pl.ds(start, size)
            many = pl.ds(pl.multiple_of(z * s.cols + start, LANES), size)
            value = product(two_t[...], gp[:, many])
            if came is not None:
                value = value + came[k, :, lanes].astype(f32)
            dst[k, :, lanes] = to_low(value)

        by_columns(s.cols, part)

    for k in range(2):
        down_panel(C.sibling_target(k), ship, k)
        C.ship(k)
    loads[2].wait()

    for j in range(4):
        if j < 3:
            tile(wc, j + 1).start()
        tile(wc, j).wait()

        def part(start, size):
            lanes = pl.ds(pl.multiple_of(j * s.cols + start, LANES), size)
            value = product(cot[...], wt[j % 2, :, pl.ds(start, size)])
            value = to_low(value * gp[:, lanes].astype(f32))
            gp[:, lanes] = value
            sums[8 + j : 9 + j, pl.ds(start, size)] = jnp.sum(
                value.astype(f32), axis=0, keepdims=True
            )

        by_columns(s.cols, part)
    tile(wb, 0).start()
    for k in range(2):
        C.wait_panel(k)
        down_panel(C.target(k), own_c, k, came)
        pl.semaphore_signal(
            credit.at[k], inc=1, device_id=net.sib, device_id_type=MESH
        )
        C.start(k)
    loads[3].wait()
    two_t[...] = two[...].T
    for k in range(2):
        C.panel(k).wait_send()
        up_panel(B.sibling_target(k), ship, k)
        pl.semaphore_wait(credit.at[k], 1)
        B.ship(k)

    for z in range(4):
        if z < 3:
            tile(wb, z + 1).start()
        tile(wb, z).wait()

        def part(start, size):
            value = nt(gp[:, z * s.cols : (z + 1) * s.cols], wt[z % 2, pl.ds(start, size), :])
            if z:
                value = value + acc[:, pl.ds(start, size)]
            acc[:, pl.ds(start, size)] = value

        by_columns(s.width, part)
        if z == 1:
            C.turn(0)
    tile(wa, 0, s.out_tile).start()
    for k in range(2):
        B.wait_panel(k)
        up_panel(B.target(k), own_b, k, came)
        if k == 0:
            C.turn(1)
    own_copy = pltpu.make_async_copy(own_b, up_own, save.at[3])
    own_copy.start()
    loads[4].wait()

    def norm(r):
        given = cot[r, :].astype(f32)
        back, gain, shift = norm_back(
            res[r, : s.width], acc[r, : s.width], vec[5:6, : s.width]
        )
        total_r = given + back
        res[r, : s.width] = total_r
        low = to_low(total_r)
        branch[r, : s.width] = low
        sums[4:5, : s.width] += jnp.sum(low.astype(f32), axis=0, keepdims=True)
        sums[5:6, : s.width] += gain
        sums[6:7, : s.width] += shift
        sums[7:8, : s.width] += jnp.sum(given, axis=0, keepdims=True)

    branch[...] = jnp.zeros_like(branch)
    by_rows(s.half, LANES, norm)
    kept = []
    for k in range(2):
        C.land(k)
        kept.append(pltpu.make_async_copy(C.block(k, net.p), down_s.at[k], keep.at[k]))
        kept[k].start()

    for z in range(4):
        if z < 3:
            tile(wa, z + 1, s.out_tile).start()
        tile(wa, z, s.out_tile).wait()
        source = z * s.out
        base = source // LANES * LANES
        size = s.cols - s.out_tile
        moved = place_run(
            branch[:, base : base + size].astype(f32), source - base, s.qkv - s.out_tile, s.out
        )
        oz[z] = to_low(moved)

        def part(start, count):
            value = nt(oz[z], wt[z % 2, pl.ds(start, count), :size])
            if z:
                value = value + acc[:, pl.ds(start, count)]
            acc[:, pl.ds(start, count)] = value

        by_columns(s.width, part)
    lane = lax.broadcasted_iota(jnp.int32, (s.half, s.wide), 1)
    branch[...] = to_low(jnp.where(lane < s.width, acc[...], 0.0))
    saves = fetch_all(((res, gres_o), (branch, gatt_o), (oz, oz_o)), save)
    C.drain(False)
    for k in range(2):
        B.panel(k).wait_send()
    for copy in saves + kept + [own_copy]:
        copy.wait()
    seq_out.wait()
    seq_out.drain()


def back_pair(s, i, q_ref, kv_ref, grad_ref, lse_ref, bias_ref, dq_ref, dkv_ref):
    lanes = pl.ds(pl.multiple_of(i * LANES, LANES), LANES)
    keys, values = kv_ref[0, :, lanes], kv_ref[1, :, lanes]
    queries, grads = q_ref[:, lanes], grad_ref[:, lanes]
    lane = lax.broadcasted_iota(jnp.int32, queries.shape, 1)
    dqs, dk, dv = [], 0.0, 0.0
    for side in range(2):
        mine = (lane >= HD) if side else (lane < HD)
        picked = jnp.where(mine, queries, jnp.zeros_like(queries)) * bf16(HD**-0.5)
        grad = jnp.where(mine, grads, jnp.zeros_like(grads))
        scores = nt(keys, picked) + bias_ref[...]
        weights = jnp.exp(scores - lse_ref[i, side : side + 1, :])
        dp = nt(values, grad)
        delta = jnp.sum(weights * dp, axis=0, keepdims=True)
        ds = (weights * (dp - delta)).astype(bf16)
        dqs.append(tn(keys[:, side * HD : (side + 1) * HD], ds) * (HD**-0.5))
        dk = dk + product(ds, picked)
        dv = dv + product(weights.astype(bf16), grad)
    dq_ref[:, lanes] = jnp.concatenate(dqs, axis=0).T.astype(bf16)
    dkv_ref[0, :, lanes] = dk.astype(bf16)
    dkv_ref[1, :, lanes] = dv.astype(bf16)


def attention_kernel(s, *refs):
    (kinfo, qinfo, lse, q_i, kv_i, grad_i, own_i, down_s) = refs[:8]
    (dq_o, dkv_o, up_s, down_o) = refs[8:12]
    (q, kv, grad, dq, dkv, came, bias, own_b, first_b, second_b, line, total, stage) = refs[12:25]
    sems = refs[25:]
    net = Net()
    B = Scatter(net, s, own_b, None, None, first_b, second_b, None, None, None, None, sems[:12])
    C = Scatter(net, s, None, None, None, None, None, line, total, down_o, down_s, sems[12:24])
    load, save, ds, dr = sems[24:28]
    loads = fetch_all(((own_i, own_b), (q_i, q), (kv_i, kv), (grad_i, grad)), load)
    enter(net)
    loads[0].wait()
    B.start(0)
    B.start(1)
    C.send(0)
    C.send(1)
    fill_bias(kinfo, qinfo, bias)
    for copy in loads[1:]:
        copy.wait()

    def pair(i, carry):
        back_pair(s, i, q, kv, grad, lse, bias, dq, dkv)

        @pl.when(i == 6)
        def _():
            B.turn(0)

        @pl.when(i == 7)
        def _():
            B.turn(1)

        return carry

    lax.fori_loop(0, s.pairs, pair, 0)
    rows = pl.ds(0, s.half)
    swap = pltpu.make_async_remote_copy(
        dkv.at[:, pl.ds(s.half, s.half)], came, ds, dr, device_id=net.sib, device_id_type=MESH
    )
    swap.start()
    saves = [pltpu.make_async_copy(dq, dq_o, save.at[0])]
    saves[0].start()
    C.collect(held=stage)
    swap.wait()

    def join(r):
        for kind in range(2):
            dkv[kind, r, :] = to_low(dkv[kind, r, :].astype(f32) + came[kind, r, :].astype(f32))

    by_rows(s.half, LANES, join)
    saves.append(pltpu.make_async_copy(dkv.at[:, rows], dkv_o, save.at[1]))
    saves[1].start()
    for k in range(2):
        B.land(k)
        saves.append(pltpu.make_async_copy(B.block(k, net.p), up_s.at[k], save.at[2 + k]))
        saves[2 + k].start()
    B.drain(False)
    C.finish()
    for copy in saves:
        copy.wait()


def attention_call(s, kinfo, qinfo, lse, q, kv, grad, own, down_s):
    dma = pltpu.SemaphoreType.DMA
    rows = s.half
    anywhere = pl.BlockSpec(memory_space=pl.ANY)
    local = pl.BlockSpec(memory_space=pltpu.VMEM)
    low = lambda *dims: jax.ShapeDtypeStruct(dims, bf16)
    block = pltpu.VMEM((s.rows, s.cols), bf16)
    return pl.pallas_call(
        partial(attention_kernel, s),
        out_shape=[
            low(rows, s.wide), low(2, rows, s.wide), low(2, s.rows, s.cols),
            jax.ShapeDtypeStruct((s.rows, s.cols), f32),
        ],
        in_specs=[local] * 3 + [anywhere] * 5,
        out_specs=[anywhere] * 4,
        scratch_shapes=[
            pltpu.VMEM((rows, s.wide), bf16),
            pltpu.VMEM((2, 2 * rows, s.wide), bf16),
            pltpu.VMEM((rows, s.wide), bf16),
            pltpu.VMEM((rows, s.wide), bf16),
            pltpu.VMEM((2, 2 * rows, s.wide), bf16),
            pltpu.VMEM((2, rows, s.wide), bf16),
            pltpu.VMEM((2 * rows, rows), f32),
            pltpu.VMEM((2, s.width, s.cols), bf16),
            pltpu.VMEM((2, 2, s.rows, s.cols), bf16),
            pltpu.VMEM((2, s.rows, s.cols), bf16),
            pltpu.VMEM((4, s.rows, s.cols), bf16),
            pltpu.VMEM((s.rows, s.cols), f32),
            block,
        ]
        + scatter_sems() * 2
        + [dma((4,)), dma((4,)), dma, dma],
        compiler_params=pltpu.CompilerParams(
            collective_id=4, has_side_effects=True, vmem_limit_bytes=60 * 2**20
        ),
        name="attention",
    )(kinfo, qinfo, lse, q, kv, grad, own, down_s)


def last_kernel(s, *refs):
    (wa, oz_i, dq_i, own_i, normed_i, att_i, x_i, gres_i, up_s, vec, sums, tops) = refs[:12]
    (qkv_o, up_o, gin_o, small_o) = refs[12:16]
    (own_d, dq, wide, qz, oz, norm_t, att_t, normed, att, x, gres, wt, acc, gin, buf, got) = refs[16:32]
    (ship, own_a, came_a, first_a, second_a, total, stage, line_a, line_b) = refs[32:41]
    sems = refs[41:]
    net = Net()
    A = Scatter(net, s, own_a, ship, came_a, first_a, second_a, line_a, total, qkv_o, None, sems[:12])
    B = Scatter(net, s, None, None, None, None, None, line_b, total, up_o, up_s, sems[18:30])
    seq_in = FromSequences(net, gin, gin_o, sems[12:14])
    load, tiles, gs, gr = sems[14:18]
    loads = fetch_all(
        ((dq_i, dq), (own_i, own_d), (normed_i, normed), (att_i, att), (oz_i, oz), (x_i, x), (gres_i, gres)),
        load,
    )
    enter(net)
    B.send(0)
    B.send(1)

    def tile(j):
        return pltpu.make_async_copy(
            wa.at[:, pl.ds(j * s.cols, s.qkv_pad)], wt.at[j % 2], tiles.at[j % 2]
        )

    tile(0).start()
    loads[2].wait()
    norm_t[...] = normed[...].T
    loads[3].wait()
    att_t[...] = att[...].T
    loads[0].wait()
    loads[1].wait()
    buf[...] = sums[...]
    wide[:, : s.wide] = dq[...].astype(f32)
    for kind in range(2):
        wide[:, (kind + 1) * s.wide : (kind + 2) * s.wide] = own_d[kind].astype(f32)
    buf[2:3, :] = jnp.sum(wide[:, : s.wide], axis=0, keepdims=True)
    buf[3:4, :] = jnp.sum(wide[:, 2 * s.wide :], axis=0, keepdims=True)
    for z in range(4):
        block = 0.0
        for source, target, count in s.qkv_runs(z):
            base = target // LANES * LANES
            moved = place_run(
                wide[:, base : base + s.qkv_pad], target - base, source, count
            )
            if moved.shape[1] < s.qkv_pad:
                moved = jnp.concatenate(
                    [moved, jnp.zeros((s.half, s.qkv_pad - moved.shape[1]), f32)], axis=1
                )
            block = block + moved
        qz[z] = to_low(block)
    loads[4].wait()

    def panel(z, dst, k, came=None):
        def put(start, size, value):
            lanes = pl.ds(start, size)
            if came is not None:
                value = value + came[k, :, lanes].astype(f32)
            dst[k, :, lanes] = to_low(value)

        def part(start, size):
            put(start, size, product(norm_t[...], qz[z, :, pl.ds(start, size)]))

        by_columns(s.out_tile, part)
        mixed = product(norm_t[...], qz[z, :, s.out_tile :]) + product(
            att_t[: s.width, :], oz[z, :, : s.qkv_pad - s.out_tile]
        )
        put(s.out_tile, s.qkv_pad - s.out_tile, mixed)
        rest = product(att_t[: s.width, :], oz[z, :, s.qkv_pad - s.out_tile :])
        put(s.qkv_pad, s.cols - s.qkv_pad, rest)

    for k in range(2):
        panel(A.sibling_target(k), ship, k)
        A.ship(k)
    for k in range(2):
        tile(k + 1).start()
        tile(k).wait()
        through(s, acc, qz, wt, k)
        A.wait_panel(k)
        panel(A.target(k), own_a, k, came_a)
        A.start(k)
    for z in range(2, 4):
        if z < 3:
            tile(z + 1).start()
        tile(z).wait()
        through(s, acc, qz, wt, z)
    loads[5].wait()
    loads[6].wait()

    def norm(r):
        back, gain, shift = norm_back(
            x[r, :].astype(f32), acc[r, : s.width], vec[0:1, : s.width]
        )
        gin[r, :] = to_low(gres[r, : s.width] + back)
        buf[0:1, : s.width] += gain
        buf[1:2, : s.width] += shift

    by_rows(s.half, LANES, norm)
    seq_in.start()

    def exchange(i, to):
        return pltpu.make_async_remote_copy(
            buf, got.at[i], gs.at[i], gr.at[i], device_id=to, device_id_type=MESH
        )

    def join(one, two):
        row = lax.broadcasted_iota(jnp.int32, one.shape, 0)
        return jnp.where(row == 12, jnp.maximum(one, two), one + two)

    row = lax.broadcasted_iota(jnp.int32, buf.shape, 0)
    buf[...] = jnp.where(row == 12, tops[0:1, :], buf[...])
    partners = (net.sib, net.x_to, net.y_to)

    def merge(i):
        exchange(i, partners[i]).wait()
        buf[...] = join(buf[...], got[i])

    exchange(0, partners[0]).start()
    A.turn(0)
    A.turn(1)
    merge(0)
    exchange(1, partners[1]).start()
    B.collect(held=stage)
    merge(1)
    exchange(2, partners[2]).start()
    A.land(0)
    A.send(0)
    merge(2)

    def around(z):
        return pltpu.make_async_remote_copy(
            buf, got.at[3 + net.z], gs.at[3 + z], gr.at[3 + net.z], device_id=(net.d, z), device_id_type=MESH
        )

    for z in range(4):

        @pl.when(z != net.z)
        def _():
            around(z).start()

        @pl.when(z == net.z)
        def _():
            pltpu.make_async_copy(buf, got.at[3 + z], gr.at[3 + z]).start()

    A.land(1)
    A.send(1)
    B.finish()
    for z in range(4):
        pltpu.make_async_copy(buf, got.at[3 + z], gr.at[3 + z]).wait()

        @pl.when(z != net.z)
        def _():
            around(z).wait_send()

    small_o[...] = join(join(got[3], got[4]), join(got[5], got[6]))
    A.collect()
    A.drain()
    A.finish()
    seq_in.wait()
    seq_in.drain()


def through(s, acc, qz, wt, z):
    def part(start, size):
        value = nt(qz[z], wt[z % 2, pl.ds(start, size), :])
        if z:
            value = value + acc[:, pl.ds(start, size)]
        acc[:, pl.ds(start, size)] = value

    by_columns(s.width, part)


def middle_call(s, shape, wa, wb, wc, cot, res, two, slope, hid, out, vec):
    dma = pltpu.SemaphoreType.DMA
    rows, full = s.half, s.ctx * s.cols
    anywhere = pl.BlockSpec(memory_space=pl.ANY)
    local = pl.BlockSpec(memory_space=pltpu.VMEM)
    low = lambda *dims: jax.ShapeDtypeStruct(dims, bf16)
    high = lambda *dims: jax.ShapeDtypeStruct(dims, f32)
    size = s.cols - s.out_tile
    return pl.pallas_call(
        partial(middle_kernel, s),
        out_shape=[
            low(2, s.rows, s.cols), low(2, s.width, s.cols), high(rows, s.wide),
            low(rows, s.wide), low(4, rows, size), high(16, s.wide), low(*shape),
        ],
        in_specs=[anywhere] * 9 + [local],
        out_specs=[anywhere] * 5 + [local, anywhere],
        scratch_shapes=[
            pltpu.VMEM((rows, s.width), bf16),
            pltpu.VMEM((rows, s.wide), f32),
            pltpu.VMEM((rows, s.width), bf16),
            pltpu.VMEM((rows, full), bf16),
            pltpu.VMEM((rows, full), bf16),
            pltpu.VMEM((s.width, rows), bf16),
            pltpu.VMEM((s.width, rows), bf16),
            pltpu.VMEM((2, s.width, s.cols), bf16),
            pltpu.VMEM((rows, s.wide), f32),
            pltpu.VMEM((rows, s.wide), bf16),
            pltpu.VMEM((4, rows, size), bf16),
        ]
        + scatter_scratch(s, 1)[:-2]
        + [pltpu.VMEM((2, s.width, s.cols), bf16)]
        + scatter_sems() * 2
        + [dma((2,)), dma((2,)), dma((5,)), dma((2,)), dma((4,)), dma((2,)), pltpu.SemaphoreType.REGULAR((2,))],
        compiler_params=pltpu.CompilerParams(
            collective_id=2, has_side_effects=True, vmem_limit_bytes=63 * 2**20
        ),
        name="middle",
    )(wa, wb, wc, cot, res, two, slope, hid, out, vec)


def last_call(s, shape, wa, oz, dq, d_own, normed, att, x, gres, up_sums, vec, sums, tops):
    dma = pltpu.SemaphoreType.DMA
    rows = s.half
    anywhere = pl.BlockSpec(memory_space=pl.ANY)
    local = pl.BlockSpec(memory_space=pltpu.VMEM)
    low = lambda *dims: jax.ShapeDtypeStruct(dims, bf16)
    high = lambda *dims: jax.ShapeDtypeStruct(dims, f32)
    size = s.cols - s.out_tile
    return pl.pallas_call(
        partial(last_kernel, s),
        out_shape=[
            high(s.rows, s.cols), high(s.rows, s.cols), low(*shape), high(16, s.wide),
        ],
        in_specs=[anywhere] * 9 + [local] * 3,
        out_specs=[anywhere, anywhere, anywhere, local],
        scratch_shapes=[
            pltpu.VMEM((2, rows, s.wide), bf16),
            pltpu.VMEM((rows, s.wide), bf16),
            pltpu.VMEM((rows, 3 * s.wide), f32),
            pltpu.VMEM((4, rows, s.qkv_pad), bf16),
            pltpu.VMEM((4, rows, size), bf16),
            pltpu.VMEM((s.width, rows), bf16),
            pltpu.VMEM((s.wide, rows), bf16),
            pltpu.VMEM((rows, s.width), bf16),
            pltpu.VMEM((rows, s.wide), bf16),
            pltpu.VMEM((rows, s.width), bf16),
            pltpu.VMEM((rows, s.wide), f32),
            pltpu.VMEM((2, s.width, s.qkv_pad), bf16),
            pltpu.VMEM((rows, s.wide), f32),
            pltpu.VMEM((rows, s.width), bf16),
            pltpu.VMEM((16, s.wide), f32),
            pltpu.VMEM((7, 16, s.wide), f32),
        ]
        + scatter_scratch(s, 1)
        + [pltpu.VMEM((4, s.rows, s.cols), bf16)] * 2
        + scatter_sems()
        + [dma((2,)), dma((2,)), dma((7,)), dma((2,)), dma((7,)), dma((7,))]
        + scatter_sems(),
        compiler_params=pltpu.CompilerParams(
            collective_id=3, has_side_effects=True, vmem_limit_bytes=63 * 2**20
        ),
        name="last",
    )(wa, oz, dq, d_own, normed, att, x, gres, up_sums, vec, sums, tops)


def slot_info(moves, segment_ids, padding, stretch_order):
    core, place, local_seqs = moves.core, moves.z, segment_ids.shape[0]
    length = segment_ids.shape[1]
    half = length // 2
    info = jnp.stack([segment_ids, padding], axis=0)
    info_there = moves.swap_core(info)
    info = jnp.where(place // local_seqs == core, info, info_there)
    info = lax.dynamic_index_in_dim(info, place % local_seqs, 1, False)
    stretches = stretch_order.shape[0]
    stretch_len = length // stretches
    info = jnp.take(info.reshape(2, stretches, stretch_len), stretch_order, axis=1)
    positions = stretch_order[:, None] * stretch_len + jnp.arange(stretch_len, dtype=jnp.int32)
    code = (info[0] * (2 * length) + positions).reshape(2, half)
    reach = (info[1] * (length - 1)).reshape(2, half)
    code_own = lax.dynamic_index_in_dim(code, core, 0, False)
    code_sib = lax.dynamic_index_in_dim(code, 1 - core, 0, False)
    reach_own = lax.dynamic_index_in_dim(reach, core, 0, False)
    reach_sib = lax.dynamic_index_in_dim(reach, 1 - core, 0, False)
    kinfo = jnp.stack(
        [jnp.concatenate([code_own, code_sib]), jnp.concatenate([reach_own, reach_sib])], axis=1
    )
    return kinfo, code_own[None]


def pack_blocks(moves, s, w_qkv, w_out, w_up, w_down, vectors, bias_up):
    rows = w_qkv.shape[0]

    def filled(values):
        return jnp.pad(values, ((0, 0), (0, s.cols - values.shape[1])))

    turned = w_down.T
    parts = jnp.concatenate(
        [
            filled(jnp.concatenate([w_qkv, w_out], axis=1)),
            filled(w_up),
            filled(jnp.concatenate([turned[:rows], turned[rows:]], axis=1)),
        ],
        axis=0,
    )
    there = moves.swap_core(parts)
    even = jnp.where(moves.core == 0, parts, there)
    odd = jnp.where(moves.core == 0, there, parts)
    own_a = jnp.concatenate([even[:rows], odd[:rows]], axis=0)
    own_b = jnp.concatenate([even[rows : 2 * rows], odd[rows : 2 * rows]], axis=0)
    ff = turned.shape[1]
    own_c = filled(
        jnp.concatenate(
            [
                jnp.concatenate([v[2 * rows :, :ff], v[2 * rows :, ff : 2 * ff]], axis=0)
                for v in (even, odd)
            ],
            axis=1,
        )
    )
    small = jnp.concatenate([jnp.pad(vectors, ((0, 0), (0, s.cols - vectors.shape[1]))), filled(bias_up[None])], axis=0)
    small = jnp.pad(small, ((0, 16 - small.shape[0]), (0, 0)))
    return own_a, own_b, own_c, small


def fast_shards(
    dp,
    ctx,
    inputs,
    cotangent,
    w_qkv,
    w_out,
    w_up,
    w_down,
    vectors,
    bias_up,
    segment_ids,
    padding,
    stretch_order,
):
    local_seqs, query_len, width = inputs.shape
    heads = width // HD
    s = Sizes(width, w_up.shape[1] * ctx, ctx, dp, segment_ids.shape[1])
    moves = Moves(dp, ctx, local_seqs)
    core, place = moves.core, moves.z
    wide = s.wide
    kinfo, qinfo = slot_info(moves, segment_ids, padding, stretch_order)
    own_a, own_b, own_c, small = pack_blocks(moves, s, w_qkv, w_out, w_up, w_down, vectors, bias_up)
    (wa, wb, wc, x, cot, vec, normed, queries, kv, attended, residual, two, slope, hidden, lse, tops, out) = forward_call(
        s, own_a, own_b, own_c, small, inputs, cotangent, kinfo, qinfo
    )
    down_sums, up_own, gres, gatt, oz, sums, output = middle_call(
        s, inputs.shape, wa, wb, wc, cot, residual, two, slope, hidden, out, vec
    )
    dq, d_own, up_sums, down_block = attention_call(
        s, kinfo, qinfo, lse, queries, kv, gatt, up_own, down_sums
    )
    block_top = jnp.max(tops, axis=2).reshape(1, -1)[:, :heads]
    block_top = jnp.pad(block_top, ((0, 7), (0, wide - heads)))
    qkv_block, up_block, grad_input, small_sums = last_call(
        s, inputs.shape, wa, oz, dq, d_own, normed, attended, x, gres, up_sums, vec, sums, block_top
    )
    rows_d = w_qkv.shape[0]
    cols_q, cols_d, cols_f = w_qkv.shape[1], w_out.shape[1], w_up.shape[1]
    ff = w_down.shape[0]

    def own_rows(block):
        return jnp.where(core == 0, block[:rows_d], block[rows_d:])

    qkv_block, up_block = own_rows(qkv_block), own_rows(up_block)
    grad_qkv, grad_out = qkv_block[:, :cols_q], qkv_block[:, cols_q : cols_q + cols_d]
    grad_up = up_block[:, :cols_f]
    grad_down = jnp.where(core == 0, down_block[:, :ff], down_block[:, ff : 2 * ff]).T
    grad_vectors = lax.dynamic_slice_in_dim(small_sums[:8, :width], place * cols_d, cols_d, 1)
    grad_bias = lax.dynamic_index_in_dim(small_sums[8:12], place, 0, False)[:cols_f]
    global_top = small_sums[12, :heads]

    factor = clip_limit / jnp.maximum(global_top, clip_limit)
    per_column = jnp.repeat(jnp.sqrt(factor), HD)
    column_scale = jnp.concatenate([per_column, per_column, jnp.ones((width,), f32)])
    local_scale = lax.dynamic_slice_in_dim(column_scale, place * cols_q, cols_q)
    clipped_qkv = to_low(w_qkv.astype(f32) * local_scale[None, :])
    bias_scale = lax.dynamic_slice_in_dim(per_column, place * cols_d, cols_d)
    clipped_bias = to_low(vectors[2].astype(f32) * bias_scale)
    return (
        output,
        grad_input.astype(f32),
        grad_qkv,
        grad_out,
        grad_up,
        grad_down,
        grad_vectors,
        grad_bias,
        clipped_qkv,
        clipped_bias,
        global_top,
    )


def shards(
    dp,
    ctx,
    inputs,
    cotangent,
    w_qkv,
    w_out,
    w_up,
    w_down,
    vectors,
    bias_up,
    segment_ids,
    padding,
    stretch_order,
):
    local_seqs, query_len, width = inputs.shape
    length = segment_ids.shape[1]
    half = length // 2
    heads = width // HD
    wide = (width + LANES - 1) // LANES * LANES
    rows_d = w_qkv.shape[0]
    cols_d = w_out.shape[1]
    cols_f = w_up.shape[1]
    ratio = w_down.shape[0] // rows_d
    hidden_width = cols_f * ctx
    moves = Moves(dp, ctx, local_seqs)
    core, place = moves.core, moves.z

    extra = jnp.concatenate([vectors.reshape(-1, cols_f), bias_up[None]], axis=0)
    first = jnp.concatenate([jnp.concatenate([w_qkv, w_out], axis=1), extra], axis=0)
    first = moves.gather_ctx(first)
    x_flat = moves.to_sequences(inputs).astype(f32)
    down_packed = jnp.swapaxes(w_down.reshape(ratio, rows_d, cols_d), 0, 1).reshape(rows_d, -1)
    second = moves.gather_ctx(jnp.concatenate([w_up, down_packed], axis=0))
    cot = moves.to_sequences(cotangent)

    def columns(blocks):
        return jnp.swapaxes(blocks, 0, 1).reshape(blocks.shape[1], -1)

    cols_q = w_qkv.shape[1]
    part_qkv = columns(first[:, :rows_d, :cols_q])
    part_out = columns(first[:, :rows_d, cols_q:])
    small = first[:, rows_d:]
    vec_rows = columns(small[:, :-1].reshape(ctx, 8, cols_d)).astype(f32)
    bias_row = small[:, -1].reshape(-1).astype(f32)
    part_up = columns(second[:, :rows_d])
    part_down = second[:, rows_d:].reshape(ctx, rows_d, ratio, cols_d)
    part_down = jnp.transpose(part_down, (2, 1, 0, 3)).reshape(ratio * rows_d, width)

    wide_qkv = moves.gather_dp(part_qkv)
    wide_out = moves.gather_dp(part_out)
    wide_up = moves.gather_dp(part_up)
    wide_down = moves.gather_dp(part_down)

    info = jnp.stack([segment_ids, padding], axis=0)
    info_there = moves.swap_core(info)
    info = jnp.where(place // local_seqs == core, info, info_there)
    info = lax.dynamic_index_in_dim(info, place % local_seqs, 1, False)
    stretches = stretch_order.shape[0]
    stretch_len = length // stretches
    info = jnp.take(info.reshape(2, stretches, stretch_len), stretch_order, axis=1)
    positions = stretch_order[:, None] * stretch_len + jnp.arange(stretch_len, dtype=jnp.int32)
    code = (info[0] * (2 * length) + positions).reshape(2, half)
    reach = (info[1] * (length - 1)).reshape(2, half)
    code_own = lax.dynamic_index_in_dim(code, core, 0, False)
    code_sib = lax.dynamic_index_in_dim(code, 1 - core, 0, False)
    reach_own = lax.dynamic_index_in_dim(reach, core, 0, False)
    reach_sib = lax.dynamic_index_in_dim(reach, 1 - core, 0, False)
    kinfo = jnp.stack(
        [jnp.concatenate([code_own, code_sib]), jnp.concatenate([reach_own, reach_sib])], axis=1
    )
    qinfo = code_own[None]

    normed = to_low(layer_norm(x_flat, vec_rows[0], vec_rows[1]))
    projected = product(normed, wide_qkv)

    def padded(values):
        return jnp.pad(to_low(values), ((0, 0), (0, wide - width)))

    queries = padded(projected[:, :width] + vec_rows[2])
    own = jnp.stack(
        [
            padded(projected[:, width : 2 * width]),
            padded(projected[:, 2 * width :] + vec_rows[3]),
        ]
    )
    sib = moves.swap_core(own)
    attended, lse, tops = attend_forward(heads, kinfo, qinfo, queries, own, sib)
    attended = attended[:, :width]
    block_top = jnp.max(tops, axis=2).reshape(-1)[:heads]
    global_top = lax.pmax(block_top, AXES)
    residual = x_flat + product(attended, wide_out) + vec_rows[4]
    normed_two = to_low(layer_norm(residual, vec_rows[5], vec_rows[6]))
    up_pre = product(normed_two, wide_up) + bias_row
    hidden = to_low(jax.nn.gelu(up_pre, approximate=True))
    output = to_low(residual + product(hidden, wide_down) + vec_rows[7])
    output = moves.from_sequences(output)

    grad_output = cot.astype(f32)
    grad_bias_two = column_sum(cot)
    sum_down = moves.weight_terms(hidden, cot)
    sum_down = moves.scatter_dp(sum_down)
    grad_hidden = contract_cols(cot, wide_down)
    unused, gelu_back = jax.vjp(partial(jax.nn.gelu, approximate=True), up_pre)
    grad_pre = to_low(gelu_back(grad_hidden)[0])
    grad_bias_up = column_sum(grad_pre)
    sum_up = moves.weight_terms(normed_two, grad_pre)
    sum_up = moves.scatter_dp(sum_up)
    unused, norm_back_two = jax.vjp(layer_norm, residual, vec_rows[5], vec_rows[6])
    back_two = norm_back_two(contract_cols(grad_pre, wide_up))
    grad_residual = grad_output + back_two[0]
    grad_branch = to_low(grad_residual)
    sum_out = moves.weight_terms(attended, grad_branch)
    sum_out = moves.scatter_dp(sum_out)
    grad_attended = padded(contract_cols(grad_branch, wide_out))
    dq, d_own, d_sib = attend_backward(
        heads, kinfo, qinfo, queries, jnp.concatenate([own, sib], axis=1), grad_attended, lse
    )
    d_came = moves.swap_core(d_sib)
    d_own = to_low(d_own.astype(f32) + d_came.astype(f32))
    grad_proj = jnp.concatenate([dq[:, :width], d_own[0, :, :width], d_own[1, :, :width]], axis=1)
    sum_qkv = moves.weight_terms(normed, grad_proj)
    sum_qkv = moves.scatter_dp(sum_qkv)
    unused, norm_back_one = jax.vjp(layer_norm, x_flat, vec_rows[0], vec_rows[1])
    back_one = norm_back_one(contract_cols(grad_proj, wide_qkv))
    grad_input = to_low(grad_residual + back_one[0])
    grad_input = moves.from_sequences(grad_input).astype(f32)
    grad_vectors = jnp.stack(
        [
            back_one[1],
            back_one[2],
            column_sum(dq[:, :width]),
            column_sum(d_own[1, :, :width]),
            column_sum(grad_branch),
            back_two[1],
            back_two[2],
            grad_bias_two,
        ]
    )

    def by_place(values):
        return jnp.swapaxes(values.reshape(values.shape[0], ctx, -1), 0, 1)

    blocks_down = sum_down.reshape(ratio, rows_d, ctx, cols_d)
    blocks_down = jnp.transpose(blocks_down, (2, 1, 0, 3)).reshape(ctx, rows_d, -1)
    later = jnp.concatenate([by_place(sum_up), blocks_down, by_place(sum_out)], axis=2)
    later = moves.scatter_ctx(later)
    grad_up = later[:, :cols_f]
    grad_down = later[:, cols_f : 2 * cols_f].reshape(rows_d, ratio, cols_d)
    grad_down = jnp.swapaxes(grad_down, 0, 1).reshape(ratio * rows_d, cols_d)
    grad_out = later[:, 2 * cols_f :]
    grad_qkv = moves.scatter_ctx(by_place(sum_qkv))

    tiny = jnp.concatenate([grad_vectors, grad_bias_up.reshape(-1, width)], axis=0)
    tiny = lax.psum(tiny, AXES)
    grad_vectors = lax.dynamic_slice_in_dim(tiny[:8], place * cols_d, cols_d, 1)
    grad_bias = lax.dynamic_slice_in_dim(tiny[8:].reshape(-1), place * cols_f, cols_f)

    factor = clip_limit / jnp.maximum(global_top, clip_limit)
    per_column = jnp.repeat(jnp.sqrt(factor), HD)
    column_scale = jnp.concatenate([per_column, per_column, jnp.ones((width,), f32)])
    local_scale = lax.dynamic_slice_in_dim(column_scale, place * cols_q, cols_q)
    clipped_qkv = to_low(w_qkv.astype(f32) * local_scale[None, :])
    bias_scale = lax.dynamic_slice_in_dim(per_column, place * cols_d, cols_d)
    clipped_bias = to_low(vectors[2].astype(f32) * bias_scale)
    return (
        output,
        grad_input,
        grad_qkv,
        grad_out,
        grad_up,
        grad_down,
        grad_vectors,
        grad_bias,
        clipped_qkv,
        clipped_bias,
        global_top,
    )


def solution(mesh):
    dp, ctx = mesh.shape["dp"], mesh.shape["ctx"]
    body = fast_shards if (dp, ctx) == (8, 4) else shards
    return jax.shard_map(
        partial(body, dp, ctx),
        mesh=mesh,
        in_specs=(
            P("dp", "ctx", None),
            P("dp", "ctx", None),
            P("dp", "ctx"),
            P("dp", "ctx"),
            P("dp", "ctx"),
            P("dp", "ctx"),
            P(None, "ctx"),
            P("ctx"),
            P("dp", None),
            P("dp", None),
            P(),
        ),
        out_specs=(
            P("dp", "ctx", None),
            P("dp", "ctx", None),
            P("dp", "ctx"),
            P("dp", "ctx"),
            P("dp", "ctx"),
            P("dp", "ctx"),
            P(None, "ctx"),
            P("ctx"),
            P("dp", "ctx"),
            P("ctx"),
            P(),
        ),
        check_vma=False,
    )
```

```python
import math
from functools import partial

import jax
import jax.numpy as jnp
from jax import lax
from jax.experimental import pallas as pl
from jax.experimental.pallas import tpu as pltpu
from jax.sharding import PartitionSpec as P

HD = 64
LANES = 128
AXES = ("dp", "ctx")

eps_norm = 1e-05
clip_limit = 5.0
masked_fill = -1e30
f32 = jnp.float32
bf16 = jnp.bfloat16


def layer_norm(values_in, gain_row, shift_row):
    average = jnp.mean(values_in, axis=-1, keepdims=True)
    centred = values_in - average
    variance = jnp.mean(centred * centred, axis=-1, keepdims=True)
    return centred * lax.rsqrt(variance + eps_norm) * gain_row + shift_row


def to_low(values_in):
    return values_in.astype(bf16)


def product(left, right):
    return jnp.dot(left, right, preferred_element_type=f32)


def contract_rows(left, right):
    return lax.dot_general(left, right, (((0,), (0,)), ((), ())), preferred_element_type=f32)


def contract_cols(left, right):
    return lax.dot_general(left, right, (((1,), (1,)), ((), ())), preferred_element_type=f32)


def column_sum(values_in):
    return jnp.sum(values_in.astype(f32), axis=0)


class Moves:
    def __init__(self, dp, ctx, local_seqs):
        self.dp, self.ctx, self.seqs = dp, ctx, local_seqs
        self.d = lax.axis_index("dp")
        self.z = lax.axis_index("ctx")
        self.core = self.d % 2
        self.cube = dp == 8 and ctx == 4
        self.x = (self.d // 2) % 2
        self.y = self.d // 4

    def permute(self, values, target):
        pairs = []
        for d in range(self.dp):
            for z in range(self.ctx):
                there = target(d, z)
                if there is not None:
                    pairs.append((d * self.ctx + z, there[0] * self.ctx + there[1]))
        return lax.ppermute(values, AXES, pairs)

    def swap_core(self, values):
        return self.permute(values, lambda d, z: (d ^ 1, z))

    def swap_x(self, values):
        return self.permute(values, lambda d, z: (d ^ 2, z))

    def swap_y(self, values):
        return self.permute(values, lambda d, z: (d ^ 4, z))

    def up(self, values):
        return self.permute(values, lambda d, z: (d, z + 1) if z + 1 < self.ctx else None)

    def down(self, values):
        return self.permute(values, lambda d, z: (d, z - 1) if z > 0 else None)

    def sequence_target(self, step):
        n = self.seqs

        def target(d, z):
            return (d - d % 2 + z // n, n * (d % 2) + (z + step) % n)

        return target

    def to_sequences(self, values):
        n = self.seqs
        came = []
        for step in range(n):
            block = lax.dynamic_index_in_dim(values, (self.z + step) % n, 0, keepdims=False)
            came.append(self.permute(block, self.sequence_target(step)))
        return jnp.concatenate([self.choose(came, (self.z - t) % n) for t in range(n)], axis=0)

    def from_sequences(self, values):
        n = self.seqs
        parts = values.reshape(n, values.shape[0] // n, values.shape[1])
        came = []
        for step in range(n):
            forward = self.sequence_target(step)
            block = lax.dynamic_index_in_dim(parts, (self.z - step) % n, 0, keepdims=False)
            back = {}
            for d in range(self.dp):
                for z in range(self.ctx):
                    back[forward(d, z)] = (d, z)
            came.append(self.permute(block, lambda d, z: back[(d, z)]))
        return jnp.stack([self.choose(came, (j - self.z) % n) for j in range(n)], axis=0)

    @staticmethod
    def choose(items, index):
        picked = items[0]
        for i in range(1, len(items)):
            picked = jnp.where(index == i, items[i], picked)
        return picked

    def gather_ctx(self, block):
        if not self.cube:
            return lax.all_gather(block, "ctx", axis=0, tiled=False)
        rising, falling = [block], [block]
        for _ in range(self.ctx - 1):
            rising.append(self.up(rising[-1]))
            falling.append(self.down(falling[-1]))
        line = jnp.stack(rising[:0:-1] + falling, axis=0)
        return lax.dynamic_slice_in_dim(line, self.ctx - 1 - self.z, self.ctx, 0)

    def gather_dp(self, block):
        if not self.cube:
            return lax.all_gather(block, "dp", axis=0, tiled=True)
        rows, cols = block.shape
        half = (cols // 2 + LANES - 1) // LANES * LANES
        from_x, from_y = self.swap_x(block), self.swap_y(block)
        far = jnp.concatenate(
            [self.swap_y(from_x[:, :half]), self.swap_x(from_y[:, half:])], axis=1
        )
        mine = jnp.zeros((4, rows, cols), block.dtype)
        here = 2 * self.y + self.x
        for step, part in enumerate((block, from_x, from_y, far)):
            mine = lax.dynamic_update_slice(mine, part[None], (here ^ step, 0, 0))
        other = self.swap_core(mine)
        first = jnp.where(self.core == 0, mine, other)
        second = jnp.where(self.core == 0, other, mine)
        return jnp.stack([first, second], axis=1).reshape(8 * rows, cols)

    def scatter_ctx(self, blocks):
        if not self.cube:
            return lax.psum_scatter(blocks, "ctx", scatter_dimension=0, tiled=False).astype(f32)

        def part(index):
            return lax.dynamic_index_in_dim(blocks, jnp.clip(index, 0, self.ctx - 1), 0, False)

        falling = rising = None
        for step in range(self.ctx - 1, 0, -1):
            low, high = part(self.z - step), part(self.z + step)
            if falling is not None:
                low = to_low(low.astype(f32) + falling.astype(f32))
                high = to_low(high.astype(f32) + rising.astype(f32))
            n = self.ctx
            falling = self.permute(
                low, lambda d, z: (d, z - 1) if z - step >= 0 else None
            )
            rising = self.permute(
                high, lambda d, z: (d, z + 1) if z + step < n else None
            )
        return part(self.z).astype(f32) + falling.astype(f32) + rising.astype(f32)

    def weight_terms(self, left, right):
        if not self.cube:
            return to_low(contract_rows(left, right))
        tokens, width = left.shape
        rows = width // self.dp
        parts = left.reshape(tokens, self.dp // 2, 2, rows)
        even = parts[:, :, 0].reshape(tokens, -1)
        odd = parts[:, :, 1].reshape(tokens, -1)
        own = jnp.where(self.core == 0, even, odd)
        sibling = jnp.where(self.core == 0, odd, even)
        came = self.swap_core(to_low(contract_rows(sibling, right)))
        return to_low(contract_rows(own, right) + came.astype(f32))

    def scatter_dp(self, terms):
        if not self.cube:
            return lax.psum_scatter(terms, "dp", scatter_dimension=0, tiled=True)
        rows, cols = terms.shape[0] // 4, terms.shape[1]
        half = (cols // 2 + LANES - 1) // LANES * LANES
        grid = terms.reshape(2, 2, rows, cols)

        def pick(values, index, axis):
            return lax.dynamic_index_in_dim(values, index, axis, False)

        def added(one, two):
            return to_low(one.astype(f32) + two.astype(f32))

        left, right = grid[..., :half], grid[..., half:]
        left_x = self.swap_x(pick(left, 1 - self.x, 1))
        right_y = self.swap_y(pick(right, 1 - self.y, 0))
        left = added(pick(left, self.x, 1), left_x)
        right = added(pick(right, self.y, 0), right_y)
        left_y = self.swap_y(pick(left, 1 - self.y, 0))
        right_x = self.swap_x(pick(right, 1 - self.x, 0))
        left = added(pick(left, self.y, 0), left_y)
        right = added(pick(right, self.x, 0), right_x)
        return jnp.concatenate([left, right], axis=1)


def nt(left, right):
    return lax.dot_general(left, right, (((1,), (1,)), ((), ())), preferred_element_type=f32)


def tn(left, right):
    return lax.dot_general(left, right, (((0,), (0,)), ((), ())), preferred_element_type=f32)


def fill_bias(kinfo_ref, qinfo_ref, bias_ref):
    diff = qinfo_ref[0:1, :] - kinfo_ref[:, 0:1]
    fine = (diff >= 0) & (diff <= kinfo_ref[:, 1:2])
    bias_ref[...] = jnp.where(fine, 0.0, masked_fill)


def attend_forward_kernel(
    heads, kinfo_ref, qinfo_ref, q_ref, own_ref, sib_ref, out_ref, lse_ref, top_ref, bias_ref
):
    step = pl.program_id(0)

    @pl.when(step == 0)
    def _():
        fill_bias(kinfo_ref, qinfo_ref, bias_ref)

    keys = jnp.concatenate([own_ref[0], sib_ref[0]], axis=0)
    values = jnp.concatenate([own_ref[1], sib_ref[1]], axis=0)
    queries = q_ref[...]
    lane = lax.broadcasted_iota(jnp.int32, queries.shape, 1)
    outs = []
    for side in range(2):
        mine = (lane >= HD) if side else (lane < HD)
        picked = jnp.where(mine, queries, jnp.zeros_like(queries)) * bf16(HD**-0.5)
        scores = nt(keys, picked) + bias_ref[...]
        top = jnp.max(scores, axis=0, keepdims=True)
        weights = jnp.exp(scores - top)
        total = jnp.sum(weights, axis=0, keepdims=True)
        mixed = tn(values[:, side * HD : (side + 1) * HD], weights.astype(bf16))
        outs.append(mixed * (1.0 / total))
        lse_ref[0, side : side + 1, :] = top + jnp.log(total)
        top_ref[0, side : side + 1, :] = top
    out_ref[...] = jnp.concatenate(outs, axis=0).T.astype(bf16)


def attend_backward_kernel(
    heads,
    kinfo_ref,
    qinfo_ref,
    q_ref,
    own_ref,
    sib_ref,
    grad_ref,
    lse_ref,
    dq_ref,
    down_ref,
    dsib_ref,
    bias_ref,
):
    step = pl.program_id(0)

    @pl.when(step == 0)
    def _():
        fill_bias(kinfo_ref, qinfo_ref, bias_ref)

    keys = jnp.concatenate([own_ref[0], sib_ref[0]], axis=0)
    values = jnp.concatenate([own_ref[1], sib_ref[1]], axis=0)
    queries, grads = q_ref[...], grad_ref[...]
    half = queries.shape[0]
    lane = lax.broadcasted_iota(jnp.int32, queries.shape, 1)
    dqs, dk, dv = [], 0.0, 0.0
    for side in range(2):
        mine = (lane >= HD) if side else (lane < HD)
        picked = jnp.where(mine, queries, jnp.zeros_like(queries)) * bf16(HD**-0.5)
        grad = jnp.where(mine, grads, jnp.zeros_like(grads))
        scores = nt(keys, picked) + bias_ref[...]
        weights = jnp.exp(scores - lse_ref[0, side : side + 1, :])
        dp = nt(values, grad)
        delta = jnp.sum(weights * dp, axis=0, keepdims=True)
        ds = (weights * (dp - delta)).astype(bf16)
        dqs.append(tn(keys[:, side * HD : (side + 1) * HD], ds) * (HD**-0.5))
        dk = dk + product(ds, picked)
        dv = dv + product(weights.astype(bf16), grad)
    dq_ref[...] = jnp.concatenate(dqs, axis=0).T.astype(bf16)
    dk, dv = dk.astype(bf16), dv.astype(bf16)
    down_ref[0] = dk[:half]
    dsib_ref[0] = dk[half:]
    down_ref[1] = dv[:half]
    dsib_ref[1] = dv[half:]


def pair_specs(rows):
    flat = pl.BlockSpec((rows, LANES), lambda i: (0, i))
    double = pl.BlockSpec((2, rows, LANES), lambda i: (0, 0, i))
    per_head = pl.BlockSpec((1, 2, rows), lambda i: (i, 0, 0))
    return flat, double, per_head


def attend_forward(heads, kinfo, qinfo, queries, own, sib):
    rows, width = queries.shape
    pairs = width // LANES
    flat, double, per_head = pair_specs(rows)
    small = jax.ShapeDtypeStruct((pairs, 2, rows), f32)
    return pl.pallas_call(
        partial(attend_forward_kernel, heads),
        grid=(pairs,),
        in_specs=[
            pl.BlockSpec(kinfo.shape, lambda i: (0, 0)),
            pl.BlockSpec(qinfo.shape, lambda i: (0, 0)),
            flat,
            double,
            double,
        ],
        out_specs=[flat, per_head, per_head],
        out_shape=[jax.ShapeDtypeStruct((rows, width), bf16), small, small],
        scratch_shapes=[pltpu.VMEM((2 * rows, rows), f32)],
        compiler_params=pltpu.CompilerParams(vmem_limit_bytes=48 * 2**20),
        cost_estimate=pl.CostEstimate(
            flops=pairs * 16 * rows * rows * LANES,
            bytes_accessed=rows * width * 12,
            transcendentals=pairs * 4 * rows * rows,
        ),
        name="attend_forward",
    )(kinfo, qinfo, queries, own, sib)


def attend_backward(heads, kinfo, qinfo, queries, kv, grad, lse):
    rows, width = queries.shape
    pairs = width // LANES
    flat, double, per_head = pair_specs(rows)
    both = jax.ShapeDtypeStruct((2, rows, width), bf16)
    return pl.pallas_call(
        partial(attend_backward_kernel, heads),
        grid=(pairs,),
        in_specs=[
            pl.BlockSpec(kinfo.shape, lambda i: (0, 0)),
            pl.BlockSpec(qinfo.shape, lambda i: (0, 0)),
            flat,
            double,
            pl.BlockSpec((2, rows, LANES), lambda i: (0, 1, i)),
            flat,
            per_head,
        ],
        out_specs=[flat, double, double],
        out_shape=[jax.ShapeDtypeStruct((rows, width), bf16), both, both],
        scratch_shapes=[pltpu.VMEM((2 * rows, rows), f32)],
        compiler_params=pltpu.CompilerParams(vmem_limit_bytes=48 * 2**20),
        cost_estimate=pl.CostEstimate(
            flops=pairs * 40 * rows * rows * LANES,
            bytes_accessed=rows * width * 22,
            transcendentals=pairs * 4 * rows * rows,
        ),
        name="attend_backward",
    )(kinfo, qinfo, queries, kv, kv, grad, lse)


MESH = pl.DeviceIdType.MESH


class Sizes:
    def __init__(self, width, hidden, ctx, dp, length):
        self.width = width
        self.wide = -(-width // LANES) * LANES
        self.ctx = ctx
        self.rows = 2 * width // dp
        self.qkv = 3 * width // ctx
        self.out = width // ctx
        self.cols = -(-(self.qkv + self.out) // LANES) * LANES
        self.up = hidden // ctx
        self.half = length // 2
        self.pairs = self.wide // LANES
        self.out_tile = self.qkv // LANES * LANES
        self.qkv_cols = 1024
        self.qkv_pad = -(-self.qkv // LANES) * LANES

    def qkv_runs(self, z):
        runs, at = [], z * self.qkv
        end = at + self.qkv
        while at < end:
            kind = at // self.width
            stop = min(end, (kind + 1) * self.width)
            runs.append((at - z * self.qkv, kind * self.wide + at - kind * self.width, stop - at))
            at = stop
        return runs


class Net:
    def __init__(self):
        self.d = lax.axis_index("dp")
        self.z = lax.axis_index("ctx")
        self.c = self.d % 2
        self.p = self.d // 2
        y, x = self.p // 2, self.p % 2
        self.px, self.py, self.pd = 2 * y + 1 - x, 2 * (1 - y) + x, 2 * (1 - y) + 1 - x
        self.x_to = (2 * self.px + self.c, self.z)
        self.y_to = (2 * self.py + self.c, self.z)
        self.sib = (2 * self.p + 1 - self.c, self.z)
        self.near = self.c + 2 * (self.z // 2)
        self.far = self.c + 2 * (1 - self.z // 2)


def enter(net):
    gate = pltpu.get_barrier_semaphore()
    for c in range(2):
        for z in range(4):

            @pl.when((c != net.c) | (z != net.z))
            def _():
                pl.semaphore_signal(gate, inc=1, device_id=(2 * net.p + c, z), device_id_type=MESH)

    for to in (net.x_to, net.y_to):
        pl.semaphore_signal(gate, inc=1, device_id=to, device_id_type=MESH)
    pl.semaphore_wait(gate, 9)


class Gather:
    def __init__(self, net, sizes, w, own, swapped, sems):
        self.n, self.s, self.w, self.own, self.swapped = net, sizes, w, own, swapped
        self.zs, self.zr, self.hs, self.hr, self.cs, self.cr, self.loc = sems

    def at(self, p, z):
        r, c = (z, p) if self.swapped else (p, z)
        s = self.s
        return self.w.at[
            pl.ds(pl.multiple_of(r * s.rows, 16), s.rows),
            pl.ds(pl.multiple_of(c * s.cols, LANES), s.cols),
        ]

    def copy(self, p, z, send, recv, to):
        block = self.at(p, z)
        return pltpu.make_async_remote_copy(
            block, block, send, recv, device_id=to, device_id_type=MESH
        )

    def zcopy(self, z, up):
        n = self.n
        to = (n.d, n.z + 1 if up else n.z - 1)
        return self.copy(n.p, z, self.zs.at[z // 2, int(up)], self.zr.at[z // 2], to)

    def hop(self, p, z, to, k):
        return self.copy(p, z, self.hs.at[z // 2, k], self.hr.at[z // 2, k], to)

    def across(self, p, z):
        return self.copy(p, z, self.cs.at[p, z // 2], self.cr.at[p, z // 2], self.n.sib)

    def begin(self):
        n = self.n

        @pl.when(n.z % 2 == n.c)
        def _():
            local = pltpu.make_async_copy(self.own, self.at(n.p, n.z), self.loc)
            local.start()
            local.wait()

            @pl.when(n.z < 3)
            def _():
                self.zcopy(n.z, True).start()

            @pl.when(n.z > 0)
            def _():
                self.zcopy(n.z, False).start()

    def arrive(self, z):
        n = self.n

        @pl.when(z != n.z)
        def _():
            self.zcopy(z, True).wait_recv()

            @pl.when((z < n.z) & (n.z < 3))
            def _():
                self.zcopy(z, True).start()

            @pl.when((z > n.z) & (n.z > 0))
            def _():
                self.zcopy(z, False).start()

        self.hop(n.p, z, n.x_to, 0).start()
        self.hop(n.p, z, n.y_to, 1).start()
        self.across(n.p, z).start()

    def turn(self, z):
        n = self.n
        self.hop(n.px, z, n.x_to, 0).wait_recv()

        @pl.when(z < 2)
        def _():
            self.hop(n.px, z, n.y_to, 2).start()

        self.across(n.px, z).start()
        self.hop(n.py, z, n.y_to, 1).wait_recv()

        @pl.when(z >= 2)
        def _():
            self.hop(n.py, z, n.x_to, 2).start()

        self.across(n.py, z).start()

    def last(self, z):
        n = self.n
        self.hop(n.pd, z, n.x_to, 2).wait_recv()
        self.across(n.pd, z).start()

    def ready(self):
        n = self.n
        for half in range(2):
            for p in range(4):
                self.across(p, 1 - n.c + 2 * half).wait_recv()

    def drain(self):
        n = self.n
        for half in range(2):
            z = n.c + 2 * half

            @pl.when((z <= n.z) & (n.z < 3))
            def _():
                self.zcopy(z, True).wait_send()

            @pl.when((z >= n.z) & (n.z > 0))
            def _():
                self.zcopy(z, False).wait_send()

            for k, to in enumerate((n.x_to, n.y_to, n.x_to)):
                self.hop(n.p, z, to, k).wait_send()
            for p in range(4):
                self.across(p, z).wait_send()


def gather_sems():
    dma = pltpu.SemaphoreType.DMA
    return [dma((2, 2)), dma((2,)), dma((2, 3)), dma((2, 3)), dma((4, 2)), dma((4, 2)), dma]


class ToSequences:
    def __init__(self, net, src, dst, sems):
        self.n, self.src, self.dst = net, src, dst
        self.ss, self.rs = sems
        self.rows = src.shape[1]

    def parts(self):
        n = self.n
        for j in range(2):
            to = (2 * n.p + n.z // 2, 2 * n.c + j)
            yield j, to, (to[0] == n.d) & (to[1] == n.z)

    def place(self, t):
        return self.dst.at[pl.ds(pl.multiple_of(t * self.rows, 16), self.rows)]

    def remote(self, j, to):
        t = self.n.z % 2
        return pltpu.make_async_remote_copy(
            self.src.at[j],
            self.place(t),
            self.ss.at[j],
            self.rs.at[t],
            device_id=to,
            device_id_type=MESH,
        )

    def start(self):
        for j, to, here in self.parts():

            @pl.when(here)
            def _():
                t = self.n.z % 2
                pltpu.make_async_copy(self.src.at[j], self.place(t), self.rs.at[t]).start()

            @pl.when(jnp.logical_not(here))
            def _():
                self.remote(j, to).start()

    def wait(self):
        for t in range(2):
            pltpu.make_async_copy(self.src.at[0], self.place(t), self.rs.at[t]).wait()

    def drain(self):
        for j, to, here in self.parts():

            @pl.when(jnp.logical_not(here))
            def _():
                self.remote(j, to).wait_send()


class FromSequences:
    def __init__(self, net, src, dst, sems):
        self.n, self.src, self.dst = net, src, dst
        self.ss, self.rs = sems
        self.rows = dst.shape[1]

    def parts(self):
        n = self.n
        for t in range(2):
            to = (2 * n.p + n.z // 2, 2 * n.c + t)
            yield t, to, (to[0] == n.d) & (to[1] == n.z)

    def piece(self, t):
        return self.src.at[pl.ds(t * self.rows, self.rows)]

    def remote(self, t, to):
        j = self.n.z % 2
        return pltpu.make_async_remote_copy(
            self.piece(t),
            self.dst.at[j],
            self.ss.at[t],
            self.rs.at[j],
            device_id=to,
            device_id_type=MESH,
        )

    def start(self):
        for t, to, here in self.parts():

            @pl.when(here)
            def _():
                j = self.n.z % 2
                pltpu.make_async_copy(self.piece(t), self.dst.at[j], self.rs.at[j]).start()

            @pl.when(jnp.logical_not(here))
            def _():
                self.remote(t, to).start()

    def wait(self):
        for j in range(2):
            pltpu.make_async_copy(self.piece(0), self.dst.at[j], self.rs.at[j]).wait()

    def drain(self):
        for t, to, here in self.parts():

            @pl.when(jnp.logical_not(here))
            def _():
                self.remote(t, to).wait_send()


def by_rows(total, step, body):
    def one(i, carry):
        body(pl.ds(pl.multiple_of(i * step, step), step))
        return carry

    lax.fori_loop(0, total // step, one, 0)


def by_columns(total, body, step=640):
    def one(i, carry):
        body(pl.multiple_of(i * step, LANES), step)
        return carry

    lax.fori_loop(0, total // step, one, 0)
    if total % step:
        body(total // step * step, total % step)


def normalised(values):
    average = jnp.mean(values, axis=-1, keepdims=True)
    centred = values - average
    variance = jnp.mean(centred * centred, axis=-1, keepdims=True)
    return centred * lax.rsqrt(variance + eps_norm)


def place_run(block, source, phase, count):
    moved = pltpu.roll(block, (phase - source) % block.shape[1], axis=1)
    tiles = -(-(phase + count) // LANES) * LANES
    moved = moved[:, :tiles]
    lane = lax.broadcasted_iota(jnp.int32, moved.shape, 1)
    return jnp.where((lane >= phase) & (lane < phase + count), moved, 0.0)


def attend_pair(s, i, q_ref, kv_ref, bias_ref, att_ref, lse_ref, top_ref):
    lanes = pl.ds(pl.multiple_of(i * LANES, LANES), LANES)
    keys, values, queries = kv_ref[0, :, lanes], kv_ref[1, :, lanes], q_ref[:, lanes]
    lane = lax.broadcasted_iota(jnp.int32, queries.shape, 1)
    outs = []
    for side in range(2):
        mine = (lane >= HD) if side else (lane < HD)
        picked = jnp.where(mine, queries, jnp.zeros_like(queries)) * bf16(HD**-0.5)
        scores = nt(keys, picked) + bias_ref[...]
        top = jnp.max(scores, axis=0, keepdims=True)
        weights = jnp.exp(scores - top)
        total = jnp.sum(weights, axis=0, keepdims=True)
        mixed = tn(values[:, side * HD : (side + 1) * HD], weights.astype(bf16))
        outs.append(mixed * (1.0 / total))
        lse_ref[i, side : side + 1, :] = top + jnp.log(total)
        top_ref[i, side : side + 1, :] = top
    att_ref[:, lanes] = jnp.concatenate(outs, axis=0).T.astype(bf16)


def forward_plan(A, B, C, near, far, seq_x, seq_cot):
    def do(method, *args):
        return partial(method, *args)

    return {
        ("start", 0): (
            do(A.arrive, near),
            do(B.begin),
            do(A.arrive, far),
            do(seq_x.start),
        ),
        ("vectors", 0): (
            do(A.turn, near),
            do(B.arrive, near),
            do(C.begin),
            do(A.turn, far),
            do(A.last, near),
            do(B.arrive, far),
            do(A.last, far),
        ),
        ("normed", 0): (do(B.turn, near),),
        ("project", 1): (do(C.arrive, near),),
        ("share", 0): (do(B.turn, far), do(B.last, near)),
        ("pair", 0): (do(C.arrive, far), do(seq_cot.start)),
        ("pair", 2): (do(B.last, far), do(C.turn, near)),
        ("pair", 6): (do(C.turn, far), do(C.last, near)),
        ("down", 0): (do(C.last, far),),
    }


def forward_kernel(s, *refs):
    (own_a, own_b, own_c, small, inp, cot, kinfo, qinfo) = refs[:8]
    (wa_o, wb_o, wc_o, x_o, cot_o, vec, normed_o, q_o, kv_o, att_o, res_o, two_o, slope_o, hid_o) = refs[8:22]
    (lse, top, out_o) = refs[22:25]
    (x, normed, q, kv, bias, att, res, two, wa, wb, wc, out, smalls) = refs[25:38]
    sems = refs[38:]
    net = Net()
    A, B, C = [
        Gather(net, s, w, own, swapped, sems[7 * g : 7 * g + 7])
        for g, (w, own, swapped) in enumerate(
            ((wa, own_a, False), (wb, own_b, False), (wc, own_c, True))
        )
    ]
    seq_x = ToSequences(net, inp, x, sems[21:23])
    seq_cot = ToSequences(net, cot, cot_o, sems[23:25])
    small_s, small_r, kv_s, kv_r, save = sems[25:30]
    near, far = net.near, net.far
    saves = []

    def keep(src, dst):
        copy = pltpu.make_async_copy(src, dst, save.at[len(saves)])
        copy.start()
        saves.append(copy)

    def small_copy(z):
        return pltpu.make_async_remote_copy(
            small,
            smalls.at[net.z],
            small_s.at[z],
            small_r.at[net.z],
            device_id=(net.d, z),
            device_id_type=MESH,
        )

    plan = forward_plan(A, B, C, near, far, seq_x, seq_cot)

    def at(name, step=0):
        for act in plan.get((name, step), ()):
            act()

    enter(net)
    A.begin()
    for z in range(4):

        @pl.when(z != net.z)
        def _():
            small_copy(z).start()

        @pl.when(z == net.z)
        def _():
            pltpu.make_async_copy(small, smalls.at[z], small_r.at[z]).start()

    at("start")
    diff = qinfo[0:1, :] - kinfo[:, 0:1]
    fine = (diff >= 0) & (diff <= kinfo[:, 1:2])
    bias[...] = jnp.where(fine, 0.0, masked_fill)
    at("vectors")

    for z in range(4):
        pltpu.make_async_copy(small, smalls.at[z], small_r.at[z]).wait()
    row = lax.broadcasted_iota(jnp.int32, (3 * LANES, s.wide), 0)
    col = lax.broadcasted_iota(jnp.int32, (3 * LANES, s.wide), 1)
    rows = 0.0
    for z in range(4):
        spread = jnp.where((col == row + z * s.out) & (row < s.out), 1.0, 0.0).astype(bf16)
        rows = rows + product(smalls[z, :, : 3 * LANES], spread)
    vec[...] = rows

    seq_x.wait()
    keep(x, x_o)
    by_rows(
        s.half,
        LANES,
        lambda r: normed.__setitem__(
            (r, slice(None)),
            to_low(
                normalised(x[r, :].astype(f32)) * vec[0:1, : s.width] + vec[1:2, : s.width]
            ),
        ),
    )
    keep(normed, normed_o)
    at("normed")
    A.ready()

    wa_saved = len(saves)
    keep(wa, wa_o)
    q[...] = jnp.zeros_like(q)
    kv[:, : s.half, :] = jnp.zeros((2, s.half, s.wide), bf16)
    places = (q, kv.at[0, pl.ds(0, s.half)], kv.at[1, pl.ds(0, s.half)])
    for z in range(4):

        def part(start, size):
            lanes = pl.ds(pl.multiple_of(z * s.cols + start, LANES), size)
            res[:, pl.ds(start, size)] = product(normed[...], wa[:, lanes])

        by_columns(s.qkv_cols, part)
        for source, target, count in s.qkv_runs(z):
            kind, first = target // s.wide, target % s.wide
            base = first // LANES * LANES
            moved = place_run(res[:, : s.qkv_cols], source, first - base, count)
            lanes = slice(base, base + moved.shape[1])
            if kind != 1:
                lane = lax.broadcasted_iota(jnp.int32, (1, moved.shape[1]), 1)
                fits = (lane >= first - base) & (lane < first - base + count)
                moved = moved + jnp.where(fits, vec[2 + kind // 2 : 3 + kind // 2, lanes], 0.0)
            place = places[kind]
            place[:, lanes] = place[:, lanes] + to_low(moved)
        at("project", z)
    share = pltpu.make_async_remote_copy(
        kv.at[:, pl.ds(0, s.half)],
        kv.at[:, pl.ds(s.half, s.half)],
        kv_s,
        kv_r,
        device_id=net.sib,
        device_id_type=MESH,
    )
    share.start()
    at("share")
    share.wait()
    keep(q, q_o)
    keep(kv, kv_o)

    def pair(i, carry):
        attend_pair(s, i, q, kv, bias, att, lse, top)

        for k in range(s.pairs):
            if ("pair", k) in plan:
                pl.when(i == k)(partial(at, "pair", k))
        return carry

    lax.fori_loop(0, s.pairs, pair, 0)
    keep(att, att_o)

    res[...] = jnp.zeros_like(res)
    for z in range(4):
        lanes = slice(z * s.cols + s.out_tile, (z + 1) * s.cols)
        block = product(att[:, : s.width], wa[:, lanes])
        target = z * s.out
        base = target // LANES * LANES
        moved = place_run(block, s.qkv - s.out_tile, target - base, s.out)
        res[:, base : base + moved.shape[1]] += moved
    at("second")
    B.ready()
    keep(wb, wb_o)

    def second(r):
        total = res[r, : s.width] + x[r, :].astype(f32) + vec[4:5, : s.width]
        res[r, : s.width] = total
        two[r, :] = to_low(normalised(total) * vec[5:6, : s.width] + vec[6:7, : s.width])

    by_rows(s.half, LANES, second)
    keep(res, res_o)
    keep(two, two_o)

    A.drain()
    saves[wa_saved].wait()
    hid, slope = wa.at[pl.ds(0, s.half)], wa.at[pl.ds(s.half, s.half)]
    for z in range(4):

        def part(start, size):
            lanes = pl.ds(pl.multiple_of(z * s.cols + start, LANES), size)
            u = product(two[...], wb[:, lanes])
            u = u + smalls[z, 8:9, pl.ds(start, size)].astype(f32)
            inner = math.sqrt(2 / math.pi) * (u + 0.044715 * u * u * u)
            t = jnp.tanh(inner)
            bend = math.sqrt(2 / math.pi) * (1 + 3 * 0.044715 * u * u)
            hid[:, lanes] = to_low(0.5 * u * (1 + t))
            slope[:, lanes] = to_low(0.5 * (1 + t) + 0.5 * u * (1 - t * t) * bend)

        by_columns(s.cols, part)
        at("up", z)
    keep(hid, hid_o)
    keep(slope, slope_o)
    at("down")
    C.ready()

    keep(wc, wc_o)
    for k in range(3):
        first, count = k * 3 * LANES, min(3 * LANES, s.width - k * 3 * LANES)
        block = nt(hid[...], wc[pl.ds(first, count), :])
        total = res[:, first : first + count] + block + vec[7:8, first : first + count]
        out[:, first : first + count] = to_low(total)
    keep(out, out_o)
    seq_cot.wait()
    for group in (B, C):
        group.drain()
    for z in range(4):

        @pl.when(z != net.z)
        def _():
            small_copy(z).wait_send()

    seq_x.drain()
    seq_cot.drain()
    for i, copy in enumerate(saves):
        if i != wa_saved:
            copy.wait()


def forward_call(s, own_a, own_b, own_c, small, inp, cot, kinfo, qinfo):
    dma = pltpu.SemaphoreType.DMA
    rows = s.half
    full = s.ctx * s.cols

    def low(*shape):
        return jax.ShapeDtypeStruct(shape, bf16)

    def high(*shape):
        return jax.ShapeDtypeStruct(shape, f32)

    out_shape = [low(s.width, full)] * 3 + [
        low(rows, s.width),
        low(rows, s.width),
        high(16, s.wide),
        low(rows, s.width),
        low(rows, s.wide),
        low(2, 2 * rows, s.wide),
        low(rows, s.wide),
        high(rows, s.wide),
        low(rows, s.width),
        low(rows, full),
        low(rows, full),
        high(s.pairs, 2, rows),
        high(s.pairs, 2, rows),
        low(rows, s.width),
    ]
    anywhere = pl.BlockSpec(memory_space=pl.ANY)
    local = pl.BlockSpec(memory_space=pltpu.VMEM)
    out_specs = [local if i in (5, 14, 15) else anywhere for i in range(len(out_shape))]
    return pl.pallas_call(
        partial(forward_kernel, s),
        out_shape=out_shape,
        in_specs=[anywhere] * 6 + [local] * 2,
        out_specs=out_specs,
        scratch_shapes=[
            pltpu.VMEM((rows, s.width), bf16),
            pltpu.VMEM((rows, s.width), bf16),
            pltpu.VMEM((rows, s.wide), bf16),
            pltpu.VMEM((2, 2 * rows, s.wide), bf16),
            pltpu.VMEM((2 * rows, rows), f32),
            pltpu.VMEM((rows, s.wide), bf16),
            pltpu.VMEM((rows, s.wide), f32),
            pltpu.VMEM((rows, s.width), bf16),
            pltpu.VMEM((s.width, full), bf16),
            pltpu.VMEM((s.width, full), bf16),
            pltpu.VMEM((s.width, full), bf16),
            pltpu.VMEM((rows, s.width), bf16),
            pltpu.VMEM((4, 16, s.wide), bf16),
        ]
        + gather_sems() * 3
        + [dma((2,))] * 4
        + [dma((4,)), dma((4,)), dma, dma, dma((14,))],
        compiler_params=pltpu.CompilerParams(
            collective_id=1, has_side_effects=True, vmem_limit_bytes=61 * 2**20
        ),
        name="forward",
    )(own_a, own_b, own_c, small, inp, cot, kinfo, qinfo)


class Scatter:
    def __init__(self, net, s, own, ship, came, first, second, line, total, out, sums, sems):
        self.n, self.s, self.sums = net, s, sums
        self.own, self.ship_ref, self.came = own, ship, came
        self.first_ref, self.second_ref, self.line = first, second, line
        self.total, self.out = total, out
        self.total_like = sums.at[0] if own is None else self.block(0, 0)
        (self.ps, self.pr, self.fs, self.fr, self.hs, self.hr, self.zs, self.zr, self.ld, self.es, self.er, self.eo) = sems

    def target(self, k):
        return (self.n.far, self.n.near)[k]

    def sibling_target(self, k):
        n = self.n
        return 1 - n.c + 2 * (n.z // 2 if k else 1 - n.z // 2)

    def route(self, h):
        n = self.n
        both = ((n.px, n.x_to), (n.py, n.y_to))
        return both[h], both[1 - h]

    def lanes(self, h):
        cut = (self.s.cols // 2 + LANES - 1) // LANES * LANES
        return pl.ds(0, cut) if h == 0 else pl.ds(cut, self.s.cols - cut)

    def block(self, k, p):
        rows = self.s.rows
        return self.own.at[k, pl.ds(pl.multiple_of(p * rows, 16), rows)]

    def remote(self, src, dst, send, recv, to):
        return pltpu.make_async_remote_copy(
            src, dst, send, recv, device_id=to, device_id_type=MESH
        )

    def panel(self, k):
        return self.remote(
            self.ship_ref.at[k], self.came.at[k], self.ps.at[k], self.pr.at[k], self.n.sib
        )

    def part(self, k, p, h):
        rows = self.s.rows
        return self.own.at[k, pl.ds(pl.multiple_of(p * rows, 16), rows), self.lanes(h)]

    def pieces(self, k, h):
        (one, to), _ = self.route(h)
        for i, p in enumerate((one, self.n.pd)):
            yield self.remote(
                self.part(k, p, h),
                self.first_ref.at[k, i, :, self.lanes(h)],
                self.fs.at[k, h, i],
                self.fr.at[k, h, i],
                to,
            )

    def piece(self, k, h):
        _, (two, to) = self.route(h)
        return self.remote(
            self.part(k, two, h),
            self.second_ref.at[k, :, self.lanes(h)],
            self.hs.at[k, h],
            self.hr.at[k, h],
            to,
        )

    def along(self, k):
        n = self.n
        src = self.block(k, n.p) if self.own is not None else self.sums.at[k]
        return self.remote(
            src, self.line.at[n.z], self.zs.at[k], self.zr.at[n.z], (n.d, self.target(k))
        )

    def ship(self, k):
        self.panel(k).start()

    def wait_panel(self, k):
        self.panel(k).wait_recv()

    def start(self, k):
        for h in range(2):
            for copy in self.pieces(k, h):
                copy.start()

    def add(self, k, p, h, other):
        rows, lanes = self.s.rows, self.lanes(h)

        def some(r):
            at = pl.ds(pl.multiple_of(p * rows + r.start, 16), r.size)
            self.own[k, at, lanes] = to_low(
                self.own[k, at, lanes].astype(f32) + other[r, lanes].astype(f32)
            )

        by_rows(rows, 16, some)

    def turn(self, k):
        for h in range(2):
            for copy in self.pieces(k, h):
                copy.wait_recv()
            _, (two, _) = self.route(h)
            self.add(k, two, h, self.first_ref.at[k, 1])
            self.piece(k, h).start()
        for h in range(2):
            self.add(k, self.n.p, h, self.first_ref.at[k, 0])

    def land(self, k):
        for h in range(2):
            self.piece(k, h).wait_recv()
            self.add(k, self.n.p, h, self.second_ref.at[k])

    def send(self, k):
        @pl.when(self.target(k) != self.n.z)
        def _():
            self.along(k).start()

    def mine(self):
        return self.n.z % 2 == self.n.c

    def collect(self, stage=None, held=None):
        n, rows = self.n, self.s.rows

        @pl.when(self.mine())
        def _():
            if self.own is None:
                load = pltpu.make_async_copy(self.sums.at[1], held, self.ld)
                load.start()
                load.wait()

            def begin(r):
                if self.own is None:
                    value = held[r, :]
                else:
                    value = self.own[1, pl.ds(pl.multiple_of(n.p * rows + r.start, 16), r.size), :]
                self.total[r, :] = value.astype(f32)

            by_rows(rows, 16, begin)
            for z in range(4):

                @pl.when(z != n.z)
                def _():
                    self.remote(
                        self.total_like, self.line.at[z], self.zs.at[0], self.zr.at[z], n.sib
                    ).wait_recv()
                    if stage is None:
                        other = self.line.at[z]
                    else:
                        other = stage
                        load = pltpu.make_async_copy(self.line.at[z], stage, self.ld)
                        load.start()
                        load.wait()

                    def more(r):
                        self.total[r, :] += other[r, :].astype(f32)

                    by_rows(rows, 16, more)

            self.kept().start()
            self.final().start()

    def share(self, core):
        rows = self.out.shape[0]
        if rows == self.s.rows:
            return self.total
        return self.total.at[pl.ds(pl.multiple_of(core * rows, 8), rows)]

    def kept(self):
        return pltpu.make_async_copy(self.share(self.n.c), self.out, self.eo)

    def final(self):
        return self.remote(self.share(1 - self.n.c), self.out, self.es, self.er, self.n.sib)

    def drain(self, panels=True):
        for k in range(2):
            if panels:
                self.panel(k).wait_send()
            for h in range(2):
                for copy in self.pieces(k, h):
                    copy.wait_send()
                self.piece(k, h).wait_send()

    def finish(self):
        for k in range(2):

            @pl.when(self.target(k) != self.n.z)
            def _():
                self.along(k).wait_send()

        @pl.when(self.mine())
        def _():
            self.kept().wait()
            self.final().wait_send()

        @pl.when(jnp.logical_not(self.mine()))
        def _():
            self.final().wait_recv()


def scatter_sems():
    dma = pltpu.SemaphoreType.DMA
    return [
        dma((2,)), dma((2,)), dma((2, 2, 2)), dma((2, 2, 2)), dma((2, 2)), dma((2, 2)),
        dma((2,)), dma((4,)), dma, dma, dma, dma,
    ]


def scatter_scratch(s, groups):
    panels = (2, s.width, s.cols)
    scratch = [pltpu.VMEM(panels, bf16)]
    for group in range(groups):
        scratch += [pltpu.VMEM(panels, bf16)] * (1 if group else 2)
        scratch += [
            pltpu.VMEM((2, 2, s.rows, s.cols), bf16),
            pltpu.VMEM((2, s.rows, s.cols), bf16),
        ]
    return scratch + [pltpu.VMEM((s.rows, s.cols), f32), pltpu.VMEM((s.rows, s.cols), bf16)]


def norm_back(values, grads, gain):
    average = jnp.mean(values, axis=-1, keepdims=True)
    centred = values - average
    variance = jnp.mean(centred * centred, axis=-1, keepdims=True)
    scale = lax.rsqrt(variance + eps_norm)
    n = centred * scale
    gn = grads * gain
    inner = jnp.mean(gn * n, axis=-1, keepdims=True)
    back = scale * (gn - jnp.mean(gn, axis=-1, keepdims=True) - n * inner)
    return back, jnp.sum(grads * n, axis=0, keepdims=True), jnp.sum(grads, axis=0, keepdims=True)


def fetch_all(pairs, sems):
    copies = [pltpu.make_async_copy(src, dst, sems.at[i]) for i, (src, dst) in enumerate(pairs)]
    for copy in copies:
        copy.start()
    return copies


def middle_kernel(s, *refs):
    (wa, wb, wc, cot_i, res_i, two_i, slope_i, hid_i, out_i, vec) = refs[:10]
    (down_s, up_own, gres_o, gatt_o, oz_o, sums, back_o) = refs[10:17]
    (cot, res, two, gp, hid, cot_t, two_t, wt, acc, branch, oz) = refs[17:28]
    (ship, own_c, came, first_c, second_c, own_b) = refs[28:34]
    sems = refs[34:]
    net = Net()
    C = Scatter(net, s, own_c, ship, came, first_c, second_c, None, None, None, None, sems[:12])
    B = Scatter(net, s, own_b, ship, came, None, None, None, None, None, None, sems[12:24])
    seq_out = FromSequences(net, out_i, back_o, sems[24:26])
    load, tiles, save, keep, credit = sems[26:31]
    loads = fetch_all(
        ((cot_i, cot), (hid_i, hid), (slope_i, gp), (two_i, two), (res_i, res)), load
    )
    enter(net)
    seq_out.start()

    def tile(w, j, first=0):
        lanes = pl.ds(j * s.cols + first, s.cols - first)
        return pltpu.make_async_copy(
            w.at[:, lanes], wt.at[j % 2, :, pl.ds(0, s.cols - first)], tiles.at[j % 2]
        )

    tile(wc, 0).start()
    loads[0].wait()
    cot_t[...] = cot[...].T
    loads[1].wait()
    sums[...] = jnp.zeros_like(sums)

    def down_panel(z, dst, k, came=None):
        rows = pl.ds(pl.multiple_of(z * s.rows, 16), s.rows)
        for p in range(4):
            at = slice(p * s.rows, (p + 1) * s.rows)

            def part(start, size):
                lanes = pl.ds(start, size)
                many = pl.ds(pl.multiple_of(p * s.cols + start, LANES), size)
                value = product(cot_t[rows, :], hid[:, many])
                if came is not None:
                    value = value + came[k, at, lanes].astype(f32)
                dst[k, at, lanes] = to_low(value)

            by_columns(s.cols, part)

    def up_panel(z, dst, k, came=None):
        def part(start, size):
            lanes = pl.ds(start, size)
            many = pl.ds(pl.multiple_of(z * s.cols + start, LANES), size)
            value = product(two_t[...], gp[:, many])
            if came is not None:
                value = value + came[k, :, lanes].astype(f32)
            dst[k, :, lanes] = to_low(value)

        by_columns(s.cols, part)

    for k in range(2):
        down_panel(C.sibling_target(k), ship, k)
        C.ship(k)
    loads[2].wait()

    for j in range(4):
        if j < 3:
            tile(wc, j + 1).start()
        tile(wc, j).wait()

        def part(start, size):
            lanes = pl.ds(pl.multiple_of(j * s.cols + start, LANES), size)
            value = product(cot[...], wt[j % 2, :, pl.ds(start, size)])
            value = to_low(value * gp[:, lanes].astype(f32))
            gp[:, lanes] = value
            sums[8 + j : 9 + j, pl.ds(start, size)] = jnp.sum(
                value.astype(f32), axis=0, keepdims=True
            )

        by_columns(s.cols, part)
    tile(wb, 0).start()
    for k in range(2):
        C.wait_panel(k)
        down_panel(C.target(k), own_c, k, came)
        pl.semaphore_signal(
            credit.at[k], inc=1, device_id=net.sib, device_id_type=MESH
        )
        C.start(k)
    loads[3].wait()
    two_t[...] = two[...].T
    for k in range(2):
        C.panel(k).wait_send()
        up_panel(B.sibling_target(k), ship, k)
        pl.semaphore_wait(credit.at[k], 1)
        B.ship(k)

    for z in range(4):
        if z < 3:
            tile(wb, z + 1).start()
        tile(wb, z).wait()

        def part(start, size):
            value = nt(gp[:, z * s.cols : (z + 1) * s.cols], wt[z % 2, pl.ds(start, size), :])
            if z:
                value = value + acc[:, pl.ds(start, size)]
            acc[:, pl.ds(start, size)] = value

        by_columns(s.width, part)
        if z == 1:
            C.turn(0)
    tile(wa, 0, s.out_tile).start()
    for k in range(2):
        B.wait_panel(k)
        up_panel(B.target(k), own_b, k, came)
        if k == 0:
            C.turn(1)
    own_copy = pltpu.make_async_copy(own_b, up_own, save.at[3])
    own_copy.start()
    loads[4].wait()

    def norm(r):
        given = cot[r, :].astype(f32)
        back, gain, shift = norm_back(
            res[r, : s.width], acc[r, : s.width], vec[5:6, : s.width]
        )
        total_r = given + back
        res[r, : s.width] = total_r
        low = to_low(total_r)
        branch[r, : s.width] = low
        sums[4:5, : s.width] += jnp.sum(low.astype(f32), axis=0, keepdims=True)
        sums[5:6, : s.width] += gain
        sums[6:7, : s.width] += shift
        sums[7:8, : s.width] += jnp.sum(given, axis=0, keepdims=True)

    branch[...] = jnp.zeros_like(branch)
    by_rows(s.half, LANES, norm)
    kept = []
    for k in range(2):
        C.land(k)
        kept.append(pltpu.make_async_copy(C.block(k, net.p), down_s.at[k], keep.at[k]))
        kept[k].start()

    for z in range(4):
        if z < 3:
            tile(wa, z + 1, s.out_tile).start()
        tile(wa, z, s.out_tile).wait()
        source = z * s.out
        base = source // LANES * LANES
        size = s.cols - s.out_tile
        moved = place_run(
            branch[:, base : base + size].astype(f32), source - base, s.qkv - s.out_tile, s.out
        )
        oz[z] = to_low(moved)

        def part(start, count):
            value = nt(oz[z], wt[z % 2, pl.ds(start, count), :size])
            if z:
                value = value + acc[:, pl.ds(start, count)]
            acc[:, pl.ds(start, count)] = value

        by_columns(s.width, part)
    lane = lax.broadcasted_iota(jnp.int32, (s.half, s.wide), 1)
    branch[...] = to_low(jnp.where(lane < s.width, acc[...], 0.0))
    saves = fetch_all(((res, gres_o), (branch, gatt_o), (oz, oz_o)), save)
    C.drain(False)
    for k in range(2):
        B.panel(k).wait_send()
    for copy in saves + kept + [own_copy]:
        copy.wait()
    seq_out.wait()
    seq_out.drain()


def back_pair(s, i, q_ref, kv_ref, grad_ref, lse_ref, bias_ref, dq_ref, dkv_ref):
    lanes = pl.ds(pl.multiple_of(i * LANES, LANES), LANES)
    keys, values = kv_ref[0, :, lanes], kv_ref[1, :, lanes]
    queries, grads = q_ref[:, lanes], grad_ref[:, lanes]
    lane = lax.broadcasted_iota(jnp.int32, queries.shape, 1)
    dqs, dk, dv = [], 0.0, 0.0
    for side in range(2):
        mine = (lane >= HD) if side else (lane < HD)
        picked = jnp.where(mine, queries, jnp.zeros_like(queries)) * bf16(HD**-0.5)
        grad = jnp.where(mine, grads, jnp.zeros_like(grads))
        scores = nt(keys, picked) + bias_ref[...]
        weights = jnp.exp(scores - lse_ref[i, side : side + 1, :])
        dp = nt(values, grad)
        delta = jnp.sum(weights * dp, axis=0, keepdims=True)
        ds = (weights * (dp - delta)).astype(bf16)
        dqs.append(tn(keys[:, side * HD : (side + 1) * HD], ds) * (HD**-0.5))
        dk = dk + product(ds, picked)
        dv = dv + product(weights.astype(bf16), grad)
    dq_ref[:, lanes] = jnp.concatenate(dqs, axis=0).T.astype(bf16)
    dkv_ref[0, :, lanes] = dk.astype(bf16)
    dkv_ref[1, :, lanes] = dv.astype(bf16)


def attention_kernel(s, *refs):
    (kinfo, qinfo, lse, q_i, kv_i, grad_i, own_i, down_s) = refs[:8]
    (dq_o, dkv_o, up_s, down_o) = refs[8:12]
    (q, kv, grad, dq, dkv, came, bias, own_b, first_b, second_b, line, total, stage) = refs[12:25]
    sems = refs[25:]
    net = Net()
    B = Scatter(net, s, own_b, None, None, first_b, second_b, None, None, None, None, sems[:12])
    C = Scatter(net, s, None, None, None, None, None, line, total, down_o, down_s, sems[12:24])
    load, save, ds, dr = sems[24:28]
    loads = fetch_all(((own_i, own_b), (q_i, q), (kv_i, kv), (grad_i, grad)), load)
    enter(net)
    loads[0].wait()
    B.start(0)
    B.start(1)
    C.send(0)
    C.send(1)
    fill_bias(kinfo, qinfo, bias)
    for copy in loads[1:]:
        copy.wait()

    def pair(i, carry):
        back_pair(s, i, q, kv, grad, lse, bias, dq, dkv)

        @pl.when(i == 6)
        def _():
            B.turn(0)

        @pl.when(i == 7)
        def _():
            B.turn(1)

        return carry

    lax.fori_loop(0, s.pairs, pair, 0)
    rows = pl.ds(0, s.half)
    swap = pltpu.make_async_remote_copy(
        dkv.at[:, pl.ds(s.half, s.half)], came, ds, dr, device_id=net.sib, device_id_type=MESH
    )
    swap.start()
    saves = [pltpu.make_async_copy(dq, dq_o, save.at[0])]
    saves[0].start()
    C.collect(held=stage)
    swap.wait()

    def join(r):
        for kind in range(2):
            dkv[kind, r, :] = to_low(dkv[kind, r, :].astype(f32) + came[kind, r, :].astype(f32))

    by_rows(s.half, LANES, join)
    saves.append(pltpu.make_async_copy(dkv.at[:, rows], dkv_o, save.at[1]))
    saves[1].start()
    for k in range(2):
        B.land(k)
        saves.append(pltpu.make_async_copy(B.block(k, net.p), up_s.at[k], save.at[2 + k]))
        saves[2 + k].start()
    B.drain(False)
    C.finish()
    for copy in saves:
        copy.wait()


def attention_call(s, kinfo, qinfo, lse, q, kv, grad, own, down_s):
    dma = pltpu.SemaphoreType.DMA
    rows = s.half
    anywhere = pl.BlockSpec(memory_space=pl.ANY)
    local = pl.BlockSpec(memory_space=pltpu.VMEM)
    low = lambda *dims: jax.ShapeDtypeStruct(dims, bf16)
    block = pltpu.VMEM((s.rows, s.cols), bf16)
    return pl.pallas_call(
        partial(attention_kernel, s),
        out_shape=[
            low(rows, s.wide), low(2, rows, s.wide), low(2, s.rows, s.cols),
            jax.ShapeDtypeStruct((s.rows, s.cols), f32),
        ],
        in_specs=[local] * 3 + [anywhere] * 5,
        out_specs=[anywhere] * 4,
        scratch_shapes=[
            pltpu.VMEM((rows, s.wide), bf16),
            pltpu.VMEM((2, 2 * rows, s.wide), bf16),
            pltpu.VMEM((rows, s.wide), bf16),
            pltpu.VMEM((rows, s.wide), bf16),
            pltpu.VMEM((2, 2 * rows, s.wide), bf16),
            pltpu.VMEM((2, rows, s.wide), bf16),
            pltpu.VMEM((2 * rows, rows), f32),
            pltpu.VMEM((2, s.width, s.cols), bf16),
            pltpu.VMEM((2, 2, s.rows, s.cols), bf16),
            pltpu.VMEM((2, s.rows, s.cols), bf16),
            pltpu.VMEM((4, s.rows, s.cols), bf16),
            pltpu.VMEM((s.rows, s.cols), f32),
            block,
        ]
        + scatter_sems() * 2
        + [dma((4,)), dma((4,)), dma, dma],
        compiler_params=pltpu.CompilerParams(
            collective_id=4, has_side_effects=True, vmem_limit_bytes=60 * 2**20
        ),
        name="attention",
    )(kinfo, qinfo, lse, q, kv, grad, own, down_s)


def last_kernel(s, *refs):
    (wa, oz_i, dq_i, own_i, normed_i, att_i, x_i, gres_i, up_s, vec, sums, tops) = refs[:12]
    (qkv_o, up_o, gin_o, small_o) = refs[12:16]
    (own_d, dq, wide, qz, oz, norm_t, att_t, normed, att, x, gres, wt, acc, gin, buf, got) = refs[16:32]
    (ship, own_a, came_a, first_a, second_a, total, stage, line_a, line_b) = refs[32:41]
    sems = refs[41:]
    net = Net()
    A = Scatter(net, s, own_a, ship, came_a, first_a, second_a, line_a, total, qkv_o, None, sems[:12])
    B = Scatter(net, s, None, None, None, None, None, line_b, total, up_o, up_s, sems[18:30])
    seq_in = FromSequences(net, gin, gin_o, sems[12:14])
    load, tiles, gs, gr = sems[14:18]
    loads = fetch_all(
        ((dq_i, dq), (own_i, own_d), (normed_i, normed), (att_i, att), (oz_i, oz), (x_i, x), (gres_i, gres)),
        load,
    )
    enter(net)
    B.send(0)
    B.send(1)

    def tile(j):
        return pltpu.make_async_copy(
            wa.at[:, pl.ds(j * s.cols, s.qkv_pad)], wt.at[j % 2], tiles.at[j % 2]
        )

    tile(0).start()
    loads[2].wait()
    norm_t[...] = normed[...].T
    loads[3].wait()
    att_t[...] = att[...].T
    loads[0].wait()
    loads[1].wait()
    buf[...] = sums[...]
    wide[:, : s.wide] = dq[...].astype(f32)
    for kind in range(2):
        wide[:, (kind + 1) * s.wide : (kind + 2) * s.wide] = own_d[kind].astype(f32)
    buf[2:3, :] = jnp.sum(wide[:, : s.wide], axis=0, keepdims=True)
    buf[3:4, :] = jnp.sum(wide[:, 2 * s.wide :], axis=0, keepdims=True)
    for z in range(4):
        block = 0.0
        for source, target, count in s.qkv_runs(z):
            base = target // LANES * LANES
            moved = place_run(
                wide[:, base : base + s.qkv_pad], target - base, source, count
            )
            if moved.shape[1] < s.qkv_pad:
                moved = jnp.concatenate(
                    [moved, jnp.zeros((s.half, s.qkv_pad - moved.shape[1]), f32)], axis=1
                )
            block = block + moved
        qz[z] = to_low(block)
    loads[4].wait()

    def panel(z, dst, k, came=None):
        def put(start, size, value):
            lanes = pl.ds(start, size)
            if came is not None:
                value = value + came[k, :, lanes].astype(f32)
            dst[k, :, lanes] = to_low(value)

        def part(start, size):
            put(start, size, product(norm_t[...], qz[z, :, pl.ds(start, size)]))

        by_columns(s.out_tile, part)
        mixed = product(norm_t[...], qz[z, :, s.out_tile :]) + product(
            att_t[: s.width, :], oz[z, :, : s.qkv_pad - s.out_tile]
        )
        put(s.out_tile, s.qkv_pad - s.out_tile, mixed)
        rest = product(att_t[: s.width, :], oz[z, :, s.qkv_pad - s.out_tile :])
        put(s.qkv_pad, s.cols - s.qkv_pad, rest)

    for k in range(2):
        panel(A.sibling_target(k), ship, k)
        A.ship(k)
    for k in range(2):
        tile(k + 1).start()
        tile(k).wait()
        through(s, acc, qz, wt, k)
        A.wait_panel(k)
        panel(A.target(k), own_a, k, came_a)
        A.start(k)
    for z in range(2, 4):
        if z < 3:
            tile(z + 1).start()
        tile(z).wait()
        through(s, acc, qz, wt, z)
    loads[5].wait()
    loads[6].wait()

    def norm(r):
        back, gain, shift = norm_back(
            x[r, :].astype(f32), acc[r, : s.width], vec[0:1, : s.width]
        )
        gin[r, :] = to_low(gres[r, : s.width] + back)
        buf[0:1, : s.width] += gain
        buf[1:2, : s.width] += shift

    by_rows(s.half, LANES, norm)
    seq_in.start()

    def exchange(i, to):
        return pltpu.make_async_remote_copy(
            buf, got.at[i], gs.at[i], gr.at[i], device_id=to, device_id_type=MESH
        )

    def join(one, two):
        row = lax.broadcasted_iota(jnp.int32, one.shape, 0)
        return jnp.where(row == 12, jnp.maximum(one, two), one + two)

    row = lax.broadcasted_iota(jnp.int32, buf.shape, 0)
    buf[...] = jnp.where(row == 12, tops[0:1, :], buf[...])
    partners = (net.sib, net.x_to, net.y_to)

    def merge(i):
        exchange(i, partners[i]).wait()
        buf[...] = join(buf[...], got[i])

    exchange(0, partners[0]).start()
    A.turn(0)
    A.turn(1)
    merge(0)
    exchange(1, partners[1]).start()
    B.collect(held=stage)
    merge(1)
    exchange(2, partners[2]).start()
    A.land(0)
    A.send(0)
    merge(2)

    def around(z):
        return pltpu.make_async_remote_copy(
            buf, got.at[3 + net.z], gs.at[3 + z], gr.at[3 + net.z], device_id=(net.d, z), device_id_type=MESH
        )

    for z in range(4):

        @pl.when(z != net.z)
        def _():
            around(z).start()

        @pl.when(z == net.z)
        def _():
            pltpu.make_async_copy(buf, got.at[3 + z], gr.at[3 + z]).start()

    A.land(1)
    A.send(1)
    B.finish()
    for z in range(4):
        pltpu.make_async_copy(buf, got.at[3 + z], gr.at[3 + z]).wait()

        @pl.when(z != net.z)
        def _():
            around(z).wait_send()

    small_o[...] = join(join(got[3], got[4]), join(got[5], got[6]))
    A.collect()
    A.drain()
    A.finish()
    seq_in.wait()
    seq_in.drain()


def through(s, acc, qz, wt, z):
    def part(start, size):
        value = nt(qz[z], wt[z % 2, pl.ds(start, size), :])
        if z:
            value = value + acc[:, pl.ds(start, size)]
        acc[:, pl.ds(start, size)] = value

    by_columns(s.width, part)


def middle_call(s, shape, wa, wb, wc, cot, res, two, slope, hid, out, vec):
    dma = pltpu.SemaphoreType.DMA
    rows, full = s.half, s.ctx * s.cols
    anywhere = pl.BlockSpec(memory_space=pl.ANY)
    local = pl.BlockSpec(memory_space=pltpu.VMEM)
    low = lambda *dims: jax.ShapeDtypeStruct(dims, bf16)
    high = lambda *dims: jax.ShapeDtypeStruct(dims, f32)
    size = s.cols - s.out_tile
    return pl.pallas_call(
        partial(middle_kernel, s),
        out_shape=[
            low(2, s.rows, s.cols), low(2, s.width, s.cols), high(rows, s.wide),
            low(rows, s.wide), low(4, rows, size), high(16, s.wide), low(*shape),
        ],
        in_specs=[anywhere] * 9 + [local],
        out_specs=[anywhere] * 5 + [local, anywhere],
        scratch_shapes=[
            pltpu.VMEM((rows, s.width), bf16),
            pltpu.VMEM((rows, s.wide), f32),
            pltpu.VMEM((rows, s.width), bf16),
            pltpu.VMEM((rows, full), bf16),
            pltpu.VMEM((rows, full), bf16),
            pltpu.VMEM((s.width, rows), bf16),
            pltpu.VMEM((s.width, rows), bf16),
            pltpu.VMEM((2, s.width, s.cols), bf16),
            pltpu.VMEM((rows, s.wide), f32),
            pltpu.VMEM((rows, s.wide), bf16),
            pltpu.VMEM((4, rows, size), bf16),
        ]
        + scatter_scratch(s, 1)[:-2]
        + [pltpu.VMEM((2, s.width, s.cols), bf16)]
        + scatter_sems() * 2
        + [dma((2,)), dma((2,)), dma((5,)), dma((2,)), dma((4,)), dma((2,)), pltpu.SemaphoreType.REGULAR((2,))],
        compiler_params=pltpu.CompilerParams(
            collective_id=2, has_side_effects=True, vmem_limit_bytes=63 * 2**20
        ),
        name="middle",
    )(wa, wb, wc, cot, res, two, slope, hid, out, vec)


def last_call(s, shape, wa, oz, dq, d_own, normed, att, x, gres, up_sums, vec, sums, tops):
    dma = pltpu.SemaphoreType.DMA
    rows = s.half
    anywhere = pl.BlockSpec(memory_space=pl.ANY)
    local = pl.BlockSpec(memory_space=pltpu.VMEM)
    low = lambda *dims: jax.ShapeDtypeStruct(dims, bf16)
    high = lambda *dims: jax.ShapeDtypeStruct(dims, f32)
    size = s.cols - s.out_tile
    return pl.pallas_call(
        partial(last_kernel, s),
        out_shape=[
            high(s.rows // 2, s.cols), high(s.rows // 2, s.cols), low(*shape), high(16, s.wide),
        ],
        in_specs=[anywhere] * 9 + [local] * 3,
        out_specs=[anywhere, anywhere, anywhere, local],
        scratch_shapes=[
            pltpu.VMEM((2, rows, s.wide), bf16),
            pltpu.VMEM((rows, s.wide), bf16),
            pltpu.VMEM((rows, 3 * s.wide), f32),
            pltpu.VMEM((4, rows, s.qkv_pad), bf16),
            pltpu.VMEM((4, rows, size), bf16),
            pltpu.VMEM((s.width, rows), bf16),
            pltpu.VMEM((s.wide, rows), bf16),
            pltpu.VMEM((rows, s.width), bf16),
            pltpu.VMEM((rows, s.wide), bf16),
            pltpu.VMEM((rows, s.width), bf16),
            pltpu.VMEM((rows, s.wide), f32),
            pltpu.VMEM((2, s.width, s.qkv_pad), bf16),
            pltpu.VMEM((rows, s.wide), f32),
            pltpu.VMEM((rows, s.width), bf16),
            pltpu.VMEM((16, s.wide), f32),
            pltpu.VMEM((7, 16, s.wide), f32),
        ]
        + scatter_scratch(s, 1)
        + [pltpu.VMEM((4, s.rows, s.cols), bf16)] * 2
        + scatter_sems()
        + [dma((2,)), dma((2,)), dma((7,)), dma((2,)), dma((7,)), dma((7,))]
        + scatter_sems(),
        compiler_params=pltpu.CompilerParams(
            collective_id=3, has_side_effects=True, vmem_limit_bytes=63 * 2**20
        ),
        name="last",
    )(wa, oz, dq, d_own, normed, att, x, gres, up_sums, vec, sums, tops)


def slot_info(moves, segment_ids, padding, stretch_order):
    core, place, local_seqs = moves.core, moves.z, segment_ids.shape[0]
    length = segment_ids.shape[1]
    half = length // 2
    info = jnp.stack([segment_ids, padding], axis=0)
    info_there = moves.swap_core(info)
    info = jnp.where(place // local_seqs == core, info, info_there)
    info = lax.dynamic_index_in_dim(info, place % local_seqs, 1, False)
    stretches = stretch_order.shape[0]
    stretch_len = length // stretches
    info = jnp.take(info.reshape(2, stretches, stretch_len), stretch_order, axis=1)
    positions = stretch_order[:, None] * stretch_len + jnp.arange(stretch_len, dtype=jnp.int32)
    code = (info[0] * (2 * length) + positions).reshape(2, half)
    reach = (info[1] * (length - 1)).reshape(2, half)
    code_own = lax.dynamic_index_in_dim(code, core, 0, False)
    code_sib = lax.dynamic_index_in_dim(code, 1 - core, 0, False)
    reach_own = lax.dynamic_index_in_dim(reach, core, 0, False)
    reach_sib = lax.dynamic_index_in_dim(reach, 1 - core, 0, False)
    kinfo = jnp.stack(
        [jnp.concatenate([code_own, code_sib]), jnp.concatenate([reach_own, reach_sib])], axis=1
    )
    return kinfo, code_own[None]


def pack_blocks(moves, s, w_qkv, w_out, w_up, w_down, vectors, bias_up):
    rows = w_qkv.shape[0]

    def filled(values):
        return jnp.pad(values, ((0, 0), (0, s.cols - values.shape[1])))

    turned = w_down.T
    parts = jnp.concatenate(
        [
            filled(jnp.concatenate([w_qkv, w_out], axis=1)),
            filled(w_up),
            filled(jnp.concatenate([turned[:rows], turned[rows:]], axis=1)),
        ],
        axis=0,
    )
    there = moves.swap_core(parts)
    even = jnp.where(moves.core == 0, parts, there)
    odd = jnp.where(moves.core == 0, there, parts)
    own_a = jnp.concatenate([even[:rows], odd[:rows]], axis=0)
    own_b = jnp.concatenate([even[rows : 2 * rows], odd[rows : 2 * rows]], axis=0)
    ff = turned.shape[1]
    own_c = filled(
        jnp.concatenate(
            [
                jnp.concatenate([v[2 * rows :, :ff], v[2 * rows :, ff : 2 * ff]], axis=0)
                for v in (even, odd)
            ],
            axis=1,
        )
    )
    small = jnp.concatenate([jnp.pad(vectors, ((0, 0), (0, s.cols - vectors.shape[1]))), filled(bias_up[None])], axis=0)
    small = jnp.pad(small, ((0, 16 - small.shape[0]), (0, 0)))
    return own_a, own_b, own_c, small


def fast_shards(
    dp,
    ctx,
    inputs,
    cotangent,
    w_qkv,
    w_out,
    w_up,
    w_down,
    vectors,
    bias_up,
    segment_ids,
    padding,
    stretch_order,
):
    local_seqs, query_len, width = inputs.shape
    heads = width // HD
    s = Sizes(width, w_up.shape[1] * ctx, ctx, dp, segment_ids.shape[1])
    moves = Moves(dp, ctx, local_seqs)
    core, place = moves.core, moves.z
    wide = s.wide
    kinfo, qinfo = slot_info(moves, segment_ids, padding, stretch_order)
    own_a, own_b, own_c, small = pack_blocks(moves, s, w_qkv, w_out, w_up, w_down, vectors, bias_up)
    (wa, wb, wc, x, cot, vec, normed, queries, kv, attended, residual, two, slope, hidden, lse, tops, out) = forward_call(
        s, own_a, own_b, own_c, small, inputs, cotangent, kinfo, qinfo
    )
    down_sums, up_own, gres, gatt, oz, sums, output = middle_call(
        s, inputs.shape, wa, wb, wc, cot, residual, two, slope, hidden, out, vec
    )
    dq, d_own, up_sums, down_block = attention_call(
        s, kinfo, qinfo, lse, queries, kv, gatt, up_own, down_sums
    )
    block_top = jnp.max(tops, axis=2).reshape(1, -1)[:, :heads]
    block_top = jnp.pad(block_top, ((0, 7), (0, wide - heads)))
    qkv_block, up_block, grad_input, small_sums = last_call(
        s, inputs.shape, wa, oz, dq, d_own, normed, attended, x, gres, up_sums, vec, sums, block_top
    )
    cols_q, cols_d, cols_f = w_qkv.shape[1], w_out.shape[1], w_up.shape[1]
    ff = w_down.shape[0]

    grad_qkv, grad_out = qkv_block[:, :cols_q], qkv_block[:, cols_q : cols_q + cols_d]
    grad_up = up_block[:, :cols_f]
    grad_down = jnp.where(core == 0, down_block[:, :ff], down_block[:, ff : 2 * ff]).T
    grad_vectors = lax.dynamic_slice_in_dim(small_sums[:8, :width], place * cols_d, cols_d, 1)
    grad_bias = lax.dynamic_index_in_dim(small_sums[8:12], place, 0, False)[:cols_f]
    global_top = small_sums[12, :heads]

    factor = clip_limit / jnp.maximum(global_top, clip_limit)
    per_column = jnp.repeat(jnp.sqrt(factor), HD)
    column_scale = jnp.concatenate([per_column, per_column, jnp.ones((width,), f32)])
    local_scale = lax.dynamic_slice_in_dim(column_scale, place * cols_q, cols_q)
    clipped_qkv = to_low(w_qkv.astype(f32) * local_scale[None, :])
    bias_scale = lax.dynamic_slice_in_dim(per_column, place * cols_d, cols_d)
    clipped_bias = to_low(vectors[2].astype(f32) * bias_scale)
    return (
        output,
        grad_input.astype(f32),
        grad_qkv,
        grad_out,
        grad_up,
        grad_down,
        grad_vectors,
        grad_bias,
        clipped_qkv,
        clipped_bias,
        global_top,
    )


def shards(
    dp,
    ctx,
    inputs,
    cotangent,
    w_qkv,
    w_out,
    w_up,
    w_down,
    vectors,
    bias_up,
    segment_ids,
    padding,
    stretch_order,
):
    local_seqs, query_len, width = inputs.shape
    length = segment_ids.shape[1]
    half = length // 2
    heads = width // HD
    wide = (width + LANES - 1) // LANES * LANES
    rows_d = w_qkv.shape[0]
    cols_d = w_out.shape[1]
    cols_f = w_up.shape[1]
    ratio = w_down.shape[0] // rows_d
    hidden_width = cols_f * ctx
    moves = Moves(dp, ctx, local_seqs)
    core, place = moves.core, moves.z

    extra = jnp.concatenate([vectors.reshape(-1, cols_f), bias_up[None]], axis=0)
    first = jnp.concatenate([jnp.concatenate([w_qkv, w_out], axis=1), extra], axis=0)
    first = moves.gather_ctx(first)
    x_flat = moves.to_sequences(inputs).astype(f32)
    down_packed = jnp.swapaxes(w_down.reshape(ratio, rows_d, cols_d), 0, 1).reshape(rows_d, -1)
    second = moves.gather_ctx(jnp.concatenate([w_up, down_packed], axis=0))
    cot = moves.to_sequences(cotangent)

    def columns(blocks):
        return jnp.swapaxes(blocks, 0, 1).reshape(blocks.shape[1], -1)

    cols_q = w_qkv.shape[1]
    part_qkv = columns(first[:, :rows_d, :cols_q])
    part_out = columns(first[:, :rows_d, cols_q:])
    small = first[:, rows_d:]
    vec_rows = columns(small[:, :-1].reshape(ctx, 8, cols_d)).astype(f32)
    bias_row = small[:, -1].reshape(-1).astype(f32)
    part_up = columns(second[:, :rows_d])
    part_down = second[:, rows_d:].reshape(ctx, rows_d, ratio, cols_d)
    part_down = jnp.transpose(part_down, (2, 1, 0, 3)).reshape(ratio * rows_d, width)

    wide_qkv = moves.gather_dp(part_qkv)
    wide_out = moves.gather_dp(part_out)
    wide_up = moves.gather_dp(part_up)
    wide_down = moves.gather_dp(part_down)

    info = jnp.stack([segment_ids, padding], axis=0)
    info_there = moves.swap_core(info)
    info = jnp.where(place // local_seqs == core, info, info_there)
    info = lax.dynamic_index_in_dim(info, place % local_seqs, 1, False)
    stretches = stretch_order.shape[0]
    stretch_len = length // stretches
    info = jnp.take(info.reshape(2, stretches, stretch_len), stretch_order, axis=1)
    positions = stretch_order[:, None] * stretch_len + jnp.arange(stretch_len, dtype=jnp.int32)
    code = (info[0] * (2 * length) + positions).reshape(2, half)
    reach = (info[1] * (length - 1)).reshape(2, half)
    code_own = lax.dynamic_index_in_dim(code, core, 0, False)
    code_sib = lax.dynamic_index_in_dim(code, 1 - core, 0, False)
    reach_own = lax.dynamic_index_in_dim(reach, core, 0, False)
    reach_sib = lax.dynamic_index_in_dim(reach, 1 - core, 0, False)
    kinfo = jnp.stack(
        [jnp.concatenate([code_own, code_sib]), jnp.concatenate([reach_own, reach_sib])], axis=1
    )
    qinfo = code_own[None]

    normed = to_low(layer_norm(x_flat, vec_rows[0], vec_rows[1]))
    projected = product(normed, wide_qkv)

    def padded(values):
        return jnp.pad(to_low(values), ((0, 0), (0, wide - width)))

    queries = padded(projected[:, :width] + vec_rows[2])
    own = jnp.stack(
        [
            padded(projected[:, width : 2 * width]),
            padded(projected[:, 2 * width :] + vec_rows[3]),
        ]
    )
    sib = moves.swap_core(own)
    attended, lse, tops = attend_forward(heads, kinfo, qinfo, queries, own, sib)
    attended = attended[:, :width]
    block_top = jnp.max(tops, axis=2).reshape(-1)[:heads]
    global_top = lax.pmax(block_top, AXES)
    residual = x_flat + product(attended, wide_out) + vec_rows[4]
    normed_two = to_low(layer_norm(residual, vec_rows[5], vec_rows[6]))
    up_pre = product(normed_two, wide_up) + bias_row
    hidden = to_low(jax.nn.gelu(up_pre, approximate=True))
    output = to_low(residual + product(hidden, wide_down) + vec_rows[7])
    output = moves.from_sequences(output)

    grad_output = cot.astype(f32)
    grad_bias_two = column_sum(cot)
    sum_down = moves.weight_terms(hidden, cot)
    sum_down = moves.scatter_dp(sum_down)
    grad_hidden = contract_cols(cot, wide_down)
    unused, gelu_back = jax.vjp(partial(jax.nn.gelu, approximate=True), up_pre)
    grad_pre = to_low(gelu_back(grad_hidden)[0])
    grad_bias_up = column_sum(grad_pre)
    sum_up = moves.weight_terms(normed_two, grad_pre)
    sum_up = moves.scatter_dp(sum_up)
    unused, norm_back_two = jax.vjp(layer_norm, residual, vec_rows[5], vec_rows[6])
    back_two = norm_back_two(contract_cols(grad_pre, wide_up))
    grad_residual = grad_output + back_two[0]
    grad_branch = to_low(grad_residual)
    sum_out = moves.weight_terms(attended, grad_branch)
    sum_out = moves.scatter_dp(sum_out)
    grad_attended = padded(contract_cols(grad_branch, wide_out))
    dq, d_own, d_sib = attend_backward(
        heads, kinfo, qinfo, queries, jnp.concatenate([own, sib], axis=1), grad_attended, lse
    )
    d_came = moves.swap_core(d_sib)
    d_own = to_low(d_own.astype(f32) + d_came.astype(f32))
    grad_proj = jnp.concatenate([dq[:, :width], d_own[0, :, :width], d_own[1, :, :width]], axis=1)
    sum_qkv = moves.weight_terms(normed, grad_proj)
    sum_qkv = moves.scatter_dp(sum_qkv)
    unused, norm_back_one = jax.vjp(layer_norm, x_flat, vec_rows[0], vec_rows[1])
    back_one = norm_back_one(contract_cols(grad_proj, wide_qkv))
    grad_input = to_low(grad_residual + back_one[0])
    grad_input = moves.from_sequences(grad_input).astype(f32)
    grad_vectors = jnp.stack(
        [
            back_one[1],
            back_one[2],
            column_sum(dq[:, :width]),
            column_sum(d_own[1, :, :width]),
            column_sum(grad_branch),
            back_two[1],
            back_two[2],
            grad_bias_two,
        ]
    )

    def by_place(values):
        return jnp.swapaxes(values.reshape(values.shape[0], ctx, -1), 0, 1)

    blocks_down = sum_down.reshape(ratio, rows_d, ctx, cols_d)
    blocks_down = jnp.transpose(blocks_down, (2, 1, 0, 3)).reshape(ctx, rows_d, -1)
    later = jnp.concatenate([by_place(sum_up), blocks_down, by_place(sum_out)], axis=2)
    later = moves.scatter_ctx(later)
    grad_up = later[:, :cols_f]
    grad_down = later[:, cols_f : 2 * cols_f].reshape(rows_d, ratio, cols_d)
    grad_down = jnp.swapaxes(grad_down, 0, 1).reshape(ratio * rows_d, cols_d)
    grad_out = later[:, 2 * cols_f :]
    grad_qkv = moves.scatter_ctx(by_place(sum_qkv))

    tiny = jnp.concatenate([grad_vectors, grad_bias_up.reshape(-1, width)], axis=0)
    tiny = lax.psum(tiny, AXES)
    grad_vectors = lax.dynamic_slice_in_dim(tiny[:8], place * cols_d, cols_d, 1)
    grad_bias = lax.dynamic_slice_in_dim(tiny[8:].reshape(-1), place * cols_f, cols_f)

    factor = clip_limit / jnp.maximum(global_top, clip_limit)
    per_column = jnp.repeat(jnp.sqrt(factor), HD)
    column_scale = jnp.concatenate([per_column, per_column, jnp.ones((width,), f32)])
    local_scale = lax.dynamic_slice_in_dim(column_scale, place * cols_q, cols_q)
    clipped_qkv = to_low(w_qkv.astype(f32) * local_scale[None, :])
    bias_scale = lax.dynamic_slice_in_dim(per_column, place * cols_d, cols_d)
    clipped_bias = to_low(vectors[2].astype(f32) * bias_scale)
    return (
        output,
        grad_input,
        grad_qkv,
        grad_out,
        grad_up,
        grad_down,
        grad_vectors,
        grad_bias,
        clipped_qkv,
        clipped_bias,
        global_top,
    )


def solution(mesh):
    dp, ctx = mesh.shape["dp"], mesh.shape["ctx"]
    body = fast_shards if (dp, ctx) == (8, 4) else shards
    return jax.shard_map(
        partial(body, dp, ctx),
        mesh=mesh,
        in_specs=(
            P("dp", "ctx", None),
            P("dp", "ctx", None),
            P("dp", "ctx"),
            P("dp", "ctx"),
            P("dp", "ctx"),
            P("dp", "ctx"),
            P(None, "ctx"),
            P("ctx"),
            P("dp", None),
            P("dp", None),
            P(),
        ),
        out_specs=(
            P("dp", "ctx", None),
            P("dp", "ctx", None),
            P("dp", "ctx"),
            P("dp", "ctx"),
            P("dp", "ctx"),
            P("dp", "ctx"),
            P(None, "ctx"),
            P("ctx"),
            P("dp", "ctx"),
            P("ctx"),
            P(),
        ),
        check_vma=False,
    )
```
